32 devices in a mesh: group: 8 (over z, x), expert: 4 (over y, core).
Axes of the slice: x: 2, y: 2, z: 4, core: 2. Of those that a mesh axis runs over, the one named last changes fastest.
Arguments:
- tokens: bfloat16 [16384, 768], P(('group', 'expert')), may hold values from -6 to 6
- gain_attn: float32 [768], replicated, may hold values from 0.5 to 1.5
- w_qkv: bfloat16 [768, 2304], replicated, may hold values from -0.21875 to 0.21875
- w_out: bfloat16 [768, 768], replicated, may hold values from -2.5 to 2.5
- gain_ffn: float32 [768], replicated, may hold values from 0.5 to 1.5
- w_router: bfloat16 [768, 16], replicated, may hold values from -0.15625 to 0.15625
- expert_gate: bfloat16 [16, 768, 2048], P('expert'), may hold values from -0.21875 to 0.21875
- expert_up: bfloat16 [16, 768, 2048], P('expert'), may hold values from -0.21875 to 0.21875
- expert_down: bfloat16 [16, 2048, 768], P('expert'), may hold values from -0.125 to 0.125
- dense_gate: bfloat16 [768, 2048], replicated, may hold values from -0.21875 to 0.21875
- dense_up: bfloat16 [768, 2048], replicated, may hold values from -0.21875 to 0.21875
- dense_down: bfloat16 [2048, 768], replicated, may hold values from -0.125 to 0.125
- expert_ids: int32 [16384, 2], P(('group', 'expert')), may hold values from 0 to 15, all different within a row
- segments: int32 [16384], P(('group', 'expert')), may hold values from 0 to 3, as said below
- cotangent: bfloat16 [16384, 768], P(('group', 'expert')), may hold values from -6 to 6
Outputs:
- mixed_out: bfloat16 [16384, 768], P(('group', 'expert'))
- grad_tokens: float32 [16384, 768], P(('group', 'expert'))
- grad_gain_attn: float32 [768], replicated
- grad_qkv: float32 [768, 2304], P('group', 'expert')
- grad_out_proj: float32 [768, 768], P('group', 'expert')
- grad_gain_ffn: float32 [768], replicated
- grad_router: float32 [768, 16], replicated
- grad_expert_gate: float32 [16, 768, 2048], P('expert', None, 'group')
- grad_expert_up: float32 [16, 768, 2048], P('expert', None, 'group')
- grad_expert_down: float32 [16, 2048, 768], P('expert', 'group')
- grad_dense_gate: float32 [768, 2048], P('group', 'expert')
- grad_dense_up: float32 [768, 2048], P('group', 'expert')
- grad_dense_down: float32 [2048, 768], P('group', 'expert')
The draws below stay inside these ranges and needn't reach their ends.
Inputs may be any that keep to these rules, and one draw needn't show every extreme that they name: `segments`: within each sequence of 2048 tokens the document numbers start at 0, never fall and rise by one at each of three boundaries, one in each of the sequence's first three quarters. `expert_ids`: the two experts of a token differ.
All inputs are finite; a program needn't handle non-finite values.
Results may differ from the reference program's by a relative error of at most 0.017.
Values may be sent and summed in bfloat16 or wider, within the bound.
A program may use at most 320 MiB of HBM per device.

```python
import jax
import jax.numpy as jnp
from jax import lax

D = 768
HEADS = 12
HEAD = 64
FF = 2048
EXPERTS = 16
WINDOW = 1024
TOK_DEV = 512
SEQ = 2048
TOKENS = 16384
CAP = 80


def draw_segments(key, part):
    key = jax.random.fold_in(key, 11)
    count_seq = TOKENS // SEQ
    quarter = SEQ // 4
    offsets = jax.random.randint(key, (count_seq, 3), 1, quarter, dtype=jnp.int32)
    bounds = offsets + jnp.arange(3, dtype=jnp.int32)[None, :] * quarter
    places = jnp.arange(SEQ, dtype=jnp.int32)
    numbers = jnp.sum((places[None, :, None] >= bounds[:, None, :]).astype(jnp.int32), axis=2)
    return numbers.reshape(TOKENS).astype(jnp.int32)


def block_scale(rng, dims, split, low, top_value):
    loudness = 1.0
    for dim, parts in split:
        steps = jax.random.uniform(jax.random.fold_in(jax.random.fold_in(rng, 6), dim), (parts,), jnp.float32, low / len(split), top_value / len(split))
        loudness = loudness * jnp.repeat(jnp.exp(steps), dims[dim] // parts).reshape((-1,) + (1,) * (len(dims) - 1 - dim))
    return loudness


def picks_of(own_key, rows, count, top, lift):
    order = jax.random.permutation(jax.random.fold_in(own_key, 1), count)
    boost = order
    for power in range(3):
        boost = boost * boost // count
    boost = boost * lift // count
    tickets = jax.random.randint(jax.random.fold_in(own_key, 2), (rows, count), 0, 4096) + boost
    holders = jax.random.permutation(jax.random.fold_in(own_key, 3), rows)[jnp.arange(count) % rows]
    tickets = jnp.where(jnp.arange(rows)[:, None] == holders[None, :], 1 << 14, tickets)
    priority = tickets * count + jnp.arange(count)
    return lax.top_k(priority.astype(jnp.int32), top)[1].astype(jnp.int32)


def scatter_about(rng, extent, scale, limit, pieces=(), kind=jnp.bfloat16):
    result = scale * jax.random.normal(rng, extent, jnp.float32)
    if pieces:
        result = result * block_scale(rng, extent, pieces, -0.22, 0.18)
    return jnp.clip(result, -limit, limit).astype(kind)


def setup_inputs(seed: int = 0) -> dict:
    arg_keys = jax.random.split(jax.random.key(seed), 16)
    return {
        "tokens": scatter_about(arg_keys[0], (TOKENS, D), 1.0, 6.0, ((0, 32),)),
        "gain_attn": jnp.clip(1.0 + 0.1 * jax.random.normal(arg_keys[1], (D,), jnp.float32), 0.5, 1.5),
        "w_qkv": scatter_about(arg_keys[2], (D, 3 * D), D ** -0.5, 0.21875),
        "w_out": scatter_about(arg_keys[3], (D, D), (max(D // 128, 1)) ** -0.5, 2.5),
        "gain_ffn": jnp.clip(1.0 + 0.1 * jax.random.normal(arg_keys[4], (D,), jnp.float32), 0.5, 1.5),
        "w_router": scatter_about(arg_keys[5], (D, EXPERTS), (2 * D) ** -0.5, 0.15625),
        "expert_gate": scatter_about(arg_keys[6], (EXPERTS, D, FF), D ** -0.5, 0.21875, ((0, 4),)),
        "expert_up": scatter_about(arg_keys[7], (EXPERTS, D, FF), D ** -0.5, 0.21875, ((0, 4),)),
        "expert_down": scatter_about(arg_keys[8], (EXPERTS, FF, D), FF ** -0.5, 0.125, ((0, 4),)),
        "dense_gate": scatter_about(arg_keys[9], (D, FF), D ** -0.5, 0.21875),
        "dense_up": scatter_about(arg_keys[10], (D, FF), D ** -0.5, 0.21875),
        "dense_down": scatter_about(arg_keys[11], (FF, D), FF ** -0.5, 0.125),
        "expert_ids": picks_of(arg_keys[12], TOKENS, EXPERTS, 2, 1024),
        "segments": draw_segments(jax.random.fold_in(arg_keys[15], 71), 0),
        "cotangent": scatter_about(arg_keys[14], (TOKENS, D), 1.0, 6.0, ((0, 32),)),
    }


highest = lax.Precision.HIGHEST
epsilon = 1e-06

@jax.custom_vjp
def low(v):
    return lax.optimization_barrier(v.astype(jnp.bfloat16)).astype(jnp.float32)

@jax.custom_vjp
def low_back(v):
    return v

def low_keep(v):
    return (low(v), None)

def low_pass(kept, grad):
    return (grad,)

def back_keep(v):
    return (v, None)

def back_low(kept, grad):
    return (low(grad),)
low.defvjp(low_keep, low_pass)
low_back.defvjp(back_keep, back_low)

def matmul(left_side, right_side):
    return jnp.dot(left_side, right_side, precision=highest, preferred_element_type=jnp.float32)

def rmsnorm(values, gain_vec):
    return values * lax.rsqrt(lax.optimization_barrier(jnp.mean(values * values, axis=-1, keepdims=True)) + epsilon) * gain_vec

def rotate(values, places):
    half_size = values.shape[-1] // 2
    powers = jnp.arange(half_size, dtype=jnp.float32) / half_size
    angles = places[:, None] * (10000.0 ** (-powers))[None, :]
    cosine = jnp.cos(angles)[:, None, :]
    sine_part = jnp.sin(angles)[:, None, :]
    first_half = values[..., :half_size]
    second_half = values[..., half_size:]
    return jnp.concatenate([first_half * cosine - second_half * sine_part, second_half * cosine + first_half * sine_part], axis=-1)

def slot_table(expert_ids):
    pair_ids = expert_ids.reshape(TOKENS // TOK_DEV, TOK_DEV * 2)
    labels = jnp.arange(EXPERTS, dtype=jnp.int32)
    onehot = (pair_ids[:, :, None] == labels[None, None, :]).astype(jnp.int32)
    earlier = jnp.cumsum(onehot, axis=1) - onehot
    return lax.optimization_barrier(jnp.sum(earlier * onehot, axis=2)).reshape(TOKENS, 2).astype(jnp.int32)

def attend(queries, keys_in, values_in, segment_row):
    reach_count = (WINDOW - 1) // TOK_DEV + 1
    margin = reach_count * TOK_DEV
    zeros_pad = jnp.zeros((margin, HEADS, HEAD), queries.dtype)
    keys_pad = jnp.concatenate([zeros_pad, keys_in], axis=0)
    values_pad = jnp.concatenate([zeros_pad, values_in], axis=0)
    segment_pad = jnp.concatenate([jnp.full((margin,), -1, jnp.int32), segment_row.astype(jnp.int32)])

    def one_block(number):
        first_row = number * TOK_DEV
        query_block = lax.dynamic_slice_in_dim(queries, first_row, TOK_DEV, 0)
        key_block = lax.dynamic_slice_in_dim(keys_pad, first_row, margin + TOK_DEV, 0)
        value_block = lax.dynamic_slice_in_dim(values_pad, first_row, margin + TOK_DEV, 0)
        query_seg = lax.dynamic_slice_in_dim(segment_row.astype(jnp.int32), first_row, TOK_DEV, 0)
        key_seg = lax.dynamic_slice_in_dim(segment_pad, first_row, margin + TOK_DEV, 0)
        query_pos = first_row + jnp.arange(TOK_DEV, dtype=jnp.int32)
        key_pos = first_row - margin + jnp.arange(margin + TOK_DEV, dtype=jnp.int32)
        offset = query_pos[:, None] - key_pos[None, :]
        allowed = (offset >= 0) & (offset < WINDOW) & (key_pos[None, :] >= 0) & (query_seg[:, None] == key_seg[None, :])
        scores = low_back(jnp.einsum('qhd,khd->hqk', query_block, key_block, precision=highest))
        scores = jnp.where(allowed[None], scores, -1e+30)
        weights = low(jax.nn.softmax(scores, axis=-1))
        return jnp.einsum('hqk,khd->qhd', weights, value_block, precision=highest)
    blocks_out = lax.map(jax.checkpoint(one_block), jnp.arange(SEQ // TOK_DEV, dtype=jnp.int32))
    return blocks_out.reshape(SEQ, HEADS, HEAD)

def swiglu_rows(rows_in, gate_w, up_w, down_w):
    gate_pre = low_back(matmul(rows_in, gate_w))
    up_pre = low_back(matmul(rows_in, up_w))
    activated = low(jax.nn.silu(gate_pre) * up_pre)
    return low_back(matmul(activated, down_w))

def expert_token_rows(members):
    return low(swiglu_rows(members[0], members[1], members[2], members[3]))

def reference(tokens, gain_attn, w_qkv, w_out, gain_ffn, w_router, expert_gate, expert_up, expert_down, dense_gate, dense_up, dense_down, expert_ids, segments, cotangent):
    slot_index = slot_table(expert_ids)
    kept_mask = slot_index < CAP
    target = jnp.where(kept_mask, expert_ids * CAP + slot_index, EXPERTS * CAP).astype(jnp.int32)
    owner_block = (jnp.arange(TOKENS, dtype=jnp.int32) // TOK_DEV).astype(jnp.int32)
    count_seq = TOKENS // SEQ
    block_count = TOKENS // TOK_DEV
    model_width = HEADS * HEAD

    def layer_forward(layer_inputs, first_norm_gain, query_key_value_weight, output_weight, second_norm_gain, router_weight, expert_gate_weight, expert_up_weight, expert_down_weight, dense_gate_weight, dense_up_weight, dense_down_weight):
        normed = low(rmsnorm(layer_inputs, first_norm_gain))
        packed = low_back(matmul(normed, query_key_value_weight))
        places = (jnp.arange(TOKENS, dtype=jnp.int32) % SEQ).astype(layer_inputs.dtype)
        shaped = packed.reshape(TOKENS, 3, HEADS, HEAD)
        queries = low(rotate(shaped[:, 0], places) * HEAD ** (-0.5))
        keys_all = low(rotate(shaped[:, 1], places))
        values_all = low(shaped[:, 2])
        attended = lax.map(lambda members: attend(members[0], members[1], members[2], members[3]), (queries.reshape(count_seq, SEQ, HEADS, HEAD), keys_all.reshape(count_seq, SEQ, HEADS, HEAD), values_all.reshape(count_seq, SEQ, HEADS, HEAD), segments.reshape(count_seq, SEQ)))
        attended = low(low_back(attended.reshape(TOKENS, model_width)))
        hidden = layer_inputs + low_back(matmul(attended, output_weight))
        normed_ffn = low(rmsnorm(hidden, second_norm_gain))
        logits = low_back(matmul(normed_ffn, router_weight))
        route_probs = jax.nn.softmax(logits, axis=-1)
        picked = jnp.take_along_axis(route_probs, expert_ids, axis=1)
        gate_share = picked / lax.optimization_barrier(jnp.sum(picked, axis=1, keepdims=True))
        buffer = jnp.zeros((block_count, EXPERTS * CAP, model_width), layer_inputs.dtype)
        for column in range(2):
            buffer = buffer.at[owner_block, target[:, column]].add(normed_ffn, mode='drop')
        dispatched = low_back(buffer).reshape(block_count, EXPERTS, CAP, model_width)
        expert_grouped = jnp.transpose(dispatched, (1, 0, 2, 3)).reshape(EXPERTS, block_count * CAP, model_width)
        layer_result = lax.map(jax.checkpoint(expert_token_rows), (expert_grouped, expert_gate_weight, expert_up_weight, expert_down_weight))
        returned = jnp.transpose(layer_result.reshape(EXPERTS, block_count, CAP, model_width), (1, 0, 2, 3))
        returned = returned.reshape(block_count, EXPERTS * CAP, model_width)
        fetched = returned[owner_block[:, None], jnp.minimum(target, EXPERTS * CAP - 1)]
        mixture = lax.optimization_barrier(jnp.sum(gate_share[:, :, None] * jnp.where(kept_mask[:, :, None], fetched, 0.0), axis=1))
        dense_out = swiglu_rows(normed_ffn, dense_gate_weight, dense_up_weight, dense_down_weight)
        return hidden + mixture + dense_out
    params = (tokens.astype(jnp.float32), gain_attn.astype(jnp.float32), w_qkv.astype(jnp.float32), w_out.astype(jnp.float32), gain_ffn.astype(jnp.float32), w_router.astype(jnp.float32), expert_gate.astype(jnp.float32), expert_up.astype(jnp.float32), expert_down.astype(jnp.float32), dense_gate.astype(jnp.float32), dense_up.astype(jnp.float32), dense_down.astype(jnp.float32))
    mixed_out, pullback = jax.vjp(layer_forward, *params)
    gradients = pullback(cotangent.astype(jnp.float32))
    return (mixed_out.astype(jnp.bfloat16), gradients[0], gradients[1], gradients[2], gradients[3], gradients[4], gradients[5], gradients[6], gradients[7], gradients[8], gradients[9], gradients[10], gradients[11])
```

```python
import jax
import jax.numpy as jnp
from jax import lax
from jax.sharding import PartitionSpec as P

HEADS = 12
HEAD = 64
EXPERTS = 16
WINDOW = 1024
CAP = 80
QUARTERS = 4

epsilon = 1e-06
F32 = jnp.float32
BF16 = jnp.bfloat16


def shifted(x, axis, by):
    count = lax.axis_size(axis)
    pairs = [(i, i + by) for i in range(count) if 0 <= i + by < count]
    return lax.ppermute(x, axis, pairs)


def swap(x, group_bits, expert_bits):
    groups, experts = lax.axis_size("group"), lax.axis_size("expert")
    pairs = [
        (g * experts + e, (g ^ group_bits) * experts + (e ^ expert_bits))
        for g in range(groups)
        for e in range(experts)
    ]
    return lax.ppermute(x, ("group", "expert"), pairs)


def pair_turn(x, by):
    groups = lax.axis_size("group")
    pairs = [(g, (g + 2 * by) % groups) for g in range(groups)]
    return lax.ppermute(x, "group", pairs)


def rmsnorm(values, gain_vec):
    return (
        values * lax.rsqrt(jnp.mean(values * values, axis=-1, keepdims=True) + epsilon) * gain_vec
    )


def rotate(values, places):
    half_size = values.shape[-1] // 2
    powers = jnp.arange(half_size, dtype=jnp.float32) / half_size
    angles = places[:, None] * (10000.0 ** (-powers))[None, :]
    cosine = jnp.cos(angles)[:, None, :]
    sine_part = jnp.sin(angles)[:, None, :]
    first_half = values[..., :half_size]
    second_half = values[..., half_size:]
    return jnp.concatenate(
        [
            first_half * cosine - second_half * sine_part,
            second_half * cosine + first_half * sine_part,
        ],
        axis=-1,
    )


def swiglu(gate_pre, up_pre):
    return jax.nn.silu(gate_pre) * up_pre


def route(logits, chosen):
    route_probs = jax.nn.softmax(logits, axis=-1)
    picked = jnp.sum(route_probs[:, None, :] * chosen, axis=2)
    return picked / jnp.sum(picked, axis=1, keepdims=True)


def dot32(spec, a, b):
    return jnp.einsum(spec, a, b, preferred_element_type=F32)


def pick(x, axis, index):
    return lax.dynamic_index_in_dim(x, index, axis, keepdims=False)


def scatter_sum(x):
    groups, experts = lax.axis_size("group"), lax.axis_size("expert")
    g, e = lax.axis_index("group"), lax.axis_index("expert")
    rows, cols = x.shape
    x = x.reshape(rows, experts, cols // experts)
    bit = 1
    while bit < experts:
        mine = (e // bit) % 2
        left = x.shape[1]
        x = x.reshape(rows, left // 2, 2, cols // experts)
        moved = swap(pick(x, 2, 1 - mine).astype(BF16), 0, bit)
        x = pick(x, 2, mine) + moved.astype(F32)
        bit *= 2
    x = x.reshape(groups, rows // groups, cols // experts)
    bit = 1
    while bit < groups:
        mine = (g // bit) % 2
        left = x.shape[0]
        x = x.reshape(left // 2, 2, rows // groups, cols // experts)
        moved = swap(pick(x, 1, 1 - mine).astype(BF16), bit, 0)
        x = pick(x, 1, mine) + moved.astype(F32)
        bit *= 2
    return x.reshape(rows // groups, cols // experts)


def local(
    tokens,
    gain_attn,
    w_qkv,
    w_out,
    gain_ffn,
    w_router,
    expert_gate,
    expert_up,
    expert_down,
    dense_gate,
    dense_up,
    dense_down,
    expert_ids,
    segments,
    cotangent,
):
    row_count, model_width = tokens.shape
    ff = dense_gate.shape[1]
    groups, experts = lax.axis_size("group"), lax.axis_size("expert")
    g, e = lax.axis_index("group"), lax.axis_index("expert")
    side, outer = g % 2, g // 2
    outers = groups // 2
    own_experts = EXPERTS // experts
    half = own_experts // 2
    peers = 2 * experts
    piece = half * CAP

    labels = jnp.arange(EXPERTS, dtype=jnp.int32)
    flat_ids = expert_ids.reshape(2 * row_count)
    onehot = (flat_ids[:, None] == labels[None, :]).astype(BF16)
    pair_no = jnp.arange(2 * row_count, dtype=jnp.int32)
    before = (pair_no[None, :] < pair_no[:, None]).astype(BF16)
    earlier = dot32("ab,be->ae", before, onehot)
    slot_index = jnp.sum(earlier * onehot.astype(F32), axis=1).astype(jnp.int32)
    slot_index = slot_index.reshape(row_count, 2)
    to_expert = expert_ids // own_experts
    to_side = (expert_ids % own_experts) // half
    relative = (to_side ^ side) * experts + (to_expert ^ e)
    target = jnp.where(
        slot_index < CAP, (relative * half + expert_ids % half) * CAP + slot_index, -1
    )
    slot_labels = jnp.arange(EXPERTS * CAP, dtype=jnp.int32)
    dispatch = (jnp.transpose(target)[:, :, None] == slot_labels[None, None, :]).astype(BF16)
    either = dispatch[0] + dispatch[1]

    def spread(rows):
        parts = rows.reshape(peers, piece, -1)
        return [
            parts[r] if r == 0 else swap(parts[r], r // experts, r % experts) for r in range(peers)
        ]

    def by_expert(parts):
        stacked = jnp.stack([part.reshape(half, CAP, -1) for part in parts], axis=1)
        return stacked.reshape(half, peers * CAP, -1)

    def give_back(rows):
        parts = jnp.transpose(rows.reshape(half, peers, CAP, -1), (1, 0, 2, 3))
        parts = parts.reshape(peers, piece, -1)
        return jnp.concatenate(
            [
                parts[r] if r == 0 else swap(parts[r], r // experts, r % experts)
                for r in range(peers)
            ],
            axis=0,
        )

    send_cot = dot32("rs,rd->sd", either, cotangent).astype(BF16)
    cot_slots = by_expert(spread(send_cot))
    cot_pieces = [cot_slots] + [pair_turn(cot_slots, k) for k in range(1, outers)]

    layer_inputs = tokens.astype(F32)
    cot_float = cotangent.astype(F32)
    normed_attn, attn_norm_pull = jax.vjp(rmsnorm, layer_inputs, gain_attn)
    normed_low = normed_attn.astype(BF16)
    packed = jnp.dot(normed_low, w_qkv, preferred_element_type=F32)
    first_row = e * row_count
    places = (first_row + jnp.arange(row_count, dtype=jnp.int32)).astype(F32)

    def embed(packed_in):
        shaped = packed_in.reshape(row_count, 3, HEADS, HEAD)
        return (
            rotate(shaped[:, 0], places) * HEAD ** (-0.5),
            rotate(shaped[:, 1], places),
            shaped[:, 2],
        )

    (queries, keys_rot, values_in), embed_pull = jax.vjp(embed, packed)
    queries_low = queries.astype(BF16)
    kv_low = jnp.concatenate(
        [keys_rot.reshape(row_count, model_width), values_in.reshape(row_count, model_width)],
        axis=1,
    ).astype(BF16)
    seg_low = segments.astype(BF16)
    per_quarter = max(experts // QUARTERS, 1)
    reach_count = min((WINDOW - 1) // row_count + 1, 2 * per_quarter - 1)
    kv_parts = []
    seg_parts = []
    for distance in range(reach_count, 0, -1):
        moved_kv, moved_seg = shifted((kv_low, seg_low), "expert", distance)
        kv_parts.append(moved_kv)
        seg_parts.append(moved_seg)
    all_kv = jnp.concatenate(kv_parts + [kv_low], axis=0)
    all_seg = jnp.concatenate(seg_parts + [seg_low], axis=0)
    key_count = all_kv.shape[0]
    key_heads = all_kv[:, :model_width].reshape(key_count, HEADS, HEAD)
    value_heads = all_kv[:, model_width:].reshape(key_count, HEADS, HEAD)
    query_pos = first_row + jnp.arange(row_count, dtype=jnp.int32)
    key_pos = first_row - reach_count * row_count + jnp.arange(key_count, dtype=jnp.int32)
    offset = query_pos[:, None] - key_pos[None, :]
    allowed = (
        (offset >= 0)
        & (offset < WINDOW)
        & (key_pos[None, :] >= 0)
        & (seg_low[:, None] == all_seg[None, :])
    )

    def masked_scores():
        raw_scores = dot32("qhd,khd->hqk", queries_low, key_heads)
        return jnp.where(allowed[None], raw_scores, -1e30)

    scores = masked_scores()
    top_score = jnp.max(scores, axis=2, keepdims=True)
    log_total = top_score + jnp.log(jnp.sum(jnp.exp(scores - top_score), axis=2, keepdims=True))
    probs_low = jnp.exp(scores - log_total).astype(BF16)
    attended = dot32("hqk,khd->qhd", probs_low, value_heads)
    attended = attended.reshape(row_count, model_width).astype(BF16)
    hidden = layer_inputs + jnp.dot(attended, w_out, preferred_element_type=F32)
    normed_ffn, ffn_norm_pull = jax.vjp(rmsnorm, hidden, gain_ffn)
    ffn_low = normed_ffn.astype(BF16)
    chosen = (expert_ids[:, :, None] == labels[None, None, :]).astype(F32)
    logits = jnp.dot(ffn_low, w_router, preferred_element_type=F32)
    gate_share, route_pull = jax.vjp(lambda logit_rows: route(logit_rows, chosen), logits)

    send_rows = dot32("rs,rd->sd", either, ffn_low).astype(BF16)
    send_share = jnp.sum(
        dispatch.astype(F32) * jnp.transpose(gate_share)[:, :, None], axis=(0, 1)
    )
    row_slots = by_expert(spread(send_rows))
    share_slots = by_expert(spread(send_share[:, None]))
    row_pieces = [row_slots] + [pair_turn(row_slots, k) for k in range(1, outers)]
    share_pieces = [share_slots] + [pair_turn(share_slots, k) for k in range(1, outers)]

    dense_gate_pre = jnp.dot(ffn_low, dense_gate, preferred_element_type=F32)
    dense_up_pre = jnp.dot(ffn_low, dense_up, preferred_element_type=F32)
    dense_act = swiglu(dense_gate_pre, dense_up_pre).astype(BF16)
    dense_out = jnp.dot(dense_act, dense_down, preferred_element_type=F32)
    grad_dense_act = dot32("rd,fd->rf", cotangent, dense_down)
    grad_dense_down = dot32("rf,rd->fd", dense_act, cotangent)
    dense_pulled = jax.vjp(swiglu, dense_gate_pre, dense_up_pre)[1](grad_dense_act)
    grad_dense_gpre = dense_pulled[0].astype(BF16)
    grad_dense_upre = dense_pulled[1].astype(BF16)
    grad_dense_gate = dot32("rd,rf->df", ffn_low, grad_dense_gpre)
    grad_dense_up = dot32("rd,rf->df", ffn_low, grad_dense_upre)
    grad_normed = dot32("rf,df->rd", grad_dense_gpre, dense_gate)
    grad_normed = grad_normed + dot32("rf,df->rd", grad_dense_upre, dense_up)
    dense_sums = (
        scatter_sum(grad_dense_gate),
        scatter_sum(grad_dense_up),
        scatter_sum(grad_dense_down),
    )

    my_gate = lax.dynamic_slice_in_dim(expert_gate, side * half, half, 0)
    my_up = lax.dynamic_slice_in_dim(expert_up, side * half, half, 0)
    my_down = lax.dynamic_slice_in_dim(expert_down, side * half, half, 0)
    grad_slots = (share_slots * cot_slots.astype(F32)).astype(BF16)
    gate_pre = dot32("erd,edf->erf", row_slots, my_gate)
    up_pre = dot32("erd,edf->erf", row_slots, my_up)
    activated = swiglu(gate_pre, up_pre).astype(BF16)
    layer_result = dot32("erf,efd->erd", activated, my_down).astype(BF16)
    came_back = give_back(layer_result)
    grad_act = dot32("erd,efd->erf", grad_slots, my_down)
    pulled = jax.vjp(swiglu, gate_pre, up_pre)[1](grad_act)
    grad_gate_pre = pulled[0].astype(BF16)
    grad_up_pre = pulled[1].astype(BF16)
    grad_rows = dot32("erf,edf->erd", grad_gate_pre, my_gate)
    grad_rows = (grad_rows + dot32("erf,edf->erd", grad_up_pre, my_up)).astype(BF16)
    grad_back = give_back(grad_rows)

    fetched = dot32("krs,sd->krd", dispatch, came_back)
    mixture = gate_share[:, 0:1] * fetched[0] + gate_share[:, 1:2] * fetched[1]
    mixed_out = (hidden + mixture + dense_out).astype(BF16)
    grad_normed = grad_normed + dot32("rs,sd->rd", either, grad_back)
    grad_gates = jnp.transpose(jnp.sum(cot_float[None] * fetched, axis=2))
    grad_logits = route_pull(grad_gates)[0].astype(BF16)
    grad_router = dot32("rd,re->de", ffn_low, grad_logits)
    grad_normed = grad_normed + dot32("re,de->rd", grad_logits, w_router)
    grad_hidden_norm, grad_gain_ffn = ffn_norm_pull(grad_normed)
    grad_hidden = cot_float + grad_hidden_norm
    grad_hidden_low = grad_hidden.astype(BF16)
    grad_out_proj = dot32("rd,re->de", attended, grad_hidden_low)
    out_sum = scatter_sum(grad_out_proj)
    grad_attended = dot32("re,de->rd", grad_hidden_low, w_out)
    grad_attended = grad_attended.astype(BF16).reshape(row_count, HEADS, HEAD)
    scores = masked_scores()
    attn_probs = jnp.exp(scores - log_total)
    probs_again = attn_probs.astype(BF16)
    grad_probs = dot32("qhd,khd->hqk", grad_attended, value_heads)
    grad_values = dot32("hqk,qhd->khd", probs_again, grad_attended)
    row_total = jnp.sum(attn_probs * grad_probs, axis=2, keepdims=True)
    grad_scores = (attn_probs * (grad_probs - row_total)).astype(BF16)
    grad_queries = dot32("hqk,khd->qhd", grad_scores, key_heads)
    grad_keys = dot32("hqk,qhd->khd", grad_scores, queries_low)
    grad_kv = jnp.concatenate(
        [grad_keys.reshape(key_count, model_width), grad_values.reshape(key_count, model_width)],
        axis=1,
    )
    own_grad = grad_kv[reach_count * row_count :]
    for distance in range(1, reach_count + 1):
        begin_at = (reach_count - distance) * row_count
        rim_part = grad_kv[begin_at : begin_at + row_count].astype(BF16)
        own_grad = own_grad + shifted(rim_part, "expert", -distance).astype(F32)
    grad_keys_own = own_grad[:, :model_width].reshape(row_count, HEADS, HEAD)
    grad_values_own = own_grad[:, model_width:].reshape(row_count, HEADS, HEAD)
    grad_packed = embed_pull((grad_queries, grad_keys_own, grad_values_own))[0].astype(BF16)
    grad_qkv = dot32("rd,re->de", normed_low, grad_packed)
    qkv_sum = scatter_sum(grad_qkv)
    grad_normed_attn = dot32("re,de->rd", grad_packed, w_qkv)
    grad_inputs_norm, grad_gain_attn = attn_norm_pull(grad_normed_attn)
    grad_tokens = grad_hidden + grad_inputs_norm
    router_sum, gains_sum = lax.psum(
        (grad_router, jnp.stack([grad_gain_attn, grad_gain_ffn])), ("group", "expert")
    )

    width = ff // outers
    cut_gate = lax.dynamic_slice_in_dim(my_gate, outer * width, width, 2)
    cut_up = lax.dynamic_slice_in_dim(my_up, outer * width, width, 2)
    cut_down = lax.dynamic_slice_in_dim(my_down, outer * width, width, 1)
    all_rows = jnp.concatenate(row_pieces, axis=1)
    all_cots = jnp.concatenate(cot_pieces, axis=1)
    all_shares = jnp.concatenate(share_pieces, axis=1)
    all_grads = (all_shares * all_cots.astype(F32)).astype(BF16)
    gate_cut = dot32("erd,edf->erf", all_rows, cut_gate)
    up_cut = dot32("erd,edf->erf", all_rows, cut_up)
    act_cut = swiglu(gate_cut, up_cut).astype(BF16)
    grad_act_cut = dot32("erd,efd->erf", all_grads, cut_down)
    pulled = jax.vjp(swiglu, gate_cut, up_cut)[1](grad_act_cut)
    grad_gate_w = dot32("erd,erf->edf", all_rows, pulled[0].astype(BF16))
    grad_up_w = dot32("erd,erf->edf", all_rows, pulled[1].astype(BF16))
    grad_down_w = dot32("erf,erd->efd", act_cut, all_grads)

    def trade(x, axis):
        size = x.shape[axis] // 2
        kept = lax.dynamic_slice_in_dim(x, side * size, size, axis)
        sent = lax.dynamic_slice_in_dim(x, (1 - side) * size, size, axis)
        got = swap(sent.astype(BF16), 1, 0).astype(F32)
        whole = jnp.zeros((2,) + kept.shape, F32)
        whole = lax.dynamic_update_index_in_dim(whole, kept, side, 0)
        whole = lax.dynamic_update_index_in_dim(whole, got, 1 - side, 0)
        return whole.reshape((2 * half,) + kept.shape[1:])

    return (
        mixed_out,
        grad_tokens,
        gains_sum[0],
        qkv_sum,
        out_sum,
        gains_sum[1],
        router_sum,
        trade(grad_gate_w, 2),
        trade(grad_up_w, 2),
        trade(grad_down_w, 1),
        dense_sums[0],
        dense_sums[1],
        dense_sums[2],
    )


def solution(mesh):
    in_specs = (
        P(("group", "expert"), None),
        P(),
        P(),
        P(),
        P(),
        P(),
        P("expert", None, None),
        P("expert", None, None),
        P("expert", None, None),
        P(),
        P(),
        P(),
        P(("group", "expert"), None),
        P(("group", "expert")),
        P(("group", "expert"), None),
    )
    out_specs = (
        P(("group", "expert"), None),
        P(("group", "expert"), None),
        P(),
        P("group", "expert"),
        P("group", "expert"),
        P(),
        P(),
        P("expert", None, "group"),
        P("expert", None, "group"),
        P("expert", "group", None),
        P("group", "expert"),
        P("group", "expert"),
        P("group", "expert"),
    )
    return jax.shard_map(local, mesh=mesh, in_specs=in_specs, out_specs=out_specs, check_vma=False)
```

```python
import functools

import jax
import jax.numpy as jnp
from jax import lax
from jax.experimental import pallas as pl
from jax.experimental.pallas import tpu as pltpu
from jax.sharding import PartitionSpec as P

HEADS = 12
HEAD = 64
EXPERTS = 16
WINDOW = 1024
CAP = 80
QUARTERS = 4
LANES = 128
TILE = 256
NEG = -1e30

epsilon = 1e-06
F32 = jnp.float32
BF16 = jnp.bfloat16
MESH = pl.DeviceIdType.MESH
VMEM = pl.BlockSpec(memory_space=pltpu.VMEM)
ANY = pl.BlockSpec(memory_space=pl.ANY)
MIB = 1 << 20


def dims(spec):
    left, right = spec
    return (((left,), (right,)), ((), ()))


NN = dims((1, 0))
NT = dims((1, 1))
TN = dims((0, 0))


def mm(a, b, how=NN):
    return lax.dot_general(a, b, how, preferred_element_type=F32)


def flipped(x, mask):
    bit = 1
    while bit <= mask:
        if mask & bit:
            x = x + bit * (1 - 2 * ((x // bit) % 2))
        bit *= 2
    return x


class Layout:
    def __init__(self, groups, experts, rows):
        self.groups, self.experts, self.rows = groups, experts, rows
        self.share = EXPERTS // experts
        self.peers = self.share * experts
        self.outers = groups // self.share
        per_quarter = max(experts // QUARTERS, 1)
        self.reach = min((WINDOW - 1) // rows + 1, 2 * per_quarter - 1)

    def peer(self, number):
        group, expert = lax.axis_index("group"), lax.axis_index("expert")
        return {
            "group": flipped(group, number // self.experts),
            "expert": flipped(expert, number % self.experts),
        }


def meet(layout):
    barrier = pltpu.get_barrier_semaphore()
    for number in range(1, layout.peers):
        pl.semaphore_signal(barrier, inc=1, device_id=layout.peer(number), device_id_type=MESH)
    pl.semaphore_wait(barrier, layout.peers - 1)


def to_peers(layout, source, target, send_sems, recv_sems):
    return [
        pltpu.make_async_remote_copy(
            src_ref=source.at[number],
            dst_ref=target.at[number],
            send_sem=send_sems.at[number],
            recv_sem=recv_sems.at[number],
            device_id=layout.peer(number),
            device_id_type=MESH,
        )
        for number in range(1, layout.peers)
    ]


def rope_turn(x, cosine, sine):
    parts = []
    for begin in range(0, x.shape[1], LANES):
        part = x[:, begin : begin + LANES]
        lane = lax.broadcasted_iota(jnp.int32, part.shape, 1)
        other = jnp.where(
            lane % HEAD < HEAD // 2,
            pltpu.roll(part, LANES - HEAD // 2, 1),
            pltpu.roll(part, HEAD // 2, 1),
        )
        parts.append(part * cosine + other * sine)
    return jnp.concatenate(parts, axis=1)


def normed(x, gain):
    return x * lax.rsqrt(jnp.mean(x * x, axis=-1, keepdims=True) + epsilon) * gain


def slot_rows(ids_row, rows):
    labels = lax.broadcasted_iota(jnp.int32, (EXPERTS, rows), 0)
    first, second = labels == ids_row[0:1], labels == ids_row[1:2]
    both = jnp.where(first | second, 1.0, 0.0).astype(BF16)
    earlier_t = lax.broadcasted_iota(jnp.int32, (rows, rows), 0)
    later_t = lax.broadcasted_iota(jnp.int32, (rows, rows), 1)
    earlier = mm(both, jnp.where(earlier_t < later_t, 1.0, 0.0).astype(BF16))
    targets = []
    for mask, ids in ((first, ids_row[0:1]), (second, ids_row[1:2])):
        slot = jnp.sum(jnp.where(mask, earlier, 0.0), axis=0, keepdims=True).astype(jnp.int32)
        targets.append(jnp.where(slot < CAP, ids * CAP + slot, -1))
    return targets


def front_kernel(
    layout,
    tokens,
    gain,
    w_qkv,
    cosine,
    sine,
    ids_row,
    seg_row,
    cot,
    q_out,
    kv_out,
    att_out,
    att_t_out,
    lse_out,
    bias_out,
    target_out,
    cots_out,
    normed_low,
    send_cot,
    seg_all,
    acc,
    top,
    total,
    kv_send,
    kv_recv,
    seg_send,
    seg_recv,
    cot_send,
    cot_recv,
    own_sem,
):
    rows, width = tokens.shape
    reach, experts = layout.reach, layout.experts
    e = lax.axis_index("expert")

    x = tokens[...].astype(F32)
    normed_low[...] = normed(x, gain[...]).astype(BF16)
    seg_all[0] = seg_row[...]

    def project(step, carry):
        for part in range(3):
            columns = pl.ds(pl.multiple_of(part * width + step * TILE, TILE), TILE)
            made = mm(normed_low[...], w_qkv[:, columns])
            columns = pl.ds(pl.multiple_of(step * TILE, TILE), TILE)
            if part == 0:
                made = rope_turn(made, cosine[...], sine[...]) * HEAD ** (-0.5)
                q_out[:, columns] = made.astype(BF16)
            elif part == 1:
                made = rope_turn(made, cosine[...], sine[...])
                kv_out[0, :, columns] = made.astype(BF16)
            else:
                columns = pl.ds(pl.multiple_of(width + step * TILE, TILE), TILE)
                kv_out[0, :, columns] = made.astype(BF16)
        return carry

    lax.fori_loop(0, width // TILE, project, 0)

    meet(layout)
    halos = []
    for distance in range(1, reach + 1):
        to = {"expert": lax.rem(e + distance, experts)}
        halos.append(
            (
                pltpu.make_async_remote_copy(
                    src_ref=kv_out.at[0],
                    dst_ref=kv_out.at[distance],
                    send_sem=kv_send.at[distance],
                    recv_sem=kv_recv.at[distance],
                    device_id=to,
                    device_id_type=MESH,
                ),
                pltpu.make_async_remote_copy(
                    src_ref=seg_all.at[0],
                    dst_ref=seg_all.at[distance],
                    send_sem=seg_send.at[distance],
                    recv_sem=seg_recv.at[distance],
                    device_id=to,
                    device_id_type=MESH,
                ),
            )
        )
        for copy in halos[-1]:
            copy.start()

    targets = slot_rows(ids_row[...], rows)
    target_out[0:1] = targets[0]
    target_out[1:2] = targets[1]
    target_out[2:8] = jnp.full((6, rows), -1, jnp.int32)
    for number in range(layout.peers):
        slots = number * CAP + lax.broadcasted_iota(jnp.int32, (CAP, rows), 0)
        chosen = (slots == targets[0]) | (slots == targets[1])
        send_cot[number] = mm(jnp.where(chosen, 1.0, 0.0).astype(BF16), cot[...]).astype(BF16)
    sends = to_peers(layout, send_cot, cots_out, cot_send, cot_recv)
    for copy in sends:
        copy.start()
    own = pltpu.make_async_copy(send_cot.at[0], cots_out.at[0], own_sem)
    own.start()

    lane = lax.broadcasted_iota(jnp.int32, (rows, LANES), 1)
    for distance in range(reach + 1):
        if distance:
            for copy in halos[distance - 1]:
                copy.wait()
        seg_col = jnp.transpose(jnp.broadcast_to(seg_all[distance, 0:1], (LANES, rows)))[:, 0:1]
        key_no = lax.broadcasted_iota(jnp.int32, (rows, rows), 0) - distance * rows
        offset = lax.broadcasted_iota(jnp.int32, (rows, rows), 1) - key_no
        allowed = (
            (offset >= 0)
            & (offset < WINDOW)
            & (key_no + e * rows >= 0)
            & (seg_col == seg_all[0, 0:1])
        )
        bias_out[distance] = jnp.where(allowed, 0.0, NEG)

        def attend(pair, carry, distance=distance):
            columns = pl.ds(pl.multiple_of(pair * LANES, LANES), LANES)
            value_columns = pl.ds(pl.multiple_of(width + pair * LANES, LANES), LANES)
            queries = q_out[:, columns]
            keys = kv_out[distance, :, columns]
            values_t = jnp.transpose(kv_out[distance, :, value_columns])
            for inner in range(2):
                head = pair * 2 + inner
                mine = jnp.where((lane // HEAD) == inner, queries, jnp.zeros_like(queries))
                value_t = values_t[inner * HEAD : (inner + 1) * HEAD]
                out_rows = pl.ds(pl.multiple_of(head * HEAD, HEAD), HEAD)
                blocks = (
                    [(slice(0, rows // 2), rows // 2), (slice(rows // 2, rows), rows)]
                    if distance == 0
                    else [(slice(0, rows), rows)]
                )
                for q_cut, key_count in blocks:
                    scores = mm(keys[:key_count], mine[q_cut], NT)
                    scores = scores + bias_out[distance, :key_count, q_cut]
                    peak = jnp.max(scores, axis=0, keepdims=True)
                    if distance:
                        before = top[pl.ds(head, 1), q_cut]
                        peak = jnp.maximum(before, peak)
                    weights = jnp.exp(scores - peak)
                    amount = jnp.sum(weights, axis=0, keepdims=True)
                    part = mm(value_t[:, :key_count], weights.astype(BF16))
                    if distance:
                        shrink = jnp.exp(before - peak)
                        amount = amount + total[pl.ds(head, 1), q_cut] * shrink
                        part = part + acc[out_rows, q_cut] * shrink
                    top[pl.ds(head, 1), q_cut] = peak
                    total[pl.ds(head, 1), q_cut] = amount
                    acc[out_rows, q_cut] = part
            return carry

        lax.fori_loop(0, HEADS // 2, attend, 0)

    lse_out[...] = top[...] + jnp.log(total[...])

    def finish(pair, carry):
        out_rows = pl.ds(pl.multiple_of(pair * LANES, LANES), LANES)
        scale = jnp.concatenate(
            [
                jnp.broadcast_to(1.0 / total[pl.ds(pair * 2 + inner, 1), :], (HEAD, rows))
                for inner in range(2)
            ],
            axis=0,
        )
        made = acc[out_rows, :] * scale
        att_t_out[out_rows, :] = made.astype(BF16)
        att_out[:, out_rows] = jnp.transpose(made).astype(BF16)
        return carry

    lax.fori_loop(0, HEADS // 2, finish, 0)
    own.wait()
    for copy in sends:
        copy.wait()


def front(layout, tokens, gain, w_qkv, cosine, sine, ids_row, seg_row, cot):
    rows, width = tokens.shape
    reach, peers = layout.reach, layout.peers
    dma = pltpu.SemaphoreType.DMA
    return pl.pallas_call(
        functools.partial(front_kernel, layout),
        out_shape=[
            jax.ShapeDtypeStruct((rows, width), BF16),
            jax.ShapeDtypeStruct((reach + 1, rows, 2 * width), BF16),
            jax.ShapeDtypeStruct((rows, width), BF16),
            jax.ShapeDtypeStruct((width, rows), BF16),
            jax.ShapeDtypeStruct((EXPERTS, rows), F32),
            jax.ShapeDtypeStruct((reach + 1, rows, rows), F32),
            jax.ShapeDtypeStruct((8, rows), jnp.int32),
            jax.ShapeDtypeStruct((peers, CAP, width), BF16),
        ],
        in_specs=[VMEM] * 8,
        out_specs=[VMEM] * 7 + [ANY],
        scratch_shapes=[
            pltpu.VMEM((rows, width), BF16),
            pltpu.VMEM((peers, CAP, width), BF16),
            pltpu.VMEM((reach + 1, 8, rows), F32),
            pltpu.VMEM((width, rows), F32),
            pltpu.VMEM((EXPERTS, rows), F32),
            pltpu.VMEM((EXPERTS, rows), F32),
            dma((reach + 1,)),
            dma((reach + 1,)),
            dma((reach + 1,)),
            dma((reach + 1,)),
            dma((peers,)),
            dma((peers,)),
            dma,
        ],
        compiler_params=pltpu.CompilerParams(
            collective_id=0, has_side_effects=True, vmem_limit_bytes=56 * MIB
        ),
        cost_estimate=pl.CostEstimate(flops=1 << 30, bytes_accessed=1 << 20, transcendentals=0),
        name="front",
    )(tokens, gain, w_qkv, cosine, sine, ids_row, seg_row, cot)


def split3(x):
    high = x.astype(BF16)
    rest = x - high.astype(F32)
    middle = rest.astype(BF16)
    return high, middle, (rest - middle.astype(F32)).astype(BF16)


def silu_parts(gate_pre):
    gate = 1.0 / (1.0 + jnp.exp(-gate_pre))
    return gate_pre * gate, gate * (1.0 + gate_pre * (1.0 - gate))


def middle_kernel(
    layout,
    att,
    tokens,
    w_out,
    gain,
    w_router_t,
    ids_row,
    target_row,
    cot,
    dense_gate,
    dense_up,
    dense_down,
    hidden_out,
    low_out,
    mixed_out,
    grad_out,
    gate_out,
    up_out,
    down_out,
    rows_out,
    shares_out,
    send_rows,
    send_shares,
    low_t,
    row_send,
    row_recv,
    share_send,
    share_recv,
    own_sems,
):
    rows, width = tokens.shape
    ff = dense_gate.shape[1]
    experts = layout.experts
    hidden_out[...] = tokens[...].astype(F32) + mm(att[...], w_out[...])
    low = normed(hidden_out[...], gain[...]).astype(BF16)
    low_out[...] = low
    logits = mm(w_router_t[...], low, NT)
    route = jnp.exp(logits - jnp.max(logits, axis=0, keepdims=True))
    route = route / jnp.sum(route, axis=0, keepdims=True)
    labels = lax.broadcasted_iota(jnp.int32, (EXPERTS, rows), 0)
    picked = [
        jnp.sum(jnp.where(labels == ids_row[k : k + 1], route, 0.0), axis=0, keepdims=True)
        for k in range(2)
    ]
    both = picked[0] + picked[1]
    shares = []
    for k in range(2):
        parts = split3(picked[k] / both)
        shares.append(
            jnp.concatenate(
                [part.astype(F32) for part in parts] + [jnp.zeros((5, rows), F32)], axis=0
            ).astype(BF16)
        )
    send_shares[...] = jnp.zeros_like(send_shares)
    for number in range(layout.peers):
        slots = number * CAP + lax.broadcasted_iota(jnp.int32, (CAP, rows), 0)
        first = jnp.where(slots == target_row[0:1], 1.0, 0.0).astype(BF16)
        second = jnp.where(slots == target_row[1:2], 1.0, 0.0).astype(BF16)
        send_rows[number] = mm(first + second, low).astype(BF16)
        share = mm(shares[0], first, NT) + mm(shares[1], second, NT)
        share = jnp.sum(share, axis=0, keepdims=True)
        send_shares[number, :, :CAP] = jnp.broadcast_to(share, (8, CAP))

    meet(layout)
    sends = to_peers(layout, send_rows, rows_out, row_send, row_recv)
    sends += to_peers(layout, send_shares, shares_out, share_send, share_recv)
    sends.append(pltpu.make_async_copy(send_rows.at[0], rows_out.at[0], own_sems.at[0]))
    sends.append(pltpu.make_async_copy(send_shares.at[0], shares_out.at[0], own_sems.at[1]))
    for copy in sends:
        copy.start()

    low_t[...] = jnp.transpose(low)
    mixed_out[...] = hidden_out[...]
    grad_out[...] = jnp.zeros_like(grad_out)
    part_width = ff // experts
    per_part = part_width // TILE

    def branch(step, carry):
        columns = pl.ds(pl.multiple_of(step * TILE, TILE), TILE)
        gate_w, up_w, down_w = dense_gate[:, columns], dense_up[:, columns], dense_down[columns, :]
        gate_pre = mm(low_out[...], gate_w)
        up_pre = mm(low_out[...], up_w)
        grad_act = mm(cot[...], down_w, NT)
        silu, slope = silu_parts(gate_pre)
        act = (silu * up_pre).astype(BF16)
        grad_gate = (grad_act * up_pre * slope).astype(BF16)
        grad_up = (grad_act * silu).astype(BF16)
        mixed_out[...] += mm(act, down_w)
        grad_out[...] += mm(grad_gate, gate_w, NT) + mm(grad_up, up_w, NT)
        inside = pl.ds(pl.multiple_of((step % per_part) * TILE, TILE), TILE)
        gate_out[step // per_part, :, inside] = mm(low_t[...], grad_gate).astype(BF16)
        up_out[step // per_part, :, inside] = mm(low_t[...], grad_up).astype(BF16)
        made = mm(act, cot[...], TN).astype(BF16)
        for part in range(experts):
            cut = width // experts
            down_out[part, columns, :] = made[:, part * cut : (part + 1) * cut]
        return carry

    lax.fori_loop(0, ff // TILE, branch, 0)
    for copy in sends:
        copy.wait()


def middle(layout, att, tokens, w_out, gain, w_router_t, ids_row, target_row, cot, dense_gate, dense_up, dense_down):
    rows, width = tokens.shape
    ff = dense_gate.shape[1]
    peers, experts = layout.peers, layout.experts
    dma = pltpu.SemaphoreType.DMA
    return pl.pallas_call(
        functools.partial(middle_kernel, layout),
        out_shape=[
            jax.ShapeDtypeStruct((rows, width), F32),
            jax.ShapeDtypeStruct((rows, width), BF16),
            jax.ShapeDtypeStruct((rows, width), F32),
            jax.ShapeDtypeStruct((rows, width), F32),
            jax.ShapeDtypeStruct((experts, width, ff // experts), BF16),
            jax.ShapeDtypeStruct((experts, width, ff // experts), BF16),
            jax.ShapeDtypeStruct((experts, ff, width // experts), BF16),
            jax.ShapeDtypeStruct((peers, CAP, width), BF16),
            jax.ShapeDtypeStruct((peers, 8, LANES), F32),
        ],
        in_specs=[VMEM] * 11,
        out_specs=[VMEM] * 7 + [ANY, ANY],
        scratch_shapes=[
            pltpu.VMEM((peers, CAP, width), BF16),
            pltpu.VMEM((peers, 8, LANES), F32),
            pltpu.VMEM((width, rows), BF16),
            dma((peers,)),
            dma((peers,)),
            dma((peers,)),
            dma((peers,)),
            dma((2,)),
        ],
        compiler_params=pltpu.CompilerParams(
            collective_id=1, has_side_effects=True, vmem_limit_bytes=56 * MIB
        ),
        cost_estimate=pl.CostEstimate(flops=1 << 30, bytes_accessed=1 << 20, transcendentals=0),
        name="middle",
    )(att, tokens, w_out, gain, w_router_t, ids_row, target_row, cot, dense_gate, dense_up, dense_down)


def share_column(share_row):
    across = lax.broadcasted_iota(jnp.int32, (CAP, CAP), 1)
    down = lax.broadcasted_iota(jnp.int32, (CAP, CAP), 0)
    return jnp.sum(jnp.where(across == down, share_row, 0.0), axis=1, keepdims=True)


def own_share(layout):
    return lax.rem(lax.axis_index("group"), layout.share)


def experts_kernel(
    layout,
    rows_in,
    cots,
    shares,
    gate_any,
    up_any,
    down_any,
    back_out,
    grad_back,
    gate_w,
    up_w,
    down_w,
    scaled,
    acc,
    grad_acc,
    send_out,
    send_grad,
    load_sems,
    out_send,
    out_recv,
    grad_send,
    grad_recv,
    own_sems,
):
    peers = layout.peers
    width, ff = gate_w.shape
    mine = own_share(layout)
    loads = [
        pltpu.make_async_copy(source.at[mine], target, load_sems.at[number])
        for number, (source, target) in enumerate(
            ((gate_any, gate_w), (up_any, up_w), (down_any, down_w))
        )
    ]
    for copy in loads:
        copy.start()
    for number in range(peers):
        column = share_column(shares[number, 0:1, :CAP])
        scaled[number] = (cots[number].astype(F32) * column).astype(BF16)
    meet(layout)
    for copy in loads:
        copy.wait()

    count = 4
    chunk = 2 * TILE
    outs = to_peers(layout, send_out, back_out, out_send, out_recv)
    grads = to_peers(layout, send_grad, grad_back, grad_send, grad_recv)
    outs.insert(0, pltpu.make_async_copy(send_out.at[0], back_out.at[0], own_sems.at[0]))
    grads.insert(0, pltpu.make_async_copy(send_grad.at[0], grad_back.at[0], own_sems.at[1]))
    for block in reversed(range(peers // count)):
        pieces = slice(block * count, (block + 1) * count)
        acc[...] = jnp.zeros_like(acc)
        grad_acc[...] = jnp.zeros_like(grad_acc)

        def turn(step, carry, pieces=pieces):
            columns = pl.ds(pl.multiple_of(step * chunk, chunk), chunk)
            n = rows_in[pieces].reshape(count * CAP, width)
            grad = scaled[pieces].reshape(count * CAP, width)
            gate_pre = mm(n, gate_w[:, columns])
            up_pre = mm(n, up_w[:, columns])
            grad_act = mm(grad, down_w[columns, :], NT)
            silu, slope = silu_parts(gate_pre)
            act = (silu * up_pre).astype(BF16)
            grad_gate = (grad_act * up_pre * slope).astype(BF16)
            grad_up = (grad_act * silu).astype(BF16)
            acc[...] += mm(act, down_w[columns, :])
            grad_acc[...] += mm(grad_gate, gate_w[:, columns], NT) + mm(
                grad_up, up_w[:, columns], NT
            )
            return carry

        lax.fori_loop(0, ff // chunk, turn, 0)
        send_out[pieces] = acc[...].astype(BF16).reshape(count, CAP, width)
        send_grad[pieces] = grad_acc[...].astype(BF16).reshape(count, CAP, width)
        for copy in outs[pieces] + grads[pieces]:
            copy.start()
    for copy in outs + grads:
        copy.wait()


def run_experts(layout, rows_in, cots, shares, expert_gate, expert_up, expert_down):
    peers = layout.peers
    _, width, ff = expert_gate.shape
    dma = pltpu.SemaphoreType.DMA
    return pl.pallas_call(
        functools.partial(experts_kernel, layout),
        out_shape=[jax.ShapeDtypeStruct((peers, CAP, width), BF16)] * 2,
        in_specs=[VMEM] * 3 + [ANY] * 3,
        out_specs=[ANY] * 2,
        scratch_shapes=[
            pltpu.VMEM((width, ff), BF16),
            pltpu.VMEM((width, ff), BF16),
            pltpu.VMEM((ff, width), BF16),
            pltpu.VMEM((peers, CAP, width), BF16),
            pltpu.VMEM((4 * CAP, width), F32),
            pltpu.VMEM((4 * CAP, width), F32),
            pltpu.VMEM((peers, CAP, width), BF16),
            pltpu.VMEM((peers, CAP, width), BF16),
            dma((3,)),
            dma((peers,)),
            dma((peers,)),
            dma((peers,)),
            dma((peers,)),
            dma((2,)),
        ],
        compiler_params=pltpu.CompilerParams(
            collective_id=2, has_side_effects=True, vmem_limit_bytes=56 * MIB
        ),
        cost_estimate=pl.CostEstimate(flops=1 << 30, bytes_accessed=1 << 20, transcendentals=0),
        name="experts",
    )(rows_in, cots, shares, expert_gate, expert_up, expert_down)


def combine_kernel(
    back,
    grad_back,
    target_row,
    ids_col,
    hidden,
    mixed_in,
    grad_in,
    low,
    cot,
    gain,
    w_router,
    w_out,
    att_t,
    mixed_out,
    grad_hidden_out,
    grad_att_out,
    proj_out,
    router_out,
    gain_out,
):
    rows, width = hidden.shape
    peers = back.shape[0]
    slots = peers * CAP
    columns = jnp.transpose(
        jnp.concatenate(
            [target_row[...].astype(F32), jnp.zeros((LANES - 8, rows), F32)], axis=0
        )
    )
    slot_no = lax.broadcasted_iota(jnp.int32, (rows, slots), 1).astype(F32)
    cot_float = cot[...].astype(F32)
    logits = mm(low[...], w_router[...])
    route = jnp.exp(logits - jnp.max(logits, axis=1, keepdims=True))
    route = route / jnp.sum(route, axis=1, keepdims=True)
    labels = lax.broadcasted_iota(jnp.int32, (rows, EXPERTS), 1)
    masks = [labels == ids_col[:, k : k + 1] for k in range(2)]
    picked = [jnp.sum(jnp.where(mask, route, 0.0), axis=1, keepdims=True) for mask in masks]
    both = picked[0] + picked[1]
    chosen, shares, grads = [], [], []
    mixed = mixed_in[...]
    for k in range(2):
        chosen.append(jnp.where(slot_no == columns[:, k : k + 1], 1.0, 0.0).astype(BF16))
        fetched = mm(chosen[k], back[...].reshape(slots, width))
        shares.append(picked[k] / both)
        mixed = mixed + shares[k] * fetched
        grads.append(jnp.sum(cot_float * fetched, axis=1, keepdims=True))
    mixed_out[...] = mixed.astype(BF16)
    mean = grads[0] * shares[0] + grads[1] * shares[1]
    grad_route = jnp.zeros_like(route)
    for k in range(2):
        grad_route = grad_route + jnp.where(masks[k], (grads[k] - mean) / both, 0.0)
    grad_logits = route * (grad_route - jnp.sum(route * grad_route, axis=1, keepdims=True))
    grad_logits = grad_logits.astype(BF16)
    router_out[...] = mm(low[...], grad_logits, TN)
    grad = grad_in[...] + mm(chosen[0] + chosen[1], grad_back[...].reshape(slots, width))
    grad = grad + mm(grad_logits, w_router[...], NT)
    h = hidden[...]
    scale = lax.rsqrt(jnp.mean(h * h, axis=-1, keepdims=True) + epsilon)
    gain_out[...] = jnp.sum(grad * h * scale, axis=0, keepdims=True)
    grad = grad * gain[...]
    grad = scale * grad - h * (scale * scale * scale) * jnp.mean(grad * h, axis=-1, keepdims=True)
    grad = cot_float + grad
    grad_hidden_out[...] = grad
    grad_low = grad.astype(BF16)
    grad_att_out[...] = mm(grad_low, w_out[...], NT).astype(BF16)
    made = mm(att_t[...], grad_low).astype(BF16)
    parts = proj_out.shape[0]
    cut = width // parts
    for part in range(parts):
        proj_out[part] = made[:, part * cut : (part + 1) * cut]


def combine(layout, back, grad_back, target_row, ids_col, hidden, mixed_in, grad_in, low, cot, gain, w_router, w_out, att_t):
    rows, width = hidden.shape
    experts = layout.experts
    return pl.pallas_call(
        combine_kernel,
        out_shape=[
            jax.ShapeDtypeStruct((rows, width), BF16),
            jax.ShapeDtypeStruct((rows, width), F32),
            jax.ShapeDtypeStruct((rows, width), BF16),
            jax.ShapeDtypeStruct((experts, width, width // experts), BF16),
            jax.ShapeDtypeStruct((width, EXPERTS), F32),
            jax.ShapeDtypeStruct((1, width), F32),
        ],
        in_specs=[VMEM] * 13,
        out_specs=[VMEM] * 6,
        compiler_params=pltpu.CompilerParams(vmem_limit_bytes=56 * MIB),
        cost_estimate=pl.CostEstimate(flops=1 << 30, bytes_accessed=1 << 20, transcendentals=0),
        name="combine",
    )(back, grad_back, target_row, ids_col, hidden, mixed_in, grad_in, low, cot, gain, w_router, w_out, att_t)


def rope_back(grad, cosine, sine):
    lane = lax.broadcasted_iota(jnp.int32, grad.shape, 1)
    turned = grad * sine
    other = jnp.where(
        lane % HEAD < HEAD // 2,
        pltpu.roll(turned, LANES - HEAD // 2, 1),
        pltpu.roll(turned, HEAD // 2, 1),
    )
    return grad * cosine + other


def back_kernel(
    layout,
    q_in,
    kv_in,
    bias,
    lse,
    att_t,
    grad_att,
    tokens,
    gain,
    w_qkv,
    cosine,
    sine,
    grad_hidden,
    tokens_out,
    qkv_out,
    gain_out,
    halo_send,
    halo_recv,
    own_kv,
    packed,
    normed_t,
    send_sems,
    recv_sems,
):
    rows, width = tokens.shape
    reach, experts = layout.reach, layout.experts
    e = lax.axis_index("expert")
    pairs = HEADS // 2
    lane = lax.broadcasted_iota(jnp.int32, (rows, LANES), 1)
    meet(layout)

    def halo(distance, pair):
        return pltpu.make_async_remote_copy(
            src_ref=halo_send.at[distance - 1, pair],
            dst_ref=halo_recv.at[distance - 1, pair],
            send_sem=send_sems.at[distance - 1, pair],
            recv_sem=recv_sems.at[distance - 1, pair],
            device_id={"expert": lax.rem(e + experts - distance, experts)},
            device_id_type=MESH,
        )

    def heads(pair, carry):
        columns = pl.ds(pl.multiple_of(pair * LANES, LANES), LANES)
        value_columns = pl.ds(pl.multiple_of(width + pair * LANES, LANES), LANES)
        queries, grads = q_in[:, columns], grad_att[:, columns]
        grads_t = jnp.transpose(grads.astype(F32))
        shrunk = grads_t * att_t[columns, :].astype(F32)
        grad_q = [None, None]
        for distance in range(reach, -1, -1):
            keys = kv_in[distance, :, columns]
            values = kv_in[distance, :, value_columns]
            keys_t = jnp.transpose(keys)
            grad_k = grad_v = None
            for inner in range(2):
                head = pair * 2 + inner
                cut = slice(inner * HEAD, (inner + 1) * HEAD)
                mine = (lane // HEAD) == inner
                query = jnp.where(mine, queries, jnp.zeros_like(queries))
                grad = jnp.where(mine, grads, jnp.zeros_like(grads))
                total = jnp.sum(shrunk[cut], axis=0, keepdims=True)
                scores = mm(keys, query, NT) + bias[distance]
                probs = jnp.exp(scores - lse[pl.ds(head, 1), :])
                grad_probs = mm(values, grad, NT)
                grad_scores = (probs * (grad_probs - total)).astype(BF16)
                part_v = mm(probs.astype(BF16), grad)
                part_k = mm(grad_scores, query)
                part_q = mm(keys_t[cut], grad_scores)
                grad_v = part_v if grad_v is None else grad_v + part_v
                grad_k = part_k if grad_k is None else grad_k + part_k
                grad_q[inner] = part_q if grad_q[inner] is None else grad_q[inner] + part_q
            if distance:
                halo_send[distance - 1, pair, 0] = grad_k.astype(BF16)
                halo_send[distance - 1, pair, 1] = grad_v.astype(BF16)
                halo(distance, pair).start()
            else:
                own_kv[pair, 0] = grad_k
                own_kv[pair, 1] = grad_v
        grad = jnp.transpose(jnp.concatenate(grad_q, axis=0)) * HEAD ** (-0.5)
        packed[:, columns] = rope_back(grad, cosine[...], sine[...]).astype(BF16)
        return carry

    lax.fori_loop(0, pairs, heads, 0)
    x = tokens[...].astype(F32)
    normed_t[...] = jnp.transpose(normed(x, gain[...])).astype(BF16)

    def merge(pair, carry):
        grad_k, grad_v = own_kv[pair, 0], own_kv[pair, 1]
        for distance in range(1, reach + 1):
            halo(distance, pair).wait()
            grad_k = grad_k + halo_recv[distance - 1, pair, 0].astype(F32)
            grad_v = grad_v + halo_recv[distance - 1, pair, 1].astype(F32)
        columns = pl.ds(pl.multiple_of(width + pair * LANES, LANES), LANES)
        packed[:, columns] = rope_back(grad_k, cosine[...], sine[...]).astype(BF16)
        columns = pl.ds(pl.multiple_of(2 * width + pair * LANES, LANES), LANES)
        packed[:, columns] = grad_v.astype(BF16)
        return carry

    lax.fori_loop(0, pairs, merge, 0)
    parts = qkv_out.shape[0]
    cut = 3 * width // parts
    for part in range(parts):
        piece = packed[:, part * cut : (part + 1) * cut]
        qkv_out[part] = mm(normed_t[...], piece).astype(BF16)
    grad = mm(packed[...], w_qkv[...], NT)
    scale = lax.rsqrt(jnp.mean(x * x, axis=-1, keepdims=True) + epsilon)
    gain_out[...] = jnp.sum(grad * x * scale, axis=0, keepdims=True)
    grad = grad * gain[...]
    grad = scale * grad - x * (scale * scale * scale) * jnp.mean(grad * x, axis=-1, keepdims=True)
    tokens_out[...] = grad_hidden[...] + grad


def back(layout, q_in, kv_in, bias, lse, att_t, grad_att, tokens, gain, w_qkv, cosine, sine, grad_hidden):
    rows, width = tokens.shape
    reach, experts = layout.reach, layout.experts
    dma = pltpu.SemaphoreType.DMA
    pairs = HEADS // 2
    return pl.pallas_call(
        functools.partial(back_kernel, layout),
        out_shape=[
            jax.ShapeDtypeStruct((rows, width), F32),
            jax.ShapeDtypeStruct((experts, width, 3 * width // experts), BF16),
            jax.ShapeDtypeStruct((1, width), F32),
        ],
        in_specs=[VMEM] * 12,
        out_specs=[VMEM] * 3,
        scratch_shapes=[
            pltpu.VMEM((reach, pairs, 2, rows, LANES), BF16),
            pltpu.VMEM((reach, pairs, 2, rows, LANES), BF16),
            pltpu.VMEM((pairs, 2, rows, LANES), F32),
            pltpu.VMEM((rows, 3 * width), BF16),
            pltpu.VMEM((width, rows), BF16),
            dma((reach, pairs)),
            dma((reach, pairs)),
        ],
        compiler_params=pltpu.CompilerParams(
            collective_id=3, has_side_effects=True, vmem_limit_bytes=56 * MIB
        ),
        cost_estimate=pl.CostEstimate(flops=1 << 30, bytes_accessed=1 << 20, transcendentals=0),
        name="back",
    )(q_in, kv_in, bias, lse, att_t, grad_att, tokens, gain, w_qkv, cosine, sine, grad_hidden)


def weights_kernel(layout, *refs):
    share, outers, peers = layout.share, layout.outers, layout.peers
    row_ins, cot_ins, share_ins = refs[:outers], refs[outers : 2 * outers], refs[2 * outers : 3 * outers]
    (
        gate_any,
        up_any,
        down_any,
        gate_out,
        up_out,
        down_out,
        gate_w,
        up_w,
        gate_t,
        up_t,
        down_w,
        rows_buf,
        cots_buf,
        shares_buf,
        accs,
        sends,
        takes,
        load_sems,
        piece_sems,
        send_sems,
        recv_sems,
    ) = refs[3 * outers :]
    width = gate_w.shape[0]
    ff = gate_any.shape[2]
    span = ff // outers
    cut = ff // layout.groups
    group = lax.axis_index("group")
    mine = own_share(layout)
    begin = pl.multiple_of((group // share) * span, span)
    loads = [
        pltpu.make_async_copy(gate_any.at[mine, :, pl.ds(begin, span)], gate_w, load_sems.at[0]),
        pltpu.make_async_copy(up_any.at[mine, :, pl.ds(begin, span)], up_w, load_sems.at[1]),
        pltpu.make_async_copy(down_any.at[mine, pl.ds(begin, span), :], down_w, load_sems.at[2]),
    ]

    def fetch(outer):
        slot = outer % 2
        return [
            pltpu.make_async_copy(source, target.at[slot], piece_sems.at[slot, number])
            for number, (source, target) in enumerate(
                (
                    (row_ins[outer], rows_buf),
                    (cot_ins[outer], cots_buf),
                    (share_ins[outer], shares_buf),
                )
            )
        ]

    for copy in loads + fetch(0):
        copy.start()
    meet(layout)
    for copy in loads:
        copy.wait()
    gate_t[...] = jnp.transpose(gate_w[...])
    up_t[...] = jnp.transpose(up_w[...])
    accs[...] = jnp.zeros_like(accs)
    count = 8
    blocks = peers // count

    def add(slot, chunk, block):
        pieces = pl.ds(block * count, count)
        n = rows_buf[slot, pieces].reshape(count * CAP, width)
        grad = cots_buf[slot, pieces].reshape(count * CAP, width)
        base = pl.multiple_of(chunk * cut, cut)
        gate_pre = mm(gate_t[pl.ds(base, cut), :], n, NT)
        up_pre = mm(up_t[pl.ds(base, cut), :], n, NT)
        grad_act = mm(down_w[pl.ds(base, cut), :], grad, NT)
        silu, slope = silu_parts(gate_pre)
        act = (silu * up_pre).astype(BF16)
        grad_gate = (grad_act * up_pre * slope).astype(BF16)
        grad_up = (grad_act * silu).astype(BF16)
        accs[chunk, 0] += mm(grad_gate, n)
        accs[chunk, 1] += mm(grad_up, n)
        accs[chunk, 2] += mm(act, grad)

    copies = []
    for outer in range(outers):
        slot = outer % 2
        for copy in fetch(outer):
            copy.wait()
        if outer + 1 < outers:
            for copy in fetch(outer + 1):
                copy.start()
        for number in range(peers):
            column = share_column(shares_buf[slot, number, 0:1, :CAP])
            cots_buf[slot, number] = (cots_buf[slot, number].astype(F32) * column).astype(BF16)
        if outer + 1 < outers:

            def step(number, carry, slot=slot):
                add(slot, number // blocks, number % blocks)
                return carry

            lax.fori_loop(0, share * blocks, step, 0)
            continue
        for turn in [*range(share - 1, 0, -1), 0]:
            owner = flipped(mine, turn)

            def step(number, carry, slot=slot, owner=owner):
                add(slot, owner, number)
                return carry

            lax.fori_loop(0, blocks, step, 0)
            if turn:
                for which in range(3):
                    sends[turn - 1, which] = accs[owner, which].astype(BF16)
                    copy = pltpu.make_async_remote_copy(
                        src_ref=sends.at[turn - 1, which],
                        dst_ref=takes.at[turn - 1, which],
                        send_sem=send_sems.at[turn - 1, which],
                        recv_sem=recv_sems.at[turn - 1, which],
                        device_id={"group": flipped(group, turn)},
                        device_id_type=MESH,
                    )
                    copy.start()
                    copies.append((turn, which, copy))
            else:
                gate_out[owner] = jnp.transpose(accs[owner, 0])
                up_out[owner] = jnp.transpose(accs[owner, 1])
                down_out[owner] = accs[owner, 2]
    for turn, which, copy in copies:
        copy.wait()
        owner = flipped(mine, turn)
        got = takes[turn - 1, which].astype(F32)
        if which == 2:
            down_out[owner] = got
        else:
            (gate_out, up_out)[which][owner] = jnp.transpose(got)


def weights(layout, row_ins, cot_ins, share_ins, expert_gate, expert_up, expert_down):
    share, outers, peers = layout.share, layout.outers, layout.peers
    experts, width, ff = expert_gate.shape
    span = ff // outers
    cut = ff // layout.groups
    dma = pltpu.SemaphoreType.DMA
    return pl.pallas_call(
        functools.partial(weights_kernel, layout),
        out_shape=[
            jax.ShapeDtypeStruct((experts, width, cut), F32),
            jax.ShapeDtypeStruct((experts, width, cut), F32),
            jax.ShapeDtypeStruct((experts, cut, width), F32),
        ],
        in_specs=[ANY] * (3 * outers + 3),
        out_specs=[VMEM] * 3,
        scratch_shapes=[
            pltpu.VMEM((width, span), BF16),
            pltpu.VMEM((width, span), BF16),
            pltpu.VMEM((span, width), BF16),
            pltpu.VMEM((span, width), BF16),
            pltpu.VMEM((span, width), BF16),
            pltpu.VMEM((2, peers, CAP, width), BF16),
            pltpu.VMEM((2, peers, CAP, width), BF16),
            pltpu.VMEM((2, peers, 8, LANES), F32),
            pltpu.VMEM((share, 3, cut, width), F32),
            pltpu.VMEM((share - 1, 3, cut, width), BF16),
            pltpu.VMEM((share - 1, 3, cut, width), BF16),
            dma((3,)),
            dma((2, 3)),
            dma((share - 1, 3)),
            dma((share - 1, 3)),
        ],
        compiler_params=pltpu.CompilerParams(
            collective_id=4, has_side_effects=True, vmem_limit_bytes=60 * MIB
        ),
        cost_estimate=pl.CostEstimate(flops=1 << 30, bytes_accessed=1 << 20, transcendentals=0),
        name="weights",
    )(*row_ins, *cot_ins, *share_ins, expert_gate, expert_up, expert_down)


def swap(x, group_bits):
    groups = lax.axis_size("group")
    return lax.ppermute(x, "group", [(g, g ^ group_bits) for g in range(groups)])


def gathered(layout, x):
    return [x] + [swap(x, layout.share * k) for k in range(1, layout.outers)]


def scatter_sum(parts):
    made = parts.reshape(-1, parts.shape[-1])
    return lax.psum_scatter(made, ("expert", "group"), scatter_dimension=0, tiled=True).astype(F32)


def local(
    tokens,
    gain_attn,
    w_qkv,
    w_out,
    gain_ffn,
    w_router,
    expert_gate,
    expert_up,
    expert_down,
    dense_gate,
    dense_up,
    dense_down,
    expert_ids,
    segments,
    cotangent,
):
    rows, width = tokens.shape
    layout = Layout(lax.axis_size("group"), lax.axis_size("expert"), rows)
    group, expert = lax.axis_index("group"), lax.axis_index("expert")
    share = layout.share
    relative = ((expert_ids % share) ^ (group % share)) * layout.experts
    relative = relative + ((expert_ids // share) ^ expert)
    fill = jnp.full((6, rows), -1, jnp.int32)
    relative_row = jnp.concatenate([jnp.transpose(relative), fill], axis=0)
    ids_row = jnp.concatenate([jnp.transpose(expert_ids), fill], axis=0)
    seg_row = jnp.broadcast_to(segments.astype(F32)[None], (8, rows))
    places = (expert * rows + jnp.arange(rows, dtype=jnp.int32)).astype(F32)
    lane = jnp.arange(LANES)
    power = (lane % (HEAD // 2)).astype(F32) / (HEAD // 2)
    angles = places[:, None] * (10000.0 ** (-power))[None]
    cosine = jnp.cos(angles)
    sine = jnp.sin(angles) * jnp.where(lane % HEAD < HEAD // 2, -1.0, 1.0)[None]

    q, kv, att, att_t, lse, bias, target, cots = front(
        layout, tokens, gain_attn[None], w_qkv, cosine, sine, relative_row, seg_row, cotangent
    )
    all_cots = gathered(layout, cots)
    hidden, low, mixed, grad_low, gate_terms, up_terms, down_terms, rows_in, shares = middle(
        layout,
        att,
        tokens,
        w_out,
        gain_ffn[None],
        jnp.transpose(w_router),
        ids_row,
        target,
        cotangent,
        dense_gate,
        dense_up,
        dense_down,
    )
    all_rows = gathered(layout, rows_in)
    all_shares = gathered(layout, shares)
    gate_sum, up_sum, down_sum = map(scatter_sum, (gate_terms, up_terms, down_terms))
    came_back, grad_back = run_experts(
        layout, rows_in, cots, shares, expert_gate, expert_up, expert_down
    )
    mixed_out, grad_hidden, grad_att, proj_terms, router_term, gain_term = combine(
        layout,
        came_back,
        grad_back,
        target,
        expert_ids,
        hidden,
        mixed,
        grad_low,
        low,
        cotangent,
        gain_ffn[None],
        w_router,
        w_out,
        att_t,
    )
    proj_sum = scatter_sum(proj_terms)
    grad_tokens, qkv_terms, attn_gain_term = back(
        layout,
        q,
        kv,
        bias,
        lse,
        att_t,
        grad_att,
        tokens,
        gain_attn[None],
        w_qkv,
        cosine,
        sine,
        grad_hidden,
    )
    qkv_sum = scatter_sum(qkv_terms)
    router_sum, gain_ffn_sum, gain_attn_sum = lax.psum(
        (router_term, gain_term, attn_gain_term), ("group", "expert")
    )
    grad_gate_w, grad_up_w, grad_down_w = weights(
        layout, all_rows, all_cots, all_shares, expert_gate, expert_up, expert_down
    )
    return (
        mixed_out,
        grad_tokens,
        gain_attn_sum[0],
        qkv_sum,
        proj_sum,
        gain_ffn_sum[0],
        router_sum,
        grad_gate_w,
        grad_up_w,
        grad_down_w,
        gate_sum,
        up_sum,
        down_sum,
    )


def solution(mesh):
    in_specs = (
        P(("group", "expert"), None),
        P(),
        P(),
        P(),
        P(),
        P(),
        P("expert", None, None),
        P("expert", None, None),
        P("expert", None, None),
        P(),
        P(),
        P(),
        P(("group", "expert"), None),
        P(("group", "expert")),
        P(("group", "expert"), None),
    )
    out_specs = (
        P(("group", "expert"), None),
        P(("group", "expert"), None),
        P(),
        P("group", "expert"),
        P("group", "expert"),
        P(),
        P(),
        P("expert", None, "group"),
        P("expert", None, "group"),
        P("expert", "group", None),
        P("group", "expert"),
        P("group", "expert"),
        P("group", "expert"),
    )
    return jax.shard_map(local, mesh=mesh, in_specs=in_specs, out_specs=out_specs, check_vma=False)
```

```python
import functools

import jax
import jax.numpy as jnp
from jax import lax
from jax.experimental import pallas as pl
from jax.experimental.pallas import tpu as pltpu
from jax.sharding import PartitionSpec as P

HEADS = 12
HEAD = 64
EXPERTS = 16
WINDOW = 1024
CAP = 80
QUARTERS = 4
LANES = 128
TILE = 256
SMALL = EXPERTS + 8
NEG = -1e30
FAR_COTS = (3, 11, 16)
FAR_ROWS = (5, 13, 16)

epsilon = 1e-06
F32 = jnp.float32
BF16 = jnp.bfloat16
MESH = pl.DeviceIdType.MESH
VMEM = pl.BlockSpec(memory_space=pltpu.VMEM)
ANY = pl.BlockSpec(memory_space=pl.ANY)
MIB = 1 << 20


def dims(spec):
    left, right = spec
    return (((left,), (right,)), ((), ()))


NN = dims((1, 0))
NT = dims((1, 1))
TN = dims((0, 0))


def mm(a, b, how=NN):
    return lax.dot_general(a, b, how, preferred_element_type=F32)


def flipped(x, mask):
    bit = 1
    while bit <= mask:
        if mask & bit:
            x = x + bit * (1 - 2 * ((x // bit) % 2))
        bit *= 2
    return x


class Layout:
    def __init__(self, groups, experts, rows):
        self.groups, self.experts, self.rows = groups, experts, rows
        self.share = EXPERTS // experts
        self.peers = self.share * experts
        self.outers = groups // self.share
        per_quarter = max(experts // QUARTERS, 1)
        self.reach = min((WINDOW - 1) // rows + 1, 2 * per_quarter - 1)

    def far(self, number):
        return {"group": flipped(lax.axis_index("group"), number * self.share)}

    def peer(self, number):
        group, expert = lax.axis_index("group"), lax.axis_index("expert")
        return {
            "group": flipped(group, number // self.experts),
            "expert": flipped(expert, number % self.experts),
        }


def meet(layout):
    barrier = pltpu.get_barrier_semaphore()
    for number in range(1, layout.peers):
        pl.semaphore_signal(barrier, inc=1, device_id=layout.peer(number), device_id_type=MESH)
    for number in range(1, layout.outers):
        pl.semaphore_signal(barrier, inc=1, device_id=layout.far(number), device_id_type=MESH)
    pl.semaphore_wait(barrier, layout.peers + layout.outers - 2)


def to_peers(layout, source, target, send_sems, recv_sems):
    return [
        pltpu.make_async_remote_copy(
            src_ref=source.at[number],
            dst_ref=target.at[number],
            send_sem=send_sems.at[number],
            recv_sem=recv_sems.at[number],
            device_id=layout.peer(number),
            device_id_type=MESH,
        )
        for number in range(1, layout.peers)
    ]


def to_far(layout, source, target, low, high, send_sems, recv_sems):
    return [
        pltpu.make_async_remote_copy(
            src_ref=source.at[low:high],
            dst_ref=target.at[number - 1],
            send_sem=send_sems.at[number - 1],
            recv_sem=recv_sems.at[number - 1],
            device_id=layout.far(number),
            device_id_type=MESH,
        )
        for number in range(1, layout.outers)
    ]


def far_shape(layout, count, width):
    return jax.ShapeDtypeStruct((layout.outers - 1, count, CAP, width), BF16)


def bit_of(axis, bit):
    return (lax.axis_index(axis) // bit) % 2


class Halving:
    def __init__(self, axis, bit, held, taken, send_sems, recv_sems):
        self.bit = bit_of(axis, bit)
        self.held, self.taken = held, taken
        self.copies = [
            pltpu.make_async_remote_copy(
                src_ref=held.at[2 * block + 1 - self.bit],
                dst_ref=taken.at[block],
                send_sem=send_sems.at[block],
                recv_sem=recv_sems.at[block],
                device_id={axis: flipped(lax.axis_index(axis), bit)},
                device_id_type=MESH,
            )
            for block in range(taken.shape[0])
        ]

    def start(self):
        for copy in self.copies:
            copy.start()

    def add(self, last=None):
        for block, copy in enumerate(self.copies):
            copy.wait()
            mine = 2 * block + self.bit
            if last is not None:
                last[...] = self.taken[block].astype(F32) + self.held[mine].astype(F32)
            elif len(self.taken.shape) == 3:
                self.taken[block] = (
                    self.taken[block].astype(F32) + self.held[mine].astype(F32)
                ).astype(BF16)
            else:

                def one(number, carry, block=block, mine=mine):
                    self.taken[block, number] = (
                        self.taken[block, number].astype(F32) + self.held[mine, number].astype(F32)
                    ).astype(BF16)
                    return carry

                lax.fori_loop(0, self.taken.shape[1], one, 0)


def rope_turn(x, cosine, sine):
    parts = []
    for begin in range(0, x.shape[1], LANES):
        part = x[:, begin : begin + LANES]
        lane = lax.broadcasted_iota(jnp.int32, part.shape, 1)
        other = jnp.where(
            lane % HEAD < HEAD // 2,
            pltpu.roll(part, LANES - HEAD // 2, 1),
            pltpu.roll(part, HEAD // 2, 1),
        )
        parts.append(part * cosine + other * sine)
    return jnp.concatenate(parts, axis=1)


def normed(x, gain):
    return x * lax.rsqrt(jnp.mean(x * x, axis=-1, keepdims=True) + epsilon) * gain


def slot_rows(ids_row, rows):
    labels = lax.broadcasted_iota(jnp.int32, (EXPERTS, rows), 0)
    first, second = labels == ids_row[0:1], labels == ids_row[1:2]
    both = jnp.where(first | second, 1.0, 0.0).astype(BF16)
    earlier_t = lax.broadcasted_iota(jnp.int32, (rows, rows), 0)
    later_t = lax.broadcasted_iota(jnp.int32, (rows, rows), 1)
    earlier = mm(both, jnp.where(earlier_t < later_t, 1.0, 0.0).astype(BF16))
    targets = []
    for mask, ids in ((first, ids_row[0:1]), (second, ids_row[1:2])):
        slot = jnp.sum(jnp.where(mask, earlier, 0.0), axis=0, keepdims=True).astype(jnp.int32)
        targets.append(jnp.where(slot < CAP, ids * CAP + slot, -1))
    return targets


def front_kernel(
    layout,
    tokens,
    gain,
    w_qkv,
    cosine,
    sine,
    ids_row,
    seg_row,
    cot,
    q_out,
    kv_out,
    att_out,
    att_t_out,
    lse_out,
    bias_out,
    target_out,
    cots_out,
    far_out,
    normed_low,
    send_cot,
    seg_all,
    acc,
    top,
    total,
    kv_send,
    kv_recv,
    seg_send,
    seg_recv,
    cot_send,
    cot_recv,
    own_sem,
    far_send,
    far_recv,
):
    rows, width = tokens.shape
    reach, experts = layout.reach, layout.experts
    e = lax.axis_index("expert")

    x = tokens[...].astype(F32)
    normed_low[...] = normed(x, gain[...]).astype(BF16)
    seg_all[0] = seg_row[...]

    def project(step, carry):
        for part in range(3):
            columns = pl.ds(pl.multiple_of(part * width + step * TILE, TILE), TILE)
            made = mm(normed_low[...], w_qkv[:, columns])
            columns = pl.ds(pl.multiple_of(step * TILE, TILE), TILE)
            if part == 0:
                made = rope_turn(made, cosine[...], sine[...]) * HEAD ** (-0.5)
                q_out[:, columns] = made.astype(BF16)
            elif part == 1:
                made = rope_turn(made, cosine[...], sine[...])
                kv_out[0, :, columns] = made.astype(BF16)
            else:
                columns = pl.ds(pl.multiple_of(width + step * TILE, TILE), TILE)
                kv_out[0, :, columns] = made.astype(BF16)
        return carry

    lax.fori_loop(0, width // TILE, project, 0)

    meet(layout)
    halos = []
    for distance in range(1, reach + 1):
        to = {"expert": lax.rem(e + distance, experts)}
        halos.append(
            (
                pltpu.make_async_remote_copy(
                    src_ref=kv_out.at[0],
                    dst_ref=kv_out.at[distance],
                    send_sem=kv_send.at[distance],
                    recv_sem=kv_recv.at[distance],
                    device_id=to,
                    device_id_type=MESH,
                ),
                pltpu.make_async_remote_copy(
                    src_ref=seg_all.at[0],
                    dst_ref=seg_all.at[distance],
                    send_sem=seg_send.at[distance],
                    recv_sem=seg_recv.at[distance],
                    device_id=to,
                    device_id_type=MESH,
                ),
            )
        )
        for copy in halos[-1]:
            copy.start()

    targets = slot_rows(ids_row[...], rows)
    target_out[0:1] = targets[0]
    target_out[1:2] = targets[1]
    target_out[2:8] = jnp.full((6, rows), -1, jnp.int32)
    for number in range(layout.peers):
        slots = number * CAP + lax.broadcasted_iota(jnp.int32, (CAP, rows), 0)
        chosen = (slots == targets[0]) | (slots == targets[1])
        send_cot[number] = mm(jnp.where(chosen, 1.0, 0.0).astype(BF16), cot[...]).astype(BF16)
    sends = to_peers(layout, send_cot, cots_out, cot_send, cot_recv)
    for copy in sends:
        copy.start()
    own = pltpu.make_async_copy(send_cot.at[0], cots_out.at[0], own_sem)
    own.start()

    lane = lax.broadcasted_iota(jnp.int32, (rows, LANES), 1)
    for distance in range(reach + 1):
        if distance:
            for copy in halos[distance - 1]:
                copy.wait()
        if distance == 1:
            own.wait()
            for copy in sends[: FAR_COTS[0] - 1]:
                copy.wait()
            far = to_far(layout, cots_out, far_out, 0, FAR_COTS[0], far_send, far_recv)
            for copy in far:
                copy.start()
        seg_col = jnp.transpose(jnp.broadcast_to(seg_all[distance, 0:1], (LANES, rows)))[:, 0:1]
        key_no = lax.broadcasted_iota(jnp.int32, (rows, rows), 0) - distance * rows
        offset = lax.broadcasted_iota(jnp.int32, (rows, rows), 1) - key_no
        allowed = (
            (offset >= 0)
            & (offset < WINDOW)
            & (key_no + e * rows >= 0)
            & (seg_col == seg_all[0, 0:1])
        )
        bias_out[distance] = jnp.where(allowed, 0.0, NEG)

        def attend(pair, carry, distance=distance):
            columns = pl.ds(pl.multiple_of(pair * LANES, LANES), LANES)
            value_columns = pl.ds(pl.multiple_of(width + pair * LANES, LANES), LANES)
            queries = q_out[:, columns]
            keys = kv_out[distance, :, columns]
            values_t = jnp.transpose(kv_out[distance, :, value_columns])
            for inner in range(2):
                head = pair * 2 + inner
                mine = jnp.where((lane // HEAD) == inner, queries, jnp.zeros_like(queries))
                value_t = values_t[inner * HEAD : (inner + 1) * HEAD]
                out_rows = pl.ds(pl.multiple_of(head * HEAD, HEAD), HEAD)
                blocks = (
                    [(slice(0, rows // 2), rows // 2), (slice(rows // 2, rows), rows)]
                    if distance == 0
                    else [(slice(0, rows), rows)]
                )
                for q_cut, key_count in blocks:
                    scores = mm(keys[:key_count], mine[q_cut], NT)
                    scores = scores + bias_out[distance, :key_count, q_cut]
                    peak = jnp.max(scores, axis=0, keepdims=True)
                    if distance:
                        before = top[pl.ds(head, 1), q_cut]
                        peak = jnp.maximum(before, peak)
                    weights = jnp.exp(scores - peak)
                    amount = jnp.sum(weights, axis=0, keepdims=True)
                    part = mm(value_t[:, :key_count], weights.astype(BF16))
                    if distance:
                        shrink = jnp.exp(before - peak)
                        amount = amount + total[pl.ds(head, 1), q_cut] * shrink
                        part = part + acc[out_rows, q_cut] * shrink
                    top[pl.ds(head, 1), q_cut] = peak
                    total[pl.ds(head, 1), q_cut] = amount
                    acc[out_rows, q_cut] = part
            return carry

        lax.fori_loop(0, HEADS // 2, attend, 0)

    lse_out[...] = top[...] + jnp.log(total[...])

    def finish(pair, carry):
        out_rows = pl.ds(pl.multiple_of(pair * LANES, LANES), LANES)
        scale = jnp.concatenate(
            [
                jnp.broadcast_to(1.0 / total[pl.ds(pair * 2 + inner, 1), :], (HEAD, rows))
                for inner in range(2)
            ],
            axis=0,
        )
        made = acc[out_rows, :] * scale
        att_t_out[out_rows, :] = made.astype(BF16)
        att_out[:, out_rows] = jnp.transpose(made).astype(BF16)
        return carry

    lax.fori_loop(0, HEADS // 2, finish, 0)
    for copy in sends[FAR_COTS[0] - 1 :] + far:
        copy.wait()


def front(layout, tokens, gain, w_qkv, cosine, sine, ids_row, seg_row, cot):
    rows, width = tokens.shape
    reach, peers = layout.reach, layout.peers
    dma = pltpu.SemaphoreType.DMA
    return pl.pallas_call(
        functools.partial(front_kernel, layout),
        out_shape=[
            jax.ShapeDtypeStruct((rows, width), BF16),
            jax.ShapeDtypeStruct((reach + 1, rows, 2 * width), BF16),
            jax.ShapeDtypeStruct((rows, width), BF16),
            jax.ShapeDtypeStruct((width, rows), BF16),
            jax.ShapeDtypeStruct((EXPERTS, rows), F32),
            jax.ShapeDtypeStruct((reach + 1, rows, rows), F32),
            jax.ShapeDtypeStruct((8, rows), jnp.int32),
            jax.ShapeDtypeStruct((peers, CAP, width), BF16),
            far_shape(layout, FAR_COTS[0], width),
        ],
        in_specs=[VMEM] * 8,
        out_specs=[VMEM] * 7 + [ANY] * 2,
        scratch_shapes=[
            pltpu.VMEM((rows, width), BF16),
            pltpu.VMEM((peers, CAP, width), BF16),
            pltpu.VMEM((reach + 1, 8, rows), F32),
            pltpu.VMEM((width, rows), F32),
            pltpu.VMEM((EXPERTS, rows), F32),
            pltpu.VMEM((EXPERTS, rows), F32),
            dma((reach + 1,)),
            dma((reach + 1,)),
            dma((reach + 1,)),
            dma((reach + 1,)),
            dma((peers,)),
            dma((peers,)),
            dma,
            dma((layout.outers - 1,)),
            dma((layout.outers - 1,)),
        ],
        compiler_params=pltpu.CompilerParams(
            collective_id=0, has_side_effects=True, vmem_limit_bytes=56 * MIB
        ),
        cost_estimate=pl.CostEstimate(flops=1 << 30, bytes_accessed=1 << 20, transcendentals=0),
        name="front",
    )(tokens, gain, w_qkv, cosine, sine, ids_row, seg_row, cot)


def split3(x):
    high = x.astype(BF16)
    rest = x - high.astype(F32)
    middle = rest.astype(BF16)
    return high, middle, (rest - middle.astype(F32)).astype(BF16)


def silu_parts(gate_pre):
    gate = 1.0 / (1.0 + jnp.exp(-gate_pre))
    return gate_pre * gate, gate * (1.0 + gate_pre * (1.0 - gate))


def middle_kernel(
    layout,
    att,
    tokens,
    w_out,
    gain,
    w_router_t,
    ids_row,
    target_row,
    cot,
    dense_gate,
    dense_up,
    dense_down,
    cots,
    hidden_out,
    low_out,
    mixed_out,
    grad_out,
    gate_out,
    up_out,
    down_out,
    rows_out,
    shares_out,
    far_out,
    send_rows,
    send_shares,
    low_t,
    gate_held,
    up_held,
    down_held,
    row_send,
    row_recv,
    share_send,
    share_recv,
    own_sems,
    far_send,
    far_recv,
    half_send,
    half_recv,
):
    rows, width = tokens.shape
    ff = dense_gate.shape[1]
    experts = layout.experts
    meet(layout)
    far = to_far(layout, cots, far_out, FAR_COTS[0], FAR_COTS[1], far_send, far_recv)
    for copy in far:
        copy.start()
    hidden_out[...] = tokens[...].astype(F32) + mm(att[...], w_out[...])
    low = normed(hidden_out[...], gain[...]).astype(BF16)
    low_out[...] = low
    logits = mm(w_router_t[...], low, NT)
    route = jnp.exp(logits - jnp.max(logits, axis=0, keepdims=True))
    route = route / jnp.sum(route, axis=0, keepdims=True)
    labels = lax.broadcasted_iota(jnp.int32, (EXPERTS, rows), 0)
    picked = [
        jnp.sum(jnp.where(labels == ids_row[k : k + 1], route, 0.0), axis=0, keepdims=True)
        for k in range(2)
    ]
    both = picked[0] + picked[1]
    shares = []
    for k in range(2):
        parts = split3(picked[k] / both)
        shares.append(
            jnp.concatenate(
                [part.astype(F32) for part in parts] + [jnp.zeros((5, rows), F32)], axis=0
            ).astype(BF16)
        )
    send_shares[...] = jnp.zeros_like(send_shares)
    for number in range(layout.peers):
        slots = number * CAP + lax.broadcasted_iota(jnp.int32, (CAP, rows), 0)
        first = jnp.where(slots == target_row[0:1], 1.0, 0.0).astype(BF16)
        second = jnp.where(slots == target_row[1:2], 1.0, 0.0).astype(BF16)
        send_rows[number] = mm(first + second, low).astype(BF16)
        share = mm(shares[0], first, NT) + mm(shares[1], second, NT)
        share = jnp.sum(share, axis=0, keepdims=True)
        send_shares[number, :, :CAP] = jnp.broadcast_to(share, (8, CAP))

    sends = to_peers(layout, send_rows, rows_out, row_send, row_recv)
    sends += to_peers(layout, send_shares, shares_out, share_send, share_recv)
    sends.append(pltpu.make_async_copy(send_rows.at[0], rows_out.at[0], own_sems.at[0]))
    sends.append(pltpu.make_async_copy(send_shares.at[0], shares_out.at[0], own_sems.at[1]))
    for copy in sends:
        copy.start()

    low_t[...] = jnp.transpose(low)
    mixed_out[...] = hidden_out[...]
    grad_out[...] = jnp.zeros_like(grad_out)
    part_width = ff // experts
    per_part = part_width // TILE
    half = experts // 2
    odd = bit_of("expert", 1)
    halvings = [
        Halving("expert", 1, held, taken, half_send.at[number], half_recv.at[number])
        for number, (held, taken) in enumerate(
            ((gate_held, gate_out), (up_held, up_out), (down_held, down_out))
        )
    ]

    def branch(step, carry):
        place = step // per_part
        part = 2 * (place % half) + (odd + 1 + place // half) % 2
        columns = pl.ds(pl.multiple_of(part * part_width + (step % per_part) * TILE, TILE), TILE)
        gate_w, up_w, down_w = dense_gate[:, columns], dense_up[:, columns], dense_down[columns, :]
        gate_pre = mm(low_out[...], gate_w)
        up_pre = mm(low_out[...], up_w)
        grad_act = mm(cot[...], down_w, NT)
        silu, slope = silu_parts(gate_pre)
        act = (silu * up_pre).astype(BF16)
        grad_gate = (grad_act * up_pre * slope).astype(BF16)
        grad_up = (grad_act * silu).astype(BF16)
        mixed_out[...] += mm(act, down_w)
        grad_out[...] += mm(grad_gate, gate_w, NT) + mm(grad_up, up_w, NT)
        inside = pl.ds(pl.multiple_of((step % per_part) * TILE, TILE), TILE)
        gate_held[part, :, inside] = mm(low_t[...], grad_gate).astype(BF16)
        up_held[part, :, inside] = mm(low_t[...], grad_up).astype(BF16)
        made = mm(act, cot[...], TN).astype(BF16)
        for other in range(experts):
            cut = width // experts
            down_held[other, columns, :] = made[:, other * cut : (other + 1) * cut]
        return carry

    lax.fori_loop(0, ff // (2 * TILE), branch, 0)
    for halving in halvings[:2]:
        halving.start()
    lax.fori_loop(ff // (2 * TILE), ff // TILE, branch, 0)
    halvings[2].start()
    for halving in halvings:
        halving.add()
    for copy in far:
        copy.wait()
    for copy in sends:
        copy.wait()


def middle(layout, att, tokens, w_out, gain, w_router_t, ids_row, target_row, cot, dense_gate, dense_up, dense_down, cots):
    rows, width = tokens.shape
    ff = dense_gate.shape[1]
    peers, experts = layout.peers, layout.experts
    dma = pltpu.SemaphoreType.DMA
    return pl.pallas_call(
        functools.partial(middle_kernel, layout),
        out_shape=[
            jax.ShapeDtypeStruct((rows, width), F32),
            jax.ShapeDtypeStruct((rows, width), BF16),
            jax.ShapeDtypeStruct((rows, width), F32),
            jax.ShapeDtypeStruct((rows, width), F32),
            jax.ShapeDtypeStruct((experts // 2, width, ff // experts), BF16),
            jax.ShapeDtypeStruct((experts // 2, width, ff // experts), BF16),
            jax.ShapeDtypeStruct((experts // 2, ff, width // experts), BF16),
            jax.ShapeDtypeStruct((peers, CAP, width), BF16),
            jax.ShapeDtypeStruct((peers, 8, LANES), F32),
            far_shape(layout, FAR_COTS[1] - FAR_COTS[0], width),
        ],
        in_specs=[VMEM] * 11 + [ANY],
        out_specs=[VMEM] * 7 + [ANY] * 3,
        scratch_shapes=[
            pltpu.VMEM((peers, CAP, width), BF16),
            pltpu.VMEM((peers, 8, LANES), F32),
            pltpu.VMEM((width, rows), BF16),
            pltpu.VMEM((experts, width, ff // experts), BF16),
            pltpu.VMEM((experts, width, ff // experts), BF16),
            pltpu.VMEM((experts, ff, width // experts), BF16),
            dma((peers,)),
            dma((peers,)),
            dma((peers,)),
            dma((peers,)),
            dma((2,)),
            dma((layout.outers - 1,)),
            dma((layout.outers - 1,)),
            dma((3, experts // 2)),
            dma((3, experts // 2)),
        ],
        compiler_params=pltpu.CompilerParams(
            collective_id=1, has_side_effects=True, vmem_limit_bytes=56 * MIB
        ),
        cost_estimate=pl.CostEstimate(flops=1 << 30, bytes_accessed=1 << 20, transcendentals=0),
        name="middle",
    )(att, tokens, w_out, gain, w_router_t, ids_row, target_row, cot, dense_gate, dense_up, dense_down, cots)


def share_column(share_row):
    across = lax.broadcasted_iota(jnp.int32, (CAP, CAP), 1)
    down = lax.broadcasted_iota(jnp.int32, (CAP, CAP), 0)
    return jnp.sum(jnp.where(across == down, share_row, 0.0), axis=1, keepdims=True)


def own_share(layout):
    return lax.rem(lax.axis_index("group"), layout.share)


def experts_kernel(
    layout,
    rows_in,
    cots,
    shares,
    gate_any,
    up_any,
    down_any,
    gate_held,
    up_held,
    down_held,
    rows_any,
    cots_any,
    shares_any,
    back_out,
    grad_back,
    gate_sum,
    up_sum,
    down_sum,
    far_cots,
    far_rows,
    far_shares,
    gate_w,
    up_w,
    down_w,
    scaled,
    acc,
    grad_acc,
    send_out,
    send_grad,
    load_sems,
    out_send,
    out_recv,
    grad_send,
    grad_recv,
    own_sems,
    far_send,
    far_recv,
    half_send,
    half_recv,
    *steps,
):
    peers = layout.peers
    width, ff = gate_w.shape
    mine = own_share(layout)
    loads = [
        pltpu.make_async_copy(source.at[mine], target, load_sems.at[number])
        for number, (source, target) in enumerate(
            ((gate_any, gate_w), (up_any, up_w), (down_any, down_w))
        )
    ]
    for copy in loads:
        copy.start()
    meet(layout)
    far = (
        to_far(layout, cots_any, far_cots, FAR_COTS[1], FAR_COTS[2], far_send.at[0], far_recv.at[0])
        + to_far(layout, rows_any, far_rows, 0, FAR_ROWS[0], far_send.at[1], far_recv.at[1])
        + to_far(layout, shares_any, far_shares, 0, peers, far_send.at[2], far_recv.at[2])
    )
    for copy in far:
        copy.start()
    chains = []
    for number, (held, made) in enumerate(
        ((gate_held, gate_sum), (up_held, up_sum), (down_held, down_sum))
    ):
        chain, bit, level = [], 2, 0
        while bit < layout.experts:
            last = 2 * bit == layout.experts
            taken = made if last else steps[number]
            chain.append(
                Halving(
                    "expert",
                    bit,
                    held,
                    taken,
                    half_send.at[number, level],
                    half_recv.at[number, level],
                )
            )
            held, bit, level = taken, 2 * bit, level + 1
        chains.append(chain)
    for chain in chains:
        chain[0].start()
    for number in range(peers):
        column = share_column(shares[number, 0:1, :CAP])
        scaled[number] = (cots[number].astype(F32) * column).astype(BF16)
    for copy in loads:
        copy.wait()

    chunk = 2 * TILE
    outs = to_peers(layout, send_out, back_out, out_send, out_recv)
    grads = to_peers(layout, send_grad, grad_back, grad_send, grad_recv)
    outs.insert(0, pltpu.make_async_copy(send_out.at[0], back_out.at[0], own_sems.at[0]))
    grads.insert(0, pltpu.make_async_copy(send_grad.at[0], grad_back.at[0], own_sems.at[1]))
    high = peers
    for count in (8, 4, 4):
        pieces = slice(high - count, high)
        high -= count
        acc[: count * CAP] = jnp.zeros((count * CAP, width), F32)
        grad_acc[: count * CAP] = jnp.zeros((count * CAP, width), F32)

        def turn(step, carry, pieces=pieces, count=count):
            columns = pl.ds(pl.multiple_of(step * chunk, chunk), chunk)
            n = rows_in[pieces].reshape(count * CAP, width)
            grad = scaled[pieces].reshape(count * CAP, width)
            gate_pre = mm(n, gate_w[:, columns])
            up_pre = mm(n, up_w[:, columns])
            grad_act = mm(grad, down_w[columns, :], NT)
            silu, slope = silu_parts(gate_pre)
            act = (silu * up_pre).astype(BF16)
            grad_gate = (grad_act * up_pre * slope).astype(BF16)
            grad_up = (grad_act * silu).astype(BF16)
            acc[: count * CAP] += mm(act, down_w[columns, :])
            grad_acc[: count * CAP] += mm(grad_gate, gate_w[:, columns], NT) + mm(
                grad_up, up_w[:, columns], NT
            )
            return carry

        lax.fori_loop(0, ff // chunk, turn, 0)
        send_out[pieces] = acc[: count * CAP].astype(BF16).reshape(count, CAP, width)
        send_grad[pieces] = grad_acc[: count * CAP].astype(BF16).reshape(count, CAP, width)
        for copy in outs[pieces] + grads[pieces]:
            copy.start()
    for level in range(len(chains[0])):
        for chain in chains:
            chain[level].add()
            if level + 1 < len(chain):
                chain[level + 1].start()
    for copy in outs + grads + far:
        copy.wait()


def run_experts(layout, rows_in, cots, shares, expert_gate, expert_up, expert_down, sums):
    peers, outers = layout.peers, layout.outers
    _, width, ff = expert_gate.shape
    dma = pltpu.SemaphoreType.DMA
    half = layout.experts // 2
    levels = half.bit_length() - 1
    last = [jax.ShapeDtypeStruct((1,) + one.shape[1:], BF16) for one in sums]
    steps = []
    if levels == 2:
        steps = [pltpu.VMEM((half // 2,) + one.shape[1:], BF16) for one in sums]
    return pl.pallas_call(
        functools.partial(experts_kernel, layout),
        out_shape=[jax.ShapeDtypeStruct((peers, CAP, width), BF16)] * 2
        + last
        + [
            far_shape(layout, FAR_COTS[2] - FAR_COTS[1], width),
            far_shape(layout, FAR_ROWS[0], width),
            jax.ShapeDtypeStruct((outers - 1, peers, 8, LANES), F32),
        ],
        in_specs=[VMEM] * 3 + [ANY] * 3 + [VMEM] * 3 + [ANY] * 3,
        out_specs=[ANY] * 2 + [VMEM] * 3 + [ANY] * 3,
        scratch_shapes=[
            pltpu.VMEM((width, ff), BF16),
            pltpu.VMEM((width, ff), BF16),
            pltpu.VMEM((ff, width), BF16),
            pltpu.VMEM((peers, CAP, width), BF16),
            pltpu.VMEM((8 * CAP, width), F32),
            pltpu.VMEM((8 * CAP, width), F32),
            pltpu.VMEM((peers, CAP, width), BF16),
            pltpu.VMEM((peers, CAP, width), BF16),
            dma((3,)),
            dma((peers,)),
            dma((peers,)),
            dma((peers,)),
            dma((peers,)),
            dma((2,)),
            dma((3, outers - 1)),
            dma((3, outers - 1)),
            dma((3, levels, half // 2)),
            dma((3, levels, half // 2)),
            *steps,
        ],
        compiler_params=pltpu.CompilerParams(
            collective_id=2, has_side_effects=True, vmem_limit_bytes=58 * MIB
        ),
        cost_estimate=pl.CostEstimate(flops=1 << 30, bytes_accessed=1 << 20, transcendentals=0),
        name="experts",
    )(
        rows_in,
        cots,
        shares,
        expert_gate,
        expert_up,
        expert_down,
        *sums,
        rows_in,
        cots,
        shares,
    )


def combine_kernel(
    back,
    grad_back,
    target_row,
    ids_col,
    hidden,
    mixed_in,
    grad_in,
    low,
    cot,
    gain,
    w_router,
    w_out,
    att_t,
    mixed_out,
    grad_hidden_out,
    grad_att_out,
    proj_out,
    small_out,
):
    rows, width = hidden.shape
    peers = back.shape[0]
    slots = peers * CAP
    columns = jnp.transpose(
        jnp.concatenate(
            [target_row[...].astype(F32), jnp.zeros((LANES - 8, rows), F32)], axis=0
        )
    )
    slot_no = lax.broadcasted_iota(jnp.int32, (rows, slots), 1).astype(F32)
    cot_float = cot[...].astype(F32)
    logits = mm(low[...], w_router[...])
    route = jnp.exp(logits - jnp.max(logits, axis=1, keepdims=True))
    route = route / jnp.sum(route, axis=1, keepdims=True)
    labels = lax.broadcasted_iota(jnp.int32, (rows, EXPERTS), 1)
    masks = [labels == ids_col[:, k : k + 1] for k in range(2)]
    picked = [jnp.sum(jnp.where(mask, route, 0.0), axis=1, keepdims=True) for mask in masks]
    both = picked[0] + picked[1]
    chosen, shares, grads = [], [], []
    mixed = mixed_in[...]
    for k in range(2):
        chosen.append(jnp.where(slot_no == columns[:, k : k + 1], 1.0, 0.0).astype(BF16))
        fetched = mm(chosen[k], back[...].reshape(slots, width))
        shares.append(picked[k] / both)
        mixed = mixed + shares[k] * fetched
        grads.append(jnp.sum(cot_float * fetched, axis=1, keepdims=True))
    mixed_out[...] = mixed.astype(BF16)
    mean = grads[0] * shares[0] + grads[1] * shares[1]
    grad_route = jnp.zeros_like(route)
    for k in range(2):
        grad_route = grad_route + jnp.where(masks[k], (grads[k] - mean) / both, 0.0)
    grad_logits = route * (grad_route - jnp.sum(route * grad_route, axis=1, keepdims=True))
    grad_logits = grad_logits.astype(BF16)
    small_out[...] = jnp.zeros_like(small_out)
    small_out[:EXPERTS] = mm(grad_logits, low[...], TN)
    grad = grad_in[...] + mm(chosen[0] + chosen[1], grad_back[...].reshape(slots, width))
    grad = grad + mm(grad_logits, w_router[...], NT)
    h = hidden[...]
    scale = lax.rsqrt(jnp.mean(h * h, axis=-1, keepdims=True) + epsilon)
    small_out[EXPERTS : EXPERTS + 1] = jnp.sum(grad * h * scale, axis=0, keepdims=True)
    grad = grad * gain[...]
    grad = scale * grad - h * (scale * scale * scale) * jnp.mean(grad * h, axis=-1, keepdims=True)
    grad = cot_float + grad
    grad_hidden_out[...] = grad
    grad_low = grad.astype(BF16)
    grad_att_out[...] = mm(grad_low, w_out[...], NT).astype(BF16)
    made = mm(att_t[...], grad_low).astype(BF16)
    parts = proj_out.shape[0]
    cut = width // parts
    for part in range(parts):
        proj_out[part] = made[:, part * cut : (part + 1) * cut]


def combine(layout, back, grad_back, target_row, ids_col, hidden, mixed_in, grad_in, low, cot, gain, w_router, w_out, att_t):
    rows, width = hidden.shape
    experts = layout.experts
    return pl.pallas_call(
        combine_kernel,
        out_shape=[
            jax.ShapeDtypeStruct((rows, width), BF16),
            jax.ShapeDtypeStruct((rows, width), F32),
            jax.ShapeDtypeStruct((rows, width), BF16),
            jax.ShapeDtypeStruct((experts, width, width // experts), BF16),
            jax.ShapeDtypeStruct((SMALL, width), F32),
        ],
        in_specs=[VMEM] * 13,
        out_specs=[VMEM] * 5,
        compiler_params=pltpu.CompilerParams(vmem_limit_bytes=56 * MIB),
        cost_estimate=pl.CostEstimate(flops=1 << 30, bytes_accessed=1 << 20, transcendentals=0),
        name="combine",
    )(back, grad_back, target_row, ids_col, hidden, mixed_in, grad_in, low, cot, gain, w_router, w_out, att_t)


def rope_back(grad, cosine, sine):
    lane = lax.broadcasted_iota(jnp.int32, grad.shape, 1)
    turned = grad * sine
    other = jnp.where(
        lane % HEAD < HEAD // 2,
        pltpu.roll(turned, LANES - HEAD // 2, 1),
        pltpu.roll(turned, HEAD // 2, 1),
    )
    return grad * cosine + other


def back_kernel(
    layout,
    q_in,
    kv_in,
    bias,
    lse,
    att_t,
    grad_att,
    tokens,
    gain,
    w_qkv,
    cosine,
    sine,
    grad_hidden,
    gate_held,
    up_held,
    down_held,
    rows_any,
    tokens_out,
    qkv_out,
    gain_out,
    gate_sum,
    up_sum,
    down_sum,
    far_out,
    halo_send,
    halo_recv,
    own_kv,
    packed,
    normed_t,
    send_sems,
    recv_sems,
    far_send,
    far_recv,
    half_send,
    half_recv,
):
    rows, width = tokens.shape
    reach, experts = layout.reach, layout.experts
    e = lax.axis_index("expert")
    pairs = HEADS // 2
    lane = lax.broadcasted_iota(jnp.int32, (rows, LANES), 1)
    meet(layout)
    far = to_far(layout, rows_any, far_out, FAR_ROWS[0], FAR_ROWS[1], far_send, far_recv)
    for copy in far:
        copy.start()
    halvings = [
        Halving("group", 1, held, taken, half_send.at[number], half_recv.at[number])
        for number, (held, taken) in enumerate(
            ((gate_held, gate_sum), (up_held, up_sum), (down_held, down_sum))
        )
    ]
    for halving in halvings:
        halving.start()

    def halo(distance, pair):
        return pltpu.make_async_remote_copy(
            src_ref=halo_send.at[distance - 1, pair],
            dst_ref=halo_recv.at[distance - 1, pair],
            send_sem=send_sems.at[distance - 1, pair],
            recv_sem=recv_sems.at[distance - 1, pair],
            device_id={"expert": lax.rem(e + experts - distance, experts)},
            device_id_type=MESH,
        )

    def heads(pair, carry):
        columns = pl.ds(pl.multiple_of(pair * LANES, LANES), LANES)
        value_columns = pl.ds(pl.multiple_of(width + pair * LANES, LANES), LANES)
        queries, grads = q_in[:, columns], grad_att[:, columns]
        grads_t = jnp.transpose(grads.astype(F32))
        shrunk = grads_t * att_t[columns, :].astype(F32)
        grad_q = [None, None]
        for distance in range(reach, -1, -1):
            keys = kv_in[distance, :, columns]
            values = kv_in[distance, :, value_columns]
            keys_t = jnp.transpose(keys)
            grad_k = grad_v = None
            for inner in range(2):
                head = pair * 2 + inner
                cut = slice(inner * HEAD, (inner + 1) * HEAD)
                mine = (lane // HEAD) == inner
                query = jnp.where(mine, queries, jnp.zeros_like(queries))
                grad = jnp.where(mine, grads, jnp.zeros_like(grads))
                total = jnp.sum(shrunk[cut], axis=0, keepdims=True)
                scores = mm(keys, query, NT) + bias[distance]
                probs = jnp.exp(scores - lse[pl.ds(head, 1), :])
                grad_probs = mm(values, grad, NT)
                grad_scores = (probs * (grad_probs - total)).astype(BF16)
                part_v = mm(probs.astype(BF16), grad)
                part_k = mm(grad_scores, query)
                part_q = mm(keys_t[cut], grad_scores)
                grad_v = part_v if grad_v is None else grad_v + part_v
                grad_k = part_k if grad_k is None else grad_k + part_k
                grad_q[inner] = part_q if grad_q[inner] is None else grad_q[inner] + part_q
            if distance:
                halo_send[distance - 1, pair, 0] = grad_k.astype(BF16)
                halo_send[distance - 1, pair, 1] = grad_v.astype(BF16)
                halo(distance, pair).start()
            else:
                own_kv[pair, 0] = grad_k
                own_kv[pair, 1] = grad_v
        grad = jnp.transpose(jnp.concatenate(grad_q, axis=0)) * HEAD ** (-0.5)
        packed[:, columns] = rope_back(grad, cosine[...], sine[...]).astype(BF16)
        return carry

    lax.fori_loop(0, pairs, heads, 0)
    x = tokens[...].astype(F32)
    normed_t[...] = jnp.transpose(normed(x, gain[...])).astype(BF16)

    def merge(pair, carry):
        grad_k, grad_v = own_kv[pair, 0], own_kv[pair, 1]
        for distance in range(1, reach + 1):
            halo(distance, pair).wait()
            grad_k = grad_k + halo_recv[distance - 1, pair, 0].astype(F32)
            grad_v = grad_v + halo_recv[distance - 1, pair, 1].astype(F32)
        columns = pl.ds(pl.multiple_of(width + pair * LANES, LANES), LANES)
        packed[:, columns] = rope_back(grad_k, cosine[...], sine[...]).astype(BF16)
        columns = pl.ds(pl.multiple_of(2 * width + pair * LANES, LANES), LANES)
        packed[:, columns] = grad_v.astype(BF16)
        return carry

    lax.fori_loop(0, pairs, merge, 0)
    parts = qkv_out.shape[0]
    cut = 3 * width // parts
    for part in range(parts):
        piece = packed[:, part * cut : (part + 1) * cut]
        qkv_out[part] = mm(normed_t[...], piece).astype(BF16)
    grad = mm(packed[...], w_qkv[...], NT)
    scale = lax.rsqrt(jnp.mean(x * x, axis=-1, keepdims=True) + epsilon)
    gain_out[...] = jnp.sum(grad * x * scale, axis=0, keepdims=True)
    grad = grad * gain[...]
    grad = scale * grad - x * (scale * scale * scale) * jnp.mean(grad * x, axis=-1, keepdims=True)
    tokens_out[...] = grad_hidden[...] + grad
    for halving in halvings:
        halving.add()
    for copy in far:
        copy.wait()


def back(layout, q_in, kv_in, bias, lse, att_t, grad_att, tokens, gain, w_qkv, cosine, sine, grad_hidden, sums, rows_in):
    rows, width = tokens.shape
    reach, experts = layout.reach, layout.experts
    dma = pltpu.SemaphoreType.DMA
    pairs = HEADS // 2
    return pl.pallas_call(
        functools.partial(back_kernel, layout),
        out_shape=[
            jax.ShapeDtypeStruct((rows, width), F32),
            jax.ShapeDtypeStruct((experts, width, 3 * width // experts), BF16),
            jax.ShapeDtypeStruct((1, width), F32),
            *[jax.ShapeDtypeStruct((layout.groups // 2,) + one.shape[1:], BF16) for one in sums],
            far_shape(layout, FAR_ROWS[1] - FAR_ROWS[0], width),
        ],
        in_specs=[VMEM] * 15 + [ANY],
        out_specs=[VMEM] * 6 + [ANY],
        scratch_shapes=[
            pltpu.VMEM((reach, pairs, 2, rows, LANES), BF16),
            pltpu.VMEM((reach, pairs, 2, rows, LANES), BF16),
            pltpu.VMEM((pairs, 2, rows, LANES), F32),
            pltpu.VMEM((rows, 3 * width), BF16),
            pltpu.VMEM((width, rows), BF16),
            dma((reach, pairs)),
            dma((reach, pairs)),
            dma((layout.outers - 1,)),
            dma((layout.outers - 1,)),
            dma((3, layout.groups // 2)),
            dma((3, layout.groups // 2)),
        ],
        compiler_params=pltpu.CompilerParams(
            collective_id=3, has_side_effects=True, vmem_limit_bytes=56 * MIB
        ),
        cost_estimate=pl.CostEstimate(flops=1 << 30, bytes_accessed=1 << 20, transcendentals=0),
        name="back",
    )(q_in, kv_in, bias, lse, att_t, grad_att, tokens, gain, w_qkv, cosine, sine, grad_hidden, *sums, rows_in)


def weights_kernel(layout, *refs):
    share, outers, peers = layout.share, layout.outers, layout.peers
    (
        rows_own,
        cots_own,
        shares_own,
        rows_a,
        rows_b,
        cots_a,
        cots_b,
        cots_c,
        shares_far,
        gate_any,
        up_any,
        down_any,
        *terms,
    ) = refs[:17]
    small_in = refs[17]
    rows_c, gate_out, up_out, down_out = refs[18:22]
    sums_out = refs[22:27]
    small_out = refs[27]
    (
        gate_w,
        up_w,
        gate_t,
        up_t,
        down_w,
        rows_buf,
        cots_buf,
        shares_buf,
        accs,
        sends,
        takes,
        small_sums,
        small_takes,
        load_sems,
        piece_sems,
        send_sems,
        recv_sems,
        far_send,
        far_recv,
        small_send,
        small_recv,
    ) = refs[28:49]
    rest = list(refs[49:])
    width = gate_w.shape[0]
    ff = gate_any.shape[2]
    span = ff // outers
    cut = ff // layout.groups
    group = lax.axis_index("group")
    mine = own_share(layout)
    begin = pl.multiple_of((group // share) * span, span)
    loads = [
        pltpu.make_async_copy(gate_any.at[mine, :, pl.ds(begin, span)], gate_w, load_sems.at[0]),
        pltpu.make_async_copy(up_any.at[mine, :, pl.ds(begin, span)], up_w, load_sems.at[1]),
        pltpu.make_async_copy(down_any.at[mine, pl.ds(begin, span), :], down_w, load_sems.at[2]),
    ]

    def fetch(turn, outer):
        slot = (turn * outers + outer) % 2
        row_cuts, cot_cuts = (0, *FAR_ROWS), (0, *FAR_COTS)
        if outer == 0:
            sources = [
                (rows_own, rows_buf.at[slot]),
                (cots_own, cots_buf.at[slot]),
                (shares_own, shares_buf.at[slot]),
            ]
        else:
            sources = [
                (one.at[outer - 1], target.at[slot, cuts[place] : cuts[place + 1]])
                for parts, cuts, target in (
                    ((rows_a, rows_b, rows_c), row_cuts, rows_buf),
                    ((cots_a, cots_b, cots_c), cot_cuts, cots_buf),
                )
                for place, one in enumerate(parts)
            ]
            sources.append((shares_far.at[outer - 1], shares_buf.at[slot]))
        return [
            pltpu.make_async_copy(source, target, piece_sems.at[slot, number])
            for number, (source, target) in enumerate(sources)
        ]

    for copy in loads + fetch(0, 0):
        copy.start()
    meet(layout)
    far = to_far(layout, rows_own, rows_c, FAR_ROWS[1], FAR_ROWS[2], far_send, far_recv)
    for copy in far:
        copy.start()

    expert_bits = [("expert", 1 << n) for n in range(layout.experts.bit_length() - 1)]
    group_bits = [("group", 1 << n) for n in range(layout.groups.bit_length() - 1)]
    chains = []
    for number, term in enumerate(terms):
        bits = group_bits[1:] if number < 3 else expert_bits + group_bits
        held, chain = term, []
        for axis, bit in bits:
            if axis == "group" and len(held.shape) == 4:
                held = held.at[0]
            taken, to_sems, from_sems = rest.pop(0), rest.pop(0), rest.pop(0)
            chain.append(Halving(axis, bit, held, taken, to_sems, from_sems))
            held = taken
        chains.append(chain)
    small_sums[0] = small_in[...]

    def small_copy(level):
        axis, bit = (expert_bits + group_bits)[level]
        return pltpu.make_async_remote_copy(
            src_ref=small_sums.at[level],
            dst_ref=small_takes.at[level],
            send_sem=small_send.at[level],
            recv_sem=small_recv.at[level],
            device_id={axis: flipped(lax.axis_index(axis), bit)},
            device_id_type=MESH,
        )

    levels = len(expert_bits + group_bits)

    def advance(level):
        for number, chain in enumerate(chains):
            if 0 < level <= len(chain):
                chain[level - 1].add(sums_out[number] if level == len(chain) else None)
            if level < len(chain):
                chain[level].start()
        if level:
            small_copy(level - 1).wait()
            made = small_sums[level - 1] + small_takes[level - 1]
            if level < levels:
                small_sums[level] = made
            else:
                small_out[...] = made
        if level < levels:
            small_copy(level).start()

    advance(0)
    points = share * outers
    marks = [max(0, (points * at) // 8 - 1) for at in (2, 6, 7, 8)]
    done = 1

    for copy in loads:
        copy.wait()
    gate_t[...] = jnp.transpose(gate_w[...])
    up_t[...] = jnp.transpose(up_w[...])
    accs[...] = jnp.zeros_like(accs)
    count = 8
    blocks = peers // count

    def add(slot, chunk, block):
        pieces = pl.ds(block * count, count)
        n = rows_buf[slot, pieces].reshape(count * CAP, width)
        grad = cots_buf[slot, pieces].reshape(count * CAP, width)
        base = pl.multiple_of(chunk * cut, cut)
        gate_pre = mm(gate_t[pl.ds(base, cut), :], n, NT)
        up_pre = mm(up_t[pl.ds(base, cut), :], n, NT)
        grad_act = mm(down_w[pl.ds(base, cut), :], grad, NT)
        silu, slope = silu_parts(gate_pre)
        act = (silu * up_pre).astype(BF16)
        grad_gate = (grad_act * up_pre * slope).astype(BF16)
        grad_up = (grad_act * silu).astype(BF16)
        accs[0] += mm(grad_gate, n)
        accs[1] += mm(grad_up, n)
        accs[2] += mm(act, grad)

    copies = []
    turns = [*range(share - 1, 0, -1), 0]
    for place, turn in enumerate(turns):
        owner = flipped(mine, turn)
        accs[...] = jnp.zeros_like(accs)
        for outer in range(outers):
            slot = (place * outers + outer) % 2
            if place == 0 and outer:
                if outer == 1:
                    for copy in far:
                        copy.wait()
                for copy in fetch(place, outer):
                    copy.start()
            for copy in fetch(place, outer):
                copy.wait()
            following = place * outers + outer + 1
            if outers <= following < points:
                for copy in fetch(following // outers, following % outers):
                    copy.start()

            def scale(number, carry, slot=slot):
                column = share_column(shares_buf[slot, number, 0:1, :CAP])
                cots_buf[slot, number] = (cots_buf[slot, number].astype(F32) * column).astype(BF16)
                return carry

            def step(number, carry, slot=slot, owner=owner):
                add(slot, owner, number)
                return carry

            lax.fori_loop(0, peers, scale, 0)
            lax.fori_loop(0, blocks, step, 0)
            while done <= len(marks) and marks[done - 1] <= place * outers + outer:
                if done < levels:
                    advance(done)
                done += 1
        if turn:
            for which in range(3):
                sends[turn - 1, which] = accs[which].astype(BF16)
                copy = pltpu.make_async_remote_copy(
                    src_ref=sends.at[turn - 1, which],
                    dst_ref=takes.at[turn - 1, which],
                    send_sem=send_sems.at[turn - 1, which],
                    recv_sem=recv_sems.at[turn - 1, which],
                    device_id={"group": flipped(group, turn)},
                    device_id_type=MESH,
                )
                copy.start()
                copies.append((turn, which, copy))
        else:
            gate_out[owner] = jnp.transpose(accs[0])
            up_out[owner] = jnp.transpose(accs[1])
            down_out[owner] = accs[2]
    for level in range(done, levels + 1):
        advance(level)
    for turn, which, copy in copies:
        copy.wait()
        owner = flipped(mine, turn)
        got = takes[turn - 1, which].astype(F32)
        if which == 2:
            down_out[owner] = got
        else:
            (gate_out, up_out)[which][owner] = jnp.transpose(got)


def weights(layout, own, rows_far, cots_far, shares_far, expert_weights, terms, small):
    share, outers, peers = layout.share, layout.outers, layout.peers
    experts, width, ff = expert_weights[0].shape
    span = ff // outers
    cut = ff // layout.groups
    dma = pltpu.SemaphoreType.DMA
    expert_levels = layout.experts.bit_length() - 1
    group_levels = layout.groups.bit_length() - 1
    levels = expert_levels + group_levels
    scratch, outs = [], []
    for number, term in enumerate(terms):
        block = term.shape[-2:]
        shapes = []
        if number >= 3:
            shapes += [
                (layout.experts >> n, layout.groups) + block for n in range(1, expert_levels + 1)
            ]
        first = 2 if number < 3 else 1
        shapes += [(layout.groups >> n,) + block for n in range(first, group_levels + 1)]
        for shape in shapes:
            scratch += [pltpu.VMEM(shape, BF16), dma((shape[0],)), dma((shape[0],))]
        outs.append(jax.ShapeDtypeStruct(block, F32))
    return pl.pallas_call(
        functools.partial(weights_kernel, layout),
        out_shape=[
            far_shape(layout, FAR_ROWS[2] - FAR_ROWS[1], width),
            jax.ShapeDtypeStruct((experts, width, cut), F32),
            jax.ShapeDtypeStruct((experts, width, cut), F32),
            jax.ShapeDtypeStruct((experts, cut, width), F32),
            *outs,
            jax.ShapeDtypeStruct((SMALL, width), F32),
        ],
        in_specs=[ANY] * 12 + [VMEM] * 6,
        out_specs=[ANY] + [VMEM] * 9,
        scratch_shapes=[
            pltpu.VMEM((width, span), BF16),
            pltpu.VMEM((width, span), BF16),
            pltpu.VMEM((span, width), BF16),
            pltpu.VMEM((span, width), BF16),
            pltpu.VMEM((span, width), BF16),
            pltpu.VMEM((2, peers, CAP, width), BF16),
            pltpu.VMEM((2, peers, CAP, width), BF16),
            pltpu.VMEM((2, peers, 8, LANES), F32),
            pltpu.VMEM((3, cut, width), F32),
            pltpu.VMEM((share - 1, 3, cut, width), BF16),
            pltpu.VMEM((share - 1, 3, cut, width), BF16),
            pltpu.VMEM((levels, SMALL, width), F32),
            pltpu.VMEM((levels, SMALL, width), F32),
            dma((3,)),
            dma((2, 7)),
            dma((share - 1, 3)),
            dma((share - 1, 3)),
            dma((outers - 1,)),
            dma((outers - 1,)),
            dma((levels,)),
            dma((levels,)),
            *scratch,
        ],
        compiler_params=pltpu.CompilerParams(
            collective_id=4, has_side_effects=True, vmem_limit_bytes=60 * MIB
        ),
        cost_estimate=pl.CostEstimate(flops=1 << 30, bytes_accessed=1 << 20, transcendentals=0),
        name="weights",
    )(*own, *rows_far, *cots_far, shares_far, *expert_weights, *terms, small)


def by_group(layout, terms):
    parts, rows, width = terms.shape
    return terms.reshape(parts, layout.groups, rows // layout.groups, width)


def local(
    tokens,
    gain_attn,
    w_qkv,
    w_out,
    gain_ffn,
    w_router,
    expert_gate,
    expert_up,
    expert_down,
    dense_gate,
    dense_up,
    dense_down,
    expert_ids,
    segments,
    cotangent,
):
    rows, width = tokens.shape
    layout = Layout(lax.axis_size("group"), lax.axis_size("expert"), rows)
    group, expert = lax.axis_index("group"), lax.axis_index("expert")
    share = layout.share
    relative = ((expert_ids % share) ^ (group % share)) * layout.experts
    relative = relative + ((expert_ids // share) ^ expert)
    fill = jnp.full((6, rows), -1, jnp.int32)
    relative_row = jnp.concatenate([jnp.transpose(relative), fill], axis=0)
    ids_row = jnp.concatenate([jnp.transpose(expert_ids), fill], axis=0)
    seg_row = jnp.broadcast_to(segments.astype(F32)[None], (8, rows))
    places = (expert * rows + jnp.arange(rows, dtype=jnp.int32)).astype(F32)
    lane = jnp.arange(LANES)
    power = (lane % (HEAD // 2)).astype(F32) / (HEAD // 2)
    angles = places[:, None] * (10000.0 ** (-power))[None]
    cosine = jnp.cos(angles)
    sine = jnp.sin(angles) * jnp.where(lane % HEAD < HEAD // 2, -1.0, 1.0)[None]

    q, kv, att, att_t, lse, bias, target, cots, cots_a = front(
        layout, tokens, gain_attn[None], w_qkv, cosine, sine, relative_row, seg_row, cotangent
    )
    hidden, low, mixed, grad_low, gate_terms, up_terms, down_terms, rows_in, shares, cots_b = middle(
        layout,
        att,
        tokens,
        w_out,
        gain_ffn[None],
        jnp.transpose(w_router),
        ids_row,
        target,
        cotangent,
        dense_gate,
        dense_up,
        dense_down,
        cots,
    )
    came_back, grad_back, *sums, cots_c, rows_a, shares_far = run_experts(
        layout,
        rows_in,
        cots,
        shares,
        expert_gate,
        expert_up,
        expert_down,
        (gate_terms, up_terms, down_terms),
    )
    mixed_out, grad_hidden, grad_att, proj_terms, small = combine(
        layout,
        came_back,
        grad_back,
        target,
        expert_ids,
        hidden,
        mixed,
        grad_low,
        low,
        cotangent,
        gain_ffn[None],
        w_router,
        w_out,
        att_t,
    )
    grad_tokens, qkv_terms, attn_gain_term, *sums, rows_b = back(
        layout,
        q,
        kv,
        bias,
        lse,
        att_t,
        grad_att,
        tokens,
        gain_attn[None],
        w_qkv,
        cosine,
        sine,
        grad_hidden,
        [by_group(layout, one)[0] for one in sums],
        rows_in,
    )
    small = lax.dynamic_update_slice(small, attn_gain_term, (EXPERTS + 1, 0))
    _, gate_w, up_w, down_w, gate_sum, up_sum, down_sum, proj_sum, qkv_sum, small = weights(
        layout,
        (rows_in, cots, shares),
        (rows_a, rows_b),
        (cots_a, cots_b, cots_c),
        shares_far,
        (expert_gate, expert_up, expert_down),
        [*sums, by_group(layout, proj_terms), by_group(layout, qkv_terms)],
        small,
    )
    return (
        mixed_out,
        grad_tokens,
        small[EXPERTS + 1],
        qkv_sum,
        proj_sum,
        small[EXPERTS],
        jnp.transpose(small[:EXPERTS]),
        gate_w,
        up_w,
        down_w,
        gate_sum,
        up_sum,
        down_sum,
    )


def solution(mesh):
    in_specs = (
        P(("group", "expert"), None),
        P(),
        P(),
        P(),
        P(),
        P(),
        P("expert", None, None),
        P("expert", None, None),
        P("expert", None, None),
        P(),
        P(),
        P(),
        P(("group", "expert"), None),
        P(("group", "expert")),
        P(("group", "expert"), None),
    )
    out_specs = (
        P(("group", "expert"), None),
        P(("group", "expert"), None),
        P(),
        P("group", "expert"),
        P("group", "expert"),
        P(),
        P(),
        P("expert", None, "group"),
        P("expert", None, "group"),
        P("expert", "group", None),
        P("group", "expert"),
        P("group", "expert"),
        P("group", "expert"),
    )
    return jax.shard_map(local, mesh=mesh, in_specs=in_specs, out_specs=out_specs, check_vma=False)
```

```python
import functools

import jax
import jax.numpy as jnp
from jax import lax
from jax.experimental import pallas as pl
from jax.experimental.pallas import tpu as pltpu
from jax.sharding import PartitionSpec as P

HEADS = 12
HEAD = 64
EXPERTS = 16
WINDOW = 1024
CAP = 80
QUARTERS = 4
LANES = 128
TILE = 256
SMALL = EXPERTS + 8
NEG = -1e30
FAR_ROWS = (4, 12, 16)

epsilon = 1e-06
F32 = jnp.float32
BF16 = jnp.bfloat16
MESH = pl.DeviceIdType.MESH
VMEM = pl.BlockSpec(memory_space=pltpu.VMEM)
ANY = pl.BlockSpec(memory_space=pl.ANY)
MIB = 1 << 20


def dims(spec):
    left, right = spec
    return (((left,), (right,)), ((), ()))


NN = dims((1, 0))
NT = dims((1, 1))
TN = dims((0, 0))


def mm(a, b, how=NN):
    return lax.dot_general(a, b, how, preferred_element_type=F32)


def flipped(x, mask):
    bit = 1
    while bit <= mask:
        if mask & bit:
            x = x + bit * (1 - 2 * ((x // bit) % 2))
        bit *= 2
    return x


def peer_number(share, group_bits, expert_bits):
    return (expert_bits // 2) * (2 * share) + group_bits * 2 + expert_bits % 2


class Layout:
    def __init__(self, groups, experts, rows):
        self.groups, self.experts, self.rows = groups, experts, rows
        self.share = EXPERTS // experts
        self.peers = self.share * experts
        self.outers = groups // self.share
        per_quarter = max(experts // QUARTERS, 1)
        self.reach = min((WINDOW - 1) // rows + 1, 2 * per_quarter - 1)

    def far(self, number):
        return {"group": flipped(lax.axis_index("group"), number * self.share)}

    def peer(self, number):
        group, expert = lax.axis_index("group"), lax.axis_index("expert")
        return {
            "group": flipped(group, (number // 2) % self.share),
            "expert": flipped(expert, number // (2 * self.share) * 2 + number % 2),
        }


def meet(layout):
    barrier = pltpu.get_barrier_semaphore()
    for number in range(1, layout.peers):
        pl.semaphore_signal(barrier, inc=1, device_id=layout.peer(number), device_id_type=MESH)
    for number in range(1, layout.outers):
        pl.semaphore_signal(barrier, inc=1, device_id=layout.far(number), device_id_type=MESH)
    pl.semaphore_wait(barrier, layout.peers + layout.outers - 2)


def to_peers(layout, source, target, send_sems, recv_sems):
    return [
        pltpu.make_async_remote_copy(
            src_ref=source.at[number],
            dst_ref=target.at[number],
            send_sem=send_sems.at[number],
            recv_sem=recv_sems.at[number],
            device_id=layout.peer(number),
            device_id_type=MESH,
        )
        for number in range(1, layout.peers)
    ]


def to_far(layout, source, target, low, high, send_sems, recv_sems):
    return [
        pltpu.make_async_remote_copy(
            src_ref=source.at[low:high],
            dst_ref=target.at[number - 1],
            send_sem=send_sems.at[number - 1],
            recv_sem=recv_sems.at[number - 1],
            device_id=layout.far(number),
            device_id_type=MESH,
        )
        for number in range(1, layout.outers)
    ]


def far_shape(layout, count, width):
    return jax.ShapeDtypeStruct((layout.outers - 1, count, CAP, width), BF16)


def bit_of(axis, bit):
    return (lax.axis_index(axis) // bit) % 2


def trade_sems(copies):
    return [pltpu.SemaphoreType.DMA((copies,)), pltpu.SemaphoreType.DMA((copies,))]


class Halving:
    def __init__(self, step, held, taken, send_sems, recv_sems):
        axis, bit = step
        odd = (lax.axis_index(axis) // bit) % 2
        self.held, self.taken = held, taken
        if axis == "expert":
            places = [((2 * n + 1 - odd,), (2 * n + odd,), (n,)) for n in range(taken.shape[0])]
        else:
            places = [
                ((m, 2 * n + 1 - odd), (m, 2 * n + odd), (m, n))
                for m in range(taken.shape[0])
                for n in range(taken.shape[1])
            ]
        self.places = [place[1:] for place in places]
        self.copies = [
            pltpu.make_async_remote_copy(
                src_ref=held.at[theirs],
                dst_ref=taken.at[target],
                send_sem=send_sems.at[number],
                recv_sem=recv_sems.at[number],
                device_id={axis: flipped(lax.axis_index(axis), bit)},
                device_id_type=MESH,
            )
            for number, (theirs, _, target) in enumerate(places)
        ]

    @staticmethod
    def shape(step, held):
        experts, groups = held[:2]
        if step[0] == "expert":
            return (experts // 2, groups) + held[2:], experts // 2
        return (experts, groups // 2) + held[2:], experts * groups // 2

    def start(self):
        for copy in self.copies:
            copy.start()

    def add(self, last=None):
        for (mine, target), copy in zip(self.places, self.copies):
            copy.wait()
            if last is not None:
                mine, target = (*mine, 0)[:2], (*target, 0)[:2]
                last[...] = self.taken[target].astype(F32) + self.held[mine].astype(F32)
            elif len(target) == 2:
                self.taken[target] = (
                    self.taken[target].astype(F32) + self.held[mine].astype(F32)
                ).astype(BF16)
            else:

                def one(number, carry, mine=mine, target=target):
                    self.taken[target[0], number] = (
                        self.taken[target[0], number].astype(F32)
                        + self.held[mine[0], number].astype(F32)
                    ).astype(BF16)
                    return carry

                lax.fori_loop(0, self.taken.shape[1], one, 0)


def halving_steps(layout):
    experts = [("expert", 1 << n) for n in range(1, layout.experts.bit_length() - 1)]
    groups = [("group", 1 << n) for n in range(layout.groups.bit_length() - 1)]
    rest = experts[1:] + groups[1:]
    by_x = [groups[0], experts[0]] + rest
    by_y = [experts[0], groups[0]] + rest
    return by_x, by_x, by_y


DONE_EXPERTS = (1, 0, 1)
DONE_LATE = (2, 1, 2)


def halving_plan(layout, shapes, first, last):
    plan = []
    for steps, shape, low, high in zip(halving_steps(layout), shapes, first, last):
        mine = []
        for step in steps[low:high]:
            shape, copies = Halving.shape(step, shape)
            mine.append((step, shape, copies))
        plan.append(mine)
    return plan


def rope_turn(x, cosine, sine):
    parts = []
    for begin in range(0, x.shape[1], LANES):
        part = x[:, begin : begin + LANES]
        lane = lax.broadcasted_iota(jnp.int32, part.shape, 1)
        other = jnp.where(
            lane % HEAD < HEAD // 2,
            pltpu.roll(part, LANES - HEAD // 2, 1),
            pltpu.roll(part, HEAD // 2, 1),
        )
        parts.append(part * cosine + other * sine)
    return jnp.concatenate(parts, axis=1)


def normed(x, gain):
    return x * lax.rsqrt(jnp.mean(x * x, axis=-1, keepdims=True) + epsilon) * gain


def slot_rows(ids_row, rows):
    labels = lax.broadcasted_iota(jnp.int32, (EXPERTS, rows), 0)
    first, second = labels == ids_row[0:1], labels == ids_row[1:2]
    both = jnp.where(first | second, 1.0, 0.0).astype(BF16)
    earlier_t = lax.broadcasted_iota(jnp.int32, (rows, rows), 0)
    later_t = lax.broadcasted_iota(jnp.int32, (rows, rows), 1)
    earlier = mm(both, jnp.where(earlier_t < later_t, 1.0, 0.0).astype(BF16))
    targets = []
    for mask, ids in ((first, ids_row[0:1]), (second, ids_row[1:2])):
        slot = jnp.sum(jnp.where(mask, earlier, 0.0), axis=0, keepdims=True)
        targets.append(jnp.where(slot < CAP, ids.astype(F32) * CAP + slot, -1.0))
    return targets


def slot_masks(number, target, rows):
    slots = (number * CAP + lax.broadcasted_iota(jnp.int32, (CAP, rows), 0)).astype(F32)
    return slots == target[0:1], slots == target[1:2]


def gather_slots(target, source, pieces, made):
    rows = source.shape[0]
    for number in range(pieces):
        first, second = slot_masks(number, target, rows)
        chosen = jnp.where(first | second, 1.0, 0.0).astype(BF16)
        made[number] = mm(chosen, source[...]).astype(BF16)


def first_kernel(
    layout,
    tokens,
    gain_attn,
    w_qkv,
    cosine,
    sine,
    relative_row,
    ids_row,
    seg_row,
    cot,
    w_out,
    gain_ffn,
    w_router_t,
    dense_gate_any,
    dense_up_any,
    dense_down_any,
    q_out,
    kv_out,
    att_t_out,
    lse_out,
    bias_out,
    target_out,
    hidden_out,
    low_out,
    mixed_out,
    grad_out,
    gate_out,
    up_out,
    down_out,
    cots_out,
    rows_out,
    shares_out,
    far_cot_out,
    far_target_out,
    normed_low,
    send_cot,
    seg_all,
    acc,
    top,
    total,
    att,
    send_rows,
    send_shares,
    dense_gate,
    dense_up,
    dense_down,
    gate_held,
    up_held,
    down_held,
    load_sems,
    kv_send,
    kv_recv,
    seg_send,
    seg_recv,
    cot_send,
    cot_recv,
    row_send,
    row_recv,
    share_send,
    share_recv,
    own_sems,
    far_send,
    far_recv,
    half_send,
    half_recv,
):
    rows, width = tokens.shape
    reach, experts = layout.reach, layout.experts
    ff = dense_gate.shape[1]
    e = lax.axis_index("expert")
    loads = [
        pltpu.make_async_copy(source, target, load_sems.at[number])
        for number, (source, target) in enumerate(
            ((dense_gate_any, dense_gate), (dense_up_any, dense_up), (dense_down_any, dense_down))
        )
    ]
    for copy in loads:
        copy.start()
    meet(layout)

    targets = slot_rows(relative_row[...], rows)
    target_out[0:1] = targets[0]
    target_out[1:2] = targets[1]
    target_out[2:8] = jnp.full((6, rows), -1.0, F32)
    far = []
    for number in range(1, layout.outers):
        for place, (source, target) in enumerate(((cot, far_cot_out), (target_out, far_target_out))):
            far.append(
                pltpu.make_async_remote_copy(
                    src_ref=source,
                    dst_ref=target.at[number - 1],
                    send_sem=far_send.at[place, number - 1],
                    recv_sem=far_recv.at[place, number - 1],
                    device_id=layout.far(number),
                    device_id_type=MESH,
                )
            )
    gather_slots(target_out[...], cot, layout.peers, send_cot)
    cot_sends = to_peers(layout, send_cot, cots_out, cot_send, cot_recv)
    near = 2 * layout.share - 1
    for copy in cot_sends[:near]:
        copy.start()
    own_cot = pltpu.make_async_copy(send_cot.at[0], cots_out.at[0], own_sems.at[0])
    own_cot.start()
    for copy in far:
        copy.start()

    x = tokens[...].astype(F32)
    normed_low[...] = normed(x, gain_attn[...]).astype(BF16)
    seg_all[0] = seg_row[...]

    def project(step, carry):
        for part in range(3):
            columns = pl.ds(pl.multiple_of(part * width + step * TILE, TILE), TILE)
            made = mm(normed_low[...], w_qkv[:, columns])
            columns = pl.ds(pl.multiple_of(step * TILE, TILE), TILE)
            if part == 0:
                made = rope_turn(made, cosine[...], sine[...]) * HEAD ** (-0.5)
                q_out[:, columns] = made.astype(BF16)
            elif part == 1:
                made = rope_turn(made, cosine[...], sine[...])
                kv_out[0, :, columns] = made.astype(BF16)
            else:
                columns = pl.ds(pl.multiple_of(width + step * TILE, TILE), TILE)
                kv_out[0, :, columns] = made.astype(BF16)
        return carry

    lax.fori_loop(0, width // TILE, project, 0)

    halos = []
    for distance in range(1, reach + 1):
        to = {"expert": lax.rem(e + distance, experts)}
        halos.append(
            [
                pltpu.make_async_remote_copy(
                    src_ref=source.at[0],
                    dst_ref=source.at[distance],
                    send_sem=sems[0].at[distance],
                    recv_sem=sems[1].at[distance],
                    device_id=to,
                    device_id_type=MESH,
                )
                for source, sems in (
                    (kv_out, (kv_send, kv_recv)),
                    (seg_all, (seg_send, seg_recv)),
                )
            ]
        )
        for copy in halos[-1]:
            copy.start()

    lane = lax.broadcasted_iota(jnp.int32, (rows, LANES), 1)
    for distance in range(reach + 1):
        if distance:
            for copy in halos[distance - 1]:
                copy.wait()
        if distance == reach:
            for copy in cot_sends[near:]:
                copy.start()
        seg_col = jnp.transpose(jnp.broadcast_to(seg_all[distance, 0:1], (LANES, rows)))[:, 0:1]
        key_no = lax.broadcasted_iota(jnp.int32, (rows, rows), 0) - distance * rows
        offset = lax.broadcasted_iota(jnp.int32, (rows, rows), 1) - key_no
        allowed = (
            (offset >= 0)
            & (offset < WINDOW)
            & (key_no + e * rows >= 0)
            & (seg_col == seg_all[0, 0:1])
        )
        bias_out[distance] = jnp.where(allowed, 0.0, NEG).astype(BF16)

        def attend(pair, carry, distance=distance):
            columns = pl.ds(pl.multiple_of(pair * LANES, LANES), LANES)
            value_columns = pl.ds(pl.multiple_of(width + pair * LANES, LANES), LANES)
            queries = q_out[:, columns]
            keys = kv_out[distance, :, columns]
            values_t = jnp.transpose(kv_out[distance, :, value_columns])
            for inner in range(2):
                head = pair * 2 + inner
                mine = jnp.where((lane // HEAD) == inner, queries, jnp.zeros_like(queries))
                value_t = values_t[inner * HEAD : (inner + 1) * HEAD]
                out_rows = pl.ds(pl.multiple_of(head * HEAD, HEAD), HEAD)
                blocks = (
                    [(slice(0, rows // 2), rows // 2), (slice(rows // 2, rows), rows)]
                    if distance == 0
                    else [(slice(0, rows), rows)]
                )
                for q_cut, key_count in blocks:
                    scores = mm(keys[:key_count], mine[q_cut], NT)
                    scores = scores + bias_out[distance, :key_count, q_cut].astype(F32)
                    peak = jnp.max(scores, axis=0, keepdims=True)
                    if distance:
                        before = top[pl.ds(head, 1), q_cut]
                        peak = jnp.maximum(before, peak)
                    weights = jnp.exp(scores - peak)
                    amount = jnp.sum(weights, axis=0, keepdims=True)
                    part = mm(value_t[:, :key_count], weights.astype(BF16))
                    if distance:
                        shrink = jnp.exp(before - peak)
                        amount = amount + total[pl.ds(head, 1), q_cut] * shrink
                        part = part + acc[out_rows, q_cut] * shrink
                    top[pl.ds(head, 1), q_cut] = peak
                    total[pl.ds(head, 1), q_cut] = amount
                    acc[out_rows, q_cut] = part
            return carry

        lax.fori_loop(0, HEADS // 2, attend, 0)

    lse_out[...] = top[...] + jnp.log(total[...])

    def finish(pair, carry):
        out_rows = pl.ds(pl.multiple_of(pair * LANES, LANES), LANES)
        scale = jnp.concatenate(
            [
                jnp.broadcast_to(1.0 / total[pl.ds(pair * 2 + inner, 1), :], (HEAD, rows))
                for inner in range(2)
            ],
            axis=0,
        )
        made = acc[out_rows, :] * scale
        att_t_out[out_rows, :] = made.astype(BF16)
        att[:, out_rows] = jnp.transpose(made).astype(BF16)
        return carry

    lax.fori_loop(0, HEADS // 2, finish, 0)

    hidden_out[...] = tokens[...].astype(F32) + mm(att[...], w_out[...])
    low = normed(hidden_out[...], gain_ffn[...]).astype(BF16)
    low_out[...] = low
    logits = mm(w_router_t[...], low, NT)
    route = jnp.exp(logits - jnp.max(logits, axis=0, keepdims=True))
    route = route / jnp.sum(route, axis=0, keepdims=True)
    labels = lax.broadcasted_iota(jnp.int32, (EXPERTS, rows), 0)
    picked = [
        jnp.sum(jnp.where(labels == ids_row[k : k + 1], route, 0.0), axis=0, keepdims=True)
        for k in range(2)
    ]
    both = picked[0] + picked[1]
    shares = []
    for k in range(2):
        parts = split3(picked[k] / both)
        shares.append(
            jnp.concatenate(
                [part.astype(F32) for part in parts] + [jnp.zeros((5, rows), F32)], axis=0
            ).astype(BF16)
        )
    send_shares[...] = jnp.zeros_like(send_shares)
    sends = to_peers(layout, send_rows, rows_out, row_send, row_recv)
    share_sends = to_peers(layout, send_shares, shares_out, share_send, share_recv)
    for number in reversed(range(layout.peers)):
        first, second = slot_masks(number, target_out[...], rows)
        first = jnp.where(first, 1.0, 0.0).astype(BF16)
        second = jnp.where(second, 1.0, 0.0).astype(BF16)
        send_rows[number] = mm(first + second, low).astype(BF16)
        share = mm(shares[0], first, NT) + mm(shares[1], second, NT)
        share = jnp.sum(share, axis=0, keepdims=True)
        send_shares[number, :, :CAP] = jnp.broadcast_to(share, (8, CAP))
        if number:
            sends[number - 1].start()
            share_sends[number - 1].start()
    sends = sends + share_sends
    for source, target, sem in (
        (send_rows, rows_out, own_sems.at[1]),
        (send_shares, shares_out, own_sems.at[2]),
    ):
        sends.append(pltpu.make_async_copy(source.at[0], target.at[0], sem))
        sends[-1].start()

    for copy in loads:
        copy.wait()
    mixed_out[...] = hidden_out[...]
    grad_out[...] = jnp.zeros_like(grad_out)
    part_width = ff // experts
    per_part = part_width // TILE
    half = experts // 2
    odd = bit_of("expert", 1)
    halvings = [
        Halving(("expert", 1), held, taken, half_send.at[number], half_recv.at[number])
        for number, (held, taken) in enumerate(
            ((gate_held, gate_out), (up_held, up_out), (down_held, down_out))
        )
    ]

    def branch(step, carry):
        place = step // per_part
        part = 2 * (place % half) + (odd + 1 + place // half) % 2
        columns = pl.ds(pl.multiple_of(part * part_width + (step % per_part) * TILE, TILE), TILE)
        gate_w, up_w, down_w = dense_gate[:, columns], dense_up[:, columns], dense_down[columns, :]
        gate_pre = mm(low_out[...], gate_w)
        up_pre = mm(low_out[...], up_w)
        grad_act = mm(cot[...], down_w, NT)
        silu, slope = silu_parts(gate_pre)
        act = (silu * up_pre).astype(BF16)
        grad_gate = (grad_act * up_pre * slope).astype(BF16)
        grad_up = (grad_act * silu).astype(BF16)
        mixed_out[...] += mm(act, down_w)
        grad_out[...] += mm(grad_gate, gate_w, NT) + mm(grad_up, up_w, NT)
        inside = pl.ds(pl.multiple_of((step % per_part) * TILE, TILE), TILE)
        for made, held in (
            (mm(low_out[...], grad_gate, TN), gate_held),
            (mm(low_out[...], grad_up, TN), up_held),
        ):
            made = made.astype(BF16)
            block = held.shape[2]
            for place in range(held.shape[1]):
                held[part, place, :, inside] = made[place * block : (place + 1) * block]
        made = mm(act, cot[...], TN).astype(BF16)
        block = down_held.shape[2]
        cut = width // experts
        low_row = part * part_width + (step % per_part) * TILE
        for inner in range(0, TILE, block):
            for other in range(experts):
                down_held[other, (low_row + inner) // block] = made[
                    inner : inner + block, other * cut : (other + 1) * cut
                ]
        return carry

    lax.fori_loop(0, ff // (2 * TILE), branch, 0)
    for halving in halvings[:2]:
        halving.start()
    lax.fori_loop(ff // (2 * TILE), ff // TILE, branch, 0)
    halvings[2].start()
    for halving in halvings:
        halving.add()
    own_cot.wait()
    for copy in cot_sends + far + sends:
        copy.wait()


def first(layout, tokens, gain_attn, w_qkv, cosine, sine, relative_row, ids_row, seg_row, cot, w_out, gain_ffn, w_router_t, dense_gate, dense_up, dense_down):
    rows, width = tokens.shape
    ff = dense_gate.shape[1]
    reach, peers, experts, groups = layout.reach, layout.peers, layout.experts, layout.groups
    half = experts // 2
    others = layout.outers - 1
    dma = pltpu.SemaphoreType.DMA
    wide = (groups, width // groups, ff // experts)
    tall = (groups, ff // groups, width // experts)
    return pl.pallas_call(
        functools.partial(first_kernel, layout),
        out_shape=[
            jax.ShapeDtypeStruct((rows, width), BF16),
            jax.ShapeDtypeStruct((reach + 1, rows, 2 * width), BF16),
            jax.ShapeDtypeStruct((width, rows), BF16),
            jax.ShapeDtypeStruct((EXPERTS, rows), F32),
            jax.ShapeDtypeStruct((reach + 1, rows, rows), BF16),
            jax.ShapeDtypeStruct((8, rows), F32),
            jax.ShapeDtypeStruct((rows, width), F32),
            jax.ShapeDtypeStruct((rows, width), BF16),
            jax.ShapeDtypeStruct((rows, width), F32),
            jax.ShapeDtypeStruct((rows, width), F32),
            jax.ShapeDtypeStruct((half,) + wide, BF16),
            jax.ShapeDtypeStruct((half,) + wide, BF16),
            jax.ShapeDtypeStruct((half,) + tall, BF16),
            jax.ShapeDtypeStruct((peers, CAP, width), BF16),
            jax.ShapeDtypeStruct((peers, CAP, width), BF16),
            jax.ShapeDtypeStruct((peers, 8, LANES), F32),
            jax.ShapeDtypeStruct((others, rows, width), BF16),
            jax.ShapeDtypeStruct((others, 8, rows), F32),
        ],
        in_specs=[VMEM] * 12 + [ANY] * 3,
        out_specs=[VMEM] * 13 + [ANY] * 5,
        scratch_shapes=[
            pltpu.VMEM((rows, width), BF16),
            pltpu.VMEM((peers, CAP, width), BF16),
            pltpu.VMEM((reach + 1, 8, rows), F32),
            pltpu.VMEM((width, rows), F32),
            pltpu.VMEM((EXPERTS, rows), F32),
            pltpu.VMEM((EXPERTS, rows), F32),
            pltpu.VMEM((rows, width), BF16),
            pltpu.VMEM((peers, CAP, width), BF16),
            pltpu.VMEM((peers, 8, LANES), F32),
            pltpu.VMEM((width, ff), BF16),
            pltpu.VMEM((width, ff), BF16),
            pltpu.VMEM((ff, width), BF16),
            pltpu.VMEM((experts,) + wide, BF16),
            pltpu.VMEM((experts,) + wide, BF16),
            pltpu.VMEM((experts,) + tall, BF16),
            dma((3,)),
            dma((reach + 1,)),
            dma((reach + 1,)),
            dma((reach + 1,)),
            dma((reach + 1,)),
            dma((peers,)),
            dma((peers,)),
            dma((peers,)),
            dma((peers,)),
            dma((peers,)),
            dma((peers,)),
            dma((3,)),
            dma((2, others)),
            dma((2, others)),
            dma((3, half)),
            dma((3, half)),
        ],
        compiler_params=pltpu.CompilerParams(
            collective_id=0, has_side_effects=True, vmem_limit_bytes=62 * MIB
        ),
        cost_estimate=pl.CostEstimate(flops=1 << 30, bytes_accessed=1 << 20, transcendentals=0),
        name="first",
    )(tokens, gain_attn, w_qkv, cosine, sine, relative_row, ids_row, seg_row, cot, w_out, gain_ffn, w_router_t, dense_gate, dense_up, dense_down)


def split3(x):
    high = x.astype(BF16)
    rest = x - high.astype(F32)
    middle = rest.astype(BF16)
    return high, middle, (rest - middle.astype(F32)).astype(BF16)


def silu_parts(gate_pre):
    gate = 1.0 / (1.0 + jnp.exp(-gate_pre))
    return gate_pre * gate, gate * (1.0 + gate_pre * (1.0 - gate))


def share_column(share_row):
    across = lax.broadcasted_iota(jnp.int32, (CAP, CAP), 1)
    down = lax.broadcasted_iota(jnp.int32, (CAP, CAP), 0)
    return jnp.sum(jnp.where(across == down, share_row, 0.0), axis=1, keepdims=True)


def own_share(layout):
    return lax.rem(lax.axis_index("group"), layout.share)


class Sums:
    def __init__(self, layout, shapes, first, last, keep):
        self.plan = halving_plan(layout, shapes, first, last)
        self.keep = keep

    def scratch(self):
        made = []
        for mine in self.plan:
            for number, (_, shape, copies) in enumerate(mine):
                made += trade_sems(copies)
                if not self.keep or number + 1 < len(mine):
                    made.append(pltpu.VMEM(shape, BF16))
        return made

    def outputs(self):
        return [jax.ShapeDtypeStruct(mine[-1][1], BF16) for mine in self.plan if mine]

    def chains(self, held_refs, outputs, scratch):
        outputs, scratch = list(outputs), list(scratch)
        chains = []
        for held, mine in zip(held_refs, self.plan):
            chain = []
            for number, (step, _, _) in enumerate(mine):
                sems = scratch.pop(0), scratch.pop(0)
                if not self.keep or number + 1 < len(mine):
                    taken = scratch.pop(0)
                else:
                    taken = outputs.pop(0)
                chain.append(Halving(step, held, taken, *sems))
                held = taken
            chains.append(chain)
        return chains


def experts_kernel(layout, sums, *refs):
    (
        rows_in,
        cots,
        shares,
        gate_any,
        up_any,
        down_any,
        rows_any,
        shares_any,
        gate_held,
        up_held,
        down_held,
        back_out,
        grad_back,
        scaled,
        far_rows,
        far_shares,
        gate_sum,
        down_sum,
        gate_w,
        up_w,
        down_w,
        acc,
        grad_acc,
        send_out,
        send_grad,
        load_sems,
        out_send,
        out_recv,
        grad_send,
        grad_recv,
        own_sems,
        far_send,
        far_recv,
        *rest,
    ) = refs
    peers = layout.peers
    width, ff = gate_w.shape
    mine = own_share(layout)
    loads = [
        pltpu.make_async_copy(source.at[mine], target, load_sems.at[number])
        for number, (source, target) in enumerate(
            ((gate_any, gate_w), (up_any, up_w), (down_any, down_w))
        )
    ]
    for copy in loads:
        copy.start()
    meet(layout)
    far = to_far(layout, rows_any, far_rows, 0, FAR_ROWS[0], far_send.at[0], far_recv.at[0])
    far += to_far(layout, shares_any, far_shares, 0, peers, far_send.at[1], far_recv.at[1])
    for copy in far:
        copy.start()
    chains = sums.chains((gate_held, up_held, down_held), (gate_sum, down_sum), rest)
    for chain in chains:
        for halving in chain[:1]:
            halving.start()

    def scale(number, carry):
        column = share_column(shares[number, 0:1, :CAP])
        scaled[number] = (cots[number].astype(F32) * column).astype(BF16)
        return carry

    lax.fori_loop(0, peers, scale, 0)
    for copy in loads:
        copy.wait()

    count = 4
    chunk = 2 * TILE
    outs = to_peers(layout, send_out, back_out, out_send, out_recv)
    grads = to_peers(layout, send_grad, grad_back, grad_send, grad_recv)
    outs.insert(0, pltpu.make_async_copy(send_out.at[0], back_out.at[0], own_sems.at[0]))
    grads.insert(0, pltpu.make_async_copy(send_grad.at[0], grad_back.at[0], own_sems.at[1]))
    for high in range(peers, 0, -count):
        pieces = slice(high - count, high)

        def turn(step, carry, pieces=pieces):
            columns = pl.ds(pl.multiple_of(step * chunk, chunk), chunk)
            n = rows_in[pieces].reshape(count * CAP, width)
            grad = scaled[pieces].reshape(count * CAP, width)
            gate_pre = mm(n, gate_w[:, columns])
            up_pre = mm(n, up_w[:, columns])
            grad_act = mm(grad, down_w[columns, :], NT)
            silu, slope = silu_parts(gate_pre)
            act = (silu * up_pre).astype(BF16)
            grad_gate = (grad_act * up_pre * slope).astype(BF16)
            grad_up = (grad_act * silu).astype(BF16)
            acc[...] += mm(act, down_w[columns, :])
            grad_acc[...] += mm(grad_gate, gate_w[:, columns], NT) + mm(
                grad_up, up_w[:, columns], NT
            )
            return carry

        acc[...] = jnp.zeros_like(acc)
        grad_acc[...] = jnp.zeros_like(grad_acc)
        lax.fori_loop(0, ff // chunk, turn, 0)
        send_out[pieces] = acc[...].astype(BF16).reshape(count, CAP, width)
        send_grad[pieces] = grad_acc[...].astype(BF16).reshape(count, CAP, width)
        for copy in reversed(outs[pieces] + grads[pieces]):
            copy.start()
    for chain in chains:
        for halving in chain:
            halving.add()
    for copy in outs + grads + far:
        copy.wait()


def run_experts(layout, rows_in, cots, shares, expert_gate, expert_up, expert_down, held):
    peers, others = layout.peers, layout.outers - 1
    _, width, ff = expert_gate.shape
    dma = pltpu.SemaphoreType.DMA
    sums = Sums(layout, [one.shape for one in held], (0, 0, 0), DONE_EXPERTS, True)
    piece = jax.ShapeDtypeStruct((peers, CAP, width), BF16)
    return pl.pallas_call(
        functools.partial(experts_kernel, layout, sums),
        out_shape=[
            piece,
            piece,
            piece,
            far_shape(layout, FAR_ROWS[0], width),
            jax.ShapeDtypeStruct((others, peers, 8, LANES), F32),
            *sums.outputs(),
        ],
        in_specs=[VMEM] * 3 + [ANY] * 5 + [VMEM] * 3,
        out_specs=[ANY] * 2 + [VMEM] + [ANY] * 2 + [VMEM] * 2,
        scratch_shapes=[
            pltpu.VMEM((width, ff), BF16),
            pltpu.VMEM((width, ff), BF16),
            pltpu.VMEM((ff, width), BF16),
            pltpu.VMEM((4 * CAP, width), F32),
            pltpu.VMEM((4 * CAP, width), F32),
            pltpu.VMEM((peers, CAP, width), BF16),
            pltpu.VMEM((peers, CAP, width), BF16),
            dma((3,)),
            dma((peers,)),
            dma((peers,)),
            dma((peers,)),
            dma((peers,)),
            dma((2,)),
            dma((2, others)),
            dma((2, others)),
            *sums.scratch(),
        ],
        compiler_params=pltpu.CompilerParams(
            collective_id=1, has_side_effects=True, vmem_limit_bytes=60 * MIB
        ),
        cost_estimate=pl.CostEstimate(flops=1 << 30, bytes_accessed=1 << 20, transcendentals=0),
        name="experts",
    )(
        rows_in,
        cots,
        shares,
        expert_gate,
        expert_up,
        expert_down,
        rows_in,
        shares,
        *held,
    )


def rope_back(grad, cosine, sine):
    lane = lax.broadcasted_iota(jnp.int32, grad.shape, 1)
    turned = grad * sine
    other = jnp.where(
        lane % HEAD < HEAD // 2,
        pltpu.roll(turned, LANES - HEAD // 2, 1),
        pltpu.roll(turned, HEAD // 2, 1),
    )
    return grad * cosine + other


def by_blocks(target, made):
    parts, places, block, cut = target.shape
    for part in range(parts):
        for place in range(places):
            target[part, place] = made[
                place * block : (place + 1) * block, part * cut : (part + 1) * cut
            ]


def combine_part(
    back,
    grad_back,
    target,
    ids_col,
    hidden,
    mixed_in,
    grad_in,
    low,
    cot,
    gain,
    w_router,
    w_out,
    att_t,
    mixed_out,
    grad_hidden_out,
    grad_att_out,
    proj_out,
    router_out,
    gain_out,
):
    rows, width = hidden.shape
    peers = back.shape[0]
    slots = peers * CAP
    columns = jnp.transpose(
        jnp.concatenate([target[...], jnp.zeros((LANES - 8, rows), F32)], axis=0)
    )
    slot_no = lax.broadcasted_iota(jnp.int32, (rows, slots), 1).astype(F32)
    cot_float = cot[...].astype(F32)
    logits = mm(low[...], w_router[...])
    route = jnp.exp(logits - jnp.max(logits, axis=1, keepdims=True))
    route = route / jnp.sum(route, axis=1, keepdims=True)
    labels = lax.broadcasted_iota(jnp.int32, (rows, EXPERTS), 1)
    masks = [labels == ids_col[:, k : k + 1] for k in range(2)]
    picked = [jnp.sum(jnp.where(mask, route, 0.0), axis=1, keepdims=True) for mask in masks]
    both = picked[0] + picked[1]
    chosen, shares, grads = [], [], []
    mixed = mixed_in[...]
    for k in range(2):
        chosen.append(jnp.where(slot_no == columns[:, k : k + 1], 1.0, 0.0).astype(BF16))
        fetched = mm(chosen[k], back[...].reshape(slots, width))
        shares.append(picked[k] / both)
        mixed = mixed + shares[k] * fetched
        grads.append(jnp.sum(cot_float * fetched, axis=1, keepdims=True))
    mixed_out[...] = mixed.astype(BF16)
    mean = grads[0] * shares[0] + grads[1] * shares[1]
    grad_route = jnp.zeros_like(route)
    for k in range(2):
        grad_route = grad_route + jnp.where(masks[k], (grads[k] - mean) / both, 0.0)
    grad_logits = route * (grad_route - jnp.sum(route * grad_route, axis=1, keepdims=True))
    grad_logits = grad_logits.astype(BF16)
    router_out[...] = mm(grad_logits, low[...], TN)
    grad = grad_in[...] + mm(chosen[0] + chosen[1], grad_back[...].reshape(slots, width))
    grad = grad + mm(grad_logits, w_router[...], NT)
    h = hidden[...]
    scale = lax.rsqrt(jnp.mean(h * h, axis=-1, keepdims=True) + epsilon)
    gain_out[...] = jnp.sum(grad * h * scale, axis=0, keepdims=True)
    grad = grad * gain[...]
    grad = scale * grad - h * (scale * scale * scale) * jnp.mean(grad * h, axis=-1, keepdims=True)
    grad = cot_float + grad
    grad_hidden_out[...] = grad
    grad_low = grad.astype(BF16)
    grad_att_out[...] = mm(grad_low, w_out[...], NT).astype(BF16)
    by_blocks(proj_out, mm(att_t[...], grad_low).astype(BF16))


def late_kernel(layout, sums, *refs):
    (
        back,
        grad_back,
        target,
        ids_col,
        hidden,
        mixed_in,
        grad_in,
        low,
        cot,
        gain_ffn,
        w_router,
        w_out,
        att_t,
        q_in,
        kv_in,
        bias,
        lse,
        tokens,
        gain,
        w_qkv,
        cosine,
        sine,
        gate_held,
        up_held,
        down_held,
        far_cot,
        far_target,
        rows_any,
        mixed_out,
        tokens_out,
        proj_out,
        qkv_out,
        small_out,
        gate_sum,
        up_sum,
        down_sum,
        far_cots_out,
        far_out,
        grad_att,
        router_term,
        gain_term,
        send_cot,
        halo_send,
        halo_recv,
        own_kv,
        packed,
        send_sems,
        recv_sems,
        cot_send,
        cot_recv,
        own_sem,
        far_send,
        far_recv,
        *rest,
    ) = refs
    rows, width = tokens.shape
    reach, experts = layout.reach, layout.experts
    e = lax.axis_index("expert")
    pairs = HEADS // 2
    lane = lax.broadcasted_iota(jnp.int32, (rows, LANES), 1)
    meet(layout)
    far = to_far(layout, rows_any, far_out, FAR_ROWS[0], FAR_ROWS[1], far_send, far_recv)
    for copy in far:
        copy.start()
    chains = sums.chains((gate_held, up_held, down_held), (gate_sum, up_sum, down_sum), rest)
    for chain in chains:
        chain[0].start()
    cot_sends = []
    for number in range(layout.outers - 1):
        for copy in cot_sends:
            copy.wait()
        load = pltpu.make_async_copy(far_cot.at[number], grad_att, own_sem.at[number])
        load.start()
        load.wait()
        gather_slots(far_target[number], grad_att, layout.peers, send_cot)
        cot_sends = to_peers(
            layout, send_cot, far_cots_out.at[number], cot_send.at[number], cot_recv.at[number]
        )
        cot_sends.append(
            pltpu.make_async_copy(
                send_cot.at[0], far_cots_out.at[number, 0], own_sem.at[number]
            )
        )
        for copy in cot_sends:
            copy.start()

    combine_part(
        back,
        grad_back,
        target,
        ids_col,
        hidden,
        mixed_in,
        grad_in,
        low,
        cot,
        gain_ffn,
        w_router,
        w_out,
        att_t,
        mixed_out,
        tokens_out,
        grad_att,
        proj_out,
        router_term,
        gain_term,
    )

    def halo(distance, pair):
        return pltpu.make_async_remote_copy(
            src_ref=halo_send.at[distance - 1, pair],
            dst_ref=halo_recv.at[distance - 1, pair],
            send_sem=send_sems.at[distance - 1, pair],
            recv_sem=recv_sems.at[distance - 1, pair],
            device_id={"expert": lax.rem(e + experts - distance, experts)},
            device_id_type=MESH,
        )

    def heads(pair, carry):
        columns = pl.ds(pl.multiple_of(pair * LANES, LANES), LANES)
        value_columns = pl.ds(pl.multiple_of(width + pair * LANES, LANES), LANES)
        queries, grads = q_in[:, columns], grad_att[:, columns]
        grads_t = jnp.transpose(grads.astype(F32))
        shrunk = grads_t * att_t[columns, :].astype(F32)
        grad_q = [None, None]
        for distance in range(reach, -1, -1):
            keys = kv_in[distance, :, columns]
            values = kv_in[distance, :, value_columns]
            keys_t = jnp.transpose(keys)
            grad_k = grad_v = None
            for inner in range(2):
                head = pair * 2 + inner
                cut = slice(inner * HEAD, (inner + 1) * HEAD)
                mine = (lane // HEAD) == inner
                query = jnp.where(mine, queries, jnp.zeros_like(queries))
                grad = jnp.where(mine, grads, jnp.zeros_like(grads))
                total = jnp.sum(shrunk[cut], axis=0, keepdims=True)
                scores = mm(keys, query, NT) + bias[distance].astype(F32)
                probs = jnp.exp(scores - lse[pl.ds(head, 1), :])
                grad_probs = mm(values, grad, NT)
                grad_scores = (probs * (grad_probs - total)).astype(BF16)
                part_v = mm(probs.astype(BF16), grad)
                part_k = mm(grad_scores, query)
                part_q = mm(keys_t[cut], grad_scores)
                grad_v = part_v if grad_v is None else grad_v + part_v
                grad_k = part_k if grad_k is None else grad_k + part_k
                grad_q[inner] = part_q if grad_q[inner] is None else grad_q[inner] + part_q
            if distance:
                halo_send[distance - 1, pair, 0] = grad_k.astype(BF16)
                halo_send[distance - 1, pair, 1] = grad_v.astype(BF16)
                halo(distance, pair).start()
            else:
                own_kv[pair, 0] = grad_k
                own_kv[pair, 1] = grad_v
        grad = jnp.transpose(jnp.concatenate(grad_q, axis=0)) * HEAD ** (-0.5)
        packed[:, columns] = rope_back(grad, cosine[...], sine[...]).astype(BF16)
        return carry

    lax.fori_loop(0, pairs, heads, 0)
    x = tokens[...].astype(F32)
    grad_att[...] = normed(x, gain[...]).astype(BF16)
    normed_low = grad_att

    def merge(pair, carry):
        grad_k, grad_v = own_kv[pair, 0], own_kv[pair, 1]
        for distance in range(1, reach + 1):
            halo(distance, pair).wait()
            grad_k = grad_k + halo_recv[distance - 1, pair, 0].astype(F32)
            grad_v = grad_v + halo_recv[distance - 1, pair, 1].astype(F32)
        columns = pl.ds(pl.multiple_of(width + pair * LANES, LANES), LANES)
        packed[:, columns] = rope_back(grad_k, cosine[...], sine[...]).astype(BF16)
        columns = pl.ds(pl.multiple_of(2 * width + pair * LANES, LANES), LANES)
        packed[:, columns] = grad_v.astype(BF16)
        return carry

    lax.fori_loop(0, pairs, merge, 0)
    for chain in chains:
        for halving in chain:
            halving.add()
    parts, places, block, cut = qkv_out.shape
    for part in range(parts):
        made = mm(normed_low[...], packed[:, part * cut : (part + 1) * cut], TN).astype(BF16)
        for place in range(places):
            qkv_out[part, place] = made[place * block : (place + 1) * block]
    grad = mm(packed[...], w_qkv[...], NT)
    scale = lax.rsqrt(jnp.mean(x * x, axis=-1, keepdims=True) + epsilon)
    gain_back = jnp.sum(grad * x * scale, axis=0, keepdims=True)
    small_out[...] = jnp.concatenate(
        [router_term[...], gain_term[...], gain_back, jnp.zeros((6, width), F32)], axis=0
    )
    grad = grad * gain[...]
    grad = scale * grad - x * (scale * scale * scale) * jnp.mean(grad * x, axis=-1, keepdims=True)
    tokens_out[...] += grad
    for copy in far + cot_sends:
        copy.wait()


def late(layout, combine_ins, back_ins, held, far_cot, far_target, rows_in):
    tokens = back_ins[4]
    rows, width = tokens.shape
    reach, peers, others = layout.reach, layout.peers, layout.outers - 1
    dma = pltpu.SemaphoreType.DMA
    pairs = HEADS // 2
    sums = Sums(layout, [one.shape for one in held], DONE_EXPERTS, DONE_LATE, True)
    blocks = (layout.experts, layout.groups, width // layout.groups)
    return pl.pallas_call(
        functools.partial(late_kernel, layout, sums),
        out_shape=[
            jax.ShapeDtypeStruct((rows, width), BF16),
            jax.ShapeDtypeStruct((rows, width), F32),
            jax.ShapeDtypeStruct(blocks + (width // layout.experts,), BF16),
            jax.ShapeDtypeStruct(blocks + (3 * width // layout.experts,), BF16),
            jax.ShapeDtypeStruct((SMALL, width), F32),
            *sums.outputs(),
            jax.ShapeDtypeStruct((others, peers, CAP, width), BF16),
            far_shape(layout, FAR_ROWS[1] - FAR_ROWS[0], width),
        ],
        in_specs=[VMEM] * 25 + [ANY, VMEM, ANY],
        out_specs=[VMEM] * 8 + [ANY] * 2,
        scratch_shapes=[
            pltpu.VMEM((rows, width), BF16),
            pltpu.VMEM((EXPERTS, width), F32),
            pltpu.VMEM((1, width), F32),
            pltpu.VMEM((peers, CAP, width), BF16),
            pltpu.VMEM((reach, pairs, 2, rows, LANES), BF16),
            pltpu.VMEM((reach, pairs, 2, rows, LANES), BF16),
            pltpu.VMEM((pairs, 2, rows, LANES), F32),
            pltpu.VMEM((rows, 3 * width), BF16),
            dma((reach, pairs)),
            dma((reach, pairs)),
            dma((others, peers)),
            dma((others, peers)),
            dma((others,)),
            dma((others,)),
            dma((others,)),
            *sums.scratch(),
        ],
        compiler_params=pltpu.CompilerParams(
            collective_id=2, has_side_effects=True, vmem_limit_bytes=63 * MIB
        ),
        cost_estimate=pl.CostEstimate(flops=1 << 30, bytes_accessed=1 << 20, transcendentals=0),
        name="late",
    )(*combine_ins, *back_ins, *held, far_cot, far_target, rows_in)


def weights_kernel(layout, sums, more, *refs):
    share, outers, peers = layout.share, layout.outers, layout.peers
    (
        rows_own,
        grads_own,
        rows_a,
        rows_b,
        cots_far,
        shares_far,
        gate_any,
        up_any,
        down_any,
        *terms,
    ) = refs[:14]
    small_in = refs[14]
    rows_c, gate_out, up_out, down_out = refs[15:19]
    sums_out = refs[19:24]
    small_out = refs[24]
    (
        gate_w,
        up_w,
        gate_t,
        up_t,
        down_w,
        rows_buf,
        cots_buf,
        shares_buf,
        accs,
        sends,
        takes,
        down_sends,
        down_takes,
        small_sums,
        small_takes,
        load_sems,
        piece_sems,
        send_sems,
        recv_sems,
        far_send,
        far_recv,
        small_send,
        small_recv,
    ) = refs[25:48]
    rest = refs[48:]
    width = gate_w.shape[0]
    ff = gate_any.shape[2]
    span = ff // outers
    cut = ff // layout.groups
    group = lax.axis_index("group")
    mine = own_share(layout)
    begin = pl.multiple_of((group // share) * span, span)
    loads = [
        pltpu.make_async_copy(gate_any.at[mine, :, pl.ds(begin, span)], gate_w, load_sems.at[0]),
        pltpu.make_async_copy(up_any.at[mine, :, pl.ds(begin, span)], up_w, load_sems.at[1]),
        pltpu.make_async_copy(down_any.at[mine, pl.ds(begin, span), :], down_w, load_sems.at[2]),
    ]

    def fetch(outer):
        slot = outer % 2
        cuts = (0, *FAR_ROWS)
        if outer == 0:
            sources = [(rows_own, rows_buf.at[slot]), (grads_own, cots_buf.at[slot])]
        else:
            sources = [
                (one.at[outer - 1], rows_buf.at[slot, cuts[place] : cuts[place + 1]])
                for place, one in enumerate((rows_a, rows_b, rows_c))
            ]
            sources.append((cots_far.at[outer - 1], cots_buf.at[slot]))
            sources.append((shares_far.at[outer - 1], shares_buf.at[slot]))
        return [
            pltpu.make_async_copy(source, target, piece_sems.at[slot, number])
            for number, (source, target) in enumerate(sources)
        ]

    for copy in loads + fetch(0):
        copy.start()
    meet(layout)
    far = to_far(layout, rows_own, rows_c, FAR_ROWS[1], FAR_ROWS[2], far_send, far_recv)
    for copy in far:
        copy.start()

    chains = sums.chains(terms[:3], (), rest)
    chains += more.chains(terms[3:], (), rest[len(sums.scratch()) :])
    steps = [("expert", 1 << n) for n in range(layout.experts.bit_length() - 1)]
    steps += [("group", 1 << n) for n in range(layout.groups.bit_length() - 1)]
    levels = len(steps)
    small_sums[0] = small_in[...]

    def small_copy(level):
        axis, bit = steps[level]
        return pltpu.make_async_remote_copy(
            src_ref=small_sums.at[level],
            dst_ref=small_takes.at[level],
            send_sem=small_send.at[level],
            recv_sem=small_recv.at[level],
            device_id={axis: flipped(lax.axis_index(axis), bit)},
            device_id_type=MESH,
        )

    def advance(level):
        for number, chain in enumerate(chains):
            if 0 < level <= len(chain):
                chain[level - 1].add(sums_out[number] if level == len(chain) else None)
            if level < len(chain):
                chain[level].start()
        if level:
            small_copy(level - 1).wait()
            made = small_sums[level - 1] + small_takes[level - 1]
            if level < levels:
                small_sums[level] = made
            else:
                small_out[...] = made
        if level < levels:
            small_copy(level).start()

    advance(0)
    points = share * outers
    marks = [max(0, (points * at) // 8 - 1) for at in (2, 6, 7, 8)]
    done = 1

    for copy in loads:
        copy.wait()
    gate_t[...] = jnp.transpose(gate_w[...])
    up_t[...] = jnp.transpose(up_w[...])
    count = 8
    blocks = peers // count

    def add(slot, chunk, block):
        pieces = pl.ds(block * count, count)
        n = rows_buf[slot, pieces].reshape(count * CAP, width)
        grad = cots_buf[slot, pieces].reshape(count * CAP, width)
        base = pl.multiple_of(chunk * cut, cut)
        gate_pre = mm(gate_t[pl.ds(base, cut), :], n, NT)
        up_pre = mm(up_t[pl.ds(base, cut), :], n, NT)
        grad_act = mm(down_w[pl.ds(base, cut), :], grad, NT)
        silu, slope = silu_parts(gate_pre)
        act = (silu * up_pre).astype(BF16)
        grad_gate = (grad_act * up_pre * slope).astype(BF16)
        grad_up = (grad_act * silu).astype(BF16)
        accs[0] += mm(grad_gate, n)
        accs[1] += mm(grad_up, n)
        accs[2] += mm(act, grad)

    copies = []
    turns = [*range(share - 1, 0, -1), 0]
    resident = outers <= 2
    for place, turn in enumerate(turns):
        owner = flipped(mine, turn)
        accs[...] = jnp.zeros_like(accs)
        for outer in range(outers):
            slot = outer % 2
            if place == 0 or not resident:
                if place == 0 and outer == 1:
                    for copy in far:
                        copy.wait()
                if place or outer:
                    for copy in fetch(outer):
                        copy.start()
                for copy in fetch(outer):
                    copy.wait()

                def scale(number, carry, slot=slot):
                    column = share_column(shares_buf[slot, number, 0:1, :CAP])
                    cots_buf[slot, number] = (cots_buf[slot, number].astype(F32) * column).astype(
                        BF16
                    )
                    return carry

                if outer:
                    lax.fori_loop(0, peers, scale, 0)

            def step(number, carry, slot=slot, owner=owner):
                add(slot, owner, number)
                return carry

            lax.fori_loop(0, blocks, step, 0)
            while done <= len(marks) and marks[done - 1] <= place * outers + outer:
                if done < levels:
                    advance(done)
                done += 1
        for which in range(3):
            made = accs[which]
            if which < 2:
                made = jnp.transpose(made)
            target = (gate_out, up_out, down_out)[which]
            if turn == 0:
                target[owner] = made
                continue
            if which < 2:
                ends = sends.at[turn - 1, which], takes.at[turn - 1, which]
            else:
                ends = down_sends.at[turn - 1], down_takes.at[turn - 1]
            ends[0][...] = made.astype(BF16)
            copy = pltpu.make_async_remote_copy(
                src_ref=ends[0],
                dst_ref=ends[1],
                send_sem=send_sems.at[turn - 1, which],
                recv_sem=recv_sems.at[turn - 1, which],
                device_id={"group": flipped(group, turn)},
                device_id_type=MESH,
            )
            copy.start()
            copies.append((turn, which, copy))
    for level in range(done, levels + 1):
        advance(level)
    for turn, which, copy in copies:
        copy.wait()
        target = (gate_out, up_out, down_out)[which]
        got = takes[turn - 1, which] if which < 2 else down_takes[turn - 1]
        target[flipped(mine, turn)] = got.astype(F32)


def weights(layout, own, rows_far, cots_far, shares_far, expert_weights, held, terms, small):
    share, outers, peers = layout.share, layout.outers, layout.peers
    experts, width, ff = expert_weights[0].shape
    span = ff // outers
    cut = ff // layout.groups
    dma = pltpu.SemaphoreType.DMA
    levels = layout.experts.bit_length() + layout.groups.bit_length() - 2
    sums = Sums(layout, [one.shape for one in held], DONE_LATE, (levels,) * 3, False)
    more = Sums(layout, [], (), (), False)
    steps = [("expert", 1 << n) for n in range(layout.experts.bit_length() - 1)]
    steps += [("group", 1 << n) for n in range(layout.groups.bit_length() - 1)]
    for term in terms:
        shape, mine = term.shape, []
        for step in steps:
            shape, copies = Halving.shape(step, shape)
            mine.append((step, shape, copies))
        more.plan.append(mine)
    return pl.pallas_call(
        functools.partial(weights_kernel, layout, sums, more),
        out_shape=[
            far_shape(layout, FAR_ROWS[2] - FAR_ROWS[1], width),
            jax.ShapeDtypeStruct((experts, width, cut), F32),
            jax.ShapeDtypeStruct((experts, width, cut), F32),
            jax.ShapeDtypeStruct((experts, cut, width), F32),
            *[jax.ShapeDtypeStruct(one.shape[2:], F32) for one in (*held, *terms)],
            jax.ShapeDtypeStruct((SMALL, width), F32),
        ],
        in_specs=[ANY] * 9 + [VMEM] * 6,
        out_specs=[ANY] + [VMEM] * 9,
        scratch_shapes=[
            pltpu.VMEM((width, span), BF16),
            pltpu.VMEM((width, span), BF16),
            pltpu.VMEM((span, width), BF16),
            pltpu.VMEM((span, width), BF16),
            pltpu.VMEM((span, width), BF16),
            pltpu.VMEM((2, peers, CAP, width), BF16),
            pltpu.VMEM((2, peers, CAP, width), BF16),
            pltpu.VMEM((2, peers, 8, LANES), F32),
            pltpu.VMEM((3, cut, width), F32),
            pltpu.VMEM((share - 1, 2, width, cut), BF16),
            pltpu.VMEM((share - 1, 2, width, cut), BF16),
            pltpu.VMEM((share - 1, cut, width), BF16),
            pltpu.VMEM((share - 1, cut, width), BF16),
            pltpu.VMEM((levels, SMALL, width), F32),
            pltpu.VMEM((levels, SMALL, width), F32),
            dma((3,)),
            dma((2, 5)),
            dma((share - 1, 3)),
            dma((share - 1, 3)),
            dma((outers - 1,)),
            dma((outers - 1,)),
            dma((levels,)),
            dma((levels,)),
            *sums.scratch(),
            *more.scratch(),
        ],
        compiler_params=pltpu.CompilerParams(
            collective_id=3, has_side_effects=True, vmem_limit_bytes=60 * MIB
        ),
        cost_estimate=pl.CostEstimate(flops=1 << 30, bytes_accessed=1 << 20, transcendentals=0),
        name="weights",
    )(*own, *rows_far, cots_far, shares_far, *expert_weights, *held, *terms, small)


def local(
    tokens,
    gain_attn,
    w_qkv,
    w_out,
    gain_ffn,
    w_router,
    expert_gate,
    expert_up,
    expert_down,
    dense_gate,
    dense_up,
    dense_down,
    expert_ids,
    segments,
    cotangent,
):
    rows, width = tokens.shape
    layout = Layout(lax.axis_size("group"), lax.axis_size("expert"), rows)
    group, expert = lax.axis_index("group"), lax.axis_index("expert")
    share = layout.share
    relative = peer_number(
        share, (expert_ids % share) ^ (group % share), (expert_ids // share) ^ expert
    )
    fill = jnp.full((6, rows), -1, jnp.int32)
    relative_row = jnp.concatenate([jnp.transpose(relative), fill], axis=0)
    ids_row = jnp.concatenate([jnp.transpose(expert_ids), fill], axis=0)
    seg_row = jnp.broadcast_to(segments.astype(F32)[None], (8, rows))
    places = (expert * rows + jnp.arange(rows, dtype=jnp.int32)).astype(F32)
    lane = jnp.arange(LANES)
    power = (lane % (HEAD // 2)).astype(F32) / (HEAD // 2)
    angles = places[:, None] * (10000.0 ** (-power))[None]
    cosine = jnp.cos(angles)
    sine = jnp.sin(angles) * jnp.where(lane % HEAD < HEAD // 2, -1.0, 1.0)[None]
    gain_attn, gain_ffn = gain_attn[None], gain_ffn[None]

    (
        q,
        kv,
        att_t,
        lse,
        bias,
        target,
        hidden,
        low,
        mixed,
        grad_low,
        gate_terms,
        up_terms,
        down_terms,
        cots,
        rows_in,
        shares,
        far_cot,
        far_target,
    ) = first(
        layout,
        tokens,
        gain_attn,
        w_qkv,
        cosine,
        sine,
        relative_row,
        ids_row,
        seg_row,
        cotangent,
        w_out,
        gain_ffn,
        jnp.transpose(w_router),
        dense_gate,
        dense_up,
        dense_down,
    )
    came_back, grad_back, grads_in, rows_a, shares_far, gate_terms, down_terms = run_experts(
        layout,
        rows_in,
        cots,
        shares,
        expert_gate,
        expert_up,
        expert_down,
        (gate_terms, up_terms, down_terms),
    )
    mixed_out, grad_tokens, proj_terms, qkv_terms, small, *sums, cots_far, rows_b = late(
        layout,
        (
            came_back,
            grad_back,
            target,
            expert_ids,
            hidden,
            mixed,
            grad_low,
            low,
            cotangent,
            gain_ffn,
            w_router,
            w_out,
            att_t,
        ),
        (q, kv, bias, lse, tokens, gain_attn, w_qkv, cosine, sine),
        (gate_terms, up_terms, down_terms),
        far_cot,
        far_target,
        rows_in,
    )
    _, gate_w, up_w, down_w, gate_sum, up_sum, down_sum, proj_sum, qkv_sum, small = weights(
        layout,
        (rows_in, grads_in),
        (rows_a, rows_b),
        cots_far,
        shares_far,
        (expert_gate, expert_up, expert_down),
        sums,
        (proj_terms, qkv_terms),
        small,
    )
    return (
        mixed_out,
        grad_tokens,
        small[EXPERTS + 1],
        qkv_sum,
        proj_sum,
        small[EXPERTS],
        jnp.transpose(small[:EXPERTS]),
        gate_w,
        up_w,
        down_w,
        gate_sum,
        up_sum,
        down_sum,
    )


def solution(mesh):
    in_specs = (
        P(("group", "expert"), None),
        P(),
        P(),
        P(),
        P(),
        P(),
        P("expert", None, None),
        P("expert", None, None),
        P("expert", None, None),
        P(),
        P(),
        P(),
        P(("group", "expert"), None),
        P(("group", "expert")),
        P(("group", "expert"), None),
    )
    out_specs = (
        P(("group", "expert"), None),
        P(("group", "expert"), None),
        P(),
        P("group", "expert"),
        P("group", "expert"),
        P(),
        P(),
        P("expert", None, "group"),
        P("expert", None, "group"),
        P("expert", "group", None),
        P("group", "expert"),
        P("group", "expert"),
        P("group", "expert"),
    )
    return jax.shard_map(local, mesh=mesh, in_specs=in_specs, out_specs=out_specs, check_vma=False)
```

```python
import functools

import jax
import jax.numpy as jnp
from jax import lax
from jax.experimental import pallas as pl
from jax.experimental.pallas import tpu as pltpu
from jax.sharding import PartitionSpec as P

HEADS = 12
HEAD = 64
EXPERTS = 16
WINDOW = 1024
CAP = 80
QUARTERS = 4
LANES = 128
TILE = 256
SMALL = EXPERTS + 8
NEG = -1e30

epsilon = 1e-06
F32 = jnp.float32
BF16 = jnp.bfloat16
MESH = pl.DeviceIdType.MESH
VMEM = pl.BlockSpec(memory_space=pltpu.VMEM)
ANY = pl.BlockSpec(memory_space=pl.ANY)
MIB = 1 << 20


def dims(spec):
    left, right = spec
    return (((left,), (right,)), ((), ()))


NN = dims((1, 0))
NT = dims((1, 1))
TN = dims((0, 0))


def mm(a, b, how=NN):
    return lax.dot_general(a, b, how, preferred_element_type=F32)


def flipped(x, mask):
    bit = 1
    while bit <= mask:
        if mask & bit:
            x = x + bit * (1 - 2 * ((x // bit) % 2))
        bit *= 2
    return x


class Layout:
    def __init__(self, groups, experts, rows):
        self.groups, self.experts, self.rows = groups, experts, rows
        self.share = EXPERTS // experts
        self.peers = self.share * experts
        self.outers = groups // self.share
        per_quarter = max(experts // QUARTERS, 1)
        self.reach = min((WINDOW - 1) // rows + 1, 2 * per_quarter - 1)

    def far(self, number):
        return {"group": flipped(lax.axis_index("group"), number * self.share)}

    def peer(self, number):
        group, expert = lax.axis_index("group"), lax.axis_index("expert")
        return {
            "group": flipped(group, number // self.experts),
            "expert": flipped(expert, number % self.experts),
        }

    def slots(self, width):
        return (self.share, self.experts, CAP, width)


def meet(layout):
    barrier = pltpu.get_barrier_semaphore()
    for number in range(1, layout.peers):
        pl.semaphore_signal(barrier, inc=1, device_id=layout.peer(number), device_id_type=MESH)
    for number in range(1, layout.outers):
        pl.semaphore_signal(barrier, inc=1, device_id=layout.far(number), device_id_type=MESH)
    pl.semaphore_wait(barrier, layout.peers + layout.outers - 2)


def remote(source, target, send_sem, recv_sem, device):
    return pltpu.make_async_remote_copy(
        src_ref=source,
        dst_ref=target,
        send_sem=send_sem,
        recv_sem=recv_sem,
        device_id=device,
        device_id_type=MESH,
    )


def to_peers(layout, source, target, send_sems, recv_sems):
    return [
        remote(
            source.at[divmod(number, layout.experts)],
            target.at[divmod(number, layout.experts)],
            send_sems.at[number],
            recv_sems.at[number],
            layout.peer(number),
        )
        for number in range(1, layout.peers)
    ]


def to_row(layout, source, target, send_sems, recv_sems):
    expert = lax.axis_index("expert")
    return [
        remote(
            source.at[:, bits],
            target.at[:, bits],
            send_sems.at[bits],
            recv_sems.at[bits],
            {"expert": flipped(expert, bits)},
        )
        for bits in range(1, layout.experts)
    ]


def to_quad(layout, source, target, send_sems, recv_sems):
    group = lax.axis_index("group")
    return [
        remote(
            source.at[bits],
            target.at[bits],
            send_sems.at[bits],
            recv_sems.at[bits],
            {"group": flipped(group, bits)},
        )
        for bits in range(1, layout.share)
    ]


def to_far(layout, source, target, low, high, send_sems, recv_sems):
    return [
        remote(
            source.at[low:high],
            target.at[number - 1],
            send_sems.at[number - 1],
            recv_sems.at[number - 1],
            layout.far(number),
        )
        for number in range(1, layout.outers)
    ]


def far_shape(layout, count, width):
    shape = (layout.outers - 1, count) + layout.slots(width)[1:]
    return jax.ShapeDtypeStruct(shape, BF16)


def bit_of(axis, bit):
    return (lax.axis_index(axis) // bit) % 2


def trade_sems(copies):
    return [pltpu.SemaphoreType.DMA((copies,)), pltpu.SemaphoreType.DMA((copies,))]


class Halving:
    def __init__(self, step, held, taken, send_sems, recv_sems):
        axis, bit = step
        odd = (lax.axis_index(axis) // bit) % 2
        self.held, self.taken = held, taken
        if axis == "expert":
            places = [((2 * n + 1 - odd,), (2 * n + odd,), (n,)) for n in range(taken.shape[0])]
        else:
            places = [
                ((m, 2 * n + 1 - odd), (m, 2 * n + odd), (m, n))
                for m in range(taken.shape[0])
                for n in range(taken.shape[1])
            ]
        self.places = [place[1:] for place in places]
        self.copies = [
            pltpu.make_async_remote_copy(
                src_ref=held.at[theirs],
                dst_ref=taken.at[target],
                send_sem=send_sems.at[number],
                recv_sem=recv_sems.at[number],
                device_id={axis: flipped(lax.axis_index(axis), bit)},
                device_id_type=MESH,
            )
            for number, (theirs, _, target) in enumerate(places)
        ]

    @staticmethod
    def shape(step, held):
        experts, groups = held[:2]
        if step[0] == "expert":
            return (experts // 2, groups) + held[2:], experts // 2
        return (experts, groups // 2) + held[2:], experts * groups // 2

    def start(self):
        for copy in self.copies:
            copy.start()

    def add(self, last=None):
        for (mine, target), copy in zip(self.places, self.copies):
            copy.wait()
            if last is not None:
                mine, target = (*mine, 0)[:2], (*target, 0)[:2]
                last[...] = self.taken[target].astype(F32) + self.held[mine].astype(F32)
            elif len(target) == 2:
                self.taken[target] = (
                    self.taken[target].astype(F32) + self.held[mine].astype(F32)
                ).astype(BF16)
            else:

                def one(number, carry, mine=mine, target=target):
                    self.taken[target[0], number] = (
                        self.taken[target[0], number].astype(F32)
                        + self.held[mine[0], number].astype(F32)
                    ).astype(BF16)
                    return carry

                lax.fori_loop(0, self.taken.shape[1], one, 0)


def halving_steps(layout):
    experts = [("expert", 1 << n) for n in range(1, layout.experts.bit_length() - 1)]
    groups = [("group", 1 << n) for n in range(layout.groups.bit_length() - 1)]
    rest = experts[1:] + groups[1:]
    by_x = [groups[0], experts[0]] + rest
    by_y = [experts[0], groups[0]] + rest
    return by_x, by_x, by_y


DONE_EXPERTS = (1, 0, 0)
DONE_LATE = (2, 1, 0)


def halving_plan(layout, shapes, first, last):
    plan = []
    for steps, shape, low, high in zip(halving_steps(layout), shapes, first, last):
        mine = []
        for step in steps[low:high]:
            shape, copies = Halving.shape(step, shape)
            mine.append((step, shape, copies))
        plan.append(mine)
    return plan


def rope_turn(x, cosine, sine):
    parts = []
    for begin in range(0, x.shape[1], LANES):
        part = x[:, begin : begin + LANES]
        lane = lax.broadcasted_iota(jnp.int32, part.shape, 1)
        other = jnp.where(
            lane % HEAD < HEAD // 2,
            pltpu.roll(part, LANES - HEAD // 2, 1),
            pltpu.roll(part, HEAD // 2, 1),
        )
        parts.append(part * cosine + other * sine)
    return jnp.concatenate(parts, axis=1)


def normed(x, gain):
    return x * lax.rsqrt(jnp.mean(x * x, axis=-1, keepdims=True) + epsilon) * gain


def slot_rows(ids_row, rows):
    labels = lax.broadcasted_iota(jnp.int32, (EXPERTS, rows), 0)
    first, second = labels == ids_row[0:1], labels == ids_row[1:2]
    both = jnp.where(first | second, 1.0, 0.0).astype(BF16)
    earlier_t = lax.broadcasted_iota(jnp.int32, (rows, rows), 0)
    later_t = lax.broadcasted_iota(jnp.int32, (rows, rows), 1)
    earlier = mm(both, jnp.where(earlier_t < later_t, 1.0, 0.0).astype(BF16))
    targets = []
    for mask, ids in ((first, ids_row[0:1]), (second, ids_row[1:2])):
        slot = jnp.sum(jnp.where(mask, earlier, 0.0), axis=0, keepdims=True)
        targets.append(jnp.where(slot < CAP, ids.astype(F32) * CAP + slot, -1.0))
    return targets


def slot_masks(number, target, rows):
    slots = (number * CAP + lax.broadcasted_iota(jnp.int32, (CAP, rows), 0)).astype(F32)
    return slots == target[0:1], slots == target[1:2]


def gather_slots(layout, target, source, made):
    rows = source.shape[0]
    for number in range(layout.peers):
        first, second = slot_masks(number, target, rows)
        chosen = jnp.where(first | second, 1.0, 0.0).astype(BF16)
        made[divmod(number, layout.experts)] = mm(chosen, source[...]).astype(BF16)


def first_kernel(
    layout,
    tokens,
    gain_attn,
    w_qkv,
    cosine,
    sine,
    relative_row,
    ids_row,
    seg_row,
    cot,
    w_out,
    gain_ffn,
    w_router_t,
    dense_gate_any,
    dense_up_any,
    dense_down_any,
    q_out,
    kv_out,
    att_t_out,
    lse_out,
    bias_out,
    target_out,
    hidden_out,
    low_out,
    mixed_out,
    grad_out,
    gate_out,
    up_out,
    down_out,
    cots_out,
    quad_out,
    rows_out,
    shares_out,
    far_cot_out,
    far_target_out,
    normed_low,
    send_cot,
    seg_all,
    acc,
    top,
    total,
    att,
    send_rows,
    send_shares,
    dense_gate,
    dense_up,
    dense_down,
    gate_held,
    up_held,
    down_held,
    load_sems,
    kv_send,
    kv_recv,
    seg_send,
    seg_recv,
    cot_send,
    cot_recv,
    quad_send,
    quad_recv,
    row_send,
    row_recv,
    share_send,
    share_recv,
    own_sems,
    far_send,
    far_recv,
    half_send,
    half_recv,
):
    rows, width = tokens.shape
    reach, experts = layout.reach, layout.experts
    ff = dense_gate.shape[1]
    e = lax.axis_index("expert")
    loads = [
        pltpu.make_async_copy(source, target, load_sems.at[number])
        for number, (source, target) in enumerate(
            ((dense_gate_any, dense_gate), (dense_up_any, dense_up), (dense_down_any, dense_down))
        )
    ]
    for copy in loads:
        copy.start()
    meet(layout)

    targets = slot_rows(relative_row[...], rows)
    target_out[0:1] = targets[0]
    target_out[1:2] = targets[1]
    target_out[2:8] = jnp.full((6, rows), -1.0, F32)
    far = [
        remote(
            source,
            target.at[number - 1],
            far_send.at[place, number - 1],
            far_recv.at[place, number - 1],
            layout.far(number),
        )
        for number in range(1, layout.outers)
        for place, (source, target) in enumerate(((cot, far_cot_out), (target_out, far_target_out)))
    ]
    for copy in far:
        copy.start()
    gather_slots(layout, target_out[...], cot, send_cot)
    cot_sends = to_row(layout, send_cot, cots_out, cot_send, cot_recv)
    own_cot = pltpu.make_async_copy(send_cot.at[:, 0], cots_out.at[:, 0], own_sems.at[0])
    own_cot.start()
    early = experts // 2
    for copy in cot_sends[:early]:
        copy.start()

    x = tokens[...].astype(F32)
    normed_low[...] = normed(x, gain_attn[...]).astype(BF16)
    seg_all[0] = seg_row[...]

    def project(step, carry):
        for part in range(3):
            columns = pl.ds(pl.multiple_of(part * width + step * TILE, TILE), TILE)
            made = mm(normed_low[...], w_qkv[:, columns])
            columns = pl.ds(pl.multiple_of(step * TILE, TILE), TILE)
            if part == 0:
                made = rope_turn(made, cosine[...], sine[...]) * HEAD ** (-0.5)
                q_out[:, columns] = made.astype(BF16)
            elif part == 1:
                made = rope_turn(made, cosine[...], sine[...])
                kv_out[0, :, columns] = made.astype(BF16)
            else:
                columns = pl.ds(pl.multiple_of(width + step * TILE, TILE), TILE)
                kv_out[0, :, columns] = made.astype(BF16)
        return carry

    lax.fori_loop(0, width // TILE, project, 0)

    halos = []
    for distance in range(1, reach + 1):
        to = {"expert": lax.rem(e + distance, experts)}
        halos.append(
            [
                pltpu.make_async_remote_copy(
                    src_ref=source.at[0],
                    dst_ref=source.at[distance],
                    send_sem=sems[0].at[distance],
                    recv_sem=sems[1].at[distance],
                    device_id=to,
                    device_id_type=MESH,
                )
                for source, sems in (
                    (kv_out, (kv_send, kv_recv)),
                    (seg_all, (seg_send, seg_recv)),
                )
            ]
        )
        for copy in halos[-1]:
            copy.start()

    lane = lax.broadcasted_iota(jnp.int32, (rows, LANES), 1)
    for distance in range(reach + 1):
        if distance:
            for copy in halos[distance - 1]:
                copy.wait()
        if distance == reach:
            for copy in cot_sends[early:]:
                copy.start()
        seg_col = jnp.transpose(jnp.broadcast_to(seg_all[distance, 0:1], (LANES, rows)))[:, 0:1]
        key_no = lax.broadcasted_iota(jnp.int32, (rows, rows), 0) - distance * rows
        offset = lax.broadcasted_iota(jnp.int32, (rows, rows), 1) - key_no
        allowed = (
            (offset >= 0)
            & (offset < WINDOW)
            & (key_no + e * rows >= 0)
            & (seg_col == seg_all[0, 0:1])
        )
        bias_out[distance] = jnp.where(allowed, 0.0, NEG).astype(BF16)

        def attend(pair, carry, distance=distance):
            columns = pl.ds(pl.multiple_of(pair * LANES, LANES), LANES)
            value_columns = pl.ds(pl.multiple_of(width + pair * LANES, LANES), LANES)
            queries = q_out[:, columns]
            keys = kv_out[distance, :, columns]
            values_t = jnp.transpose(kv_out[distance, :, value_columns])
            for inner in range(2):
                head = pair * 2 + inner
                mine = jnp.where((lane // HEAD) == inner, queries, jnp.zeros_like(queries))
                value_t = values_t[inner * HEAD : (inner + 1) * HEAD]
                out_rows = pl.ds(pl.multiple_of(head * HEAD, HEAD), HEAD)
                blocks = (
                    [(slice(0, rows // 2), rows // 2), (slice(rows // 2, rows), rows)]
                    if distance == 0
                    else [(slice(0, rows), rows)]
                )
                for q_cut, key_count in blocks:
                    scores = mm(keys[:key_count], mine[q_cut], NT)
                    scores = scores + bias_out[distance, :key_count, q_cut].astype(F32)
                    peak = jnp.max(scores, axis=0, keepdims=True)
                    if distance:
                        before = top[pl.ds(head, 1), q_cut]
                        peak = jnp.maximum(before, peak)
                    weights = jnp.exp(scores - peak)
                    amount = jnp.sum(weights, axis=0, keepdims=True)
                    part = mm(value_t[:, :key_count], weights.astype(BF16))
                    if distance:
                        shrink = jnp.exp(before - peak)
                        amount = amount + total[pl.ds(head, 1), q_cut] * shrink
                        part = part + acc[out_rows, q_cut] * shrink
                    top[pl.ds(head, 1), q_cut] = peak
                    total[pl.ds(head, 1), q_cut] = amount
                    acc[out_rows, q_cut] = part
            return carry

        lax.fori_loop(0, HEADS // 2, attend, 0)

    lse_out[...] = top[...] + jnp.log(total[...])

    def finish(pair, carry):
        out_rows = pl.ds(pl.multiple_of(pair * LANES, LANES), LANES)
        scale = jnp.concatenate(
            [
                jnp.broadcast_to(1.0 / total[pl.ds(pair * 2 + inner, 1), :], (HEAD, rows))
                for inner in range(2)
            ],
            axis=0,
        )
        made = acc[out_rows, :] * scale
        att_t_out[out_rows, :] = made.astype(BF16)
        att[:, out_rows] = jnp.transpose(made).astype(BF16)
        return carry

    lax.fori_loop(0, HEADS // 2, finish, 0)

    hidden_out[...] = tokens[...].astype(F32) + mm(att[...], w_out[...])
    low = normed(hidden_out[...], gain_ffn[...]).astype(BF16)
    low_out[...] = low
    logits = mm(w_router_t[...], low, NT)
    route = jnp.exp(logits - jnp.max(logits, axis=0, keepdims=True))
    route = route / jnp.sum(route, axis=0, keepdims=True)
    labels = lax.broadcasted_iota(jnp.int32, (EXPERTS, rows), 0)
    picked = [
        jnp.sum(jnp.where(labels == ids_row[k : k + 1], route, 0.0), axis=0, keepdims=True)
        for k in range(2)
    ]
    both = picked[0] + picked[1]
    shares = []
    for k in range(2):
        parts = split3(picked[k] / both)
        shares.append(
            jnp.concatenate(
                [part.astype(F32) for part in parts] + [jnp.zeros((5, rows), F32)], axis=0
            ).astype(BF16)
        )
    send_shares[...] = jnp.zeros_like(send_shares)
    for number in range(layout.peers):
        first, second = slot_masks(number, target_out[...], rows)
        first = jnp.where(first, 1.0, 0.0).astype(BF16)
        second = jnp.where(second, 1.0, 0.0).astype(BF16)
        place = divmod(number, experts)
        send_rows[place] = mm(first + second, low).astype(BF16)
        share = mm(shares[0], first, NT) + mm(shares[1], second, NT)
        share = jnp.sum(share, axis=0, keepdims=True)
        send_shares[place + (slice(None), slice(0, CAP))] = jnp.broadcast_to(share, (8, CAP))
    sends = to_row(layout, send_rows, rows_out, row_send, row_recv)
    sends += to_row(layout, send_shares, shares_out, share_send, share_recv)
    for source, target, sem in (
        (send_rows, rows_out, own_sems.at[1]),
        (send_shares, shares_out, own_sems.at[2]),
    ):
        sends.append(pltpu.make_async_copy(source.at[:, 0], target.at[:, 0], sem))
    for copy in reversed(sends):
        copy.start()
    own_cot.wait()
    for copy in cot_sends:
        copy.wait()
    sends += to_quad(layout, cots_out, quad_out, quad_send, quad_recv)
    sends.append(pltpu.make_async_copy(cots_out.at[0], quad_out.at[0], own_sems.at[3]))
    for copy in sends[-layout.share :]:
        copy.start()

    for copy in loads:
        copy.wait()
    mixed_out[...] = hidden_out[...]
    grad_out[...] = jnp.zeros_like(grad_out)
    part_width = ff // experts
    per_part = part_width // TILE
    half = experts // 2
    odd = bit_of("expert", 1)
    halvings = [
        Halving(("expert", 1), held, taken, half_send.at[number], half_recv.at[number])
        for number, (held, taken) in enumerate(
            ((gate_held, gate_out), (up_held, up_out), (down_held, down_out))
        )
    ]

    def branch(step, carry):
        place = step // per_part
        part = 2 * (place % half) + (odd + 1 + place // half) % 2
        columns = pl.ds(pl.multiple_of(part * part_width + (step % per_part) * TILE, TILE), TILE)
        gate_w, up_w, down_w = dense_gate[:, columns], dense_up[:, columns], dense_down[columns, :]
        gate_pre = mm(low_out[...], gate_w)
        up_pre = mm(low_out[...], up_w)
        grad_act = mm(cot[...], down_w, NT)
        silu, slope = silu_parts(gate_pre)
        act = (silu * up_pre).astype(BF16)
        grad_gate = (grad_act * up_pre * slope).astype(BF16)
        grad_up = (grad_act * silu).astype(BF16)
        mixed_out[...] += mm(act, down_w)
        grad_out[...] += mm(grad_gate, gate_w, NT) + mm(grad_up, up_w, NT)
        inside = pl.ds(pl.multiple_of((step % per_part) * TILE, TILE), TILE)
        for made, held in (
            (mm(low_out[...], grad_gate, TN), gate_held),
            (mm(low_out[...], grad_up, TN), up_held),
        ):
            made = made.astype(BF16)
            block = held.shape[2]
            for place in range(held.shape[1]):
                held[part, place, :, inside] = made[place * block : (place + 1) * block]
        made = mm(act, cot[...], TN).astype(BF16)
        block = down_held.shape[2]
        cut = width // experts
        low_row = part * part_width + (step % per_part) * TILE
        for inner in range(0, TILE, block):
            for other in range(experts):
                down_held[other, (low_row + inner) // block] = made[
                    inner : inner + block, other * cut : (other + 1) * cut
                ]
        return carry

    lax.fori_loop(0, ff // (2 * TILE), branch, 0)
    for halving in halvings[:2]:
        halving.start()
    lax.fori_loop(ff // (2 * TILE), ff // TILE, branch, 0)
    halvings[2].start()
    for halving in halvings:
        halving.add()
    for copy in far + sends:
        copy.wait()


def first(layout, tokens, gain_attn, w_qkv, cosine, sine, relative_row, ids_row, seg_row, cot, w_out, gain_ffn, w_router_t, dense_gate, dense_up, dense_down):
    rows, width = tokens.shape
    ff = dense_gate.shape[1]
    reach, experts, groups = layout.reach, layout.experts, layout.groups
    half = experts // 2
    others = layout.outers - 1
    dma = pltpu.SemaphoreType.DMA
    wide = (groups, width // groups, ff // experts)
    tall = (groups, ff // groups, width // experts)
    return pl.pallas_call(
        functools.partial(first_kernel, layout),
        out_shape=[
            jax.ShapeDtypeStruct((rows, width), BF16),
            jax.ShapeDtypeStruct((reach + 1, rows, 2 * width), BF16),
            jax.ShapeDtypeStruct((width, rows), BF16),
            jax.ShapeDtypeStruct((EXPERTS, rows), F32),
            jax.ShapeDtypeStruct((reach + 1, rows, rows), BF16),
            jax.ShapeDtypeStruct((8, rows), F32),
            jax.ShapeDtypeStruct((rows, width), F32),
            jax.ShapeDtypeStruct((rows, width), BF16),
            jax.ShapeDtypeStruct((rows, width), F32),
            jax.ShapeDtypeStruct((rows, width), F32),
            jax.ShapeDtypeStruct((half,) + wide, BF16),
            jax.ShapeDtypeStruct((half,) + wide, BF16),
            jax.ShapeDtypeStruct((half,) + tall, BF16),
            jax.ShapeDtypeStruct(layout.slots(width), BF16),
            jax.ShapeDtypeStruct(layout.slots(width), BF16),
            jax.ShapeDtypeStruct(layout.slots(width), BF16),
            jax.ShapeDtypeStruct((layout.share, experts, 8, LANES), F32),
            jax.ShapeDtypeStruct((others, rows, width), BF16),
            jax.ShapeDtypeStruct((others, 8, rows), F32),
        ],
        in_specs=[VMEM] * 12 + [ANY] * 3,
        out_specs=[VMEM] * 13 + [ANY] * 6,
        scratch_shapes=[
            pltpu.VMEM((rows, width), BF16),
            pltpu.VMEM(layout.slots(width), BF16),
            pltpu.VMEM((reach + 1, 8, rows), F32),
            pltpu.VMEM((width, rows), F32),
            pltpu.VMEM((EXPERTS, rows), F32),
            pltpu.VMEM((EXPERTS, rows), F32),
            pltpu.VMEM((rows, width), BF16),
            pltpu.VMEM(layout.slots(width), BF16),
            pltpu.VMEM((layout.share, experts, 8, LANES), F32),
            pltpu.VMEM((width, ff), BF16),
            pltpu.VMEM((width, ff), BF16),
            pltpu.VMEM((ff, width), BF16),
            pltpu.VMEM((experts,) + wide, BF16),
            pltpu.VMEM((experts,) + wide, BF16),
            pltpu.VMEM((experts,) + tall, BF16),
            dma((3,)),
            dma((reach + 1,)),
            dma((reach + 1,)),
            dma((reach + 1,)),
            dma((reach + 1,)),
            dma((experts,)),
            dma((experts,)),
            dma((layout.share,)),
            dma((layout.share,)),
            dma((experts,)),
            dma((experts,)),
            dma((experts,)),
            dma((experts,)),
            dma((4,)),
            dma((2, others)),
            dma((2, others)),
            dma((3, half)),
            dma((3, half)),
        ],
        compiler_params=pltpu.CompilerParams(
            collective_id=0, has_side_effects=True, vmem_limit_bytes=62 * MIB
        ),
        cost_estimate=pl.CostEstimate(flops=1 << 30, bytes_accessed=1 << 20, transcendentals=0),
        name="first",
    )(tokens, gain_attn, w_qkv, cosine, sine, relative_row, ids_row, seg_row, cot, w_out, gain_ffn, w_router_t, dense_gate, dense_up, dense_down)


def split3(x):
    high = x.astype(BF16)
    rest = x - high.astype(F32)
    middle = rest.astype(BF16)
    return high, middle, (rest - middle.astype(F32)).astype(BF16)


def silu_parts(gate_pre):
    gate = 1.0 / (1.0 + jnp.exp(-gate_pre))
    return gate_pre * gate, gate * (1.0 + gate_pre * (1.0 - gate))


def share_column(share_row):
    across = lax.broadcasted_iota(jnp.int32, (CAP, CAP), 1)
    down = lax.broadcasted_iota(jnp.int32, (CAP, CAP), 0)
    return jnp.sum(jnp.where(across == down, share_row, 0.0), axis=1, keepdims=True)


def own_share(layout):
    return lax.rem(lax.axis_index("group"), layout.share)


class Sums:
    def __init__(self, layout, shapes, first, last, keep):
        self.plan = halving_plan(layout, shapes, first, last)
        self.keep = keep

    def scratch(self):
        made = []
        for mine in self.plan:
            for number, (_, shape, copies) in enumerate(mine):
                made += trade_sems(copies)
                if not self.keep or number + 1 < len(mine):
                    made.append(pltpu.VMEM(shape, BF16))
        return made

    def outputs(self):
        return [jax.ShapeDtypeStruct(mine[-1][1], BF16) for mine in self.plan if mine]

    def chains(self, held_refs, outputs, scratch):
        outputs, scratch = list(outputs), list(scratch)
        chains = []
        for held, mine in zip(held_refs, self.plan):
            chain = []
            for number, (step, _, _) in enumerate(mine):
                sems = scratch.pop(0), scratch.pop(0)
                if not self.keep or number + 1 < len(mine):
                    taken = scratch.pop(0)
                else:
                    taken = outputs.pop(0)
                chain.append(Halving(step, held, taken, *sems))
                held = taken
            chains.append(chain)
        return chains


def experts_kernel(layout, sums, *refs):
    (
        rows_in,
        cots,
        shares,
        gate_any,
        up_any,
        down_any,
        rows_any,
        shares_any,
        gate_held,
        up_held,
        down_held,
        back_out,
        grad_back,
        quad_rows,
        quad_shares,
        far_rows,
        gate_sum,
        gate_w,
        up_w,
        down_w,
        scaled,
        acc,
        grad_acc,
        send_out,
        send_grad,
        load_sems,
        back_send,
        back_recv,
        quad_send,
        quad_recv,
        own_sems,
        far_send,
        far_recv,
        *rest,
    ) = refs
    share, experts = layout.share, layout.experts
    width, ff = gate_w.shape[1:]
    mine = own_share(layout)

    def load(turn):
        return [
            pltpu.make_async_copy(
                source.at[flipped(mine, turn)], target.at[turn % 2], load_sems.at[turn % 2, number]
            )
            for number, (source, target) in enumerate(
                ((gate_any, gate_w), (up_any, up_w), (down_any, down_w))
            )
        ]

    for copy in load(0):
        copy.start()
    meet(layout)
    quads = to_quad(layout, rows_any, quad_rows, quad_send.at[0], quad_recv.at[0])
    quads += to_quad(layout, shares_any, quad_shares, quad_send.at[1], quad_recv.at[1])
    own = [
        pltpu.make_async_copy(rows_any.at[0], quad_rows.at[0], own_sems.at[2]),
        pltpu.make_async_copy(shares_any.at[0], quad_shares.at[0], own_sems.at[3]),
    ]
    far_low, far_high = far_parts(layout)[0]
    fars = [
        to_far(layout, rows_any, far_rows.at[:, 0:1], 0, 1, far_send.at[0], far_recv.at[0]),
        to_far(layout, quad_rows, far_rows.at[:, 1:], 1, far_high, far_send.at[1], far_recv.at[1])
        if far_high > 1
        else [],
    ]
    for copy in quads + own + fars[0]:
        copy.start()
    chains = sums.chains((gate_held, up_held, down_held), (gate_sum,), rest)
    for chain in chains:
        for halving in chain[:1]:
            halving.start()

    chunk = 2 * TILE
    copies = list(own)
    for turn in range(share):
        for copy in load(turn):
            copy.wait()
        if turn + 1 < share:
            for copy in load(turn + 1):
                copy.start()
        slot = turn % 2
        for number in range(experts):
            column = share_column(shares[turn, number, 0:1, :CAP])
            scaled[number] = (cots[turn, number].astype(F32) * column).astype(BF16)

        def step(number, carry, turn=turn, slot=slot):
            columns = pl.ds(pl.multiple_of(number * chunk, chunk), chunk)
            n = rows_in[turn].reshape(experts * CAP, width)
            grad = scaled[...].reshape(experts * CAP, width)
            gate_pre = mm(n, gate_w[slot, :, columns])
            up_pre = mm(n, up_w[slot, :, columns])
            grad_act = mm(grad, down_w[slot, columns, :], NT)
            silu, slope = silu_parts(gate_pre)
            act = (silu * up_pre).astype(BF16)
            grad_gate = (grad_act * up_pre * slope).astype(BF16)
            grad_up = (grad_act * silu).astype(BF16)
            acc[...] += mm(act, down_w[slot, columns, :])
            grad_acc[...] += mm(grad_gate, gate_w[slot, :, columns], NT) + mm(
                grad_up, up_w[slot, :, columns], NT
            )
            return carry

        acc[...] = jnp.zeros_like(acc)
        grad_acc[...] = jnp.zeros_like(grad_acc)
        lax.fori_loop(0, ff // chunk, step, 0)
        send_out[turn] = acc[...].astype(BF16).reshape(experts, CAP, width)
        send_grad[turn] = grad_acc[...].astype(BF16).reshape(experts, CAP, width)
        for bits in reversed(range(experts)):
            for which, (source, target) in enumerate(
                ((send_out, back_out), (send_grad, grad_back))
            ):
                ends = source.at[turn, bits], target.at[turn, bits]
                sem = which, turn, bits
                if bits:
                    device = {"expert": flipped(lax.axis_index("expert"), bits)}
                    copies.append(remote(*ends, back_send.at[sem], back_recv.at[sem], device))
                else:
                    copies.append(pltpu.make_async_copy(*ends, back_send.at[sem]))
                copies[-1].start()
        if turn == share // 2:
            for copy in quads:
                copy.wait()
            for copy in fars[1]:
                copy.start()
    for chain in chains:
        for halving in chain:
            halving.add()
    for copy in copies + fars[0] + fars[1]:
        copy.wait()


def far_parts(layout):
    middle = max(layout.share // 2, 1)
    return (0, middle), (middle, layout.share)


def run_experts(layout, rows_in, cots, shares, expert_gate, expert_up, expert_down, held):
    share, experts, others = layout.share, layout.experts, layout.outers - 1
    _, width, ff = expert_gate.shape
    dma = pltpu.SemaphoreType.DMA
    sums = Sums(layout, [one.shape for one in held], (0, 0, 0), DONE_EXPERTS, True)
    slots = jax.ShapeDtypeStruct(layout.slots(width), BF16)
    return pl.pallas_call(
        functools.partial(experts_kernel, layout, sums),
        out_shape=[
            slots,
            slots,
            slots,
            jax.ShapeDtypeStruct(shares.shape, F32),
            far_shape(layout, far_parts(layout)[0][1], width),
            *sums.outputs(),
        ],
        in_specs=[VMEM] * 3 + [ANY] * 5 + [VMEM] * 3,
        out_specs=[ANY] * 5 + [VMEM],
        scratch_shapes=[
            pltpu.VMEM((2, width, ff), BF16),
            pltpu.VMEM((2, width, ff), BF16),
            pltpu.VMEM((2, ff, width), BF16),
            pltpu.VMEM((experts, CAP, width), BF16),
            pltpu.VMEM((experts * CAP, width), F32),
            pltpu.VMEM((experts * CAP, width), F32),
            pltpu.VMEM(layout.slots(width), BF16),
            pltpu.VMEM(layout.slots(width), BF16),
            dma((2, 3)),
            dma((2, share, experts)),
            dma((2, share, experts)),
            dma((2, share)),
            dma((2, share)),
            dma((4,)),
            dma((2, others)),
            dma((2, others)),
            *sums.scratch(),
        ],
        compiler_params=pltpu.CompilerParams(
            collective_id=1, has_side_effects=True, vmem_limit_bytes=60 * MIB
        ),
        cost_estimate=pl.CostEstimate(flops=1 << 30, bytes_accessed=1 << 20, transcendentals=0),
        name="experts",
    )(
        rows_in,
        cots,
        shares,
        expert_gate,
        expert_up,
        expert_down,
        rows_in,
        shares,
        *held,
    )


def rope_back(grad, cosine, sine):
    lane = lax.broadcasted_iota(jnp.int32, grad.shape, 1)
    turned = grad * sine
    other = jnp.where(
        lane % HEAD < HEAD // 2,
        pltpu.roll(turned, LANES - HEAD // 2, 1),
        pltpu.roll(turned, HEAD // 2, 1),
    )
    return grad * cosine + other


def by_blocks(target, made):
    parts, places, block, cut = target.shape
    for part in range(parts):
        for place in range(places):
            target[part, place] = made[
                place * block : (place + 1) * block, part * cut : (part + 1) * cut
            ]


def combine_part(
    back,
    grad_back,
    target,
    ids_col,
    hidden,
    mixed_in,
    grad_in,
    low,
    cot,
    gain,
    w_router,
    w_out,
    att_t,
    mixed_out,
    grad_hidden_out,
    grad_att_out,
    proj_out,
    router_out,
    gain_out,
):
    rows, width = hidden.shape
    slots = back.shape[0] * back.shape[1] * CAP
    columns = jnp.transpose(
        jnp.concatenate([target[...], jnp.zeros((LANES - 8, rows), F32)], axis=0)
    )
    slot_no = lax.broadcasted_iota(jnp.int32, (rows, slots), 1).astype(F32)
    cot_float = cot[...].astype(F32)
    logits = mm(low[...], w_router[...])
    route = jnp.exp(logits - jnp.max(logits, axis=1, keepdims=True))
    route = route / jnp.sum(route, axis=1, keepdims=True)
    labels = lax.broadcasted_iota(jnp.int32, (rows, EXPERTS), 1)
    masks = [labels == ids_col[:, k : k + 1] for k in range(2)]
    picked = [jnp.sum(jnp.where(mask, route, 0.0), axis=1, keepdims=True) for mask in masks]
    both = picked[0] + picked[1]
    chosen, shares, grads = [], [], []
    mixed = mixed_in[...]
    for k in range(2):
        chosen.append(jnp.where(slot_no == columns[:, k : k + 1], 1.0, 0.0).astype(BF16))
        fetched = mm(chosen[k], back[...].reshape(slots, width))
        shares.append(picked[k] / both)
        mixed = mixed + shares[k] * fetched
        grads.append(jnp.sum(cot_float * fetched, axis=1, keepdims=True))
    mixed_out[...] = mixed.astype(BF16)
    mean = grads[0] * shares[0] + grads[1] * shares[1]
    grad_route = jnp.zeros_like(route)
    for k in range(2):
        grad_route = grad_route + jnp.where(masks[k], (grads[k] - mean) / both, 0.0)
    grad_logits = route * (grad_route - jnp.sum(route * grad_route, axis=1, keepdims=True))
    grad_logits = grad_logits.astype(BF16)
    router_out[...] = mm(grad_logits, low[...], TN)
    grad = grad_in[...] + mm(chosen[0] + chosen[1], grad_back[...].reshape(slots, width))
    grad = grad + mm(grad_logits, w_router[...], NT)
    h = hidden[...]
    scale = lax.rsqrt(jnp.mean(h * h, axis=-1, keepdims=True) + epsilon)
    gain_out[...] = jnp.sum(grad * h * scale, axis=0, keepdims=True)
    grad = grad * gain[...]
    grad = scale * grad - h * (scale * scale * scale) * jnp.mean(grad * h, axis=-1, keepdims=True)
    grad = cot_float + grad
    grad_hidden_out[...] = grad
    grad_low = grad.astype(BF16)
    grad_att_out[...] = mm(grad_low, w_out[...], NT).astype(BF16)
    by_blocks(proj_out, mm(att_t[...], grad_low).astype(BF16))


def late_kernel(layout, sums, *refs):
    (
        back,
        grad_back,
        target,
        ids_col,
        hidden,
        mixed_in,
        grad_in,
        low,
        cot,
        gain_ffn,
        w_router,
        w_out,
        att_t,
        q_in,
        kv_in,
        bias,
        lse,
        tokens,
        gain,
        w_qkv,
        cosine,
        sine,
        gate_held,
        up_held,
        down_held,
        far_cot,
        far_target,
        rows_any,
        shares_any,
        mixed_out,
        tokens_out,
        proj_out,
        qkv_out,
        small_out,
        gate_sum,
        up_sum,
        far_cots_out,
        far_out,
        far_shares_out,
        grad_att,
        router_term,
        gain_term,
        send_cot,
        halo_send,
        halo_recv,
        own_kv,
        packed,
        send_sems,
        recv_sems,
        cot_send,
        cot_recv,
        own_sem,
        far_send,
        far_recv,
        *rest,
    ) = refs
    rows, width = tokens.shape
    reach, experts = layout.reach, layout.experts
    e = lax.axis_index("expert")
    pairs = HEADS // 2
    lane = lax.broadcasted_iota(jnp.int32, (rows, LANES), 1)
    meet(layout)
    far_low, far_high = far_parts(layout)[1]
    far = to_far(layout, rows_any, far_out, far_low, far_high, far_send.at[0], far_recv.at[0])
    far += to_far(
        layout, shares_any, far_shares_out, 0, layout.share, far_send.at[1], far_recv.at[1]
    )
    for copy in far:
        copy.start()
    chains = sums.chains((gate_held, up_held, down_held), (gate_sum, up_sum), rest)
    for chain in chains:
        for halving in chain[:1]:
            halving.start()
    cot_sends = []
    for number in range(layout.outers - 1):
        for copy in cot_sends:
            copy.wait()
        load = pltpu.make_async_copy(far_cot.at[number], grad_att, own_sem.at[number])
        load.start()
        load.wait()
        gather_slots(layout, far_target[number], grad_att, send_cot)
        cot_sends = to_peers(
            layout, send_cot, far_cots_out.at[number], cot_send.at[number], cot_recv.at[number]
        )
        cot_sends.append(
            pltpu.make_async_copy(
                send_cot.at[0, 0], far_cots_out.at[number, 0, 0], own_sem.at[number]
            )
        )
        for copy in cot_sends:
            copy.start()

    combine_part(
        back,
        grad_back,
        target,
        ids_col,
        hidden,
        mixed_in,
        grad_in,
        low,
        cot,
        gain_ffn,
        w_router,
        w_out,
        att_t,
        mixed_out,
        tokens_out,
        grad_att,
        proj_out,
        router_term,
        gain_term,
    )

    def halo(distance, pair):
        return pltpu.make_async_remote_copy(
            src_ref=halo_send.at[distance - 1, pair],
            dst_ref=halo_recv.at[distance - 1, pair],
            send_sem=send_sems.at[distance - 1, pair],
            recv_sem=recv_sems.at[distance - 1, pair],
            device_id={"expert": lax.rem(e + experts - distance, experts)},
            device_id_type=MESH,
        )

    def heads(pair, carry):
        columns = pl.ds(pl.multiple_of(pair * LANES, LANES), LANES)
        value_columns = pl.ds(pl.multiple_of(width + pair * LANES, LANES), LANES)
        queries, grads = q_in[:, columns], grad_att[:, columns]
        grads_t = jnp.transpose(grads.astype(F32))
        shrunk = grads_t * att_t[columns, :].astype(F32)
        grad_q = [None, None]
        for distance in range(reach, -1, -1):
            keys = kv_in[distance, :, columns]
            values = kv_in[distance, :, value_columns]
            keys_t = jnp.transpose(keys)
            grad_k = grad_v = None
            for inner in range(2):
                head = pair * 2 + inner
                cut = slice(inner * HEAD, (inner + 1) * HEAD)
                mine = (lane // HEAD) == inner
                query = jnp.where(mine, queries, jnp.zeros_like(queries))
                grad = jnp.where(mine, grads, jnp.zeros_like(grads))
                total = jnp.sum(shrunk[cut], axis=0, keepdims=True)
                scores = mm(keys, query, NT) + bias[distance].astype(F32)
                probs = jnp.exp(scores - lse[pl.ds(head, 1), :])
                grad_probs = mm(values, grad, NT)
                grad_scores = (probs * (grad_probs - total)).astype(BF16)
                part_v = mm(probs.astype(BF16), grad)
                part_k = mm(grad_scores, query)
                part_q = mm(keys_t[cut], grad_scores)
                grad_v = part_v if grad_v is None else grad_v + part_v
                grad_k = part_k if grad_k is None else grad_k + part_k
                grad_q[inner] = part_q if grad_q[inner] is None else grad_q[inner] + part_q
            if distance:
                halo_send[distance - 1, pair, 0] = grad_k.astype(BF16)
                halo_send[distance - 1, pair, 1] = grad_v.astype(BF16)
                halo(distance, pair).start()
            else:
                own_kv[pair, 0] = grad_k
                own_kv[pair, 1] = grad_v
        grad = jnp.transpose(jnp.concatenate(grad_q, axis=0)) * HEAD ** (-0.5)
        packed[:, columns] = rope_back(grad, cosine[...], sine[...]).astype(BF16)
        return carry

    lax.fori_loop(0, pairs, heads, 0)
    x = tokens[...].astype(F32)
    grad_att[...] = normed(x, gain[...]).astype(BF16)
    normed_low = grad_att

    def merge(pair, carry):
        grad_k, grad_v = own_kv[pair, 0], own_kv[pair, 1]
        for distance in range(1, reach + 1):
            halo(distance, pair).wait()
            grad_k = grad_k + halo_recv[distance - 1, pair, 0].astype(F32)
            grad_v = grad_v + halo_recv[distance - 1, pair, 1].astype(F32)
        columns = pl.ds(pl.multiple_of(width + pair * LANES, LANES), LANES)
        packed[:, columns] = rope_back(grad_k, cosine[...], sine[...]).astype(BF16)
        columns = pl.ds(pl.multiple_of(2 * width + pair * LANES, LANES), LANES)
        packed[:, columns] = grad_v.astype(BF16)
        return carry

    lax.fori_loop(0, pairs, merge, 0)
    for chain in chains:
        for halving in chain:
            halving.add()
    parts, places, block, cut = qkv_out.shape
    for part in range(parts):
        made = mm(normed_low[...], packed[:, part * cut : (part + 1) * cut], TN).astype(BF16)
        for place in range(places):
            qkv_out[part, place] = made[place * block : (place + 1) * block]
    grad = mm(packed[...], w_qkv[...], NT)
    scale = lax.rsqrt(jnp.mean(x * x, axis=-1, keepdims=True) + epsilon)
    gain_back = jnp.sum(grad * x * scale, axis=0, keepdims=True)
    small_out[...] = jnp.concatenate(
        [router_term[...], gain_term[...], gain_back, jnp.zeros((6, width), F32)], axis=0
    )
    grad = grad * gain[...]
    grad = scale * grad - x * (scale * scale * scale) * jnp.mean(grad * x, axis=-1, keepdims=True)
    tokens_out[...] += grad
    for copy in far + cot_sends:
        copy.wait()


def late(layout, combine_ins, back_ins, held, far_cot, far_target, rows_in, shares):
    tokens = back_ins[4]
    rows, width = tokens.shape
    reach, peers, others = layout.reach, layout.peers, layout.outers - 1
    dma = pltpu.SemaphoreType.DMA
    pairs = HEADS // 2
    sums = Sums(layout, [one.shape for one in held], DONE_EXPERTS, DONE_LATE, True)
    blocks = (layout.experts, layout.groups, width // layout.groups)
    far_low, far_high = far_parts(layout)[1]
    return pl.pallas_call(
        functools.partial(late_kernel, layout, sums),
        out_shape=[
            jax.ShapeDtypeStruct((rows, width), BF16),
            jax.ShapeDtypeStruct((rows, width), F32),
            jax.ShapeDtypeStruct(blocks + (width // layout.experts,), BF16),
            jax.ShapeDtypeStruct(blocks + (3 * width // layout.experts,), BF16),
            jax.ShapeDtypeStruct((SMALL, width), F32),
            *sums.outputs(),
            jax.ShapeDtypeStruct((others,) + layout.slots(width), BF16),
            far_shape(layout, far_high - far_low, width),
            jax.ShapeDtypeStruct((others,) + shares.shape, F32),
        ],
        in_specs=[VMEM] * 25 + [ANY, VMEM, ANY, ANY],
        out_specs=[VMEM] * 7 + [ANY] * 3,
        scratch_shapes=[
            pltpu.VMEM((rows, width), BF16),
            pltpu.VMEM((EXPERTS, width), F32),
            pltpu.VMEM((1, width), F32),
            pltpu.VMEM(layout.slots(width), BF16),
            pltpu.VMEM((reach, pairs, 2, rows, LANES), BF16),
            pltpu.VMEM((reach, pairs, 2, rows, LANES), BF16),
            pltpu.VMEM((pairs, 2, rows, LANES), F32),
            pltpu.VMEM((rows, 3 * width), BF16),
            dma((reach, pairs)),
            dma((reach, pairs)),
            dma((others, peers)),
            dma((others, peers)),
            dma((others,)),
            dma((2, others)),
            dma((2, others)),
            *sums.scratch(),
        ],
        compiler_params=pltpu.CompilerParams(
            collective_id=2, has_side_effects=True, vmem_limit_bytes=63 * MIB
        ),
        cost_estimate=pl.CostEstimate(flops=1 << 30, bytes_accessed=1 << 20, transcendentals=0),
        name="late",
    )(*combine_ins, *back_ins, *held, far_cot, far_target, rows_in, shares)


def weights_kernel(layout, sums, more, *refs):
    share, outers, peers = layout.share, layout.outers, layout.peers
    (
        rows_own,
        cots_own,
        shares_own,
        rows_a,
        rows_b,
        cots_far,
        shares_far,
        gate_any,
        up_any,
        down_any,
        *terms,
    ) = refs[:15]
    small_in = refs[15]
    gate_out, up_out, down_out = refs[16:19]
    sums_out = refs[19:24]
    small_out = refs[24]
    (
        gate_w,
        up_w,
        gate_t,
        up_t,
        down_w,
        rows_buf,
        cots_buf,
        shares_buf,
        accs,
        sends,
        takes,
        down_sends,
        down_takes,
        small_sums,
        small_takes,
        load_sems,
        piece_sems,
        send_sems,
        recv_sems,
        small_send,
        small_recv,
    ) = refs[25:46]
    rest = refs[46:]
    width = gate_w.shape[0]
    ff = gate_any.shape[2]
    span = ff // outers
    cut = ff // layout.groups
    group = lax.axis_index("group")
    mine = own_share(layout)
    begin = pl.multiple_of((group // share) * span, span)
    loads = [
        pltpu.make_async_copy(gate_any.at[mine, :, pl.ds(begin, span)], gate_w, load_sems.at[0]),
        pltpu.make_async_copy(up_any.at[mine, :, pl.ds(begin, span)], up_w, load_sems.at[1]),
        pltpu.make_async_copy(down_any.at[mine, pl.ds(begin, span), :], down_w, load_sems.at[2]),
    ]

    def fetch(outer):
        slot = outer % 2
        if outer == 0:
            sources = [
                (rows_own, rows_buf.at[slot]),
                (cots_own, cots_buf.at[slot]),
                (shares_own, shares_buf.at[slot]),
            ]
        else:
            sources = [
                (one.at[outer - 1], rows_buf.at[slot, low:high])
                for one, (low, high) in zip((rows_a, rows_b), far_parts(layout))
            ]
            sources.append((cots_far.at[outer - 1], cots_buf.at[slot]))
            sources.append((shares_far.at[outer - 1], shares_buf.at[slot]))
        return [
            pltpu.make_async_copy(source, target, piece_sems.at[slot, number])
            for number, (source, target) in enumerate(sources)
        ]

    for copy in loads + fetch(0):
        copy.start()
    meet(layout)

    chains = sums.chains(terms[:3], (), rest)
    chains += more.chains(terms[3:], (), rest[len(sums.scratch()) :])
    steps = [("expert", 1 << n) for n in range(layout.experts.bit_length() - 1)]
    steps += [("group", 1 << n) for n in range(layout.groups.bit_length() - 1)]
    levels = len(steps)
    small_sums[0] = small_in[...]

    def small_copy(level):
        axis, bit = steps[level]
        return pltpu.make_async_remote_copy(
            src_ref=small_sums.at[level],
            dst_ref=small_takes.at[level],
            send_sem=small_send.at[level],
            recv_sem=small_recv.at[level],
            device_id={axis: flipped(lax.axis_index(axis), bit)},
            device_id_type=MESH,
        )

    def advance(level):
        for number, chain in enumerate(chains):
            if 0 < level <= len(chain):
                chain[level - 1].add(sums_out[number] if level == len(chain) else None)
            if level < len(chain):
                chain[level].start()
        if level:
            small_copy(level - 1).wait()
            made = small_sums[level - 1] + small_takes[level - 1]
            if level < levels:
                small_sums[level] = made
            else:
                small_out[...] = made
        if level < levels:
            small_copy(level).start()

    advance(0)
    points = share * outers
    marks = [max(0, (points * at) // 8 - 1) for at in (2, 6, 7, 8)]
    done = 1

    for copy in loads:
        copy.wait()
    gate_t[...] = jnp.transpose(gate_w[...])
    up_t[...] = jnp.transpose(up_w[...])
    experts = layout.experts
    count = max(8 // experts, 1)
    blocks = share // count

    def add(slot, chunk, block):
        parts = pl.ds(block * count, count)
        n = rows_buf[slot, parts].reshape(count * experts * CAP, width)
        grad = cots_buf[slot, parts].reshape(count * experts * CAP, width)
        base = pl.multiple_of(chunk * cut, cut)
        gate_pre = mm(gate_t[pl.ds(base, cut), :], n, NT)
        up_pre = mm(up_t[pl.ds(base, cut), :], n, NT)
        grad_act = mm(down_w[pl.ds(base, cut), :], grad, NT)
        silu, slope = silu_parts(gate_pre)
        act = (silu * up_pre).astype(BF16)
        grad_gate = (grad_act * up_pre * slope).astype(BF16)
        grad_up = (grad_act * silu).astype(BF16)
        accs[0] += mm(grad_gate, n)
        accs[1] += mm(grad_up, n)
        accs[2] += mm(act, grad)

    copies = []
    turns = [*range(share - 1, 0, -1), 0]
    resident = outers <= 2
    for place, turn in enumerate(turns):
        owner = flipped(mine, turn)
        accs[...] = jnp.zeros_like(accs)
        for outer in range(outers):
            slot = outer % 2
            if place == 0 or not resident:
                if place or outer:
                    for copy in fetch(outer):
                        copy.start()
                for copy in fetch(outer):
                    copy.wait()

                def scale(number, carry, slot=slot):
                    at = slot, number // experts, number % experts
                    column = share_column(shares_buf[at + (slice(0, 1), slice(0, CAP))])
                    cots_buf[at] = (cots_buf[at].astype(F32) * column).astype(BF16)
                    return carry

                lax.fori_loop(0, peers, scale, 0)

            def step(number, carry, slot=slot, owner=owner):
                add(slot, owner, number)
                return carry

            lax.fori_loop(0, blocks, step, 0)
            while done <= len(marks) and marks[done - 1] <= place * outers + outer:
                if done < levels:
                    advance(done)
                done += 1
        for which in range(3):
            made = accs[which]
            if which < 2:
                made = jnp.transpose(made)
            target = (gate_out, up_out, down_out)[which]
            if turn == 0:
                target[owner] = made
                continue
            if which < 2:
                ends = sends.at[turn - 1, which], takes.at[turn - 1, which]
            else:
                ends = down_sends.at[turn - 1], down_takes.at[turn - 1]
            ends[0][...] = made.astype(BF16)
            copy = pltpu.make_async_remote_copy(
                src_ref=ends[0],
                dst_ref=ends[1],
                send_sem=send_sems.at[turn - 1, which],
                recv_sem=recv_sems.at[turn - 1, which],
                device_id={"group": flipped(group, turn)},
                device_id_type=MESH,
            )
            copy.start()
            copies.append((turn, which, copy))
    for level in range(done, levels + 1):
        advance(level)
    for turn, which, copy in copies:
        copy.wait()
        target = (gate_out, up_out, down_out)[which]
        got = takes[turn - 1, which] if which < 2 else down_takes[turn - 1]
        target[flipped(mine, turn)] = got.astype(F32)


def weights(layout, own, rows_far, cots_far, shares_far, expert_weights, held, terms, small):
    share, outers = layout.share, layout.outers
    experts, width, ff = expert_weights[0].shape
    span = ff // outers
    cut = ff // layout.groups
    dma = pltpu.SemaphoreType.DMA
    levels = layout.experts.bit_length() + layout.groups.bit_length() - 2
    sums = Sums(layout, [one.shape for one in held], DONE_LATE, (levels,) * 3, False)
    more = Sums(layout, [], (), (), False)
    steps = [("expert", 1 << n) for n in range(layout.experts.bit_length() - 1)]
    steps += [("group", 1 << n) for n in range(layout.groups.bit_length() - 1)]
    for term in terms:
        shape, mine = term.shape, []
        for step in steps:
            shape, copies = Halving.shape(step, shape)
            mine.append((step, shape, copies))
        more.plan.append(mine)
    return pl.pallas_call(
        functools.partial(weights_kernel, layout, sums, more),
        out_shape=[
            jax.ShapeDtypeStruct((experts, width, cut), F32),
            jax.ShapeDtypeStruct((experts, width, cut), F32),
            jax.ShapeDtypeStruct((experts, cut, width), F32),
            *[jax.ShapeDtypeStruct(one.shape[2:], F32) for one in (*held, *terms)],
            jax.ShapeDtypeStruct((SMALL, width), F32),
        ],
        in_specs=[ANY] * 10 + [VMEM] * 6,
        out_specs=[VMEM] * 9,
        scratch_shapes=[
            pltpu.VMEM((width, span), BF16),
            pltpu.VMEM((width, span), BF16),
            pltpu.VMEM((span, width), BF16),
            pltpu.VMEM((span, width), BF16),
            pltpu.VMEM((span, width), BF16),
            pltpu.VMEM((2,) + layout.slots(width), BF16),
            pltpu.VMEM((2,) + layout.slots(width), BF16),
            pltpu.VMEM((2, share, layout.experts, 8, LANES), F32),
            pltpu.VMEM((3, cut, width), F32),
            pltpu.VMEM((share - 1, 2, width, cut), BF16),
            pltpu.VMEM((share - 1, 2, width, cut), BF16),
            pltpu.VMEM((share - 1, cut, width), BF16),
            pltpu.VMEM((share - 1, cut, width), BF16),
            pltpu.VMEM((levels, SMALL, width), F32),
            pltpu.VMEM((levels, SMALL, width), F32),
            dma((3,)),
            dma((2, 5)),
            dma((share - 1, 3)),
            dma((share - 1, 3)),
            dma((levels,)),
            dma((levels,)),
            *sums.scratch(),
            *more.scratch(),
        ],
        compiler_params=pltpu.CompilerParams(
            collective_id=3, has_side_effects=True, vmem_limit_bytes=60 * MIB
        ),
        cost_estimate=pl.CostEstimate(flops=1 << 30, bytes_accessed=1 << 20, transcendentals=0),
        name="weights",
    )(*own, *rows_far, cots_far, shares_far, *expert_weights, *held, *terms, small)


def local(
    tokens,
    gain_attn,
    w_qkv,
    w_out,
    gain_ffn,
    w_router,
    expert_gate,
    expert_up,
    expert_down,
    dense_gate,
    dense_up,
    dense_down,
    expert_ids,
    segments,
    cotangent,
):
    rows, width = tokens.shape
    layout = Layout(lax.axis_size("group"), lax.axis_size("expert"), rows)
    group, expert = lax.axis_index("group"), lax.axis_index("expert")
    share = layout.share
    relative = ((expert_ids % share) ^ (group % share)) * layout.experts
    relative = relative + ((expert_ids // share) ^ expert)
    fill = jnp.full((6, rows), -1, jnp.int32)
    relative_row = jnp.concatenate([jnp.transpose(relative), fill], axis=0)
    ids_row = jnp.concatenate([jnp.transpose(expert_ids), fill], axis=0)
    seg_row = jnp.broadcast_to(segments.astype(F32)[None], (8, rows))
    places = (expert * rows + jnp.arange(rows, dtype=jnp.int32)).astype(F32)
    lane = jnp.arange(LANES)
    power = (lane % (HEAD // 2)).astype(F32) / (HEAD // 2)
    angles = places[:, None] * (10000.0 ** (-power))[None]
    cosine = jnp.cos(angles)
    sine = jnp.sin(angles) * jnp.where(lane % HEAD < HEAD // 2, -1.0, 1.0)[None]
    gain_attn, gain_ffn = gain_attn[None], gain_ffn[None]

    (
        q,
        kv,
        att_t,
        lse,
        bias,
        target,
        hidden,
        low,
        mixed,
        grad_low,
        gate_terms,
        up_terms,
        down_terms,
        cots,
        quad_cots,
        rows_in,
        shares,
        far_cot,
        far_target,
    ) = first(
        layout,
        tokens,
        gain_attn,
        w_qkv,
        cosine,
        sine,
        relative_row,
        ids_row,
        seg_row,
        cotangent,
        w_out,
        gain_ffn,
        jnp.transpose(w_router),
        dense_gate,
        dense_up,
        dense_down,
    )
    came_back, grad_back, quad_rows, quad_shares, rows_a, gate_terms = run_experts(
        layout,
        rows_in,
        cots,
        shares,
        expert_gate,
        expert_up,
        expert_down,
        (gate_terms, up_terms, down_terms),
    )
    mixed_out, grad_tokens, proj_terms, qkv_terms, small, gate_terms, up_terms, cots_far, rows_b, shares_far = late(
        layout,
        (
            came_back,
            grad_back,
            target,
            expert_ids,
            hidden,
            mixed,
            grad_low,
            low,
            cotangent,
            gain_ffn,
            w_router,
            w_out,
            att_t,
        ),
        (q, kv, bias, lse, tokens, gain_attn, w_qkv, cosine, sine),
        (gate_terms, up_terms, down_terms),
        far_cot,
        far_target,
        quad_rows,
        quad_shares,
    )
    gate_w, up_w, down_w, gate_sum, up_sum, down_sum, proj_sum, qkv_sum, small = weights(
        layout,
        (quad_rows, quad_cots, quad_shares),
        (rows_a, rows_b),
        cots_far,
        shares_far,
        (expert_gate, expert_up, expert_down),
        (gate_terms, up_terms, down_terms),
        (proj_terms, qkv_terms),
        small,
    )
    return (
        mixed_out,
        grad_tokens,
        small[EXPERTS + 1],
        qkv_sum,
        proj_sum,
        small[EXPERTS],
        jnp.transpose(small[:EXPERTS]),
        gate_w,
        up_w,
        down_w,
        gate_sum,
        up_sum,
        down_sum,
    )


def solution(mesh):
    in_specs = (
        P(("group", "expert"), None),
        P(),
        P(),
        P(),
        P(),
        P(),
        P("expert", None, None),
        P("expert", None, None),
        P("expert", None, None),
        P(),
        P(),
        P(),
        P(("group", "expert"), None),
        P(("group", "expert")),
        P(("group", "expert"), None),
    )
    out_specs = (
        P(("group", "expert"), None),
        P(("group", "expert"), None),
        P(),
        P("group", "expert"),
        P("group", "expert"),
        P(),
        P(),
        P("expert", None, "group"),
        P("expert", None, "group"),
        P("expert", "group", None),
        P("group", "expert"),
        P("group", "expert"),
        P("group", "expert"),
    )
    return jax.shard_map(local, mesh=mesh, in_specs=in_specs, out_specs=out_specs, check_vma=False)
```

```python
import functools

import jax
import jax.numpy as jnp
from jax import lax
from jax.experimental import pallas as pl
from jax.experimental.pallas import tpu as pltpu
from jax.sharding import PartitionSpec as P

HEADS = 12
HEAD = 64
EXPERTS = 16
WINDOW = 1024
CAP = 80
QUARTERS = 4
LANES = 128
TILE = 256
SMALL = EXPERTS + 8
NEG = -1e30

epsilon = 1e-06
F32 = jnp.float32
BF16 = jnp.bfloat16
MESH = pl.DeviceIdType.MESH
VMEM = pl.BlockSpec(memory_space=pltpu.VMEM)
ANY = pl.BlockSpec(memory_space=pl.ANY)
MIB = 1 << 20


def dims(spec):
    left, right = spec
    return (((left,), (right,)), ((), ()))


NN = dims((1, 0))
NT = dims((1, 1))
TN = dims((0, 0))


def mm(a, b, how=NN):
    return lax.dot_general(a, b, how, preferred_element_type=F32)


def flipped(x, mask):
    bit = 1
    while bit <= mask:
        if mask & bit:
            x = x + bit * (1 - 2 * ((x // bit) % 2))
        bit *= 2
    return x


class Layout:
    def __init__(self, groups, experts, rows):
        self.groups, self.experts, self.rows = groups, experts, rows
        self.share = EXPERTS // experts
        self.peers = self.share * experts
        self.outers = groups // self.share
        per_quarter = max(experts // QUARTERS, 1)
        self.reach = min((WINDOW - 1) // rows + 1, 2 * per_quarter - 1)

    def far(self, number):
        return {"group": flipped(lax.axis_index("group"), number * self.share)}

    def peer(self, number):
        group, expert = lax.axis_index("group"), lax.axis_index("expert")
        return {
            "group": flipped(group, number // self.experts),
            "expert": flipped(expert, number % self.experts),
        }

    def slots(self, width):
        return (self.share, self.experts, CAP, width)


def meet(layout):
    barrier = pltpu.get_barrier_semaphore()
    for number in range(1, layout.peers):
        pl.semaphore_signal(barrier, inc=1, device_id=layout.peer(number), device_id_type=MESH)
    for number in range(1, layout.outers):
        pl.semaphore_signal(barrier, inc=1, device_id=layout.far(number), device_id_type=MESH)
    pl.semaphore_wait(barrier, layout.peers + layout.outers - 2)


def remote(source, target, send_sem, recv_sem, device):
    return pltpu.make_async_remote_copy(
        src_ref=source,
        dst_ref=target,
        send_sem=send_sem,
        recv_sem=recv_sem,
        device_id=device,
        device_id_type=MESH,
    )


def to_peers(layout, source, target, send_sems, recv_sems):
    return [
        remote(
            source.at[divmod(number, layout.experts)],
            target.at[divmod(number, layout.experts)],
            send_sems.at[number],
            recv_sems.at[number],
            layout.peer(number),
        )
        for number in range(1, layout.peers)
    ]


def to_row(layout, source, target, send_sems, recv_sems):
    expert = lax.axis_index("expert")
    return [
        remote(
            source.at[:, bits],
            target.at[:, bits],
            send_sems.at[bits],
            recv_sems.at[bits],
            {"expert": flipped(expert, bits)},
        )
        for bits in range(1, layout.experts)
    ]


def to_quad(layout, source, target, send_sems, recv_sems):
    group = lax.axis_index("group")
    return [
        remote(
            source.at[bits],
            target.at[bits],
            send_sems.at[bits],
            recv_sems.at[bits],
            {"group": flipped(group, bits)},
        )
        for bits in range(1, layout.share)
    ]


def to_far(layout, source, target, low, high, send_sems, recv_sems):
    return [
        remote(
            source.at[low:high],
            target.at[number - 1],
            send_sems.at[number - 1],
            recv_sems.at[number - 1],
            layout.far(number),
        )
        for number in range(1, layout.outers)
    ]


def far_shape(layout, count, width):
    shape = (layout.outers - 1, count) + layout.slots(width)[1:]
    return jax.ShapeDtypeStruct(shape, BF16)


def bit_of(axis, bit):
    return (lax.axis_index(axis) // bit) % 2


def trade_sems(copies):
    return [pltpu.SemaphoreType.DMA((copies,)), pltpu.SemaphoreType.DMA((copies,))]


def packed_shape(rows, columns):
    if columns % LANES == LANES // 2 and rows % 32 == 0:
        return rows * columns // LANES, LANES
    return rows, columns


def pack(block):
    rows, columns = block.shape
    if packed_shape(rows, columns) == block.shape:
        return block
    whole = columns // LANES * LANES
    parts = [block[:, low : low + LANES] for low in range(0, whole, LANES)]
    parts.append(jnp.concatenate([block[: rows // 2, whole:], block[rows // 2 :, whole:]], axis=1))
    return jnp.concatenate(parts, axis=0)


def unpack(made, target, low, columns):
    rows = target.shape[0]
    if made.shape == (rows, columns):
        target[:, low : low + columns] = made
        return
    count = columns // LANES
    for part in range(count):
        target[:, low + part * LANES : low + (part + 1) * LANES] = made[
            part * rows : (part + 1) * rows
        ]
    at = slice(low + count * LANES, low + columns)
    target[: rows // 2, at] = made[count * rows :, : LANES // 2]
    target[rows // 2 :, at] = made[count * rows :, LANES // 2 :]


class Halving:
    def __init__(self, step, held, taken, send_sems, recv_sems):
        axis, bit, below = step
        odd = (lax.axis_index(axis) // bit) % 2
        self.held, self.taken = held, taken
        unit = 1 << below

        def place(number, value):
            return number // unit * (2 * unit) + value * unit + number % unit

        if axis == "expert":
            places = [
                ((place(n, 1 - odd),), (place(n, odd),), (n,)) for n in range(taken.shape[0])
            ]
        else:
            places = [
                ((m, place(n, 1 - odd)), (m, place(n, odd)), (m, n))
                for m in range(taken.shape[0])
                for n in range(taken.shape[1])
            ]
        self.places = [place[1:] for place in places]
        self.copies = [
            remote(
                held.at[theirs],
                taken.at[target],
                send_sems.at[number],
                recv_sems.at[number],
                {axis: flipped(lax.axis_index(axis), bit)},
            )
            for number, (theirs, _, target) in enumerate(places)
        ]

    def start(self):
        for copy in self.copies:
            copy.start()

    def add(self, last=None):
        for (mine, target), copy in zip(self.places, self.copies):
            copy.wait()
            if last is not None:
                mine, target = (*mine, 0)[:2], (*target, 0)[:2]
                unpack(self.taken[target].astype(F32) + self.held[mine].astype(F32), *last)
            elif len(target) == 2:
                self.taken[target] = (
                    self.taken[target].astype(F32) + self.held[mine].astype(F32)
                ).astype(BF16)
            else:

                def one(number, carry, mine=mine, target=target):
                    self.taken[target[0], number] = (
                        self.taken[target[0], number].astype(F32)
                        + self.held[mine[0], number].astype(F32)
                    ).astype(BF16)
                    return carry

                lax.fori_loop(0, self.taken.shape[1], one, 0)


def step_orders(layout):
    core, y, *experts = [("expert", 1 << n) for n in range(layout.experts.bit_length() - 1)]
    x, z, *groups = [("group", 1 << n) for n in range(layout.groups.bit_length() - 1)]
    rest = experts + groups
    return (
        [core, x, z, y] + rest,
        [core, x, y, z] + rest,
        [core, y, x, z] + rest,
        [core, y, x, z] + rest,
        [core, x, y, z] + rest,
        [core, y, z, x] + rest,
        [core, z, x, y] + rest,
    )


DONE_FIRST = (1, 1, 1)
DONE_EXPERTS = (2, 1, 1)
DONE_LATE = (3, 2, 1)
DONE_NONE = (0, 0, 0, 0)


def halving_plan(layout, orders, shapes, first, last):
    plan = []
    for steps, shape, low, high in zip(orders, shapes, first, last):
        mine, left = [], sorted(steps, key=lambda step: step[1])
        for number, step in enumerate(steps[:high]):
            axis, bit = step
            below = sum(1 for other in left if other[0] == axis and other[1] < bit)
            left.remove(step)
            if number < low:
                continue
            experts, groups = shape[:2]
            if axis == "expert":
                shape, copies = (experts // 2, groups) + shape[2:], experts // 2
            else:
                shape, copies = (experts, groups // 2) + shape[2:], experts * groups // 2
            mine.append(((axis, bit, below), shape, copies))
        plan.append(mine)
    return plan


def rope_turn(x, cosine, sine):
    parts = []
    for begin in range(0, x.shape[1], LANES):
        part = x[:, begin : begin + LANES]
        lane = lax.broadcasted_iota(jnp.int32, part.shape, 1)
        other = jnp.where(
            lane % HEAD < HEAD // 2,
            pltpu.roll(part, LANES - HEAD // 2, 1),
            pltpu.roll(part, HEAD // 2, 1),
        )
        parts.append(part * cosine + other * sine)
    return jnp.concatenate(parts, axis=1)


def normed(x, gain):
    return x * lax.rsqrt(jnp.mean(x * x, axis=-1, keepdims=True) + epsilon) * gain


def other_bits(x, mask, count):
    made, bit = 0, 1
    while bit < count:
        mine, theirs = (x // bit) % 2, (mask // bit) % 2
        made = made + bit * (mine + theirs - 2 * mine * theirs)
        bit *= 2
    return made


def slot_rows(ids_row, rows):
    labels = lax.broadcasted_iota(jnp.int32, (EXPERTS, rows), 0)
    first, second = labels == ids_row[0:1], labels == ids_row[1:2]
    both = jnp.where(first | second, 1.0, 0.0).astype(BF16)
    earlier_t = lax.broadcasted_iota(jnp.int32, (rows, rows), 0)
    later_t = lax.broadcasted_iota(jnp.int32, (rows, rows), 1)
    earlier = mm(both, jnp.where(earlier_t < later_t, 1.0, 0.0).astype(BF16))
    targets = []
    for mask, ids in ((first, ids_row[0:1]), (second, ids_row[1:2])):
        slot = jnp.sum(jnp.where(mask, earlier, 0.0), axis=0, keepdims=True)
        targets.append(jnp.where(slot < CAP, ids.astype(F32) * CAP + slot, -1.0))
    return targets


def slot_masks(number, target, rows):
    slots = (number * CAP + lax.broadcasted_iota(jnp.int32, (CAP, rows), 0)).astype(F32)
    return slots == target[0:1], slots == target[1:2]


def gather_slots(layout, target, source, made):
    rows = source.shape[0]
    for number in range(layout.peers):
        first, second = slot_masks(number, target, rows)
        chosen = jnp.where(first | second, 1.0, 0.0).astype(BF16)
        made[divmod(number, layout.experts)] = mm(chosen, source[...]).astype(BF16)


def first_kernel(
    layout,
    tokens,
    gain_attn,
    w_qkv,
    cosine,
    sine,
    ids_row,
    seg_row,
    cot,
    w_out,
    gain_ffn,
    w_router_t,
    dense_gate_any,
    dense_up_any,
    dense_down_any,
    q_out,
    kv_out,
    att_t_out,
    lse_out,
    bias_out,
    target_out,
    hidden_out,
    low_out,
    mixed_out,
    grad_out,
    gate_out,
    up_out,
    down_out,
    cots_out,
    quad_out,
    rows_out,
    shares_out,
    far_cot_out,
    far_target_out,
    normed_low,
    send_cot,
    seg_all,
    acc,
    top,
    total,
    att,
    send_rows,
    send_shares,
    dense_gate,
    dense_up,
    dense_down,
    gate_held,
    up_held,
    down_held,
    load_sems,
    kv_send,
    kv_recv,
    seg_send,
    seg_recv,
    cot_send,
    cot_recv,
    quad_send,
    quad_recv,
    row_send,
    row_recv,
    share_send,
    share_recv,
    own_sems,
    far_send,
    far_recv,
    half_send,
    half_recv,
):
    rows, width = tokens.shape
    reach, experts = layout.reach, layout.experts
    ff = dense_gate.shape[1]
    e = lax.axis_index("expert")
    loads = [
        pltpu.make_async_copy(source, target, load_sems.at[number])
        for number, (source, target) in enumerate(
            ((dense_gate_any, dense_gate), (dense_up_any, dense_up), (dense_down_any, dense_down))
        )
    ]
    for copy in loads:
        copy.start()
    meet(layout)

    share = layout.share
    ids = ids_row[...]
    relative = other_bits(ids % share, own_share(layout), share) * experts
    targets = slot_rows(relative + other_bits(ids // share, e, experts), rows)
    target_out[0:1] = targets[0]
    target_out[1:2] = targets[1]
    target_out[2:8] = jnp.full((6, rows), -1.0, F32)
    far = [
        remote(
            source,
            target.at[number - 1],
            far_send.at[place, number - 1],
            far_recv.at[place, number - 1],
            layout.far(number),
        )
        for number in range(1, layout.outers)
        for place, (source, target) in enumerate(((cot, far_cot_out), (target_out, far_target_out)))
    ]
    for copy in far:
        copy.start()
    gather_slots(layout, target_out[...], cot, send_cot)
    cot_sends = to_row(layout, send_cot, cots_out, cot_send, cot_recv)
    own_cot = pltpu.make_async_copy(send_cot.at[:, 0], cots_out.at[:, 0], own_sems.at[0])
    own_cot.start()
    early = experts // 2
    for copy in cot_sends[:early]:
        copy.start()

    x = tokens[...].astype(F32)
    normed_low[...] = normed(x, gain_attn[...].reshape(1, width)).astype(BF16)
    seg_all[0] = jnp.broadcast_to(seg_row[...].astype(F32).reshape(1, rows), (8, rows))

    def project(step, carry):
        for part in range(3):
            columns = pl.ds(pl.multiple_of(part * width + step * TILE, TILE), TILE)
            made = mm(normed_low[...], w_qkv[:, columns])
            columns = pl.ds(pl.multiple_of(step * TILE, TILE), TILE)
            if part == 0:
                made = rope_turn(made, cosine[...], sine[...]) * HEAD ** (-0.5)
                q_out[:, columns] = made.astype(BF16)
            elif part == 1:
                made = rope_turn(made, cosine[...], sine[...])
                kv_out[0, :, columns] = made.astype(BF16)
            else:
                columns = pl.ds(pl.multiple_of(width + step * TILE, TILE), TILE)
                kv_out[0, :, columns] = made.astype(BF16)
        return carry

    lax.fori_loop(0, width // TILE, project, 0)

    halos = []
    for distance in range(1, reach + 1):
        to = {"expert": lax.rem(e + distance, experts)}
        halos.append(
            [
                pltpu.make_async_remote_copy(
                    src_ref=source.at[0],
                    dst_ref=source.at[distance],
                    send_sem=sems[0].at[distance],
                    recv_sem=sems[1].at[distance],
                    device_id=to,
                    device_id_type=MESH,
                )
                for source, sems in (
                    (kv_out, (kv_send, kv_recv)),
                    (seg_all, (seg_send, seg_recv)),
                )
            ]
        )
        for copy in halos[-1]:
            copy.start()

    lane = lax.broadcasted_iota(jnp.int32, (rows, LANES), 1)
    for distance in range(reach + 1):
        if distance:
            for copy in halos[distance - 1]:
                copy.wait()
        if distance == reach:
            for copy in cot_sends[early:]:
                copy.start()
        seg_col = jnp.transpose(jnp.broadcast_to(seg_all[distance, 0:1], (LANES, rows)))[:, 0:1]
        key_no = lax.broadcasted_iota(jnp.int32, (rows, rows), 0) - distance * rows
        offset = lax.broadcasted_iota(jnp.int32, (rows, rows), 1) - key_no
        allowed = (
            (offset >= 0)
            & (offset < WINDOW)
            & (key_no + e * rows >= 0)
            & (seg_col == seg_all[0, 0:1])
        )
        bias_out[distance] = jnp.where(allowed, 0.0, NEG).astype(BF16)

        def attend(pair, carry, distance=distance):
            columns = pl.ds(pl.multiple_of(pair * LANES, LANES), LANES)
            value_columns = pl.ds(pl.multiple_of(width + pair * LANES, LANES), LANES)
            queries = q_out[:, columns]
            keys = kv_out[distance, :, columns]
            values_t = jnp.transpose(kv_out[distance, :, value_columns])
            for inner in range(2):
                head = pair * 2 + inner
                mine = jnp.where((lane // HEAD) == inner, queries, jnp.zeros_like(queries))
                value_t = values_t[inner * HEAD : (inner + 1) * HEAD]
                out_rows = pl.ds(pl.multiple_of(head * HEAD, HEAD), HEAD)
                blocks = (
                    [(slice(0, rows // 2), rows // 2), (slice(rows // 2, rows), rows)]
                    if distance == 0
                    else [(slice(0, rows), rows)]
                )
                for q_cut, key_count in blocks:
                    scores = mm(keys[:key_count], mine[q_cut], NT)
                    scores = scores + bias_out[distance, :key_count, q_cut].astype(F32)
                    peak = jnp.max(scores, axis=0, keepdims=True)
                    if distance:
                        before = top[pl.ds(head, 1), q_cut]
                        peak = jnp.maximum(before, peak)
                    weights = jnp.exp(scores - peak)
                    amount = jnp.sum(weights, axis=0, keepdims=True)
                    part = mm(value_t[:, :key_count], weights.astype(BF16))
                    if distance:
                        shrink = jnp.exp(before - peak)
                        amount = amount + total[pl.ds(head, 1), q_cut] * shrink
                        part = part + acc[out_rows, q_cut] * shrink
                    top[pl.ds(head, 1), q_cut] = peak
                    total[pl.ds(head, 1), q_cut] = amount
                    acc[out_rows, q_cut] = part
            return carry

        lax.fori_loop(0, HEADS // 2, attend, 0)

    lse_out[...] = top[...] + jnp.log(total[...])

    def finish(pair, carry):
        out_rows = pl.ds(pl.multiple_of(pair * LANES, LANES), LANES)
        scale = jnp.concatenate(
            [
                jnp.broadcast_to(1.0 / total[pl.ds(pair * 2 + inner, 1), :], (HEAD, rows))
                for inner in range(2)
            ],
            axis=0,
        )
        made = acc[out_rows, :] * scale
        att_t_out[out_rows, :] = made.astype(BF16)
        att[:, out_rows] = jnp.transpose(made).astype(BF16)
        return carry

    lax.fori_loop(0, HEADS // 2, finish, 0)

    hidden_out[...] = tokens[...].astype(F32) + mm(att[...], w_out[...])
    low = normed(hidden_out[...], gain_ffn[...].reshape(1, width)).astype(BF16)
    low_out[...] = low
    logits = mm(w_router_t[...], low, NT)
    route = jnp.exp(logits - jnp.max(logits, axis=0, keepdims=True))
    route = route / jnp.sum(route, axis=0, keepdims=True)
    labels = lax.broadcasted_iota(jnp.int32, (EXPERTS, rows), 0)
    picked = [
        jnp.sum(jnp.where(labels == ids_row[k : k + 1], route, 0.0), axis=0, keepdims=True)
        for k in range(2)
    ]
    both = picked[0] + picked[1]
    shares = []
    for k in range(2):
        parts = split3(picked[k] / both)
        shares.append(
            jnp.concatenate(
                [part.astype(F32) for part in parts] + [jnp.zeros((5, rows), F32)], axis=0
            ).astype(BF16)
        )
    send_shares[...] = jnp.zeros_like(send_shares)
    for number in range(layout.peers):
        first, second = slot_masks(number, target_out[...], rows)
        first = jnp.where(first, 1.0, 0.0).astype(BF16)
        second = jnp.where(second, 1.0, 0.0).astype(BF16)
        place = divmod(number, experts)
        send_rows[place] = mm(first + second, low).astype(BF16)
        share = mm(shares[0], first, NT) + mm(shares[1], second, NT)
        share = jnp.sum(share, axis=0, keepdims=True)
        send_shares[place + (slice(None), slice(0, CAP))] = jnp.broadcast_to(share, (8, CAP))
    sends = to_row(layout, send_rows, rows_out, row_send, row_recv)
    sends += to_row(layout, send_shares, shares_out, share_send, share_recv)
    for source, target, sem in (
        (send_rows, rows_out, own_sems.at[1]),
        (send_shares, shares_out, own_sems.at[2]),
    ):
        sends.append(pltpu.make_async_copy(source.at[:, 0], target.at[:, 0], sem))
    for copy in reversed(sends):
        copy.start()
    own_cot.wait()
    for copy in cot_sends:
        copy.wait()
    sends += to_quad(layout, cots_out, quad_out, quad_send, quad_recv)
    sends.append(pltpu.make_async_copy(cots_out.at[0], quad_out.at[0], own_sems.at[3]))
    for copy in sends[-layout.share :]:
        copy.start()

    for copy in loads:
        copy.wait()
    mixed_out[...] = hidden_out[...]
    grad_out[...] = jnp.zeros_like(grad_out)
    part_width = ff // experts
    per_part = part_width // TILE
    half = experts // 2
    odd = bit_of("expert", 1)
    halvings = [
        Halving(("expert", 1, 0), held, taken, half_send.at[number], half_recv.at[number])
        for number, (held, taken) in enumerate(
            ((gate_held, gate_out), (up_held, up_out), (down_held, down_out))
        )
    ]

    def branch(step, carry):
        place = step // per_part
        part = 2 * (place % half) + (odd + 1 + place // half) % 2
        columns = pl.ds(pl.multiple_of(part * part_width + (step % per_part) * TILE, TILE), TILE)
        gate_w, up_w, down_w = dense_gate[:, columns], dense_up[:, columns], dense_down[columns, :]
        gate_pre = mm(low_out[...], gate_w)
        up_pre = mm(low_out[...], up_w)
        grad_act = mm(cot[...], down_w, NT)
        silu, slope = silu_parts(gate_pre)
        act = (silu * up_pre).astype(BF16)
        grad_gate = (grad_act * up_pre * slope).astype(BF16)
        grad_up = (grad_act * silu).astype(BF16)
        mixed_out[...] += mm(act, down_w)
        grad_out[...] += mm(grad_gate, gate_w, NT) + mm(grad_up, up_w, NT)
        inside = pl.ds(pl.multiple_of((step % per_part) * TILE, TILE), TILE)
        for made, held in (
            (mm(low_out[...], grad_gate, TN), gate_held),
            (mm(low_out[...], grad_up, TN), up_held),
        ):
            made = made.astype(BF16)
            block = held.shape[2]
            for place in range(held.shape[1]):
                held[part, place, :, inside] = made[place * block : (place + 1) * block]
        made = mm(act, cot[...], TN).astype(BF16)
        block = ff // layout.groups
        cut = width // experts
        low_row = part * part_width + (step % per_part) * TILE
        for inner in range(0, TILE, block):
            for other in range(experts):
                down_held[other, (low_row + inner) // block] = pack(
                    made[inner : inner + block, other * cut : (other + 1) * cut]
                )
        return carry

    lax.fori_loop(0, ff // (2 * TILE), branch, 0)
    for halving in halvings[:2]:
        halving.start()
    lax.fori_loop(ff // (2 * TILE), ff // TILE, branch, 0)
    halvings[2].start()
    for halving in halvings:
        halving.add()
    for copy in far + sends:
        copy.wait()


def first(layout, tokens, gain_attn, w_qkv, cosine, sine, ids_row, seg_row, cot, w_out, gain_ffn, w_router_t, dense_gate, dense_up, dense_down):
    rows, width = tokens.shape
    ff = dense_gate.shape[1]
    reach, experts, groups = layout.reach, layout.experts, layout.groups
    half = experts // 2
    others = layout.outers - 1
    dma = pltpu.SemaphoreType.DMA
    wide = (groups, width // groups, ff // experts)
    tall = (groups,) + packed_shape(ff // groups, width // experts)
    return pl.pallas_call(
        functools.partial(first_kernel, layout),
        out_shape=[
            jax.ShapeDtypeStruct((rows, width), BF16),
            jax.ShapeDtypeStruct((reach + 1, rows, 2 * width), BF16),
            jax.ShapeDtypeStruct((width, rows), BF16),
            jax.ShapeDtypeStruct((EXPERTS, rows), F32),
            jax.ShapeDtypeStruct((reach + 1, rows, rows), BF16),
            jax.ShapeDtypeStruct((8, rows), F32),
            jax.ShapeDtypeStruct((rows, width), F32),
            jax.ShapeDtypeStruct((rows, width), BF16),
            jax.ShapeDtypeStruct((rows, width), F32),
            jax.ShapeDtypeStruct((rows, width), F32),
            jax.ShapeDtypeStruct((half,) + wide, BF16),
            jax.ShapeDtypeStruct((half,) + wide, BF16),
            jax.ShapeDtypeStruct((half,) + tall, BF16),
            jax.ShapeDtypeStruct(layout.slots(width), BF16),
            jax.ShapeDtypeStruct(layout.slots(width), BF16),
            jax.ShapeDtypeStruct(layout.slots(width), BF16),
            jax.ShapeDtypeStruct((layout.share, experts, 8, LANES), F32),
            jax.ShapeDtypeStruct((others, rows, width), BF16),
            jax.ShapeDtypeStruct((others, 8, rows), F32),
        ],
        in_specs=[VMEM] * 11 + [ANY] * 3,
        out_specs=[VMEM] * 13 + [ANY] * 6,
        scratch_shapes=[
            pltpu.VMEM((rows, width), BF16),
            pltpu.VMEM(layout.slots(width), BF16),
            pltpu.VMEM((reach + 1, 8, rows), F32),
            pltpu.VMEM((width, rows), F32),
            pltpu.VMEM((EXPERTS, rows), F32),
            pltpu.VMEM((EXPERTS, rows), F32),
            pltpu.VMEM((rows, width), BF16),
            pltpu.VMEM(layout.slots(width), BF16),
            pltpu.VMEM((layout.share, experts, 8, LANES), F32),
            pltpu.VMEM((width, ff), BF16),
            pltpu.VMEM((width, ff), BF16),
            pltpu.VMEM((ff, width), BF16),
            pltpu.VMEM((experts,) + wide, BF16),
            pltpu.VMEM((experts,) + wide, BF16),
            pltpu.VMEM((experts,) + tall, BF16),
            dma((3,)),
            dma((reach + 1,)),
            dma((reach + 1,)),
            dma((reach + 1,)),
            dma((reach + 1,)),
            dma((experts,)),
            dma((experts,)),
            dma((layout.share,)),
            dma((layout.share,)),
            dma((experts,)),
            dma((experts,)),
            dma((experts,)),
            dma((experts,)),
            dma((4,)),
            dma((2, others)),
            dma((2, others)),
            dma((3, half)),
            dma((3, half)),
        ],
        compiler_params=pltpu.CompilerParams(
            collective_id=0, has_side_effects=True, vmem_limit_bytes=62 * MIB
        ),
        cost_estimate=pl.CostEstimate(flops=1 << 30, bytes_accessed=1 << 20, transcendentals=0),
        name="first",
    )(tokens, gain_attn, w_qkv, cosine, sine, ids_row, seg_row, cot, w_out, gain_ffn, w_router_t, dense_gate, dense_up, dense_down)


def split3(x):
    high = x.astype(BF16)
    rest = x - high.astype(F32)
    middle = rest.astype(BF16)
    return high, middle, (rest - middle.astype(F32)).astype(BF16)


def silu_parts(gate_pre):
    gate = 1.0 / (1.0 + jnp.exp(-gate_pre))
    return gate_pre * gate, gate * (1.0 + gate_pre * (1.0 - gate))


def share_column(share_row):
    across = lax.broadcasted_iota(jnp.int32, (CAP, CAP), 1)
    down = lax.broadcasted_iota(jnp.int32, (CAP, CAP), 0)
    return jnp.sum(jnp.where(across == down, share_row, 0.0), axis=1, keepdims=True)


def own_share(layout):
    return lax.rem(lax.axis_index("group"), layout.share)


class Sums:
    def __init__(self, layout, orders, arrays, first, last, keep):
        self.plan = halving_plan(layout, orders, [one.shape for one in arrays], first, last)
        self.keep = keep

    def scratch(self):
        made = []
        for mine in self.plan:
            for number, (_, shape, copies) in enumerate(mine):
                made += trade_sems(copies)
                if not self.keep or number + 1 < len(mine):
                    made.append(pltpu.VMEM(shape, BF16))
        return made

    def outputs(self):
        return [jax.ShapeDtypeStruct(mine[-1][1], BF16) for mine in self.plan if mine]

    def chains(self, held_refs, outputs, scratch):
        outputs, scratch = list(outputs), list(scratch)
        chains = []
        for held, mine in zip(held_refs, self.plan):
            chain = []
            for number, (step, _, _) in enumerate(mine):
                sems = scratch.pop(0), scratch.pop(0)
                if not self.keep or number + 1 < len(mine):
                    taken = scratch.pop(0)
                else:
                    taken = outputs.pop(0)
                chain.append(Halving(step, held, taken, *sems))
                held = taken
            chains.append(chain)
        return chains


def experts_kernel(layout, sums, *refs):
    (
        rows_in,
        cots,
        shares,
        gate_any,
        up_any,
        down_any,
        rows_any,
        shares_any,
        gate_held,
        up_held,
        down_held,
        back_out,
        grad_back,
        quad_rows,
        quad_shares,
        far_rows,
        gate_sum,
        gate_w,
        up_w,
        down_w,
        scaled,
        acc,
        grad_acc,
        send_out,
        send_grad,
        load_sems,
        back_send,
        back_recv,
        quad_send,
        quad_recv,
        own_sems,
        far_send,
        far_recv,
        *rest,
    ) = refs
    share, experts = layout.share, layout.experts
    width, ff = gate_w.shape[1:]
    mine = own_share(layout)

    def load(turn):
        return [
            pltpu.make_async_copy(
                source.at[flipped(mine, turn)], target.at[turn % 2], load_sems.at[turn % 2, number]
            )
            for number, (source, target) in enumerate(
                ((gate_any, gate_w), (up_any, up_w), (down_any, down_w))
            )
        ]

    for copy in load(0):
        copy.start()
    meet(layout)
    quads = to_quad(layout, rows_any, quad_rows, quad_send.at[0], quad_recv.at[0])
    quads += to_quad(layout, shares_any, quad_shares, quad_send.at[1], quad_recv.at[1])
    own = [
        pltpu.make_async_copy(rows_any.at[0], quad_rows.at[0], own_sems.at[2]),
        pltpu.make_async_copy(shares_any.at[0], quad_shares.at[0], own_sems.at[3]),
    ]
    far_low, far_high = far_parts(layout)[0]
    fars = [
        to_far(layout, rows_any, far_rows.at[:, 0:1], 0, 1, far_send.at[0], far_recv.at[0]),
        to_far(layout, quad_rows, far_rows.at[:, 1:], 1, far_high, far_send.at[1], far_recv.at[1])
        if far_high > 1
        else [],
    ]
    for copy in quads + own + fars[0]:
        copy.start()
    chains = sums.chains((gate_held, up_held, down_held), (gate_sum,), rest)
    for chain in chains:
        for halving in chain[:1]:
            halving.start()

    chunk = 2 * TILE
    copies = list(own)
    for turn in range(share):
        for copy in load(turn):
            copy.wait()
        if turn + 1 < share:
            for copy in load(turn + 1):
                copy.start()
        slot = turn % 2
        for number in range(experts):
            column = share_column(shares[turn, number, 0:1, :CAP])
            scaled[number] = (cots[turn, number].astype(F32) * column).astype(BF16)

        def step(number, carry, turn=turn, slot=slot):
            columns = pl.ds(pl.multiple_of(number * chunk, chunk), chunk)
            n = rows_in[turn].reshape(experts * CAP, width)
            grad = scaled[...].reshape(experts * CAP, width)
            gate_pre = mm(n, gate_w[slot, :, columns])
            up_pre = mm(n, up_w[slot, :, columns])
            grad_act = mm(grad, down_w[slot, columns, :], NT)
            silu, slope = silu_parts(gate_pre)
            act = (silu * up_pre).astype(BF16)
            grad_gate = (grad_act * up_pre * slope).astype(BF16)
            grad_up = (grad_act * silu).astype(BF16)
            acc[...] += mm(act, down_w[slot, columns, :])
            grad_acc[...] += mm(grad_gate, gate_w[slot, :, columns], NT) + mm(
                grad_up, up_w[slot, :, columns], NT
            )
            return carry

        acc[...] = jnp.zeros_like(acc)
        grad_acc[...] = jnp.zeros_like(grad_acc)
        lax.fori_loop(0, ff // chunk, step, 0)
        send_out[turn] = acc[...].astype(BF16).reshape(experts, CAP, width)
        send_grad[turn] = grad_acc[...].astype(BF16).reshape(experts, CAP, width)
        for bits in reversed(range(experts)):
            for which, (source, target) in enumerate(
                ((send_out, back_out), (send_grad, grad_back))
            ):
                ends = source.at[turn, bits], target.at[turn, bits]
                sem = which, turn, bits
                if bits:
                    device = {"expert": flipped(lax.axis_index("expert"), bits)}
                    copies.append(remote(*ends, back_send.at[sem], back_recv.at[sem], device))
                else:
                    copies.append(pltpu.make_async_copy(*ends, back_send.at[sem]))
                copies[-1].start()
        if turn == share // 2:
            for copy in quads:
                copy.wait()
            for copy in fars[1]:
                copy.start()
    for chain in chains:
        for halving in chain:
            halving.add()
    for copy in copies + fars[0] + fars[1]:
        copy.wait()


def far_parts(layout):
    middle = max(layout.share // 2, 1)
    return (0, middle), (middle, layout.share)


def run_experts(layout, rows_in, cots, shares, expert_gate, expert_up, expert_down, held):
    share, experts, others = layout.share, layout.experts, layout.outers - 1
    _, width, ff = expert_gate.shape
    dma = pltpu.SemaphoreType.DMA
    sums = Sums(layout, step_orders(layout)[:3], held, DONE_FIRST, DONE_EXPERTS, True)
    slots = jax.ShapeDtypeStruct(layout.slots(width), BF16)
    return pl.pallas_call(
        functools.partial(experts_kernel, layout, sums),
        out_shape=[
            slots,
            slots,
            slots,
            jax.ShapeDtypeStruct(shares.shape, F32),
            far_shape(layout, far_parts(layout)[0][1], width),
            *sums.outputs(),
        ],
        in_specs=[VMEM] * 3 + [ANY] * 5 + [VMEM] * 3,
        out_specs=[ANY] * 5 + [VMEM],
        scratch_shapes=[
            pltpu.VMEM((2, width, ff), BF16),
            pltpu.VMEM((2, width, ff), BF16),
            pltpu.VMEM((2, ff, width), BF16),
            pltpu.VMEM((experts, CAP, width), BF16),
            pltpu.VMEM((experts * CAP, width), F32),
            pltpu.VMEM((experts * CAP, width), F32),
            pltpu.VMEM(layout.slots(width), BF16),
            pltpu.VMEM(layout.slots(width), BF16),
            dma((2, 3)),
            dma((2, share, experts)),
            dma((2, share, experts)),
            dma((2, share)),
            dma((2, share)),
            dma((4,)),
            dma((2, others)),
            dma((2, others)),
            *sums.scratch(),
        ],
        compiler_params=pltpu.CompilerParams(
            collective_id=1, has_side_effects=True, vmem_limit_bytes=60 * MIB
        ),
        cost_estimate=pl.CostEstimate(flops=1 << 30, bytes_accessed=1 << 20, transcendentals=0),
        name="experts",
    )(
        rows_in,
        cots,
        shares,
        expert_gate,
        expert_up,
        expert_down,
        rows_in,
        shares,
        *held,
    )


def rope_back(grad, cosine, sine):
    lane = lax.broadcasted_iota(jnp.int32, grad.shape, 1)
    turned = grad * sine
    other = jnp.where(
        lane % HEAD < HEAD // 2,
        pltpu.roll(turned, LANES - HEAD // 2, 1),
        pltpu.roll(turned, HEAD // 2, 1),
    )
    return grad * cosine + other


def by_blocks(target, made):
    parts, places = target.shape[:2]
    block, cut = made.shape[0] // places, made.shape[1] // parts
    for part in range(parts):
        for place in range(places):
            target[part, place] = pack(
                made[place * block : (place + 1) * block, part * cut : (part + 1) * cut]
            )


def combine_part(
    back,
    grad_back,
    target,
    ids_row,
    hidden,
    mixed_in,
    grad_in,
    low,
    cot,
    gain,
    w_router_t,
    w_out,
    att_t,
    mixed_out,
    grad_hidden_out,
    grad_att_out,
    proj_out,
    router_out,
    gain_out,
):
    rows, width = hidden.shape
    slots = back.shape[0] * back.shape[1] * CAP
    columns = jnp.transpose(
        jnp.concatenate(
            [target[...], ids_row[...].astype(F32), jnp.zeros((LANES - 10, rows), F32)], axis=0
        )
    )
    slot_no = lax.broadcasted_iota(jnp.int32, (rows, slots), 1).astype(F32)
    cot_float = cot[...].astype(F32)
    logits = mm(low[...], w_router_t[...], NT)
    route = jnp.exp(logits - jnp.max(logits, axis=1, keepdims=True))
    route = route / jnp.sum(route, axis=1, keepdims=True)
    labels = lax.broadcasted_iota(jnp.int32, (rows, EXPERTS), 1).astype(F32)
    masks = [labels == columns[:, 8 + k : 9 + k] for k in range(2)]
    picked = [jnp.sum(jnp.where(mask, route, 0.0), axis=1, keepdims=True) for mask in masks]
    both = picked[0] + picked[1]
    chosen, shares, grads = [], [], []
    mixed = mixed_in[...]
    for k in range(2):
        chosen.append(jnp.where(slot_no == columns[:, k : k + 1], 1.0, 0.0).astype(BF16))
        fetched = mm(chosen[k], back[...].reshape(slots, width))
        shares.append(picked[k] / both)
        mixed = mixed + shares[k] * fetched
        grads.append(jnp.sum(cot_float * fetched, axis=1, keepdims=True))
    mixed_out[...] = mixed.astype(BF16)
    mean = grads[0] * shares[0] + grads[1] * shares[1]
    grad_route = jnp.zeros_like(route)
    for k in range(2):
        grad_route = grad_route + jnp.where(masks[k], (grads[k] - mean) / both, 0.0)
    grad_logits = route * (grad_route - jnp.sum(route * grad_route, axis=1, keepdims=True))
    grad_logits = grad_logits.astype(BF16)
    router_out[...] = mm(grad_logits, low[...], TN)
    grad = grad_in[...] + mm(chosen[0] + chosen[1], grad_back[...].reshape(slots, width))
    grad = grad + mm(grad_logits, w_router_t[...])
    h = hidden[...]
    scale = lax.rsqrt(jnp.mean(h * h, axis=-1, keepdims=True) + epsilon)
    gain_out[...] = jnp.sum(grad * h * scale, axis=0, keepdims=True)
    grad = grad * gain[...].reshape(1, width)
    grad = scale * grad - h * (scale * scale * scale) * jnp.mean(grad * h, axis=-1, keepdims=True)
    grad = cot_float + grad
    grad_hidden_out[...] = grad
    grad_low = grad.astype(BF16)
    grad_att_out[...] = mm(grad_low, w_out[...], NT).astype(BF16)
    by_blocks(proj_out, mm(att_t[...], grad_low).astype(BF16))


def late_kernel(layout, sums, *refs):
    (
        back,
        grad_back,
        target,
        ids_row,
        hidden,
        mixed_in,
        grad_in,
        low,
        cot,
        gain_ffn,
        w_router_t,
        w_out,
        att_t,
        q_in,
        kv_in,
        bias,
        lse,
        tokens,
        gain,
        w_qkv,
        cosine,
        sine,
        gate_held,
        up_held,
        down_held,
        far_cot,
        far_target,
        rows_any,
        shares_any,
        mixed_out,
        tokens_out,
        proj_out,
        qkv_out,
        small_out,
        gate_sum,
        up_sum,
        far_cots_out,
        far_out,
        far_shares_out,
        grad_att,
        router_term,
        gain_term,
        send_cot,
        halo_send,
        halo_recv,
        own_kv,
        packed,
        send_sems,
        recv_sems,
        cot_send,
        cot_recv,
        own_sem,
        mixed_sem,
        far_send,
        far_recv,
        *rest,
    ) = refs
    rows, width = tokens.shape
    reach, experts = layout.reach, layout.experts
    e = lax.axis_index("expert")
    pairs = HEADS // 2
    lane = lax.broadcasted_iota(jnp.int32, (rows, LANES), 1)
    load = pltpu.make_async_copy(grad_in, tokens_out, mixed_sem)
    load.start()
    meet(layout)
    far_low, far_high = far_parts(layout)[1]
    far = to_far(layout, rows_any, far_out, far_low, far_high, far_send.at[0], far_recv.at[0])
    far += to_far(
        layout, shares_any, far_shares_out, 0, layout.share, far_send.at[1], far_recv.at[1]
    )
    for copy in far:
        copy.start()
    chains = sums.chains((gate_held, up_held, down_held), (gate_sum, up_sum), rest)
    for chain in chains:
        for halving in chain[:1]:
            halving.start()
    cot_sends = []
    for number in range(layout.outers - 1):
        for copy in cot_sends:
            copy.wait()
        fetch = pltpu.make_async_copy(far_cot.at[number], grad_att, own_sem.at[number])
        fetch.start()
        fetch.wait()
        gather_slots(layout, far_target[number], grad_att, send_cot)
        cot_sends = to_peers(
            layout, send_cot, far_cots_out.at[number], cot_send.at[number], cot_recv.at[number]
        )
        cot_sends.append(
            pltpu.make_async_copy(
                send_cot.at[0, 0], far_cots_out.at[number, 0, 0], own_sem.at[number]
            )
        )
        for copy in cot_sends:
            copy.start()

    load.wait()
    combine_part(
        back,
        grad_back,
        target,
        ids_row,
        hidden,
        mixed_in,
        tokens_out,
        low,
        cot,
        gain_ffn,
        w_router_t,
        w_out,
        att_t,
        packed.at[:, :width],
        tokens_out,
        grad_att,
        proj_out,
        router_term,
        gain_term,
    )
    mixed = pltpu.make_async_copy(packed.at[:, :width], mixed_out, mixed_sem)
    mixed.start()
    mixed.wait()

    def halo(distance, pair):
        return pltpu.make_async_remote_copy(
            src_ref=halo_send.at[distance - 1, pair],
            dst_ref=halo_recv.at[distance - 1, pair],
            send_sem=send_sems.at[distance - 1, pair],
            recv_sem=recv_sems.at[distance - 1, pair],
            device_id={"expert": lax.rem(e + experts - distance, experts)},
            device_id_type=MESH,
        )

    def heads(pair, carry):
        columns = pl.ds(pl.multiple_of(pair * LANES, LANES), LANES)
        value_columns = pl.ds(pl.multiple_of(width + pair * LANES, LANES), LANES)
        queries, grads = q_in[:, columns], grad_att[:, columns]
        grads_t = jnp.transpose(grads.astype(F32))
        shrunk = grads_t * att_t[columns, :].astype(F32)
        grad_q = [None, None]
        for distance in range(reach, -1, -1):
            keys = kv_in[distance, :, columns]
            values = kv_in[distance, :, value_columns]
            keys_t = jnp.transpose(keys)
            grad_k = grad_v = None
            for inner in range(2):
                head = pair * 2 + inner
                cut = slice(inner * HEAD, (inner + 1) * HEAD)
                mine = (lane // HEAD) == inner
                query = jnp.where(mine, queries, jnp.zeros_like(queries))
                grad = jnp.where(mine, grads, jnp.zeros_like(grads))
                total = jnp.sum(shrunk[cut], axis=0, keepdims=True)
                scores = mm(keys, query, NT) + bias[distance].astype(F32)
                probs = jnp.exp(scores - lse[pl.ds(head, 1), :])
                grad_probs = mm(values, grad, NT)
                grad_scores = (probs * (grad_probs - total)).astype(BF16)
                part_v = mm(probs.astype(BF16), grad)
                part_k = mm(grad_scores, query)
                part_q = mm(keys_t[cut], grad_scores)
                grad_v = part_v if grad_v is None else grad_v + part_v
                grad_k = part_k if grad_k is None else grad_k + part_k
                grad_q[inner] = part_q if grad_q[inner] is None else grad_q[inner] + part_q
            if distance:
                halo_send[distance - 1, pair, 0] = grad_k.astype(BF16)
                halo_send[distance - 1, pair, 1] = grad_v.astype(BF16)
                halo(distance, pair).start()
            else:
                own_kv[pair, 0] = grad_k.astype(BF16)
                own_kv[pair, 1] = grad_v.astype(BF16)
        grad = jnp.transpose(jnp.concatenate(grad_q, axis=0)) * HEAD ** (-0.5)
        packed[:, columns] = rope_back(grad, cosine[...], sine[...]).astype(BF16)
        return carry

    lax.fori_loop(0, pairs, heads, 0)
    x = tokens[...].astype(F32)
    grad_att[...] = normed(x, gain[...].reshape(1, width)).astype(BF16)
    normed_low = grad_att

    def merge(pair, carry):
        grad_k, grad_v = own_kv[pair, 0].astype(F32), own_kv[pair, 1].astype(F32)
        for distance in range(1, reach + 1):
            halo(distance, pair).wait()
            grad_k = grad_k + halo_recv[distance - 1, pair, 0].astype(F32)
            grad_v = grad_v + halo_recv[distance - 1, pair, 1].astype(F32)
        columns = pl.ds(pl.multiple_of(width + pair * LANES, LANES), LANES)
        packed[:, columns] = rope_back(grad_k, cosine[...], sine[...]).astype(BF16)
        columns = pl.ds(pl.multiple_of(2 * width + pair * LANES, LANES), LANES)
        packed[:, columns] = grad_v.astype(BF16)
        return carry

    lax.fori_loop(0, pairs, merge, 0)
    for chain in chains:
        for halving in chain:
            halving.add()
    thirds, parts, places = qkv_out.shape[:3]
    block, cut = width // places, width // parts
    for part in range(parts):
        columns = slice(part * thirds * cut, (part + 1) * thirds * cut)
        made = mm(normed_low[...], packed[:, columns], TN).astype(BF16)
        for third in range(thirds):
            for place in range(places):
                qkv_out[third, part, place] = pack(
                    made[place * block : (place + 1) * block, third * cut : (third + 1) * cut]
                )
    grad = mm(packed[...], w_qkv[...], NT)
    scale = lax.rsqrt(jnp.mean(x * x, axis=-1, keepdims=True) + epsilon)
    gain_back = jnp.sum(grad * x * scale, axis=0, keepdims=True)
    small_out[...] = jnp.concatenate(
        [router_term[...], gain_term[...], gain_back, jnp.zeros((6, width), F32)], axis=0
    )
    grad = grad * gain[...].reshape(1, width)
    grad = scale * grad - x * (scale * scale * scale) * jnp.mean(grad * x, axis=-1, keepdims=True)
    tokens_out[...] += grad
    for copy in far + cot_sends:
        copy.wait()


def late(layout, combine_ins, back_ins, held, far_cot, far_target, rows_in, shares):
    tokens = back_ins[4]
    rows, width = tokens.shape
    reach, peers, others = layout.reach, layout.peers, layout.outers - 1
    dma = pltpu.SemaphoreType.DMA
    pairs = HEADS // 2
    sums = Sums(layout, step_orders(layout)[:3], held, DONE_EXPERTS, DONE_LATE, True)
    blocks = (layout.experts, layout.groups)
    blocks += packed_shape(width // layout.groups, width // layout.experts)
    far_low, far_high = far_parts(layout)[1]
    return pl.pallas_call(
        functools.partial(late_kernel, layout, sums),
        out_shape=[
            jax.ShapeDtypeStruct((rows, width), BF16),
            jax.ShapeDtypeStruct((rows, width), F32),
            jax.ShapeDtypeStruct(blocks, BF16),
            jax.ShapeDtypeStruct((3,) + blocks, BF16),
            jax.ShapeDtypeStruct((SMALL, width), F32),
            *sums.outputs(),
            jax.ShapeDtypeStruct((others,) + layout.slots(width), BF16),
            far_shape(layout, far_high - far_low, width),
            jax.ShapeDtypeStruct((others,) + shares.shape, F32),
        ],
        in_specs=[VMEM] * 6 + [ANY] + [VMEM] * 18 + [ANY, VMEM, ANY, ANY],
        out_specs=[ANY] + [VMEM] * 6 + [ANY] * 3,
        scratch_shapes=[
            pltpu.VMEM((rows, width), BF16),
            pltpu.VMEM((EXPERTS, width), F32),
            pltpu.VMEM((1, width), F32),
            pltpu.VMEM(layout.slots(width), BF16),
            pltpu.VMEM((reach, pairs, 2, rows, LANES), BF16),
            pltpu.VMEM((reach, pairs, 2, rows, LANES), BF16),
            pltpu.VMEM((pairs, 2, rows, LANES), BF16),
            pltpu.VMEM((rows, 3 * width), BF16),
            dma((reach, pairs)),
            dma((reach, pairs)),
            dma((others, peers)),
            dma((others, peers)),
            dma((others,)),
            dma,
            dma((2, others)),
            dma((2, others)),
            *sums.scratch(),
        ],
        compiler_params=pltpu.CompilerParams(
            collective_id=2, has_side_effects=True, vmem_limit_bytes=63 * MIB
        ),
        cost_estimate=pl.CostEstimate(flops=1 << 30, bytes_accessed=1 << 20, transcendentals=0),
        name="late",
    )(*combine_ins, *back_ins, *held, far_cot, far_target, rows_in, shares)


def weights_kernel(layout, sums, *refs):
    share, outers, peers = layout.share, layout.outers, layout.peers
    (
        rows_own,
        cots_own,
        shares_own,
        rows_a,
        rows_b,
        cots_far,
        shares_far,
        gate_any,
        up_any,
        down_any,
        *terms,
        qkv_terms,
        small_in,
        gate_out,
        up_out,
        down_out,
        gate_sum,
        up_sum,
        down_sum,
        proj_sum,
        qkv_sum,
        router_out,
        gain_ffn_out,
        gain_attn_out,
    ) = refs[:27]
    (
        gate_w,
        up_w,
        gate_t,
        up_t,
        down_w,
        rows_buf,
        cots_buf,
        shares_buf,
        accs,
        sends,
        takes,
        down_sends,
        down_takes,
        small_sums,
        small_takes,
        load_sems,
        piece_sems,
        send_sems,
        recv_sems,
        small_send,
        small_recv,
    ) = refs[27:48]
    rest = refs[48:]
    width = gate_w.shape[0]
    ff = gate_any.shape[2]
    span = ff // outers
    cut = ff // layout.groups
    group = lax.axis_index("group")
    mine = own_share(layout)
    begin = pl.multiple_of((group // share) * span, span)
    loads = [
        pltpu.make_async_copy(gate_any.at[mine, :, pl.ds(begin, span)], gate_w, load_sems.at[0]),
        pltpu.make_async_copy(up_any.at[mine, :, pl.ds(begin, span)], up_w, load_sems.at[1]),
        pltpu.make_async_copy(down_any.at[mine, pl.ds(begin, span), :], down_w, load_sems.at[2]),
    ]

    def fetch(outer):
        slot = outer % 2
        if outer == 0:
            sources = [
                (rows_own, rows_buf.at[slot]),
                (cots_own, cots_buf.at[slot]),
                (shares_own, shares_buf.at[slot]),
            ]
        else:
            sources = [
                (one.at[outer - 1], rows_buf.at[slot, low:high])
                for one, (low, high) in zip((rows_a, rows_b), far_parts(layout))
            ]
            sources.append((cots_far.at[outer - 1], cots_buf.at[slot]))
            sources.append((shares_far.at[outer - 1], shares_buf.at[slot]))
        return [
            pltpu.make_async_copy(source, target, piece_sems.at[slot, number])
            for number, (source, target) in enumerate(sources)
        ]

    for copy in loads + fetch(0):
        copy.start()
    meet(layout)

    third = qkv_sum.shape[1] // 3
    chains = sums.chains([*terms, *[qkv_terms.at[n] for n in range(3)]], (), rest)
    results = [(one, 0, one.shape[1]) for one in (gate_sum, up_sum, down_sum, proj_sum)]
    results += [(qkv_sum, n * third, third) for n in range(3)]
    steps = [("expert", 1 << n) for n in range(layout.experts.bit_length() - 1)]
    steps += [("group", 1 << n) for n in range(layout.groups.bit_length() - 1)]
    levels = len(steps)
    small_sums[0] = small_in[...]

    def small_copy(level):
        axis, bit = steps[level]
        return pltpu.make_async_remote_copy(
            src_ref=small_sums.at[level],
            dst_ref=small_takes.at[level],
            send_sem=small_send.at[level],
            recv_sem=small_recv.at[level],
            device_id={axis: flipped(lax.axis_index(axis), bit)},
            device_id_type=MESH,
        )

    reached = [0] * len(chains)

    def advance(*numbers):
        for number in numbers:
            chain, level = chains[number], reached[number]
            if 0 < level <= len(chain):
                chain[level - 1].add(results[number] if level == len(chain) else None)
            if level < len(chain):
                chain[level].start()
            reached[number] += 1

    def advance_small(level):
        if level:
            small_copy(level - 1).wait()
            made = small_sums[level - 1] + small_takes[level - 1]
            if level < levels:
                small_sums[level] = made
            else:
                router_out[...] = made[:EXPERTS]
                gain_ffn_out[...] = made[EXPERTS : EXPERTS + 1]
                gain_attn_out[...] = made[EXPERTS + 1 : EXPERTS + 2]
        if level < levels:
            small_copy(level).start()

    attention, shared = (3, 4, 5, 6), (1, 2, 0)
    points = share * outers
    marks = {
        0: [attention],
        5 * points // 8: [shared, attention],
        points - 1: [shared, attention],
    }
    small_level = 1
    advance(*attention, *shared)
    advance_small(0)

    for copy in loads:
        copy.wait()
    gate_t[...] = jnp.transpose(gate_w[...])
    up_t[...] = jnp.transpose(up_w[...])
    experts = layout.experts
    count = max(8 // experts, 1)
    blocks = share // count

    def add(slot, chunk, block):
        parts = pl.ds(block * count, count)
        n = rows_buf[slot, parts].reshape(count * experts * CAP, width)
        grad = cots_buf[slot, parts].reshape(count * experts * CAP, width)
        base = pl.multiple_of(chunk * cut, cut)
        gate_pre = mm(gate_t[pl.ds(base, cut), :], n, NT)
        up_pre = mm(up_t[pl.ds(base, cut), :], n, NT)
        grad_act = mm(down_w[pl.ds(base, cut), :], grad, NT)
        silu, slope = silu_parts(gate_pre)
        act = (silu * up_pre).astype(BF16)
        grad_gate = (grad_act * up_pre * slope).astype(BF16)
        grad_up = (grad_act * silu).astype(BF16)
        accs[0] += mm(grad_gate, n)
        accs[1] += mm(grad_up, n)
        accs[2] += mm(act, grad)

    copies = []
    turns = [*range(share - 1, 0, -1), 0]
    resident = outers <= 2
    for place, turn in enumerate(turns):
        owner = flipped(mine, turn)
        accs[...] = jnp.zeros_like(accs)
        for outer in range(outers):
            slot = outer % 2
            if place == 0 or not resident:
                if place or outer:
                    for copy in fetch(outer):
                        copy.start()
                for copy in fetch(outer):
                    copy.wait()

                def scale(number, carry, slot=slot):
                    at = slot, number // experts, number % experts
                    column = share_column(shares_buf[at + (slice(0, 1), slice(0, CAP))])
                    cots_buf[at] = (cots_buf[at].astype(F32) * column).astype(BF16)
                    return carry

                lax.fori_loop(0, peers, scale, 0)

            def step(number, carry, slot=slot, owner=owner):
                add(slot, owner, number)
                return carry

            lax.fori_loop(0, blocks, step, 0)
            if place * outers + outer in marks:
                for numbers in marks[place * outers + outer]:
                    advance(*numbers)
                if small_level <= levels:
                    advance_small(small_level)
                    small_level += 1
        for which in range(3):
            made = accs[which]
            if which < 2:
                made = jnp.transpose(made)
            target = (gate_out, up_out, down_out)[which]
            if turn == 0:
                target[owner] = made
                continue
            if which < 2:
                ends = sends.at[turn - 1, which], takes.at[turn - 1, which]
            else:
                ends = down_sends.at[turn - 1], down_takes.at[turn - 1]
            ends[0][...] = made.astype(BF16)
            copy = pltpu.make_async_remote_copy(
                src_ref=ends[0],
                dst_ref=ends[1],
                send_sem=send_sems.at[turn - 1, which],
                recv_sem=recv_sems.at[turn - 1, which],
                device_id={"group": flipped(group, turn)},
                device_id_type=MESH,
            )
            copy.start()
            copies.append((turn, which, copy))
    while any(at <= len(chain) for at, chain in zip(reached, chains)) or small_level <= levels:
        advance(*attention)
        if small_level <= levels:
            advance_small(small_level)
            small_level += 1
        advance(*shared)
    for turn, which, copy in copies:
        copy.wait()
        target = (gate_out, up_out, down_out)[which]
        got = takes[turn - 1, which] if which < 2 else down_takes[turn - 1]
        target[flipped(mine, turn)] = got.astype(F32)


def weights(layout, own, rows_far, cots_far, shares_far, expert_weights, held, terms, small):
    share, outers = layout.share, layout.outers
    experts, width, ff = expert_weights[0].shape
    span = ff // outers
    cut = ff // layout.groups
    dma = pltpu.SemaphoreType.DMA
    levels = layout.experts.bit_length() + layout.groups.bit_length() - 2
    proj_terms, qkv_terms = terms
    thirds = [jax.ShapeDtypeStruct(qkv_terms.shape[1:], BF16)] * 3
    sums = Sums(
        layout,
        step_orders(layout),
        (*held, proj_terms, *thirds),
        DONE_LATE + DONE_NONE,
        (levels,) * 7,
        False,
    )
    wide = width // layout.groups, ff // layout.experts
    tall = cut, width // layout.experts
    narrow = width // layout.groups, width // layout.experts
    results = wide, wide, tall, narrow, (narrow[0], 3 * narrow[1])
    return pl.pallas_call(
        functools.partial(weights_kernel, layout, sums),
        out_shape=[
            jax.ShapeDtypeStruct((experts, width, cut), F32),
            jax.ShapeDtypeStruct((experts, width, cut), F32),
            jax.ShapeDtypeStruct((experts, cut, width), F32),
            *[jax.ShapeDtypeStruct(shape, F32) for shape in results],
            jax.ShapeDtypeStruct((EXPERTS, width), F32),
            jax.ShapeDtypeStruct((1, width), F32),
            jax.ShapeDtypeStruct((1, width), F32),
        ],
        in_specs=[ANY] * 10 + [VMEM] * 6,
        out_specs=[VMEM] * 11,
        scratch_shapes=[
            pltpu.VMEM((width, span), BF16),
            pltpu.VMEM((width, span), BF16),
            pltpu.VMEM((span, width), BF16),
            pltpu.VMEM((span, width), BF16),
            pltpu.VMEM((span, width), BF16),
            pltpu.VMEM((2,) + layout.slots(width), BF16),
            pltpu.VMEM((2,) + layout.slots(width), BF16),
            pltpu.VMEM((2, share, layout.experts, 8, LANES), F32),
            pltpu.VMEM((3, cut, width), F32),
            pltpu.VMEM((share - 1, 2, width, cut), BF16),
            pltpu.VMEM((share - 1, 2, width, cut), BF16),
            pltpu.VMEM((share - 1, cut, width), BF16),
            pltpu.VMEM((share - 1, cut, width), BF16),
            pltpu.VMEM((levels, SMALL, width), F32),
            pltpu.VMEM((levels, SMALL, width), F32),
            dma((3,)),
            dma((2, 5)),
            dma((share - 1, 3)),
            dma((share - 1, 3)),
            dma((levels,)),
            dma((levels,)),
            *sums.scratch(),
        ],
        compiler_params=pltpu.CompilerParams(
            collective_id=3, has_side_effects=True, vmem_limit_bytes=60 * MIB
        ),
        cost_estimate=pl.CostEstimate(flops=1 << 30, bytes_accessed=1 << 20, transcendentals=0),
        name="weights",
    )(*own, *rows_far, cots_far, shares_far, *expert_weights, *held, *terms, small)


def local(
    tokens,
    gain_attn,
    w_qkv,
    w_out,
    gain_ffn,
    w_router,
    expert_gate,
    expert_up,
    expert_down,
    dense_gate,
    dense_up,
    dense_down,
    expert_ids,
    segments,
    cotangent,
):
    rows, width = tokens.shape
    layout = Layout(lax.axis_size("group"), lax.axis_size("expert"), rows)
    expert = lax.axis_index("expert")
    ids_row, w_router_t = jnp.transpose(expert_ids), jnp.transpose(w_router)
    places = (expert * rows + jnp.arange(rows, dtype=jnp.int32)).astype(F32)
    lane = jnp.arange(LANES)
    power = (lane % (HEAD // 2)).astype(F32) / (HEAD // 2)
    angles = places[:, None] * (10000.0 ** (-power))[None]
    cosine = jnp.cos(angles)
    sine = jnp.sin(angles) * jnp.where(lane % HEAD < HEAD // 2, -1.0, 1.0)[None]

    (
        q,
        kv,
        att_t,
        lse,
        bias,
        target,
        hidden,
        low,
        mixed,
        grad_low,
        gate_terms,
        up_terms,
        down_terms,
        cots,
        quad_cots,
        rows_in,
        shares,
        far_cot,
        far_target,
    ) = first(
        layout,
        tokens,
        gain_attn,
        w_qkv,
        cosine,
        sine,
        ids_row,
        segments,
        cotangent,
        w_out,
        gain_ffn,
        w_router_t,
        dense_gate,
        dense_up,
        dense_down,
    )
    came_back, grad_back, quad_rows, quad_shares, rows_a, gate_terms = run_experts(
        layout,
        rows_in,
        cots,
        shares,
        expert_gate,
        expert_up,
        expert_down,
        (gate_terms, up_terms, down_terms),
    )
    mixed_out, grad_tokens, proj_terms, qkv_terms, small, gate_terms, up_terms, cots_far, rows_b, shares_far = late(
        layout,
        (
            came_back,
            grad_back,
            target,
            ids_row,
            hidden,
            mixed,
            grad_low,
            low,
            cotangent,
            gain_ffn,
            w_router_t,
            w_out,
            att_t,
        ),
        (q, kv, bias, lse, tokens, gain_attn, w_qkv, cosine, sine),
        (gate_terms, up_terms, down_terms),
        far_cot,
        far_target,
        quad_rows,
        quad_shares,
    )
    gate_w, up_w, down_w, gate_sum, up_sum, down_sum, proj_sum, qkv_sum, *small = weights(
        layout,
        (quad_rows, quad_cots, quad_shares),
        (rows_a, rows_b),
        cots_far,
        shares_far,
        (expert_gate, expert_up, expert_down),
        (gate_terms, up_terms, down_terms),
        (proj_terms, qkv_terms),
        small,
    )
    return (
        mixed_out,
        grad_tokens,
        small[2][0],
        qkv_sum,
        proj_sum,
        small[1][0],
        jnp.transpose(small[0]),
        gate_w,
        up_w,
        down_w,
        gate_sum,
        up_sum,
        down_sum,
    )


def solution(mesh):
    in_specs = (
        P(("group", "expert"), None),
        P(),
        P(),
        P(),
        P(),
        P(),
        P("expert", None, None),
        P("expert", None, None),
        P("expert", None, None),
        P(),
        P(),
        P(),
        P(("group", "expert"), None),
        P(("group", "expert")),
        P(("group", "expert"), None),
    )
    out_specs = (
        P(("group", "expert"), None),
        P(("group", "expert"), None),
        P(),
        P("group", "expert"),
        P("group", "expert"),
        P(),
        P(),
        P("expert", None, "group"),
        P("expert", None, "group"),
        P("expert", "group", None),
        P("group", "expert"),
        P("group", "expert"),
        P("group", "expert"),
    )
    return jax.shard_map(local, mesh=mesh, in_specs=in_specs, out_specs=out_specs, check_vma=False)
```

```python
import functools

import jax
import jax.numpy as jnp
from jax import lax
from jax.experimental import pallas as pl
from jax.experimental.pallas import tpu as pltpu
from jax.sharding import PartitionSpec as P

HEADS = 12
HEAD = 64
EXPERTS = 16
WINDOW = 1024
CAP = 80
QUARTERS = 4
LANES = 128
TILE = 256
SMALL = EXPERTS + 8
NEG = -1e30

epsilon = 1e-06
F32 = jnp.float32
BF16 = jnp.bfloat16
MESH = pl.DeviceIdType.MESH
VMEM = pl.BlockSpec(memory_space=pltpu.VMEM)
ANY = pl.BlockSpec(memory_space=pl.ANY)
MIB = 1 << 20


def dims(spec):
    left, right = spec
    return (((left,), (right,)), ((), ()))


NN = dims((1, 0))
NT = dims((1, 1))
TN = dims((0, 0))


def mm(a, b, how=NN):
    return lax.dot_general(a, b, how, preferred_element_type=F32)


def flipped(x, mask):
    bit = 1
    while bit <= mask:
        if mask & bit:
            x = x + bit * (1 - 2 * ((x // bit) % 2))
        bit *= 2
    return x


class Layout:
    def __init__(self, groups, experts, rows):
        self.groups, self.experts, self.rows = groups, experts, rows
        self.share = EXPERTS // experts
        self.peers = self.share * experts
        self.outers = groups // self.share
        per_quarter = max(experts // QUARTERS, 1)
        self.reach = min((WINDOW - 1) // rows + 1, 2 * per_quarter - 1)

    def far(self, number):
        return {"group": flipped(lax.axis_index("group"), number * self.share)}

    def peer(self, number):
        group, expert = lax.axis_index("group"), lax.axis_index("expert")
        return {
            "group": flipped(group, number // self.experts),
            "expert": flipped(expert, number % self.experts),
        }

    def slots(self, width):
        return (self.share, self.experts, CAP, width)


def meet(layout):
    barrier = pltpu.get_barrier_semaphore()
    for number in range(1, layout.peers):
        pl.semaphore_signal(barrier, inc=1, device_id=layout.peer(number), device_id_type=MESH)
    for number in range(1, layout.outers):
        pl.semaphore_signal(barrier, inc=1, device_id=layout.far(number), device_id_type=MESH)
    pl.semaphore_wait(barrier, layout.peers + layout.outers - 2)


def remote(source, target, send_sem, recv_sem, device):
    return pltpu.make_async_remote_copy(
        src_ref=source,
        dst_ref=target,
        send_sem=send_sem,
        recv_sem=recv_sem,
        device_id=device,
        device_id_type=MESH,
    )


def to_peers(layout, source, target, send_sems, recv_sems):
    return [
        remote(
            source.at[divmod(number, layout.experts)],
            target.at[divmod(number, layout.experts)],
            send_sems.at[number],
            recv_sems.at[number],
            layout.peer(number),
        )
        for number in range(1, layout.peers)
    ]


def to_row(layout, source, target, send_sems, recv_sems):
    expert = lax.axis_index("expert")
    return [
        remote(
            source.at[:, bits],
            target.at[:, bits],
            send_sems.at[bits],
            recv_sems.at[bits],
            {"expert": flipped(expert, bits)},
        )
        for bits in range(1, layout.experts)
    ]


def to_quad(layout, source, target, send_sems, recv_sems):
    group = lax.axis_index("group")
    return [
        remote(
            source.at[bits],
            target.at[bits],
            send_sems.at[bits],
            recv_sems.at[bits],
            {"group": flipped(group, bits)},
        )
        for bits in range(1, layout.share)
    ]


def to_far(layout, source, target, low, high, send_sems, recv_sems):
    return [
        remote(
            source.at[low:high],
            target.at[number - 1],
            send_sems.at[number - 1],
            recv_sems.at[number - 1],
            layout.far(number),
        )
        for number in range(1, layout.outers)
    ]


def far_shape(layout, count, width):
    shape = (layout.outers - 1, count) + layout.slots(width)[1:]
    return jax.ShapeDtypeStruct(shape, BF16)


def bit_of(axis, bit):
    return (lax.axis_index(axis) // bit) % 2


def trade_sems(copies):
    return [pltpu.SemaphoreType.DMA((copies,)), pltpu.SemaphoreType.DMA((copies,))]


def packed_shape(rows, columns):
    if columns % LANES == LANES // 2 and rows % 32 == 0:
        return rows * columns // LANES, LANES
    return rows, columns


def pack(block):
    rows, columns = block.shape
    if packed_shape(rows, columns) == block.shape:
        return block
    whole = columns // LANES * LANES
    parts = [block[:, low : low + LANES] for low in range(0, whole, LANES)]
    parts.append(jnp.concatenate([block[: rows // 2, whole:], block[rows // 2 :, whole:]], axis=1))
    return jnp.concatenate(parts, axis=0)


def unpack(made, target, low, columns):
    rows = target.shape[0]
    if made.shape == (rows, columns):
        target[:, low : low + columns] = made
        return
    count = columns // LANES
    for part in range(count):
        target[:, low + part * LANES : low + (part + 1) * LANES] = made[
            part * rows : (part + 1) * rows
        ]
    at = slice(low + count * LANES, low + columns)
    target[: rows // 2, at] = made[count * rows :, : LANES // 2]
    target[rows // 2 :, at] = made[count * rows :, LANES // 2 :]


class Halving:
    def __init__(self, step, held, taken, send_sems, recv_sems):
        axis, bit, below = step
        odd = (lax.axis_index(axis) // bit) % 2
        self.held, self.taken = held, taken
        unit = 1 << below

        def place(number, value):
            return number // unit * (2 * unit) + value * unit + number % unit

        if axis == "expert":
            places = [
                ((place(n, 1 - odd),), (place(n, odd),), (n,)) for n in range(taken.shape[0])
            ]
        else:
            places = [
                ((m, place(n, 1 - odd)), (m, place(n, odd)), (m, n))
                for m in range(taken.shape[0])
                for n in range(taken.shape[1])
            ]
        self.places = [place[1:] for place in places]
        self.copies = [
            remote(
                held.at[theirs],
                taken.at[target],
                send_sems.at[number],
                recv_sems.at[number],
                {axis: flipped(lax.axis_index(axis), bit)},
            )
            for number, (theirs, _, target) in enumerate(places)
        ]

    def start(self):
        for copy in self.copies:
            copy.start()

    def add(self, last=None):
        for (mine, target), copy in zip(self.places, self.copies):
            copy.wait()
            if last is not None:
                mine, target = (*mine, 0)[:2], (*target, 0)[:2]
                unpack(self.taken[target].astype(F32) + self.held[mine].astype(F32), *last)
            elif len(target) == 2:
                self.taken[target] = (
                    self.taken[target].astype(F32) + self.held[mine].astype(F32)
                ).astype(BF16)
            else:

                def one(number, carry, mine=mine, target=target):
                    self.taken[target[0], number] = (
                        self.taken[target[0], number].astype(F32)
                        + self.held[mine[0], number].astype(F32)
                    ).astype(BF16)
                    return carry

                lax.fori_loop(0, self.taken.shape[1], one, 0)


def step_orders(layout):
    core, y, *experts = [("expert", 1 << n) for n in range(layout.experts.bit_length() - 1)]
    x, z, *groups = [("group", 1 << n) for n in range(layout.groups.bit_length() - 1)]
    rest = experts + groups
    return (
        [core, x, z, y] + rest,
        [core, x, y, z] + rest,
        [core, y, x, z] + rest,
        [core, y, x, z] + rest,
        [core, x, y, z] + rest,
        [core, y, z, x] + rest,
        [core, z, x, y] + rest,
    )


DONE_FIRST = (1, 1, 1)
DONE_EXPERTS = (2, 1, 1)
DONE_LATE = (3, 2, 1)
DONE_NONE = (0, 0, 0, 0)


def halving_plan(layout, orders, shapes, first, last):
    plan = []
    for steps, shape, low, high in zip(orders, shapes, first, last):
        mine, left = [], sorted(steps, key=lambda step: step[1])
        for number, step in enumerate(steps[:high]):
            axis, bit = step
            below = sum(1 for other in left if other[0] == axis and other[1] < bit)
            left.remove(step)
            if number < low:
                continue
            experts, groups = shape[:2]
            if axis == "expert":
                shape, copies = (experts // 2, groups) + shape[2:], experts // 2
            else:
                shape, copies = (experts, groups // 2) + shape[2:], experts * groups // 2
            mine.append(((axis, bit, below), shape, copies))
        plan.append(mine)
    return plan


def rope_turn(x, cosine, sine):
    parts = []
    for begin in range(0, x.shape[1], LANES):
        part = x[:, begin : begin + LANES]
        lane = lax.broadcasted_iota(jnp.int32, part.shape, 1)
        other = jnp.where(
            lane % HEAD < HEAD // 2,
            pltpu.roll(part, LANES - HEAD // 2, 1),
            pltpu.roll(part, HEAD // 2, 1),
        )
        parts.append(part * cosine + other * sine)
    return jnp.concatenate(parts, axis=1)


def normed(x, gain):
    return x * lax.rsqrt(jnp.mean(x * x, axis=-1, keepdims=True) + epsilon) * gain


def other_bits(x, mask, count):
    made, bit = 0, 1
    while bit < count:
        mine, theirs = (x // bit) % 2, (mask // bit) % 2
        made = made + bit * (mine + theirs - 2 * mine * theirs)
        bit *= 2
    return made


def slot_rows(ids_row, rows):
    labels = lax.broadcasted_iota(jnp.int32, (EXPERTS, rows), 0)
    first, second = labels == ids_row[0:1], labels == ids_row[1:2]
    both = jnp.where(first | second, 1.0, 0.0).astype(BF16)
    earlier_t = lax.broadcasted_iota(jnp.int32, (rows, rows), 0)
    later_t = lax.broadcasted_iota(jnp.int32, (rows, rows), 1)
    earlier = mm(both, jnp.where(earlier_t < later_t, 1.0, 0.0).astype(BF16))
    targets = []
    for mask, ids in ((first, ids_row[0:1]), (second, ids_row[1:2])):
        slot = jnp.sum(jnp.where(mask, earlier, 0.0), axis=0, keepdims=True)
        targets.append(jnp.where(slot < CAP, ids.astype(F32) * CAP + slot, -1.0))
    return targets


def slot_masks(number, target, rows):
    slots = (number * CAP + lax.broadcasted_iota(jnp.int32, (CAP, rows), 0)).astype(F32)
    return slots == target[0:1], slots == target[1:2]


def gather_slots(layout, target, source, made):
    rows = source.shape[0]
    for number in range(layout.peers):
        first, second = slot_masks(number, target, rows)
        chosen = jnp.where(first | second, 1.0, 0.0).astype(BF16)
        made[divmod(number, layout.experts)] = mm(chosen, source[...]).astype(BF16)


def first_kernel(
    layout,
    tokens,
    gain_attn,
    w_qkv,
    cosine,
    sine,
    ids_row,
    seg_row,
    cot,
    w_out,
    gain_ffn,
    w_router_t,
    dense_gate_any,
    dense_up_any,
    dense_down_any,
    q_out,
    kv_out,
    att_t_out,
    lse_out,
    bias_out,
    target_out,
    hidden_out,
    low_out,
    mixed_out,
    grad_out,
    gate_out,
    up_out,
    down_out,
    cots_out,
    quad_out,
    rows_out,
    shares_out,
    far_cot_out,
    far_target_out,
    normed_low,
    send_cot,
    seg_all,
    acc,
    top,
    total,
    att,
    send_rows,
    send_shares,
    dense_gate,
    dense_up,
    dense_down,
    gate_held,
    up_held,
    down_held,
    load_sems,
    kv_send,
    kv_recv,
    seg_send,
    seg_recv,
    cot_send,
    cot_recv,
    quad_send,
    quad_recv,
    row_send,
    row_recv,
    share_send,
    share_recv,
    own_sems,
    far_send,
    far_recv,
    half_send,
    half_recv,
):
    rows, width = tokens.shape
    reach, experts = layout.reach, layout.experts
    ff = dense_gate.shape[1]
    e = lax.axis_index("expert")
    loads = [
        pltpu.make_async_copy(source, target, load_sems.at[number])
        for number, (source, target) in enumerate(
            ((dense_gate_any, dense_gate), (dense_up_any, dense_up), (dense_down_any, dense_down))
        )
    ]
    for copy in loads:
        copy.start()
    meet(layout)

    share = layout.share
    ids = ids_row[...]
    relative = other_bits(ids % share, own_share(layout), share) * experts
    targets = slot_rows(relative + other_bits(ids // share, e, experts), rows)
    target_out[0:1] = targets[0]
    target_out[1:2] = targets[1]
    target_out[2:8] = jnp.full((6, rows), -1.0, F32)
    far = [
        remote(
            source,
            target.at[number - 1],
            far_send.at[place, number - 1],
            far_recv.at[place, number - 1],
            layout.far(number),
        )
        for number in range(1, layout.outers)
        for place, (source, target) in enumerate(((cot, far_cot_out), (target_out, far_target_out)))
    ]
    for copy in far:
        copy.start()
    gather_slots(layout, target_out[...], cot, send_cot)
    cot_sends = to_row(layout, send_cot, cots_out, cot_send, cot_recv)
    own_cot = pltpu.make_async_copy(send_cot.at[:, 0], cots_out.at[:, 0], own_sems.at[0])
    own_cot.start()
    early = experts // 2
    for copy in cot_sends[:early]:
        copy.start()

    x = tokens[...].astype(F32)
    normed_low[...] = normed(x, gain_attn[...].reshape(1, width)).astype(BF16)
    seg_all[0] = jnp.broadcast_to(seg_row[...].astype(F32).reshape(1, rows), (8, rows))

    def project(step, carry):
        for part in range(3):
            columns = pl.ds(pl.multiple_of(part * width + step * TILE, TILE), TILE)
            made = mm(normed_low[...], w_qkv[:, columns])
            columns = pl.ds(pl.multiple_of(step * TILE, TILE), TILE)
            if part == 0:
                made = rope_turn(made, cosine[...], sine[...]) * HEAD ** (-0.5)
                q_out[:, columns] = made.astype(BF16)
            elif part == 1:
                made = rope_turn(made, cosine[...], sine[...])
                kv_out[0, :, columns] = made.astype(BF16)
            else:
                columns = pl.ds(pl.multiple_of(width + step * TILE, TILE), TILE)
                kv_out[0, :, columns] = made.astype(BF16)
        return carry

    lax.fori_loop(0, width // TILE, project, 0)

    halos = []
    for distance in range(1, reach + 1):
        to = {"expert": lax.rem(e + distance, experts)}
        halos.append(
            [
                pltpu.make_async_remote_copy(
                    src_ref=source.at[0],
                    dst_ref=source.at[distance],
                    send_sem=sems[0].at[distance],
                    recv_sem=sems[1].at[distance],
                    device_id=to,
                    device_id_type=MESH,
                )
                for source, sems in (
                    (kv_out, (kv_send, kv_recv)),
                    (seg_all, (seg_send, seg_recv)),
                )
            ]
        )
        for copy in halos[-1]:
            copy.start()

    lane = lax.broadcasted_iota(jnp.int32, (rows, LANES), 1)
    for distance in range(reach + 1):
        if distance:
            for copy in halos[distance - 1]:
                copy.wait()
        if distance == reach:
            for copy in cot_sends[early:]:
                copy.start()
        seg_col = jnp.transpose(jnp.broadcast_to(seg_all[distance, 0:1], (LANES, rows)))[:, 0:1]
        key_no = lax.broadcasted_iota(jnp.int32, (rows, rows), 0) - distance * rows
        offset = lax.broadcasted_iota(jnp.int32, (rows, rows), 1) - key_no
        allowed = (
            (offset >= 0)
            & (offset < WINDOW)
            & (key_no + e * rows >= 0)
            & (seg_col == seg_all[0, 0:1])
        )
        bias_out[distance] = jnp.where(allowed, 0.0, NEG).astype(BF16)

        def attend(pair, carry, distance=distance):
            columns = pl.ds(pl.multiple_of(pair * LANES, LANES), LANES)
            value_columns = pl.ds(pl.multiple_of(width + pair * LANES, LANES), LANES)
            queries = q_out[:, columns]
            keys = kv_out[distance, :, columns]
            values_t = jnp.transpose(kv_out[distance, :, value_columns])
            for inner in range(2):
                head = pair * 2 + inner
                mine = jnp.where((lane // HEAD) == inner, queries, jnp.zeros_like(queries))
                value_t = values_t[inner * HEAD : (inner + 1) * HEAD]
                out_rows = pl.ds(pl.multiple_of(head * HEAD, HEAD), HEAD)
                blocks = (
                    [(slice(0, rows // 2), rows // 2), (slice(rows // 2, rows), rows)]
                    if distance == 0
                    else [(slice(0, rows), rows)]
                )
                for q_cut, key_count in blocks:
                    scores = mm(keys[:key_count], mine[q_cut], NT)
                    scores = scores + bias_out[distance, :key_count, q_cut].astype(F32)
                    peak = jnp.max(scores, axis=0, keepdims=True)
                    if distance:
                        before = top[pl.ds(head, 1), q_cut]
                        peak = jnp.maximum(before, peak)
                    weights = jnp.exp(scores - peak)
                    amount = jnp.sum(weights, axis=0, keepdims=True)
                    part = mm(value_t[:, :key_count], weights.astype(BF16))
                    if distance:
                        shrink = jnp.exp(before - peak)
                        amount = amount + total[pl.ds(head, 1), q_cut] * shrink
                        part = part + acc[out_rows, q_cut] * shrink
                    top[pl.ds(head, 1), q_cut] = peak
                    total[pl.ds(head, 1), q_cut] = amount
                    acc[out_rows, q_cut] = part
            return carry

        lax.fori_loop(0, HEADS // 2, attend, 0)

    lse_out[...] = top[...] + jnp.log(total[...])

    def finish(pair, carry):
        out_rows = pl.ds(pl.multiple_of(pair * LANES, LANES), LANES)
        scale = jnp.concatenate(
            [
                jnp.broadcast_to(1.0 / total[pl.ds(pair * 2 + inner, 1), :], (HEAD, rows))
                for inner in range(2)
            ],
            axis=0,
        )
        made = acc[out_rows, :] * scale
        att_t_out[out_rows, :] = made.astype(BF16)
        att[:, out_rows] = jnp.transpose(made).astype(BF16)
        return carry

    lax.fori_loop(0, HEADS // 2, finish, 0)

    hidden_out[...] = tokens[...].astype(F32) + mm(att[...], w_out[...])
    low = normed(hidden_out[...], gain_ffn[...].reshape(1, width)).astype(BF16)
    low_out[...] = low
    logits = mm(w_router_t[...], low, NT)
    route = jnp.exp(logits - jnp.max(logits, axis=0, keepdims=True))
    route = route / jnp.sum(route, axis=0, keepdims=True)
    labels = lax.broadcasted_iota(jnp.int32, (EXPERTS, rows), 0)
    picked = [
        jnp.sum(jnp.where(labels == ids_row[k : k + 1], route, 0.0), axis=0, keepdims=True)
        for k in range(2)
    ]
    both = picked[0] + picked[1]
    shares = []
    for k in range(2):
        parts = split3(picked[k] / both)
        shares.append(
            jnp.concatenate(
                [part.astype(F32) for part in parts] + [jnp.zeros((5, rows), F32)], axis=0
            ).astype(BF16)
        )
    send_shares[...] = jnp.zeros_like(send_shares)
    for number in range(layout.peers):
        first, second = slot_masks(number, target_out[...], rows)
        first = jnp.where(first, 1.0, 0.0).astype(BF16)
        second = jnp.where(second, 1.0, 0.0).astype(BF16)
        place = divmod(number, experts)
        send_rows[place] = mm(first + second, low).astype(BF16)
        share = mm(shares[0], first, NT) + mm(shares[1], second, NT)
        share = jnp.sum(share, axis=0, keepdims=True)
        send_shares[place + (slice(None), slice(0, CAP))] = jnp.broadcast_to(share, (8, CAP))
    sends = to_row(layout, send_rows, rows_out, row_send, row_recv)
    sends += to_row(layout, send_shares, shares_out, share_send, share_recv)
    for source, target, sem in (
        (send_rows, rows_out, own_sems.at[1]),
        (send_shares, shares_out, own_sems.at[2]),
    ):
        sends.append(pltpu.make_async_copy(source.at[:, 0], target.at[:, 0], sem))
    for copy in reversed(sends):
        copy.start()
    own_cot.wait()
    for copy in cot_sends:
        copy.wait()
    sends += to_quad(layout, cots_out, quad_out, quad_send, quad_recv)
    sends.append(pltpu.make_async_copy(cots_out.at[0], quad_out.at[0], own_sems.at[3]))
    for copy in sends[-layout.share :]:
        copy.start()

    for copy in loads:
        copy.wait()
    mixed_out[...] = hidden_out[...]
    grad_out[...] = jnp.zeros_like(grad_out)
    part_width = ff // experts
    per_part = part_width // TILE
    half = experts // 2
    odd = bit_of("expert", 1)
    halvings = [
        Halving(("expert", 1, 0), held, taken, half_send.at[number], half_recv.at[number])
        for number, (held, taken) in enumerate(
            ((gate_held, gate_out), (up_held, up_out), (down_held, down_out))
        )
    ]

    def branch(step, carry):
        place = step // per_part
        part = 2 * (place % half) + (odd + 1 + place // half) % 2
        columns = pl.ds(pl.multiple_of(part * part_width + (step % per_part) * TILE, TILE), TILE)
        gate_w, up_w, down_w = dense_gate[:, columns], dense_up[:, columns], dense_down[columns, :]
        gate_pre = mm(low_out[...], gate_w)
        up_pre = mm(low_out[...], up_w)
        grad_act = mm(cot[...], down_w, NT)
        silu, slope = silu_parts(gate_pre)
        act = (silu * up_pre).astype(BF16)
        grad_gate = (grad_act * up_pre * slope).astype(BF16)
        grad_up = (grad_act * silu).astype(BF16)
        mixed_out[...] += mm(act, down_w)
        grad_out[...] += mm(grad_gate, gate_w, NT) + mm(grad_up, up_w, NT)
        inside = pl.ds(pl.multiple_of((step % per_part) * TILE, TILE), TILE)
        for made, held in (
            (mm(low_out[...], grad_gate, TN), gate_held),
            (mm(low_out[...], grad_up, TN), up_held),
        ):
            made = made.astype(BF16)
            block = held.shape[2]
            for place in range(held.shape[1]):
                held[part, place, :, inside] = made[place * block : (place + 1) * block]
        made = mm(act, cot[...], TN).astype(BF16)
        block = ff // layout.groups
        cut = width // experts
        low_row = part * part_width + (step % per_part) * TILE
        for inner in range(0, TILE, block):
            for other in range(experts):
                down_held[other, (low_row + inner) // block] = pack(
                    made[inner : inner + block, other * cut : (other + 1) * cut]
                )
        return carry

    lax.fori_loop(0, ff // (2 * TILE), branch, 0)
    for halving in halvings[:2]:
        halving.start()
    lax.fori_loop(ff // (2 * TILE), ff // TILE, branch, 0)
    halvings[2].start()
    for halving in halvings:
        halving.add()
    for copy in far + sends:
        copy.wait()


def first(layout, tokens, gain_attn, w_qkv, cosine, sine, ids_row, seg_row, cot, w_out, gain_ffn, w_router_t, dense_gate, dense_up, dense_down):
    rows, width = tokens.shape
    ff = dense_gate.shape[1]
    reach, experts, groups = layout.reach, layout.experts, layout.groups
    half = experts // 2
    others = layout.outers - 1
    dma = pltpu.SemaphoreType.DMA
    wide = (groups, width // groups, ff // experts)
    tall = (groups,) + packed_shape(ff // groups, width // experts)
    return pl.pallas_call(
        functools.partial(first_kernel, layout),
        out_shape=[
            jax.ShapeDtypeStruct((rows, width), BF16),
            jax.ShapeDtypeStruct((reach + 1, rows, 2 * width), BF16),
            jax.ShapeDtypeStruct((width, rows), BF16),
            jax.ShapeDtypeStruct((EXPERTS, rows), F32),
            jax.ShapeDtypeStruct((reach + 1, rows, rows), BF16),
            jax.ShapeDtypeStruct((8, rows), F32),
            jax.ShapeDtypeStruct((rows, width), F32),
            jax.ShapeDtypeStruct((rows, width), BF16),
            jax.ShapeDtypeStruct((rows, width), F32),
            jax.ShapeDtypeStruct((rows, width), F32),
            jax.ShapeDtypeStruct((half,) + wide, BF16),
            jax.ShapeDtypeStruct((half,) + wide, BF16),
            jax.ShapeDtypeStruct((half,) + tall, BF16),
            jax.ShapeDtypeStruct(layout.slots(width), BF16),
            jax.ShapeDtypeStruct(layout.slots(width), BF16),
            jax.ShapeDtypeStruct(layout.slots(width), BF16),
            jax.ShapeDtypeStruct((layout.share, experts, 8, LANES), F32),
            jax.ShapeDtypeStruct((others, rows, width), BF16),
            jax.ShapeDtypeStruct((others, 8, rows), F32),
        ],
        in_specs=[VMEM] * 11 + [ANY] * 3,
        out_specs=[VMEM] * 13 + [ANY] * 6,
        scratch_shapes=[
            pltpu.VMEM((rows, width), BF16),
            pltpu.VMEM(layout.slots(width), BF16),
            pltpu.VMEM((reach + 1, 8, rows), F32),
            pltpu.VMEM((width, rows), F32),
            pltpu.VMEM((EXPERTS, rows), F32),
            pltpu.VMEM((EXPERTS, rows), F32),
            pltpu.VMEM((rows, width), BF16),
            pltpu.VMEM(layout.slots(width), BF16),
            pltpu.VMEM((layout.share, experts, 8, LANES), F32),
            pltpu.VMEM((width, ff), BF16),
            pltpu.VMEM((width, ff), BF16),
            pltpu.VMEM((ff, width), BF16),
            pltpu.VMEM((experts,) + wide, BF16),
            pltpu.VMEM((experts,) + wide, BF16),
            pltpu.VMEM((experts,) + tall, BF16),
            dma((3,)),
            dma((reach + 1,)),
            dma((reach + 1,)),
            dma((reach + 1,)),
            dma((reach + 1,)),
            dma((experts,)),
            dma((experts,)),
            dma((layout.share,)),
            dma((layout.share,)),
            dma((experts,)),
            dma((experts,)),
            dma((experts,)),
            dma((experts,)),
            dma((4,)),
            dma((2, others)),
            dma((2, others)),
            dma((3, half)),
            dma((3, half)),
        ],
        compiler_params=pltpu.CompilerParams(
            collective_id=0, has_side_effects=True, vmem_limit_bytes=62 * MIB
        ),
        cost_estimate=pl.CostEstimate(flops=1 << 30, bytes_accessed=1 << 20, transcendentals=0),
        name="first",
    )(tokens, gain_attn, w_qkv, cosine, sine, ids_row, seg_row, cot, w_out, gain_ffn, w_router_t, dense_gate, dense_up, dense_down)


def split3(x):
    high = x.astype(BF16)
    rest = x - high.astype(F32)
    middle = rest.astype(BF16)
    return high, middle, (rest - middle.astype(F32)).astype(BF16)


def silu_parts(gate_pre):
    gate = 1.0 / (1.0 + jnp.exp(-gate_pre))
    return gate_pre * gate, gate * (1.0 + gate_pre * (1.0 - gate))


def share_column(share_row):
    across = lax.broadcasted_iota(jnp.int32, (CAP, CAP), 1)
    down = lax.broadcasted_iota(jnp.int32, (CAP, CAP), 0)
    return jnp.sum(jnp.where(across == down, share_row, 0.0), axis=1, keepdims=True)


def own_share(layout):
    return lax.rem(lax.axis_index("group"), layout.share)


class Sums:
    def __init__(self, layout, orders, arrays, first, last, keep):
        self.plan = halving_plan(layout, orders, [one.shape for one in arrays], first, last)
        self.keep = keep

    def scratch(self):
        made = []
        for mine in self.plan:
            for number, (_, shape, copies) in enumerate(mine):
                made += trade_sems(copies)
                if not self.keep or number + 1 < len(mine):
                    made.append(pltpu.VMEM(shape, BF16))
        return made

    def outputs(self):
        return [jax.ShapeDtypeStruct(mine[-1][1], BF16) for mine in self.plan if mine]

    def chains(self, held_refs, outputs, scratch):
        outputs, scratch = list(outputs), list(scratch)
        chains = []
        for held, mine in zip(held_refs, self.plan):
            chain = []
            for number, (step, _, _) in enumerate(mine):
                sems = scratch.pop(0), scratch.pop(0)
                if not self.keep or number + 1 < len(mine):
                    taken = scratch.pop(0)
                else:
                    taken = outputs.pop(0)
                chain.append(Halving(step, held, taken, *sems))
                held = taken
            chains.append(chain)
        return chains


def experts_kernel(layout, sums, *refs):
    (
        rows_in,
        cots,
        shares,
        gate_any,
        up_any,
        down_any,
        rows_any,
        shares_any,
        gate_held,
        up_held,
        down_held,
        back_out,
        grad_back,
        quad_rows,
        quad_shares,
        far_rows,
        gate_sum,
        gate_w,
        up_w,
        down_w,
        scaled,
        acc,
        grad_acc,
        send_out,
        send_grad,
        load_sems,
        back_send,
        back_recv,
        quad_send,
        quad_recv,
        own_sems,
        far_send,
        far_recv,
        *rest,
    ) = refs
    share, experts = layout.share, layout.experts
    width, ff = gate_w.shape[1:]
    mine = own_share(layout)

    def load(place):
        slot = place % 2
        return [
            pltpu.make_async_copy(
                source.at[flipped(mine, place % share)], target.at[slot], load_sems.at[slot, number]
            )
            for number, (source, target) in enumerate(
                ((gate_any, gate_w), (up_any, up_w), (down_any, down_w))
            )
        ]

    for copy in load(0):
        copy.start()
    meet(layout)
    quads = to_quad(layout, rows_any, quad_rows, quad_send.at[0], quad_recv.at[0])
    share_quads = to_quad(layout, shares_any, quad_shares, quad_send.at[1], quad_recv.at[1])
    own = [
        pltpu.make_async_copy(rows_any.at[0], quad_rows.at[0], own_sems.at[2]),
        pltpu.make_async_copy(shares_any.at[0], quad_shares.at[0], own_sems.at[3]),
    ]
    far_low, far_high = far_parts(layout)[0]
    fars = [
        to_far(layout, rows_any, far_rows.at[:, 0:1], 0, 1, far_send.at[0], far_recv.at[0]),
        to_far(layout, quad_rows, far_rows.at[:, 1:], 1, far_high, far_send.at[1], far_recv.at[1])
        if far_high > 1
        else [],
    ]
    early = max(far_high, 2)
    for copy in quads[:early] + share_quads + own + fars[0]:
        copy.start()
    chains = sums.chains((gate_held, up_held, down_held), (gate_sum,), rest)
    chunk = 2 * TILE
    copies = list(own)
    half = experts // 2
    for place in range(2 * share):
        turn, low = place % share, half * (1 - place // share)
        for copy in load(place):
            copy.wait()
        if place + 1 < 2 * share:
            for copy in load(place + 1):
                copy.start()
        slot = place % 2
        for number in range(half):
            column = share_column(shares[turn, low + number, 0:1, :CAP])
            scaled[number] = (cots[turn, low + number].astype(F32) * column).astype(BF16)

        def step(number, carry, turn=turn, slot=slot, low=low):
            columns = pl.ds(pl.multiple_of(number * chunk, chunk), chunk)
            n = rows_in[turn, low : low + half].reshape(half * CAP, width)
            grad = scaled[...].reshape(half * CAP, width)
            gate_pre = mm(n, gate_w[slot, :, columns])
            up_pre = mm(n, up_w[slot, :, columns])
            grad_act = mm(grad, down_w[slot, columns, :], NT)
            silu, slope = silu_parts(gate_pre)
            act = (silu * up_pre).astype(BF16)
            grad_gate = (grad_act * up_pre * slope).astype(BF16)
            grad_up = (grad_act * silu).astype(BF16)
            acc[...] += mm(act, down_w[slot, columns, :])
            grad_acc[...] += mm(grad_gate, gate_w[slot, :, columns], NT) + mm(
                grad_up, up_w[slot, :, columns], NT
            )
            return carry

        acc[...] = jnp.zeros_like(acc)
        grad_acc[...] = jnp.zeros_like(grad_acc)
        lax.fori_loop(0, ff // chunk, step, 0)
        send_out[turn, low : low + half] = acc[...].astype(BF16).reshape(half, CAP, width)
        send_grad[turn, low : low + half] = grad_acc[...].astype(BF16).reshape(half, CAP, width)
        for bits in range(low, low + half):
            for which, (source, target) in enumerate(
                ((send_out, back_out), (send_grad, grad_back))
            ):
                ends = source.at[turn, bits], target.at[turn, bits]
                sem = which, turn, bits
                if bits:
                    device = {"expert": flipped(lax.axis_index("expert"), bits)}
                    copies.append(remote(*ends, back_send.at[sem], back_recv.at[sem], device))
                else:
                    copies.append(pltpu.make_async_copy(*ends, back_send.at[sem]))
                copies[-1].start()
        if place == share // 2:
            for copy in quads[: far_high - 1]:
                copy.wait()
            for copy in fars[1] + quads[early:]:
                copy.start()
            for chain in chains:
                for halving in chain[:1]:
                    halving.start()
    for chain in chains:
        for halving in chain:
            halving.add()
    for copy in copies + quads[far_high - 1 :] + share_quads + fars[0] + fars[1]:
        copy.wait()


def far_parts(layout):
    middle = max(layout.share // 2, 1)
    return (0, middle), (middle, layout.share)


def run_experts(layout, rows_in, cots, shares, expert_gate, expert_up, expert_down, held):
    share, experts, others = layout.share, layout.experts, layout.outers - 1
    _, width, ff = expert_gate.shape
    dma = pltpu.SemaphoreType.DMA
    sums = Sums(layout, step_orders(layout)[:3], held, DONE_FIRST, DONE_EXPERTS, True)
    slots = jax.ShapeDtypeStruct(layout.slots(width), BF16)
    return pl.pallas_call(
        functools.partial(experts_kernel, layout, sums),
        out_shape=[
            slots,
            slots,
            slots,
            jax.ShapeDtypeStruct(shares.shape, F32),
            far_shape(layout, far_parts(layout)[0][1], width),
            *sums.outputs(),
        ],
        in_specs=[VMEM] * 3 + [ANY] * 5 + [VMEM] * 3,
        out_specs=[ANY] * 5 + [VMEM],
        scratch_shapes=[
            pltpu.VMEM((2, width, ff), BF16),
            pltpu.VMEM((2, width, ff), BF16),
            pltpu.VMEM((2, ff, width), BF16),
            pltpu.VMEM((experts // 2, CAP, width), BF16),
            pltpu.VMEM((experts // 2 * CAP, width), F32),
            pltpu.VMEM((experts // 2 * CAP, width), F32),
            pltpu.VMEM(layout.slots(width), BF16),
            pltpu.VMEM(layout.slots(width), BF16),
            dma((2, 3)),
            dma((2, share, experts)),
            dma((2, share, experts)),
            dma((2, share)),
            dma((2, share)),
            dma((4,)),
            dma((2, others)),
            dma((2, others)),
            *sums.scratch(),
        ],
        compiler_params=pltpu.CompilerParams(
            collective_id=1, has_side_effects=True, vmem_limit_bytes=60 * MIB
        ),
        cost_estimate=pl.CostEstimate(flops=1 << 30, bytes_accessed=1 << 20, transcendentals=0),
        name="experts",
    )(
        rows_in,
        cots,
        shares,
        expert_gate,
        expert_up,
        expert_down,
        rows_in,
        shares,
        *held,
    )


def rope_back(grad, cosine, sine):
    lane = lax.broadcasted_iota(jnp.int32, grad.shape, 1)
    turned = grad * sine
    other = jnp.where(
        lane % HEAD < HEAD // 2,
        pltpu.roll(turned, LANES - HEAD // 2, 1),
        pltpu.roll(turned, HEAD // 2, 1),
    )
    return grad * cosine + other


def by_blocks(target, made):
    parts, places = target.shape[:2]
    block, cut = made.shape[0] // places, made.shape[1] // parts
    for part in range(parts):
        for place in range(places):
            target[part, place] = pack(
                made[place * block : (place + 1) * block, part * cut : (part + 1) * cut]
            )


def combine_part(
    back,
    grad_back,
    target,
    ids_row,
    hidden,
    mixed_in,
    grad_in,
    low,
    cot,
    gain,
    w_router_t,
    w_out,
    att_t,
    mixed_out,
    grad_hidden_out,
    grad_att_out,
    proj_out,
    router_out,
    gain_out,
):
    rows, width = hidden.shape
    slots = back.shape[0] * back.shape[1] * CAP
    columns = jnp.transpose(
        jnp.concatenate(
            [target[...], ids_row[...].astype(F32), jnp.zeros((LANES - 10, rows), F32)], axis=0
        )
    )
    slot_no = lax.broadcasted_iota(jnp.int32, (rows, slots), 1).astype(F32)
    cot_float = cot[...].astype(F32)
    logits = mm(low[...], w_router_t[...], NT)
    route = jnp.exp(logits - jnp.max(logits, axis=1, keepdims=True))
    route = route / jnp.sum(route, axis=1, keepdims=True)
    labels = lax.broadcasted_iota(jnp.int32, (rows, EXPERTS), 1).astype(F32)
    masks = [labels == columns[:, 8 + k : 9 + k] for k in range(2)]
    picked = [jnp.sum(jnp.where(mask, route, 0.0), axis=1, keepdims=True) for mask in masks]
    both = picked[0] + picked[1]
    chosen, shares, grads = [], [], []
    mixed = mixed_in[...]
    for k in range(2):
        chosen.append(jnp.where(slot_no == columns[:, k : k + 1], 1.0, 0.0).astype(BF16))
        fetched = mm(chosen[k], back[...].reshape(slots, width))
        shares.append(picked[k] / both)
        mixed = mixed + shares[k] * fetched
        grads.append(jnp.sum(cot_float * fetched, axis=1, keepdims=True))
    mixed_out[...] = mixed.astype(BF16)
    mean = grads[0] * shares[0] + grads[1] * shares[1]
    grad_route = jnp.zeros_like(route)
    for k in range(2):
        grad_route = grad_route + jnp.where(masks[k], (grads[k] - mean) / both, 0.0)
    grad_logits = route * (grad_route - jnp.sum(route * grad_route, axis=1, keepdims=True))
    grad_logits = grad_logits.astype(BF16)
    router_out[...] = mm(grad_logits, low[...], TN)
    grad = grad_in[...] + mm(chosen[0] + chosen[1], grad_back[...].reshape(slots, width))
    grad = grad + mm(grad_logits, w_router_t[...])
    h = hidden[...]
    scale = lax.rsqrt(jnp.mean(h * h, axis=-1, keepdims=True) + epsilon)
    gain_out[...] = jnp.sum(grad * h * scale, axis=0, keepdims=True)
    grad = grad * gain[...].reshape(1, width)
    grad = scale * grad - h * (scale * scale * scale) * jnp.mean(grad * h, axis=-1, keepdims=True)
    grad = cot_float + grad
    grad_hidden_out[...] = grad
    grad_low = grad.astype(BF16)
    grad_att_out[...] = mm(grad_low, w_out[...], NT).astype(BF16)
    by_blocks(proj_out, mm(att_t[...], grad_low).astype(BF16))


def late_kernel(layout, sums, *refs):
    (
        back,
        grad_back,
        target,
        ids_row,
        hidden,
        mixed_in,
        grad_in,
        low,
        cot,
        gain_ffn,
        w_router_t,
        w_out,
        att_t,
        q_in,
        kv_in,
        bias,
        lse,
        tokens,
        gain,
        w_qkv,
        cosine,
        sine,
        gate_held,
        up_held,
        down_held,
        far_cot,
        far_target,
        rows_any,
        shares_any,
        mixed_out,
        tokens_out,
        proj_out,
        qkv_out,
        small_out,
        gate_sum,
        up_sum,
        far_cots_out,
        far_out,
        far_shares_out,
        grad_att,
        router_term,
        gain_term,
        send_cot,
        halo_send,
        halo_recv,
        own_kv,
        packed,
        send_sems,
        recv_sems,
        cot_send,
        cot_recv,
        own_sem,
        mixed_sem,
        far_send,
        far_recv,
        *rest,
    ) = refs
    rows, width = tokens.shape
    reach, experts = layout.reach, layout.experts
    e = lax.axis_index("expert")
    pairs = HEADS // 2
    lane = lax.broadcasted_iota(jnp.int32, (rows, LANES), 1)
    load = pltpu.make_async_copy(grad_in, tokens_out, mixed_sem)
    load.start()
    meet(layout)
    far_low, far_high = far_parts(layout)[1]
    far = to_far(layout, rows_any, far_out, far_low, far_high, far_send.at[0], far_recv.at[0])
    far += to_far(
        layout, shares_any, far_shares_out, 0, layout.share, far_send.at[1], far_recv.at[1]
    )
    for copy in far:
        copy.start()
    chains = sums.chains((gate_held, up_held, down_held), (gate_sum, up_sum), rest)
    for chain in chains:
        for halving in chain[:1]:
            halving.start()
    cot_sends = []
    for number in range(layout.outers - 1):
        for copy in cot_sends:
            copy.wait()
        fetch = pltpu.make_async_copy(far_cot.at[number], grad_att, own_sem.at[number])
        fetch.start()
        fetch.wait()
        gather_slots(layout, far_target[number], grad_att, send_cot)
        cot_sends = to_peers(
            layout, send_cot, far_cots_out.at[number], cot_send.at[number], cot_recv.at[number]
        )
        cot_sends.append(
            pltpu.make_async_copy(
                send_cot.at[0, 0], far_cots_out.at[number, 0, 0], own_sem.at[number]
            )
        )
        for copy in cot_sends:
            copy.start()

    load.wait()
    combine_part(
        back,
        grad_back,
        target,
        ids_row,
        hidden,
        mixed_in,
        tokens_out,
        low,
        cot,
        gain_ffn,
        w_router_t,
        w_out,
        att_t,
        packed.at[:, :width],
        tokens_out,
        grad_att,
        proj_out,
        router_term,
        gain_term,
    )
    mixed = pltpu.make_async_copy(packed.at[:, :width], mixed_out, mixed_sem)
    mixed.start()
    mixed.wait()

    def halo(distance, pair):
        return pltpu.make_async_remote_copy(
            src_ref=halo_send.at[distance - 1, pair],
            dst_ref=halo_recv.at[distance - 1, pair],
            send_sem=send_sems.at[distance - 1, pair],
            recv_sem=recv_sems.at[distance - 1, pair],
            device_id={"expert": lax.rem(e + experts - distance, experts)},
            device_id_type=MESH,
        )

    def heads(pair, carry):
        columns = pl.ds(pl.multiple_of(pair * LANES, LANES), LANES)
        value_columns = pl.ds(pl.multiple_of(width + pair * LANES, LANES), LANES)
        queries, grads = q_in[:, columns], grad_att[:, columns]
        grads_t = jnp.transpose(grads.astype(F32))
        shrunk = grads_t * att_t[columns, :].astype(F32)
        grad_q = [None, None]
        for distance in range(reach, -1, -1):
            keys = kv_in[distance, :, columns]
            values = kv_in[distance, :, value_columns]
            keys_t = jnp.transpose(keys)
            grad_k = grad_v = None
            for inner in range(2):
                head = pair * 2 + inner
                cut = slice(inner * HEAD, (inner + 1) * HEAD)
                mine = (lane // HEAD) == inner
                query = jnp.where(mine, queries, jnp.zeros_like(queries))
                grad = jnp.where(mine, grads, jnp.zeros_like(grads))
                total = jnp.sum(shrunk[cut], axis=0, keepdims=True)
                scores = mm(keys, query, NT) + bias[distance].astype(F32)
                probs = jnp.exp(scores - lse[pl.ds(head, 1), :])
                grad_probs = mm(values, grad, NT)
                grad_scores = (probs * (grad_probs - total)).astype(BF16)
                part_v = mm(probs.astype(BF16), grad)
                part_k = mm(grad_scores, query)
                part_q = mm(keys_t[cut], grad_scores)
                grad_v = part_v if grad_v is None else grad_v + part_v
                grad_k = part_k if grad_k is None else grad_k + part_k
                grad_q[inner] = part_q if grad_q[inner] is None else grad_q[inner] + part_q
            if distance:
                halo_send[distance - 1, pair, 0] = grad_k.astype(BF16)
                halo_send[distance - 1, pair, 1] = grad_v.astype(BF16)
                halo(distance, pair).start()
            else:
                own_kv[pair, 0] = grad_k.astype(BF16)
                own_kv[pair, 1] = grad_v.astype(BF16)
        grad = jnp.transpose(jnp.concatenate(grad_q, axis=0)) * HEAD ** (-0.5)
        packed[:, columns] = rope_back(grad, cosine[...], sine[...]).astype(BF16)
        return carry

    lax.fori_loop(0, pairs, heads, 0)
    x = tokens[...].astype(F32)
    grad_att[...] = normed(x, gain[...].reshape(1, width)).astype(BF16)
    normed_low = grad_att

    def merge(pair, carry):
        grad_k, grad_v = own_kv[pair, 0].astype(F32), own_kv[pair, 1].astype(F32)
        for distance in range(1, reach + 1):
            halo(distance, pair).wait()
            grad_k = grad_k + halo_recv[distance - 1, pair, 0].astype(F32)
            grad_v = grad_v + halo_recv[distance - 1, pair, 1].astype(F32)
        columns = pl.ds(pl.multiple_of(width + pair * LANES, LANES), LANES)
        packed[:, columns] = rope_back(grad_k, cosine[...], sine[...]).astype(BF16)
        columns = pl.ds(pl.multiple_of(2 * width + pair * LANES, LANES), LANES)
        packed[:, columns] = grad_v.astype(BF16)
        return carry

    lax.fori_loop(0, pairs, merge, 0)
    for chain in chains:
        for halving in chain:
            halving.add()
    thirds, parts, places = qkv_out.shape[:3]
    block, cut = width // places, width // parts
    for part in range(parts):
        columns = slice(part * thirds * cut, (part + 1) * thirds * cut)
        made = mm(normed_low[...], packed[:, columns], TN).astype(BF16)
        for third in range(thirds):
            for place in range(places):
                qkv_out[third, part, place] = pack(
                    made[place * block : (place + 1) * block, third * cut : (third + 1) * cut]
                )
    grad = mm(packed[...], w_qkv[...], NT)
    scale = lax.rsqrt(jnp.mean(x * x, axis=-1, keepdims=True) + epsilon)
    gain_back = jnp.sum(grad * x * scale, axis=0, keepdims=True)
    small_out[...] = jnp.concatenate(
        [router_term[...], gain_term[...], gain_back, jnp.zeros((6, width), F32)], axis=0
    )
    grad = grad * gain[...].reshape(1, width)
    grad = scale * grad - x * (scale * scale * scale) * jnp.mean(grad * x, axis=-1, keepdims=True)
    tokens_out[...] += grad
    for copy in far + cot_sends:
        copy.wait()


def late(layout, combine_ins, back_ins, held, far_cot, far_target, rows_in, shares):
    tokens = back_ins[4]
    rows, width = tokens.shape
    reach, peers, others = layout.reach, layout.peers, layout.outers - 1
    dma = pltpu.SemaphoreType.DMA
    pairs = HEADS // 2
    sums = Sums(layout, step_orders(layout)[:3], held, DONE_EXPERTS, DONE_LATE, True)
    blocks = (layout.experts, layout.groups)
    blocks += packed_shape(width // layout.groups, width // layout.experts)
    far_low, far_high = far_parts(layout)[1]
    return pl.pallas_call(
        functools.partial(late_kernel, layout, sums),
        out_shape=[
            jax.ShapeDtypeStruct((rows, width), BF16),
            jax.ShapeDtypeStruct((rows, width), F32),
            jax.ShapeDtypeStruct(blocks, BF16),
            jax.ShapeDtypeStruct((3,) + blocks, BF16),
            jax.ShapeDtypeStruct((SMALL, width), F32),
            *sums.outputs(),
            jax.ShapeDtypeStruct((others,) + layout.slots(width), BF16),
            far_shape(layout, far_high - far_low, width),
            jax.ShapeDtypeStruct((others,) + shares.shape, F32),
        ],
        in_specs=[VMEM] * 6 + [ANY] + [VMEM] * 18 + [ANY, VMEM, ANY, ANY],
        out_specs=[ANY] + [VMEM] * 6 + [ANY] * 3,
        scratch_shapes=[
            pltpu.VMEM((rows, width), BF16),
            pltpu.VMEM((EXPERTS, width), F32),
            pltpu.VMEM((1, width), F32),
            pltpu.VMEM(layout.slots(width), BF16),
            pltpu.VMEM((reach, pairs, 2, rows, LANES), BF16),
            pltpu.VMEM((reach, pairs, 2, rows, LANES), BF16),
            pltpu.VMEM((pairs, 2, rows, LANES), BF16),
            pltpu.VMEM((rows, 3 * width), BF16),
            dma((reach, pairs)),
            dma((reach, pairs)),
            dma((others, peers)),
            dma((others, peers)),
            dma((others,)),
            dma,
            dma((2, others)),
            dma((2, others)),
            *sums.scratch(),
        ],
        compiler_params=pltpu.CompilerParams(
            collective_id=2, has_side_effects=True, vmem_limit_bytes=63 * MIB
        ),
        cost_estimate=pl.CostEstimate(flops=1 << 30, bytes_accessed=1 << 20, transcendentals=0),
        name="late",
    )(*combine_ins, *back_ins, *held, far_cot, far_target, rows_in, shares)


def weights_kernel(layout, sums, *refs):
    share, outers, peers = layout.share, layout.outers, layout.peers
    (
        rows_own,
        cots_own,
        shares_own,
        rows_a,
        rows_b,
        cots_far,
        shares_far,
        gate_any,
        up_any,
        down_any,
        *terms,
        qkv_terms,
        small_in,
        gate_out,
        up_out,
        down_out,
        gate_sum,
        up_sum,
        down_sum,
        proj_sum,
        qkv_sum,
        router_out,
        gain_ffn_out,
        gain_attn_out,
    ) = refs[:27]
    (
        gate_w,
        up_w,
        gate_t,
        up_t,
        down_w,
        rows_buf,
        cots_buf,
        shares_buf,
        accs,
        sends,
        down_sends,
        small_sums,
        small_takes,
        load_sems,
        piece_sems,
        send_sems,
        recv_sems,
        small_send,
        small_recv,
    ) = refs[27:46]
    rest = refs[46:]
    width = gate_w.shape[0]
    ff = gate_any.shape[2]
    span = ff // outers
    cut = ff // layout.groups
    group = lax.axis_index("group")
    mine = own_share(layout)
    begin = pl.multiple_of((group // share) * span, span)
    loads = [
        pltpu.make_async_copy(gate_any.at[mine, :, pl.ds(begin, span)], gate_w, load_sems.at[0]),
        pltpu.make_async_copy(up_any.at[mine, :, pl.ds(begin, span)], up_w, load_sems.at[1]),
        pltpu.make_async_copy(down_any.at[mine, pl.ds(begin, span), :], down_w, load_sems.at[2]),
    ]

    def fetch(outer):
        slot = outer % 2
        if outer == 0:
            sources = [
                (rows_own, rows_buf.at[slot]),
                (cots_own, cots_buf.at[slot]),
                (shares_own, shares_buf.at[slot]),
            ]
        else:
            sources = [
                (one.at[outer - 1], rows_buf.at[slot, low:high])
                for one, (low, high) in zip((rows_a, rows_b), far_parts(layout))
            ]
            sources.append((cots_far.at[outer - 1], cots_buf.at[slot]))
            sources.append((shares_far.at[outer - 1], shares_buf.at[slot]))
        return [
            pltpu.make_async_copy(source, target, piece_sems.at[slot, number])
            for number, (source, target) in enumerate(sources)
        ]

    for copy in loads + fetch(0):
        copy.start()
    meet(layout)

    third = qkv_sum.shape[1] // 3
    chains = sums.chains([*terms, *[qkv_terms.at[n] for n in range(3)]], (), rest)
    results = [(one, 0, one.shape[1]) for one in (gate_sum, up_sum, down_sum, proj_sum)]
    results += [(qkv_sum, n * third, third) for n in range(3)]
    steps = [("expert", 1 << n) for n in range(layout.experts.bit_length() - 1)]
    steps += [("group", 1 << n) for n in range(layout.groups.bit_length() - 1)]
    levels = len(steps)
    small_sums[0] = small_in[...]

    def small_copy(level):
        axis, bit = steps[level]
        return pltpu.make_async_remote_copy(
            src_ref=small_sums.at[level],
            dst_ref=small_takes.at[level],
            send_sem=small_send.at[level],
            recv_sem=small_recv.at[level],
            device_id={axis: flipped(lax.axis_index(axis), bit)},
            device_id_type=MESH,
        )

    reached = [0] * len(chains)

    def advance(*numbers):
        for number in numbers:
            chain, level = chains[number], reached[number]
            if 0 < level <= len(chain):
                chain[level - 1].add(results[number] if level == len(chain) else None)
            if level < len(chain):
                chain[level].start()
            reached[number] += 1

    def advance_small(level):
        if level:
            small_copy(level - 1).wait()
            made = small_sums[level - 1] + small_takes[level - 1]
            if level < levels:
                small_sums[level] = made
            else:
                router_out[...] = made[:EXPERTS]
                gain_ffn_out[...] = made[EXPERTS : EXPERTS + 1].reshape(width)
                gain_attn_out[...] = made[EXPERTS + 1 : EXPERTS + 2].reshape(width)
        if level < levels:
            small_copy(level).start()

    attention, shared = (3, 4, 5, 6), (1, 2, 0)
    points = share * outers
    marks = {
        0: [attention],
        3 * points // 8: [attention],
        5 * points // 8: [shared],
        6 * points // 8: [attention],
        points - 1: [shared, attention],
    }
    small_level = 1
    advance(*attention, *shared)
    advance_small(0)

    for copy in loads:
        copy.wait()
    gate_t[...] = jnp.transpose(gate_w[...])
    up_t[...] = jnp.transpose(up_w[...])
    experts = layout.experts
    count = max(8 // experts, 1)
    blocks = share // count

    def add(slot, chunk, block):
        parts = pl.ds(block * count, count)
        n = rows_buf[slot, parts].reshape(count * experts * CAP, width)
        grad = cots_buf[slot, parts].reshape(count * experts * CAP, width)
        base = pl.multiple_of(chunk * cut, cut)
        gate_pre = mm(gate_t[pl.ds(base, cut), :], n, NT)
        up_pre = mm(up_t[pl.ds(base, cut), :], n, NT)
        grad_act = mm(down_w[pl.ds(base, cut), :], grad, NT)
        silu, slope = silu_parts(gate_pre)
        act = (silu * up_pre).astype(BF16)
        grad_gate = (grad_act * up_pre * slope).astype(BF16)
        grad_up = (grad_act * silu).astype(BF16)
        accs[0] += mm(grad_gate, n)
        accs[1] += mm(grad_up, n)
        accs[2] += mm(act, grad)

    copies = []
    turns = [*range(share - 1, 0, -1), 0]
    resident = outers <= 2
    for place, turn in enumerate(turns):
        owner = flipped(mine, turn)
        accs[...] = jnp.zeros_like(accs)
        for outer in range(outers):
            slot = outer % 2
            if place == 0 or not resident:
                if place or outer:
                    for copy in fetch(outer):
                        copy.start()
                for copy in fetch(outer):
                    copy.wait()

                def scale(number, carry, slot=slot):
                    at = slot, number // experts, number % experts
                    column = share_column(shares_buf[at + (slice(0, 1), slice(0, CAP))])
                    cots_buf[at] = (cots_buf[at].astype(F32) * column).astype(BF16)
                    return carry

                lax.fori_loop(0, peers, scale, 0)

            def step(number, carry, slot=slot, owner=owner):
                add(slot, owner, number)
                return carry

            lax.fori_loop(0, blocks, step, 0)
            if place * outers + outer in marks:
                for numbers in marks[place * outers + outer]:
                    advance(*numbers)
                if small_level <= levels:
                    advance_small(small_level)
                    small_level += 1
        for which, target in enumerate((gate_out, up_out, down_out)):
            made = accs[which]
            if which < 2:
                made = jnp.transpose(made)
                source = sends.at[turn, which]
            else:
                source = down_sends.at[turn]
            source[...] = made.astype(BF16)
            if turn:
                device = {"group": flipped(group, turn)}
                sems = send_sems.at[turn, which], recv_sems.at[turn, which]
                copies.append(remote(source, target.at[mine], *sems, device))
            else:
                copies.append(
                    pltpu.make_async_copy(source, target.at[mine], send_sems.at[turn, which])
                )
            copies[-1].start()
    while any(at <= len(chain) for at, chain in zip(reached, chains)) or small_level <= levels:
        advance(*attention)
        if small_level <= levels:
            advance_small(small_level)
            small_level += 1
        advance(*shared)
    for copy in copies:
        copy.wait()


def weights(layout, own, rows_far, cots_far, shares_far, expert_weights, held, terms, small):
    share, outers = layout.share, layout.outers
    experts, width, ff = expert_weights[0].shape
    span = ff // outers
    cut = ff // layout.groups
    dma = pltpu.SemaphoreType.DMA
    levels = layout.experts.bit_length() + layout.groups.bit_length() - 2
    proj_terms, qkv_terms = terms
    thirds = [jax.ShapeDtypeStruct(qkv_terms.shape[1:], BF16)] * 3
    sums = Sums(
        layout,
        step_orders(layout),
        (*held, proj_terms, *thirds),
        DONE_LATE + DONE_NONE,
        (levels,) * 7,
        False,
    )
    wide = width // layout.groups, ff // layout.experts
    tall = cut, width // layout.experts
    narrow = width // layout.groups, width // layout.experts
    results = wide, wide, tall, narrow, (narrow[0], 3 * narrow[1])
    return pl.pallas_call(
        functools.partial(weights_kernel, layout, sums),
        out_shape=[
            jax.ShapeDtypeStruct((experts, width, cut), BF16),
            jax.ShapeDtypeStruct((experts, width, cut), BF16),
            jax.ShapeDtypeStruct((experts, cut, width), BF16),
            *[jax.ShapeDtypeStruct(shape, F32) for shape in results],
            jax.ShapeDtypeStruct((EXPERTS, width), F32),
            jax.ShapeDtypeStruct((width,), F32),
            jax.ShapeDtypeStruct((width,), F32),
        ],
        in_specs=[ANY] * 10 + [VMEM] * 6,
        out_specs=[ANY] * 3 + [VMEM] * 8,
        scratch_shapes=[
            pltpu.VMEM((width, span), BF16),
            pltpu.VMEM((width, span), BF16),
            pltpu.VMEM((span, width), BF16),
            pltpu.VMEM((span, width), BF16),
            pltpu.VMEM((span, width), BF16),
            pltpu.VMEM((2,) + layout.slots(width), BF16),
            pltpu.VMEM((2,) + layout.slots(width), BF16),
            pltpu.VMEM((2, share, layout.experts, 8, LANES), F32),
            pltpu.VMEM((3, cut, width), F32),
            pltpu.VMEM((share, 2, width, cut), BF16),
            pltpu.VMEM((share, cut, width), BF16),
            pltpu.VMEM((levels, SMALL, width), F32),
            pltpu.VMEM((levels, SMALL, width), F32),
            dma((3,)),
            dma((2, 5)),
            dma((share, 3)),
            dma((share, 3)),
            dma((levels,)),
            dma((levels,)),
            *sums.scratch(),
        ],
        compiler_params=pltpu.CompilerParams(
            collective_id=3, has_side_effects=True, vmem_limit_bytes=60 * MIB
        ),
        cost_estimate=pl.CostEstimate(flops=1 << 30, bytes_accessed=1 << 20, transcendentals=0),
        name="weights",
    )(*own, *rows_far, cots_far, shares_far, *expert_weights, *held, *terms, small)


def local(
    tokens,
    gain_attn,
    w_qkv,
    w_out,
    gain_ffn,
    w_router,
    expert_gate,
    expert_up,
    expert_down,
    dense_gate,
    dense_up,
    dense_down,
    expert_ids,
    segments,
    cotangent,
):
    rows, width = tokens.shape
    layout = Layout(lax.axis_size("group"), lax.axis_size("expert"), rows)
    expert = lax.axis_index("expert")
    ids_row, w_router_t = jnp.transpose(expert_ids), jnp.transpose(w_router)
    places = (expert * rows + jnp.arange(rows, dtype=jnp.int32)).astype(F32)
    lane = jnp.arange(LANES)
    power = (lane % (HEAD // 2)).astype(F32) / (HEAD // 2)
    angles = places[:, None] * (10000.0 ** (-power))[None]
    cosine = jnp.cos(angles)
    sine = jnp.sin(angles) * jnp.where(lane % HEAD < HEAD // 2, -1.0, 1.0)[None]

    (
        q,
        kv,
        att_t,
        lse,
        bias,
        target,
        hidden,
        low,
        mixed,
        grad_low,
        gate_terms,
        up_terms,
        down_terms,
        cots,
        quad_cots,
        rows_in,
        shares,
        far_cot,
        far_target,
    ) = first(
        layout,
        tokens,
        gain_attn,
        w_qkv,
        cosine,
        sine,
        ids_row,
        segments,
        cotangent,
        w_out,
        gain_ffn,
        w_router_t,
        dense_gate,
        dense_up,
        dense_down,
    )
    came_back, grad_back, quad_rows, quad_shares, rows_a, gate_terms = run_experts(
        layout,
        rows_in,
        cots,
        shares,
        expert_gate,
        expert_up,
        expert_down,
        (gate_terms, up_terms, down_terms),
    )
    mixed_out, grad_tokens, proj_terms, qkv_terms, small, gate_terms, up_terms, cots_far, rows_b, shares_far = late(
        layout,
        (
            came_back,
            grad_back,
            target,
            ids_row,
            hidden,
            mixed,
            grad_low,
            low,
            cotangent,
            gain_ffn,
            w_router_t,
            w_out,
            att_t,
        ),
        (q, kv, bias, lse, tokens, gain_attn, w_qkv, cosine, sine),
        (gate_terms, up_terms, down_terms),
        far_cot,
        far_target,
        quad_rows,
        quad_shares,
    )
    gate_w, up_w, down_w, gate_sum, up_sum, down_sum, proj_sum, qkv_sum, *small = weights(
        layout,
        (quad_rows, quad_cots, quad_shares),
        (rows_a, rows_b),
        cots_far,
        shares_far,
        (expert_gate, expert_up, expert_down),
        (gate_terms, up_terms, down_terms),
        (proj_terms, qkv_terms),
        small,
    )
    return (
        mixed_out,
        grad_tokens,
        small[2],
        qkv_sum,
        proj_sum,
        small[1],
        jnp.transpose(small[0]),
        gate_w.astype(F32),
        up_w.astype(F32),
        down_w.astype(F32),
        gate_sum,
        up_sum,
        down_sum,
    )


def solution(mesh):
    in_specs = (
        P(("group", "expert"), None),
        P(),
        P(),
        P(),
        P(),
        P(),
        P("expert", None, None),
        P("expert", None, None),
        P("expert", None, None),
        P(),
        P(),
        P(),
        P(("group", "expert"), None),
        P(("group", "expert")),
        P(("group", "expert"), None),
    )
    out_specs = (
        P(("group", "expert"), None),
        P(("group", "expert"), None),
        P(),
        P("group", "expert"),
        P("group", "expert"),
        P(),
        P(),
        P("expert", None, "group"),
        P("expert", None, "group"),
        P("expert", "group", None),
        P("group", "expert"),
        P("group", "expert"),
        P("group", "expert"),
    )
    return jax.shard_map(local, mesh=mesh, in_specs=in_specs, out_specs=out_specs, check_vma=False)
```

```python
import functools

import jax
import jax.numpy as jnp
from jax import lax
from jax.experimental import pallas as pl
from jax.experimental.pallas import tpu as pltpu
from jax.sharding import PartitionSpec as P

HEADS = 12
HEAD = 64
EXPERTS = 16
WINDOW = 1024
CAP = 80
QUARTERS = 4
LANES = 128
TILE = 256
SMALL = EXPERTS + 8
NEG = -1e30

epsilon = 1e-06
F32 = jnp.float32
BF16 = jnp.bfloat16
MESH = pl.DeviceIdType.MESH
VMEM = pl.BlockSpec(memory_space=pltpu.VMEM)
ANY = pl.BlockSpec(memory_space=pl.ANY)
MIB = 1 << 20


def dims(spec):
    left, right = spec
    return (((left,), (right,)), ((), ()))


NN = dims((1, 0))
NT = dims((1, 1))
TN = dims((0, 0))


def mm(a, b, how=NN):
    return lax.dot_general(a, b, how, preferred_element_type=F32)


def flipped(x, mask):
    bit = 1
    while bit <= mask:
        if mask & bit:
            x = x + bit * (1 - 2 * ((x // bit) % 2))
        bit *= 2
    return x


class Layout:
    def __init__(self, groups, experts, rows):
        self.groups, self.experts, self.rows = groups, experts, rows
        self.share = EXPERTS // experts
        self.peers = self.share * experts
        self.outers = groups // self.share
        per_quarter = max(experts // QUARTERS, 1)
        self.reach = min((WINDOW - 1) // rows + 1, 2 * per_quarter - 1)

    def far(self, number):
        return {"group": flipped(lax.axis_index("group"), number * self.share)}

    def peer(self, number):
        group, expert = lax.axis_index("group"), lax.axis_index("expert")
        return {
            "group": flipped(group, number // self.experts),
            "expert": flipped(expert, number % self.experts),
        }

    def slots(self, width):
        return (self.share, self.experts, CAP, width)


def meet(layout):
    barrier = pltpu.get_barrier_semaphore()
    for number in range(1, layout.peers):
        pl.semaphore_signal(barrier, inc=1, device_id=layout.peer(number), device_id_type=MESH)
    for number in range(1, layout.outers):
        pl.semaphore_signal(barrier, inc=1, device_id=layout.far(number), device_id_type=MESH)
    pl.semaphore_wait(barrier, layout.peers + layout.outers - 2)


def remote(source, target, send_sem, recv_sem, device):
    return pltpu.make_async_remote_copy(
        src_ref=source,
        dst_ref=target,
        send_sem=send_sem,
        recv_sem=recv_sem,
        device_id=device,
        device_id_type=MESH,
    )


def to_peers(layout, source, target, send_sems, recv_sems):
    return [
        remote(
            source.at[divmod(number, layout.experts)],
            target.at[divmod(number, layout.experts)],
            send_sems.at[number],
            recv_sems.at[number],
            layout.peer(number),
        )
        for number in range(1, layout.peers)
    ]


def to_row(layout, source, target, send_sems, recv_sems):
    expert = lax.axis_index("expert")
    return [
        remote(
            source.at[:, bits],
            target.at[:, bits],
            send_sems.at[bits],
            recv_sems.at[bits],
            {"expert": flipped(expert, bits)},
        )
        for bits in range(1, layout.experts)
    ]


def to_quad(layout, source, target, send_sems, recv_sems):
    group = lax.axis_index("group")
    return [
        remote(
            source.at[bits],
            target.at[bits],
            send_sems.at[bits],
            recv_sems.at[bits],
            {"group": flipped(group, bits)},
        )
        for bits in range(1, layout.share)
    ]


def to_far(layout, source, target, low, high, send_sems, recv_sems):
    return [
        remote(
            source.at[low:high],
            target.at[number - 1],
            send_sems.at[number - 1],
            recv_sems.at[number - 1],
            layout.far(number),
        )
        for number in range(1, layout.outers)
    ]


def far_shape(layout, count, width):
    shape = (layout.outers - 1, count) + layout.slots(width)[1:]
    return jax.ShapeDtypeStruct(shape, BF16)


def bit_of(axis, bit):
    return (lax.axis_index(axis) // bit) % 2


def trade_sems(copies):
    return [pltpu.SemaphoreType.DMA((copies,)), pltpu.SemaphoreType.DMA((copies,))]


def packed_shape(rows, columns):
    if columns % LANES == LANES // 2 and rows % 32 == 0:
        return rows * columns // LANES, LANES
    return rows, columns


def pack(block):
    rows, columns = block.shape
    if packed_shape(rows, columns) == block.shape:
        return block
    whole = columns // LANES * LANES
    parts = [block[:, low : low + LANES] for low in range(0, whole, LANES)]
    parts.append(jnp.concatenate([block[: rows // 2, whole:], block[rows // 2 :, whole:]], axis=1))
    return jnp.concatenate(parts, axis=0)


def unpack(made, target, low, columns):
    rows = target.shape[0]
    if made.shape == (rows, columns):
        target[:, low : low + columns] = made
        return
    count = columns // LANES
    for part in range(count):
        target[:, low + part * LANES : low + (part + 1) * LANES] = made[
            part * rows : (part + 1) * rows
        ]
    at = slice(low + count * LANES, low + columns)
    target[: rows // 2, at] = made[count * rows :, : LANES // 2]
    target[rows // 2 :, at] = made[count * rows :, LANES // 2 :]


class Halving:
    def __init__(self, step, held, taken, send_sems, recv_sems):
        axis, bit, below = step
        odd = (lax.axis_index(axis) // bit) % 2
        self.held, self.taken = held, taken
        unit = 1 << below

        def place(number, value):
            return number // unit * (2 * unit) + value * unit + number % unit

        if axis == "expert":
            places = [
                ((place(n, 1 - odd),), (place(n, odd),), (n,)) for n in range(taken.shape[0])
            ]
        else:
            places = [
                ((m, place(n, 1 - odd)), (m, place(n, odd)), (m, n))
                for m in range(taken.shape[0])
                for n in range(taken.shape[1])
            ]
        self.places = [place[1:] for place in places]
        self.copies = [
            remote(
                held.at[theirs],
                taken.at[target],
                send_sems.at[number],
                recv_sems.at[number],
                {axis: flipped(lax.axis_index(axis), bit)},
            )
            for number, (theirs, _, target) in enumerate(places)
        ]

    def start(self):
        for copy in self.copies:
            copy.start()

    def add(self, last=None):
        for (mine, target), copy in zip(self.places, self.copies):
            copy.wait()
            if last is not None:
                mine, target = (*mine, 0)[:2], (*target, 0)[:2]
                unpack(self.taken[target].astype(F32) + self.held[mine].astype(F32), *last)
            elif len(target) == 2:
                self.taken[target] = (
                    self.taken[target].astype(F32) + self.held[mine].astype(F32)
                ).astype(BF16)
            else:

                def one(number, carry, mine=mine, target=target):
                    self.taken[target[0], number] = (
                        self.taken[target[0], number].astype(F32)
                        + self.held[mine[0], number].astype(F32)
                    ).astype(BF16)
                    return carry

                lax.fori_loop(0, self.taken.shape[1], one, 0)


def step_orders(layout):
    core, y, *experts = [("expert", 1 << n) for n in range(layout.experts.bit_length() - 1)]
    x, z, *groups = [("group", 1 << n) for n in range(layout.groups.bit_length() - 1)]
    rest = experts + groups
    return (
        [core, x, z, y] + rest,
        [core, x, y, z] + rest,
        [core, y, x, z] + rest,
        [core, y, x, z] + rest,
        [core, x, y, z] + rest,
        [core, y, z, x] + rest,
        [core, z, x, y] + rest,
    )


DONE_FIRST = (1, 1, 1)
DONE_EXPERTS = (2, 1, 1)
DONE_LATE = (3, 2, 1)
DONE_NONE = (0, 0, 0, 0)


def halving_plan(layout, orders, shapes, first, last):
    plan = []
    for steps, shape, low, high in zip(orders, shapes, first, last):
        mine, left = [], sorted(steps, key=lambda step: step[1])
        for number, step in enumerate(steps[:high]):
            axis, bit = step
            below = sum(1 for other in left if other[0] == axis and other[1] < bit)
            left.remove(step)
            if number < low:
                continue
            experts, groups = shape[:2]
            if axis == "expert":
                shape, copies = (experts // 2, groups) + shape[2:], experts // 2
            else:
                shape, copies = (experts, groups // 2) + shape[2:], experts * groups // 2
            mine.append(((axis, bit, below), shape, copies))
        plan.append(mine)
    return plan


def rope_turn(x, cosine, sine):
    parts = []
    for begin in range(0, x.shape[1], LANES):
        part = x[:, begin : begin + LANES]
        lane = lax.broadcasted_iota(jnp.int32, part.shape, 1)
        other = jnp.where(
            lane % HEAD < HEAD // 2,
            pltpu.roll(part, LANES - HEAD // 2, 1),
            pltpu.roll(part, HEAD // 2, 1),
        )
        parts.append(part * cosine + other * sine)
    return jnp.concatenate(parts, axis=1)


def normed(x, gain):
    return x * lax.rsqrt(jnp.mean(x * x, axis=-1, keepdims=True) + epsilon) * gain


def other_bits(x, mask, count):
    made, bit = 0, 1
    while bit < count:
        mine, theirs = (x // bit) % 2, (mask // bit) % 2
        made = made + bit * (mine + theirs - 2 * mine * theirs)
        bit *= 2
    return made


def slot_rows(ids_row, rows):
    labels = lax.broadcasted_iota(jnp.int32, (EXPERTS, rows), 0)
    first, second = labels == ids_row[0:1], labels == ids_row[1:2]
    both = jnp.where(first | second, 1.0, 0.0).astype(BF16)
    earlier_t = lax.broadcasted_iota(jnp.int32, (rows, rows), 0)
    later_t = lax.broadcasted_iota(jnp.int32, (rows, rows), 1)
    earlier = mm(both, jnp.where(earlier_t < later_t, 1.0, 0.0).astype(BF16))
    targets = []
    for mask, ids in ((first, ids_row[0:1]), (second, ids_row[1:2])):
        slot = jnp.sum(jnp.where(mask, earlier, 0.0), axis=0, keepdims=True)
        targets.append(jnp.where(slot < CAP, ids.astype(F32) * CAP + slot, -1.0))
    return targets


def slot_masks(number, target, rows):
    slots = (number * CAP + lax.broadcasted_iota(jnp.int32, (CAP, rows), 0)).astype(F32)
    return slots == target[0:1], slots == target[1:2]


def gather_slots(layout, target, source, made):
    rows = source.shape[0]
    for number in range(layout.peers):
        first, second = slot_masks(number, target, rows)
        chosen = jnp.where(first | second, 1.0, 0.0).astype(BF16)
        made[divmod(number, layout.experts)] = mm(chosen, source[...]).astype(BF16)


def first_kernel(
    layout,
    tokens,
    gain_attn,
    w_qkv,
    cosine,
    sine,
    ids_row,
    seg_row,
    cot,
    w_out,
    gain_ffn,
    w_router_t,
    dense_gate_any,
    dense_up_any,
    dense_down_any,
    q_out,
    kv_out,
    att_t_out,
    lse_out,
    bias_out,
    target_out,
    hidden_out,
    low_out,
    mixed_out,
    grad_out,
    gate_out,
    up_out,
    down_out,
    cots_out,
    quad_out,
    rows_out,
    shares_out,
    far_cot_out,
    far_target_out,
    normed_low,
    send_cot,
    seg_all,
    acc,
    top,
    total,
    att,
    send_rows,
    send_shares,
    dense_gate,
    dense_up,
    dense_down,
    gate_held,
    up_held,
    down_held,
    load_sems,
    kv_send,
    kv_recv,
    seg_send,
    seg_recv,
    cot_send,
    cot_recv,
    quad_send,
    quad_recv,
    row_send,
    row_recv,
    share_send,
    share_recv,
    own_sems,
    far_send,
    far_recv,
    half_send,
    half_recv,
):
    rows, width = tokens.shape
    reach, experts = layout.reach, layout.experts
    ff = dense_gate.shape[1]
    e = lax.axis_index("expert")
    loads = [
        pltpu.make_async_copy(source, target, load_sems.at[number])
        for number, (source, target) in enumerate(
            ((dense_gate_any, dense_gate), (dense_up_any, dense_up), (dense_down_any, dense_down))
        )
    ]
    for copy in loads:
        copy.start()
    meet(layout)

    share = layout.share
    ids = ids_row[...]
    relative = other_bits(ids % share, own_share(layout), share) * experts
    targets = slot_rows(relative + other_bits(ids // share, e, experts), rows)
    target_out[0:1] = targets[0]
    target_out[1:2] = targets[1]
    target_out[2:8] = jnp.full((6, rows), -1.0, F32)
    far = [
        remote(
            source,
            target.at[number - 1],
            far_send.at[place, number - 1],
            far_recv.at[place, number - 1],
            layout.far(number),
        )
        for number in range(1, layout.outers)
        for place, (source, target) in enumerate(((cot, far_cot_out), (target_out, far_target_out)))
    ]
    for copy in far:
        copy.start()
    gather_slots(layout, target_out[...], cot, send_cot)
    cot_sends = to_row(layout, send_cot, cots_out, cot_send, cot_recv)
    own_cot = pltpu.make_async_copy(send_cot.at[:, 0], cots_out.at[:, 0], own_sems.at[0])
    own_cot.start()
    early = experts // 2
    for copy in cot_sends[:early]:
        copy.start()

    x = tokens[...].astype(F32)
    normed_low[...] = normed(x, gain_attn[...].reshape(1, width)).astype(BF16)
    seg_all[0] = jnp.broadcast_to(seg_row[...].astype(F32).reshape(1, rows), (8, rows))

    def project(step, carry):
        for part in range(3):
            columns = pl.ds(pl.multiple_of(part * width + step * TILE, TILE), TILE)
            made = mm(normed_low[...], w_qkv[:, columns])
            columns = pl.ds(pl.multiple_of(step * TILE, TILE), TILE)
            if part == 0:
                made = rope_turn(made, cosine[...], sine[...]) * HEAD ** (-0.5)
                q_out[:, columns] = made.astype(BF16)
            elif part == 1:
                made = rope_turn(made, cosine[...], sine[...])
                kv_out[0, :, columns] = made.astype(BF16)
            else:
                columns = pl.ds(pl.multiple_of(width + step * TILE, TILE), TILE)
                kv_out[0, :, columns] = made.astype(BF16)
        return carry

    lax.fori_loop(0, width // TILE, project, 0)

    halos = []
    for distance in range(1, reach + 1):
        to = {"expert": lax.rem(e + distance, experts)}
        halos.append(
            [
                pltpu.make_async_remote_copy(
                    src_ref=source.at[0],
                    dst_ref=source.at[distance],
                    send_sem=sems[0].at[distance],
                    recv_sem=sems[1].at[distance],
                    device_id=to,
                    device_id_type=MESH,
                )
                for source, sems in (
                    (kv_out, (kv_send, kv_recv)),
                    (seg_all, (seg_send, seg_recv)),
                )
            ]
        )
        for copy in halos[-1]:
            copy.start()

    lane = lax.broadcasted_iota(jnp.int32, (rows, LANES), 1)
    for distance in range(reach + 1):
        if distance:
            for copy in halos[distance - 1]:
                copy.wait()
        if distance == reach:
            for copy in cot_sends[early:]:
                copy.start()
        seg_col = jnp.transpose(jnp.broadcast_to(seg_all[distance, 0:1], (LANES, rows)))[:, 0:1]
        key_no = lax.broadcasted_iota(jnp.int32, (rows, rows), 0) - distance * rows
        offset = lax.broadcasted_iota(jnp.int32, (rows, rows), 1) - key_no
        allowed = (
            (offset >= 0)
            & (offset < WINDOW)
            & (key_no + e * rows >= 0)
            & (seg_col == seg_all[0, 0:1])
        )
        bias_out[distance] = jnp.where(allowed, 0.0, NEG).astype(BF16)

        def attend(pair, carry, distance=distance):
            columns = pl.ds(pl.multiple_of(pair * LANES, LANES), LANES)
            value_columns = pl.ds(pl.multiple_of(width + pair * LANES, LANES), LANES)
            queries = q_out[:, columns]
            keys = kv_out[distance, :, columns]
            values_t = jnp.transpose(kv_out[distance, :, value_columns])
            for inner in range(2):
                head = pair * 2 + inner
                mine = jnp.where((lane // HEAD) == inner, queries, jnp.zeros_like(queries))
                value_t = values_t[inner * HEAD : (inner + 1) * HEAD]
                out_rows = pl.ds(pl.multiple_of(head * HEAD, HEAD), HEAD)
                blocks = (
                    [(slice(0, rows // 2), rows // 2), (slice(rows // 2, rows), rows)]
                    if distance == 0
                    else [(slice(0, rows), rows)]
                )
                for q_cut, key_count in blocks:
                    scores = mm(keys[:key_count], mine[q_cut], NT)
                    scores = scores + bias_out[distance, :key_count, q_cut].astype(F32)
                    peak = jnp.max(scores, axis=0, keepdims=True)
                    if distance:
                        before = top[pl.ds(head, 1), q_cut]
                        peak = jnp.maximum(before, peak)
                    weights = jnp.exp(scores - peak)
                    amount = jnp.sum(weights, axis=0, keepdims=True)
                    part = mm(value_t[:, :key_count], weights.astype(BF16))
                    if distance:
                        shrink = jnp.exp(before - peak)
                        amount = amount + total[pl.ds(head, 1), q_cut] * shrink
                        part = part + acc[out_rows, q_cut] * shrink
                    top[pl.ds(head, 1), q_cut] = peak
                    total[pl.ds(head, 1), q_cut] = amount
                    acc[out_rows, q_cut] = part
            return carry

        lax.fori_loop(0, HEADS // 2, attend, 0)

    lse_out[...] = top[...] + jnp.log(total[...])

    def finish(pair, carry):
        out_rows = pl.ds(pl.multiple_of(pair * LANES, LANES), LANES)
        scale = jnp.concatenate(
            [
                jnp.broadcast_to(1.0 / total[pl.ds(pair * 2 + inner, 1), :], (HEAD, rows))
                for inner in range(2)
            ],
            axis=0,
        )
        made = acc[out_rows, :] * scale
        att_t_out[out_rows, :] = made.astype(BF16)
        att[:, out_rows] = jnp.transpose(made).astype(BF16)
        return carry

    lax.fori_loop(0, HEADS // 2, finish, 0)

    hidden_out[...] = tokens[...].astype(F32) + mm(att[...], w_out[...])
    low = normed(hidden_out[...], gain_ffn[...].reshape(1, width)).astype(BF16)
    low_out[...] = low
    logits = mm(w_router_t[...], low, NT)
    route = jnp.exp(logits - jnp.max(logits, axis=0, keepdims=True))
    route = route / jnp.sum(route, axis=0, keepdims=True)
    labels = lax.broadcasted_iota(jnp.int32, (EXPERTS, rows), 0)
    picked = [
        jnp.sum(jnp.where(labels == ids_row[k : k + 1], route, 0.0), axis=0, keepdims=True)
        for k in range(2)
    ]
    both = picked[0] + picked[1]
    shares = []
    for k in range(2):
        parts = split3(picked[k] / both)
        shares.append(
            jnp.concatenate(
                [part.astype(F32) for part in parts] + [jnp.zeros((5, rows), F32)], axis=0
            ).astype(BF16)
        )
    send_shares[...] = jnp.zeros_like(send_shares)
    for number in range(layout.peers):
        first, second = slot_masks(number, target_out[...], rows)
        first = jnp.where(first, 1.0, 0.0).astype(BF16)
        second = jnp.where(second, 1.0, 0.0).astype(BF16)
        place = divmod(number, experts)
        send_rows[place] = mm(first + second, low).astype(BF16)
        share = mm(shares[0], first, NT) + mm(shares[1], second, NT)
        share = jnp.sum(share, axis=0, keepdims=True)
        send_shares[place + (slice(None), slice(0, CAP))] = jnp.broadcast_to(share, (8, CAP))
    sends = to_row(layout, send_rows, rows_out, row_send, row_recv)
    sends += to_row(layout, send_shares, shares_out, share_send, share_recv)
    for source, target, sem in (
        (send_rows, rows_out, own_sems.at[1]),
        (send_shares, shares_out, own_sems.at[2]),
    ):
        sends.append(pltpu.make_async_copy(source.at[:, 0], target.at[:, 0], sem))
    for copy in reversed(sends):
        copy.start()
    own_cot.wait()
    for copy in cot_sends:
        copy.wait()
    sends += to_quad(layout, cots_out, quad_out, quad_send, quad_recv)
    sends.append(pltpu.make_async_copy(cots_out.at[0], quad_out.at[0], own_sems.at[3]))
    for copy in sends[-layout.share :]:
        copy.start()

    for copy in loads:
        copy.wait()
    mixed_out[...] = hidden_out[...]
    grad_out[...] = jnp.zeros_like(grad_out)
    part_width = ff // experts
    per_part = part_width // TILE
    half = experts // 2
    odd = bit_of("expert", 1)
    halvings = [
        Halving(("expert", 1, 0), held, taken, half_send.at[number], half_recv.at[number])
        for number, (held, taken) in enumerate(
            ((gate_held, gate_out), (up_held, up_out), (down_held, down_out))
        )
    ]

    def branch(step, carry):
        place = step // per_part
        part = 2 * (place % half) + (odd + 1 + place // half) % 2
        columns = pl.ds(pl.multiple_of(part * part_width + (step % per_part) * TILE, TILE), TILE)
        gate_w, up_w, down_w = dense_gate[:, columns], dense_up[:, columns], dense_down[columns, :]
        gate_pre = mm(low_out[...], gate_w)
        up_pre = mm(low_out[...], up_w)
        grad_act = mm(cot[...], down_w, NT)
        silu, slope = silu_parts(gate_pre)
        act = (silu * up_pre).astype(BF16)
        grad_gate = (grad_act * up_pre * slope).astype(BF16)
        grad_up = (grad_act * silu).astype(BF16)
        mixed_out[...] += mm(act, down_w)
        grad_out[...] += mm(grad_gate, gate_w, NT) + mm(grad_up, up_w, NT)
        inside = pl.ds(pl.multiple_of((step % per_part) * TILE, TILE), TILE)
        for made, held in (
            (mm(low_out[...], grad_gate, TN), gate_held),
            (mm(low_out[...], grad_up, TN), up_held),
        ):
            made = made.astype(BF16)
            block = held.shape[2]
            for place in range(held.shape[1]):
                held[part, place, :, inside] = made[place * block : (place + 1) * block]
        made = mm(act, cot[...], TN).astype(BF16)
        block = ff // layout.groups
        cut = width // experts
        low_row = part * part_width + (step % per_part) * TILE
        for inner in range(0, TILE, block):
            for other in range(experts):
                down_held[other, (low_row + inner) // block] = pack(
                    made[inner : inner + block, other * cut : (other + 1) * cut]
                )
        return carry

    lax.fori_loop(0, ff // (2 * TILE), branch, 0)
    for halving in halvings[:2]:
        halving.start()
    lax.fori_loop(ff // (2 * TILE), ff // TILE, branch, 0)
    halvings[2].start()
    for halving in halvings:
        halving.add()
    for copy in far + sends:
        copy.wait()


def first(layout, tokens, gain_attn, w_qkv, cosine, sine, ids_row, seg_row, cot, w_out, gain_ffn, w_router_t, dense_gate, dense_up, dense_down):
    rows, width = tokens.shape
    ff = dense_gate.shape[1]
    reach, experts, groups = layout.reach, layout.experts, layout.groups
    half = experts // 2
    others = layout.outers - 1
    dma = pltpu.SemaphoreType.DMA
    wide = (groups, width // groups, ff // experts)
    tall = (groups,) + packed_shape(ff // groups, width // experts)
    return pl.pallas_call(
        functools.partial(first_kernel, layout),
        out_shape=[
            jax.ShapeDtypeStruct((rows, width), BF16),
            jax.ShapeDtypeStruct((reach + 1, rows, 2 * width), BF16),
            jax.ShapeDtypeStruct((width, rows), BF16),
            jax.ShapeDtypeStruct((EXPERTS, rows), F32),
            jax.ShapeDtypeStruct((reach + 1, rows, rows), BF16),
            jax.ShapeDtypeStruct((8, rows), F32),
            jax.ShapeDtypeStruct((rows, width), F32),
            jax.ShapeDtypeStruct((rows, width), BF16),
            jax.ShapeDtypeStruct((rows, width), F32),
            jax.ShapeDtypeStruct((rows, width), F32),
            jax.ShapeDtypeStruct((half,) + wide, BF16),
            jax.ShapeDtypeStruct((half,) + wide, BF16),
            jax.ShapeDtypeStruct((half,) + tall, BF16),
            jax.ShapeDtypeStruct(layout.slots(width), BF16),
            jax.ShapeDtypeStruct(layout.slots(width), BF16),
            jax.ShapeDtypeStruct(layout.slots(width), BF16),
            jax.ShapeDtypeStruct((layout.share, experts, 8, LANES), F32),
            jax.ShapeDtypeStruct((others, rows, width), BF16),
            jax.ShapeDtypeStruct((others, 8, rows), F32),
        ],
        in_specs=[VMEM] * 11 + [ANY] * 3,
        out_specs=[VMEM] * 13 + [ANY] * 6,
        scratch_shapes=[
            pltpu.VMEM((rows, width), BF16),
            pltpu.VMEM(layout.slots(width), BF16),
            pltpu.VMEM((reach + 1, 8, rows), F32),
            pltpu.VMEM((width, rows), F32),
            pltpu.VMEM((EXPERTS, rows), F32),
            pltpu.VMEM((EXPERTS, rows), F32),
            pltpu.VMEM((rows, width), BF16),
            pltpu.VMEM(layout.slots(width), BF16),
            pltpu.VMEM((layout.share, experts, 8, LANES), F32),
            pltpu.VMEM((width, ff), BF16),
            pltpu.VMEM((width, ff), BF16),
            pltpu.VMEM((ff, width), BF16),
            pltpu.VMEM((experts,) + wide, BF16),
            pltpu.VMEM((experts,) + wide, BF16),
            pltpu.VMEM((experts,) + tall, BF16),
            dma((3,)),
            dma((reach + 1,)),
            dma((reach + 1,)),
            dma((reach + 1,)),
            dma((reach + 1,)),
            dma((experts,)),
            dma((experts,)),
            dma((layout.share,)),
            dma((layout.share,)),
            dma((experts,)),
            dma((experts,)),
            dma((experts,)),
            dma((experts,)),
            dma((4,)),
            dma((2, others)),
            dma((2, others)),
            dma((3, half)),
            dma((3, half)),
        ],
        compiler_params=pltpu.CompilerParams(
            collective_id=0, has_side_effects=True, vmem_limit_bytes=62 * MIB
        ),
        cost_estimate=pl.CostEstimate(flops=1 << 30, bytes_accessed=1 << 20, transcendentals=0),
        name="first",
    )(tokens, gain_attn, w_qkv, cosine, sine, ids_row, seg_row, cot, w_out, gain_ffn, w_router_t, dense_gate, dense_up, dense_down)


def split3(x):
    high = x.astype(BF16)
    rest = x - high.astype(F32)
    middle = rest.astype(BF16)
    return high, middle, (rest - middle.astype(F32)).astype(BF16)


def silu_parts(gate_pre):
    gate = 1.0 / (1.0 + jnp.exp(-gate_pre))
    return gate_pre * gate, gate * (1.0 + gate_pre * (1.0 - gate))


def share_column(share_row):
    across = lax.broadcasted_iota(jnp.int32, (CAP, CAP), 1)
    down = lax.broadcasted_iota(jnp.int32, (CAP, CAP), 0)
    return jnp.sum(jnp.where(across == down, share_row, 0.0), axis=1, keepdims=True)


def own_share(layout):
    return lax.rem(lax.axis_index("group"), layout.share)


class Sums:
    def __init__(self, layout, orders, arrays, first, last, keep):
        self.plan = halving_plan(layout, orders, [one.shape for one in arrays], first, last)
        self.keep = keep

    def scratch(self):
        made = []
        for mine in self.plan:
            for number, (_, shape, copies) in enumerate(mine):
                made += trade_sems(copies)
                if not self.keep or number + 1 < len(mine):
                    made.append(pltpu.VMEM(shape, BF16))
        return made

    def outputs(self):
        return [jax.ShapeDtypeStruct(mine[-1][1], BF16) for mine in self.plan if mine]

    def chains(self, held_refs, outputs, scratch):
        outputs, scratch = list(outputs), list(scratch)
        chains = []
        for held, mine in zip(held_refs, self.plan):
            chain = []
            for number, (step, _, _) in enumerate(mine):
                sems = scratch.pop(0), scratch.pop(0)
                if not self.keep or number + 1 < len(mine):
                    taken = scratch.pop(0)
                else:
                    taken = outputs.pop(0)
                chain.append(Halving(step, held, taken, *sems))
                held = taken
            chains.append(chain)
        return chains


def experts_kernel(layout, sums, *refs):
    (
        rows_in,
        cots,
        shares,
        gate_any,
        up_any,
        down_any,
        rows_any,
        shares_any,
        gate_held,
        up_held,
        down_held,
        back_out,
        grad_back,
        quad_rows,
        quad_shares,
        far_rows,
        gate_sum,
        gate_w,
        up_w,
        down_w,
        scaled,
        acc,
        grad_acc,
        send_out,
        send_grad,
        load_sems,
        back_send,
        back_recv,
        quad_send,
        quad_recv,
        own_sems,
        far_send,
        far_recv,
        *rest,
    ) = refs
    share, experts = layout.share, layout.experts
    width, ff = gate_w.shape[1:]
    mine = own_share(layout)

    def load(place):
        slot = place % 2
        return [
            pltpu.make_async_copy(
                source.at[flipped(mine, place % share)], target.at[slot], load_sems.at[slot, number]
            )
            for number, (source, target) in enumerate(
                ((gate_any, gate_w), (up_any, up_w), (down_any, down_w))
            )
        ]

    for copy in load(0):
        copy.start()
    meet(layout)
    quads = to_quad(layout, rows_any, quad_rows, quad_send.at[0], quad_recv.at[0])
    share_quads = to_quad(layout, shares_any, quad_shares, quad_send.at[1], quad_recv.at[1])
    own = [
        pltpu.make_async_copy(rows_any.at[0], quad_rows.at[0], own_sems.at[2]),
        pltpu.make_async_copy(shares_any.at[0], quad_shares.at[0], own_sems.at[3]),
    ]
    far_low, far_high = far_parts(layout)[0]
    fars = [
        to_far(layout, rows_any, far_rows.at[:, 0:1], 0, 1, far_send.at[0], far_recv.at[0]),
        to_far(layout, quad_rows, far_rows.at[:, 1:], 1, far_high, far_send.at[1], far_recv.at[1])
        if far_high > 1
        else [],
    ]
    early = max(far_high, 2)
    for copy in quads[:early] + share_quads + own + fars[0]:
        copy.start()
    chains = sums.chains((gate_held, up_held, down_held), (gate_sum,), rest)
    chunk = 2 * TILE
    copies = list(own)
    half = experts // 2
    for place in range(2 * share):
        turn, low = place % share, half * (1 - place // share)
        for copy in load(place):
            copy.wait()
        if place + 1 < 2 * share:
            for copy in load(place + 1):
                copy.start()
        slot = place % 2
        for number in range(half):
            column = share_column(shares[turn, low + number, 0:1, :CAP])
            scaled[number] = (cots[turn, low + number].astype(F32) * column).astype(BF16)

        def step(number, carry, turn=turn, slot=slot, low=low):
            columns = pl.ds(pl.multiple_of(number * chunk, chunk), chunk)
            n = rows_in[turn, low : low + half].reshape(half * CAP, width)
            grad = scaled[...].reshape(half * CAP, width)
            gate_pre = mm(n, gate_w[slot, :, columns])
            up_pre = mm(n, up_w[slot, :, columns])
            grad_act = mm(grad, down_w[slot, columns, :], NT)
            silu, slope = silu_parts(gate_pre)
            act = (silu * up_pre).astype(BF16)
            grad_gate = (grad_act * up_pre * slope).astype(BF16)
            grad_up = (grad_act * silu).astype(BF16)
            acc[...] += mm(act, down_w[slot, columns, :])
            grad_acc[...] += mm(grad_gate, gate_w[slot, :, columns], NT) + mm(
                grad_up, up_w[slot, :, columns], NT
            )
            return carry

        acc[...] = jnp.zeros_like(acc)
        grad_acc[...] = jnp.zeros_like(grad_acc)
        lax.fori_loop(0, ff // chunk, step, 0)
        send_out[turn, low : low + half] = acc[...].astype(BF16).reshape(half, CAP, width)
        send_grad[turn, low : low + half] = grad_acc[...].astype(BF16).reshape(half, CAP, width)
        for bits in range(low, low + half):
            for which, (source, target) in enumerate(
                ((send_out, back_out), (send_grad, grad_back))
            ):
                ends = source.at[turn, bits], target.at[turn, bits]
                sem = which, turn, bits
                if bits:
                    device = {"expert": flipped(lax.axis_index("expert"), bits)}
                    copies.append(remote(*ends, back_send.at[sem], back_recv.at[sem], device))
                else:
                    copies.append(pltpu.make_async_copy(*ends, back_send.at[sem]))
                copies[-1].start()
        if place == share // 2:
            for copy in quads[: far_high - 1]:
                copy.wait()
            for copy in fars[1] + quads[early:]:
                copy.start()
            for chain in chains:
                for halving in chain[:1]:
                    halving.start()
    for chain in chains:
        for halving in chain:
            halving.add()
    for copy in copies + quads[far_high - 1 :] + share_quads + fars[0] + fars[1]:
        copy.wait()


def far_parts(layout):
    middle = max(layout.share // 2, 1)
    return (0, middle), (middle, layout.share)


def run_experts(layout, rows_in, cots, shares, expert_gate, expert_up, expert_down, held):
    share, experts, others = layout.share, layout.experts, layout.outers - 1
    _, width, ff = expert_gate.shape
    dma = pltpu.SemaphoreType.DMA
    sums = Sums(layout, step_orders(layout)[:3], held, DONE_FIRST, DONE_EXPERTS, True)
    slots = jax.ShapeDtypeStruct(layout.slots(width), BF16)
    return pl.pallas_call(
        functools.partial(experts_kernel, layout, sums),
        out_shape=[
            slots,
            slots,
            slots,
            jax.ShapeDtypeStruct(shares.shape, F32),
            far_shape(layout, far_parts(layout)[0][1], width),
            *sums.outputs(),
        ],
        in_specs=[VMEM] * 3 + [ANY] * 5 + [VMEM] * 3,
        out_specs=[ANY] * 5 + [VMEM],
        scratch_shapes=[
            pltpu.VMEM((2, width, ff), BF16),
            pltpu.VMEM((2, width, ff), BF16),
            pltpu.VMEM((2, ff, width), BF16),
            pltpu.VMEM((experts // 2, CAP, width), BF16),
            pltpu.VMEM((experts // 2 * CAP, width), F32),
            pltpu.VMEM((experts // 2 * CAP, width), F32),
            pltpu.VMEM(layout.slots(width), BF16),
            pltpu.VMEM(layout.slots(width), BF16),
            dma((2, 3)),
            dma((2, share, experts)),
            dma((2, share, experts)),
            dma((2, share)),
            dma((2, share)),
            dma((4,)),
            dma((2, others)),
            dma((2, others)),
            *sums.scratch(),
        ],
        compiler_params=pltpu.CompilerParams(
            collective_id=1, has_side_effects=True, vmem_limit_bytes=60 * MIB
        ),
        cost_estimate=pl.CostEstimate(flops=1 << 30, bytes_accessed=1 << 20, transcendentals=0),
        name="experts",
    )(
        rows_in,
        cots,
        shares,
        expert_gate,
        expert_up,
        expert_down,
        rows_in,
        shares,
        *held,
    )


def rope_back(grad, cosine, sine):
    lane = lax.broadcasted_iota(jnp.int32, grad.shape, 1)
    turned = grad * sine
    other = jnp.where(
        lane % HEAD < HEAD // 2,
        pltpu.roll(turned, LANES - HEAD // 2, 1),
        pltpu.roll(turned, HEAD // 2, 1),
    )
    return grad * cosine + other


def by_blocks(target, made):
    parts, places = target.shape[:2]
    block, cut = made.shape[0] // places, made.shape[1] // parts
    for part in range(parts):
        for place in range(places):
            target[part, place] = pack(
                made[place * block : (place + 1) * block, part * cut : (part + 1) * cut]
            )


def combine_part(
    back,
    grad_back,
    target,
    ids_row,
    hidden,
    mixed_in,
    grad_in,
    low,
    cot,
    gain,
    w_router_t,
    w_out,
    att_t,
    mixed_out,
    grad_hidden_out,
    grad_att_out,
    proj_out,
    router_out,
    gain_out,
):
    rows, width = hidden.shape
    slots = back.shape[0] * back.shape[1] * CAP
    columns = jnp.transpose(
        jnp.concatenate(
            [target[...], ids_row[...].astype(F32), jnp.zeros((LANES - 10, rows), F32)], axis=0
        )
    )
    slot_no = lax.broadcasted_iota(jnp.int32, (rows, slots), 1).astype(F32)
    cot_float = cot[...].astype(F32)
    logits = mm(low[...], w_router_t[...], NT)
    route = jnp.exp(logits - jnp.max(logits, axis=1, keepdims=True))
    route = route / jnp.sum(route, axis=1, keepdims=True)
    labels = lax.broadcasted_iota(jnp.int32, (rows, EXPERTS), 1).astype(F32)
    masks = [labels == columns[:, 8 + k : 9 + k] for k in range(2)]
    picked = [jnp.sum(jnp.where(mask, route, 0.0), axis=1, keepdims=True) for mask in masks]
    both = picked[0] + picked[1]
    chosen, shares, grads = [], [], []
    mixed = mixed_in[...]
    for k in range(2):
        chosen.append(jnp.where(slot_no == columns[:, k : k + 1], 1.0, 0.0).astype(BF16))
        fetched = mm(chosen[k], back[...].reshape(slots, width))
        shares.append(picked[k] / both)
        mixed = mixed + shares[k] * fetched
        grads.append(jnp.sum(cot_float * fetched, axis=1, keepdims=True))
    mixed_out[...] = mixed.astype(BF16)
    mean = grads[0] * shares[0] + grads[1] * shares[1]
    grad_route = jnp.zeros_like(route)
    for k in range(2):
        grad_route = grad_route + jnp.where(masks[k], (grads[k] - mean) / both, 0.0)
    grad_logits = route * (grad_route - jnp.sum(route * grad_route, axis=1, keepdims=True))
    grad_logits = grad_logits.astype(BF16)
    router_out[...] = mm(grad_logits, low[...], TN)
    grad = grad_in[...] + mm(chosen[0] + chosen[1], grad_back[...].reshape(slots, width))
    grad = grad + mm(grad_logits, w_router_t[...])
    h = hidden[...]
    scale = lax.rsqrt(jnp.mean(h * h, axis=-1, keepdims=True) + epsilon)
    gain_out[...] = jnp.sum(grad * h * scale, axis=0, keepdims=True)
    grad = grad * gain[...].reshape(1, width)
    grad = scale * grad - h * (scale * scale * scale) * jnp.mean(grad * h, axis=-1, keepdims=True)
    grad = cot_float + grad
    grad_hidden_out[...] = grad
    grad_low = grad.astype(BF16)
    grad_att_out[...] = mm(grad_low, w_out[...], NT).astype(BF16)
    by_blocks(proj_out, mm(att_t[...], grad_low).astype(BF16))


def late_kernel(layout, sums, *refs):
    (
        back,
        grad_back,
        target,
        ids_row,
        hidden,
        mixed_in,
        grad_in,
        low,
        cot,
        gain_ffn,
        w_router_t,
        w_out,
        att_t,
        q_in,
        kv_in,
        bias,
        lse,
        tokens,
        gain,
        w_qkv,
        cosine,
        sine,
        gate_held,
        up_held,
        down_held,
        far_cot,
        far_target,
        rows_any,
        shares_any,
        mixed_out,
        tokens_out,
        proj_out,
        qkv_out,
        small_out,
        gate_sum,
        up_sum,
        far_cots_out,
        far_out,
        far_shares_out,
        grad_att,
        router_term,
        gain_term,
        send_cot,
        halo_send,
        halo_recv,
        own_kv,
        packed,
        send_sems,
        recv_sems,
        cot_send,
        cot_recv,
        own_sem,
        mixed_sem,
        far_send,
        far_recv,
        *rest,
    ) = refs
    rows, width = tokens.shape
    reach, experts = layout.reach, layout.experts
    e = lax.axis_index("expert")
    pairs = HEADS // 2
    lane = lax.broadcasted_iota(jnp.int32, (rows, LANES), 1)
    load = pltpu.make_async_copy(grad_in, tokens_out, mixed_sem)
    load.start()
    meet(layout)
    far_low, far_high = far_parts(layout)[1]
    far = to_far(layout, rows_any, far_out, far_low, far_high, far_send.at[0], far_recv.at[0])
    far += to_far(
        layout, shares_any, far_shares_out, 0, layout.share, far_send.at[1], far_recv.at[1]
    )
    for copy in far:
        copy.start()
    chains = sums.chains((gate_held, up_held, down_held), (gate_sum, up_sum), rest)
    for chain in chains:
        for halving in chain[:1]:
            halving.start()
    cot_sends = []
    for number in range(layout.outers - 1):
        for copy in cot_sends:
            copy.wait()
        fetch = pltpu.make_async_copy(far_cot.at[number], grad_att, own_sem.at[number])
        fetch.start()
        fetch.wait()
        gather_slots(layout, far_target[number], grad_att, send_cot)
        cot_sends = to_peers(
            layout, send_cot, far_cots_out.at[number], cot_send.at[number], cot_recv.at[number]
        )
        cot_sends.append(
            pltpu.make_async_copy(
                send_cot.at[0, 0], far_cots_out.at[number, 0, 0], own_sem.at[number]
            )
        )
        for copy in cot_sends:
            copy.start()

    load.wait()
    combine_part(
        back,
        grad_back,
        target,
        ids_row,
        hidden,
        mixed_in,
        tokens_out,
        low,
        cot,
        gain_ffn,
        w_router_t,
        w_out,
        att_t,
        packed.at[:, :width],
        tokens_out,
        grad_att,
        proj_out,
        router_term,
        gain_term,
    )
    mixed = pltpu.make_async_copy(packed.at[:, :width], mixed_out, mixed_sem)
    mixed.start()
    mixed.wait()

    def halo(distance, pair):
        return pltpu.make_async_remote_copy(
            src_ref=halo_send.at[distance - 1, pair],
            dst_ref=halo_recv.at[distance - 1, pair],
            send_sem=send_sems.at[distance - 1, pair],
            recv_sem=recv_sems.at[distance - 1, pair],
            device_id={"expert": lax.rem(e + experts - distance, experts)},
            device_id_type=MESH,
        )

    def heads(pair, carry):
        columns = pl.ds(pl.multiple_of(pair * LANES, LANES), LANES)
        value_columns = pl.ds(pl.multiple_of(width + pair * LANES, LANES), LANES)
        queries, grads = q_in[:, columns], grad_att[:, columns]
        grads_t = jnp.transpose(grads.astype(F32))
        shrunk = grads_t * att_t[columns, :].astype(F32)
        grad_q = [None, None]
        for distance in range(reach, -1, -1):
            keys = kv_in[distance, :, columns]
            values = kv_in[distance, :, value_columns]
            keys_t = jnp.transpose(keys)
            grad_k = grad_v = None
            for inner in range(2):
                head = pair * 2 + inner
                cut = slice(inner * HEAD, (inner + 1) * HEAD)
                mine = (lane // HEAD) == inner
                query = jnp.where(mine, queries, jnp.zeros_like(queries))
                grad = jnp.where(mine, grads, jnp.zeros_like(grads))
                total = jnp.sum(shrunk[cut], axis=0, keepdims=True)
                scores = mm(keys, query, NT) + bias[distance].astype(F32)
                probs = jnp.exp(scores - lse[pl.ds(head, 1), :])
                grad_probs = mm(values, grad, NT)
                grad_scores = (probs * (grad_probs - total)).astype(BF16)
                part_v = mm(probs.astype(BF16), grad)
                part_k = mm(grad_scores, query)
                part_q = mm(keys_t[cut], grad_scores)
                grad_v = part_v if grad_v is None else grad_v + part_v
                grad_k = part_k if grad_k is None else grad_k + part_k
                grad_q[inner] = part_q if grad_q[inner] is None else grad_q[inner] + part_q
            if distance:
                halo_send[distance - 1, pair, 0] = grad_k.astype(BF16)
                halo_send[distance - 1, pair, 1] = grad_v.astype(BF16)
                halo(distance, pair).start()
            else:
                own_kv[pair, 0] = grad_k.astype(BF16)
                own_kv[pair, 1] = grad_v.astype(BF16)
        grad = jnp.transpose(jnp.concatenate(grad_q, axis=0)) * HEAD ** (-0.5)
        packed[:, columns] = rope_back(grad, cosine[...], sine[...]).astype(BF16)
        return carry

    lax.fori_loop(0, pairs, heads, 0)
    x = tokens[...].astype(F32)
    grad_att[...] = normed(x, gain[...].reshape(1, width)).astype(BF16)
    normed_low = grad_att

    def merge(pair, carry):
        grad_k, grad_v = own_kv[pair, 0].astype(F32), own_kv[pair, 1].astype(F32)
        for distance in range(1, reach + 1):
            halo(distance, pair).wait()
            grad_k = grad_k + halo_recv[distance - 1, pair, 0].astype(F32)
            grad_v = grad_v + halo_recv[distance - 1, pair, 1].astype(F32)
        columns = pl.ds(pl.multiple_of(width + pair * LANES, LANES), LANES)
        packed[:, columns] = rope_back(grad_k, cosine[...], sine[...]).astype(BF16)
        columns = pl.ds(pl.multiple_of(2 * width + pair * LANES, LANES), LANES)
        packed[:, columns] = grad_v.astype(BF16)
        return carry

    lax.fori_loop(0, pairs, merge, 0)
    for chain in chains:
        for halving in chain:
            halving.add()
    thirds, parts, places = qkv_out.shape[:3]
    block, cut = width // places, width // parts
    for part in range(parts):
        columns = slice(part * thirds * cut, (part + 1) * thirds * cut)
        made = mm(normed_low[...], packed[:, columns], TN).astype(BF16)
        for third in range(thirds):
            for place in range(places):
                qkv_out[third, part, place] = pack(
                    made[place * block : (place + 1) * block, third * cut : (third + 1) * cut]
                )
    grad = mm(packed[...], w_qkv[...], NT)
    scale = lax.rsqrt(jnp.mean(x * x, axis=-1, keepdims=True) + epsilon)
    gain_back = jnp.sum(grad * x * scale, axis=0, keepdims=True)
    small_out[...] = jnp.concatenate(
        [router_term[...], gain_term[...], gain_back, jnp.zeros((6, width), F32)], axis=0
    )
    grad = grad * gain[...].reshape(1, width)
    grad = scale * grad - x * (scale * scale * scale) * jnp.mean(grad * x, axis=-1, keepdims=True)
    tokens_out[...] += grad
    for copy in far + cot_sends:
        copy.wait()


def late(layout, combine_ins, back_ins, held, far_cot, far_target, rows_in, shares):
    tokens = back_ins[4]
    rows, width = tokens.shape
    reach, peers, others = layout.reach, layout.peers, layout.outers - 1
    dma = pltpu.SemaphoreType.DMA
    pairs = HEADS // 2
    sums = Sums(layout, step_orders(layout)[:3], held, DONE_EXPERTS, DONE_LATE, True)
    blocks = (layout.experts, layout.groups)
    blocks += packed_shape(width // layout.groups, width // layout.experts)
    far_low, far_high = far_parts(layout)[1]
    return pl.pallas_call(
        functools.partial(late_kernel, layout, sums),
        out_shape=[
            jax.ShapeDtypeStruct((rows, width), BF16),
            jax.ShapeDtypeStruct((rows, width), F32),
            jax.ShapeDtypeStruct(blocks, BF16),
            jax.ShapeDtypeStruct((3,) + blocks, BF16),
            jax.ShapeDtypeStruct((SMALL, width), F32),
            *sums.outputs(),
            jax.ShapeDtypeStruct((others,) + layout.slots(width), BF16),
            far_shape(layout, far_high - far_low, width),
            jax.ShapeDtypeStruct((others,) + shares.shape, F32),
        ],
        in_specs=[VMEM] * 6 + [ANY] + [VMEM] * 18 + [ANY, VMEM, ANY, ANY],
        out_specs=[ANY] + [VMEM] * 6 + [ANY] * 3,
        scratch_shapes=[
            pltpu.VMEM((rows, width), BF16),
            pltpu.VMEM((EXPERTS, width), F32),
            pltpu.VMEM((1, width), F32),
            pltpu.VMEM(layout.slots(width), BF16),
            pltpu.VMEM((reach, pairs, 2, rows, LANES), BF16),
            pltpu.VMEM((reach, pairs, 2, rows, LANES), BF16),
            pltpu.VMEM((pairs, 2, rows, LANES), BF16),
            pltpu.VMEM((rows, 3 * width), BF16),
            dma((reach, pairs)),
            dma((reach, pairs)),
            dma((others, peers)),
            dma((others, peers)),
            dma((others,)),
            dma,
            dma((2, others)),
            dma((2, others)),
            *sums.scratch(),
        ],
        compiler_params=pltpu.CompilerParams(
            collective_id=2, has_side_effects=True, vmem_limit_bytes=63 * MIB
        ),
        cost_estimate=pl.CostEstimate(flops=1 << 30, bytes_accessed=1 << 20, transcendentals=0),
        name="late",
    )(*combine_ins, *back_ins, *held, far_cot, far_target, rows_in, shares)


def weights_kernel(layout, sums, *refs):
    share, outers, peers = layout.share, layout.outers, layout.peers
    (
        rows_own,
        cots_own,
        shares_own,
        rows_a,
        rows_b,
        cots_far,
        shares_far,
        gate_any,
        up_any,
        down_any,
        *terms,
        qkv_terms,
        small_in,
        gate_out,
        up_out,
        down_out,
        gate_sum,
        up_sum,
        down_sum,
        proj_sum,
        qkv_sum,
        router_out,
        gain_ffn_out,
        gain_attn_out,
    ) = refs[:27]
    (
        gate_w,
        up_w,
        gate_t,
        up_t,
        down_w,
        rows_buf,
        cots_buf,
        shares_buf,
        accs,
        sends,
        down_sends,
        small_sums,
        small_takes,
        load_sems,
        piece_sems,
        send_sems,
        recv_sems,
        small_send,
        small_recv,
    ) = refs[27:46]
    rest = refs[46:]
    width = gate_w.shape[0]
    ff = gate_any.shape[2]
    span = ff // outers
    cut = ff // layout.groups
    group = lax.axis_index("group")
    mine = own_share(layout)
    begin = pl.multiple_of((group // share) * span, span)
    loads = [
        pltpu.make_async_copy(gate_any.at[mine, :, pl.ds(begin, span)], gate_w, load_sems.at[0]),
        pltpu.make_async_copy(up_any.at[mine, :, pl.ds(begin, span)], up_w, load_sems.at[1]),
        pltpu.make_async_copy(down_any.at[mine, pl.ds(begin, span), :], down_w, load_sems.at[2]),
    ]

    def fetch(outer):
        slot = outer % 2
        if outer == 0:
            sources = [
                (rows_own, rows_buf.at[slot]),
                (cots_own, cots_buf.at[slot]),
                (shares_own, shares_buf.at[slot]),
            ]
        else:
            sources = [
                (one.at[outer - 1], rows_buf.at[slot, low:high])
                for one, (low, high) in zip((rows_a, rows_b), far_parts(layout))
            ]
            sources.append((cots_far.at[outer - 1], cots_buf.at[slot]))
            sources.append((shares_far.at[outer - 1], shares_buf.at[slot]))
        return [
            pltpu.make_async_copy(source, target, piece_sems.at[slot, number])
            for number, (source, target) in enumerate(sources)
        ]

    for copy in loads + fetch(0):
        copy.start()
    meet(layout)

    third = qkv_sum.shape[1] // 3
    chains = sums.chains([*terms, *[qkv_terms.at[n] for n in range(3)]], (), rest)
    results = [(one, 0, one.shape[1]) for one in (gate_sum, up_sum, down_sum, proj_sum)]
    results += [(qkv_sum, n * third, third) for n in range(3)]
    steps = [("expert", 1 << n) for n in range(layout.experts.bit_length() - 1)]
    steps += [("group", 1 << n) for n in range(layout.groups.bit_length() - 1)]
    levels = len(steps)
    small_sums[0] = small_in[...]

    def small_copy(level):
        axis, bit = steps[level]
        return pltpu.make_async_remote_copy(
            src_ref=small_sums.at[level],
            dst_ref=small_takes.at[level],
            send_sem=small_send.at[level],
            recv_sem=small_recv.at[level],
            device_id={axis: flipped(lax.axis_index(axis), bit)},
            device_id_type=MESH,
        )

    reached = [0] * len(chains)

    def advance(*numbers):
        for number in numbers:
            chain, level = chains[number], reached[number]
            if 0 < level <= len(chain):
                chain[level - 1].add(results[number] if level == len(chain) else None)
            if level < len(chain):
                chain[level].start()
            reached[number] += 1

    def advance_small(level):
        if level:
            small_copy(level - 1).wait()
            made = small_sums[level - 1] + small_takes[level - 1]
            if level < levels:
                small_sums[level] = made
            else:
                router_out[...] = made[:EXPERTS]
                gain_ffn_out[...] = made[EXPERTS : EXPERTS + 1].reshape(width)
                gain_attn_out[...] = made[EXPERTS + 1 : EXPERTS + 2].reshape(width)
        if level < levels:
            small_copy(level).start()

    attention, shared = (3, 4, 5, 6), (1, 2, 0)
    points = share * outers
    marks = {
        0: [attention],
        3 * points // 8: [attention],
        5 * points // 8: [shared],
        6 * points // 8: [attention],
        points - 1: [shared, attention],
    }
    small_level = 1
    advance(*attention, *shared)
    advance_small(0)

    for copy in loads:
        copy.wait()
    gate_t[...] = jnp.transpose(gate_w[...])
    up_t[...] = jnp.transpose(up_w[...])
    experts = layout.experts
    count = max(16 // experts, 1)
    blocks = share // count

    def add(slot, chunk, block):
        parts = pl.ds(block * count, count)
        n = rows_buf[slot, parts].reshape(count * experts * CAP, width)
        grad = cots_buf[slot, parts].reshape(count * experts * CAP, width)
        base = pl.multiple_of(chunk * cut, cut)
        gate_pre = mm(gate_t[pl.ds(base, cut), :], n, NT)
        up_pre = mm(up_t[pl.ds(base, cut), :], n, NT)
        grad_act = mm(down_w[pl.ds(base, cut), :], grad, NT)
        silu, slope = silu_parts(gate_pre)
        act = (silu * up_pre).astype(BF16)
        grad_gate = (grad_act * up_pre * slope).astype(BF16)
        grad_up = (grad_act * silu).astype(BF16)
        accs[0] += mm(grad_gate, n)
        accs[1] += mm(grad_up, n)
        accs[2] += mm(act, grad)

    copies = []
    turns = [*range(share - 1, 0, -1), 0]
    resident = outers <= 2
    for place, turn in enumerate(turns):
        owner = flipped(mine, turn)
        accs[...] = jnp.zeros_like(accs)
        for outer in range(outers):
            slot = outer % 2
            if place == 0 or not resident:
                if place or outer:
                    for copy in fetch(outer):
                        copy.start()
                for copy in fetch(outer):
                    copy.wait()

                def scale(number, carry, slot=slot):
                    at = slot, number // experts, number % experts
                    column = share_column(shares_buf[at + (slice(0, 1), slice(0, CAP))])
                    cots_buf[at] = (cots_buf[at].astype(F32) * column).astype(BF16)
                    return carry

                lax.fori_loop(0, peers, scale, 0)

            def step(number, carry, slot=slot, owner=owner):
                add(slot, owner, number)
                return carry

            lax.fori_loop(0, blocks, step, 0)
            if place * outers + outer in marks:
                for numbers in marks[place * outers + outer]:
                    advance(*numbers)
                if small_level <= levels:
                    advance_small(small_level)
                    small_level += 1
        for which, target in enumerate((gate_out, up_out, down_out)):
            made = accs[which]
            if which < 2:
                made = jnp.transpose(made)
                source = sends.at[turn, which]
            else:
                source = down_sends.at[turn]
            source[...] = made.astype(BF16)
            if turn:
                device = {"group": flipped(group, turn)}
                sems = send_sems.at[turn, which], recv_sems.at[turn, which]
                copies.append(remote(source, target.at[mine], *sems, device))
            else:
                copies.append(
                    pltpu.make_async_copy(source, target.at[mine], send_sems.at[turn, which])
                )
            copies[-1].start()
    while any(at <= len(chain) for at, chain in zip(reached, chains)) or small_level <= levels:
        advance(*attention)
        if small_level <= levels:
            advance_small(small_level)
            small_level += 1
        advance(*shared)
    for copy in copies:
        copy.wait()


def weights(layout, own, rows_far, cots_far, shares_far, expert_weights, held, terms, small):
    share, outers = layout.share, layout.outers
    experts, width, ff = expert_weights[0].shape
    span = ff // outers
    cut = ff // layout.groups
    dma = pltpu.SemaphoreType.DMA
    levels = layout.experts.bit_length() + layout.groups.bit_length() - 2
    proj_terms, qkv_terms = terms
    thirds = [jax.ShapeDtypeStruct(qkv_terms.shape[1:], BF16)] * 3
    sums = Sums(
        layout,
        step_orders(layout),
        (*held, proj_terms, *thirds),
        DONE_LATE + DONE_NONE,
        (levels,) * 7,
        False,
    )
    wide = width // layout.groups, ff // layout.experts
    tall = cut, width // layout.experts
    narrow = width // layout.groups, width // layout.experts
    results = wide, wide, tall, narrow, (narrow[0], 3 * narrow[1])
    return pl.pallas_call(
        functools.partial(weights_kernel, layout, sums),
        out_shape=[
            jax.ShapeDtypeStruct((experts, width, cut), BF16),
            jax.ShapeDtypeStruct((experts, width, cut), BF16),
            jax.ShapeDtypeStruct((experts, cut, width), BF16),
            *[jax.ShapeDtypeStruct(shape, F32) for shape in results],
            jax.ShapeDtypeStruct((EXPERTS, width), F32),
            jax.ShapeDtypeStruct((width,), F32),
            jax.ShapeDtypeStruct((width,), F32),
        ],
        in_specs=[ANY] * 10 + [VMEM] * 6,
        out_specs=[ANY] * 3 + [VMEM] * 8,
        scratch_shapes=[
            pltpu.VMEM((width, span), BF16),
            pltpu.VMEM((width, span), BF16),
            pltpu.VMEM((span, width), BF16),
            pltpu.VMEM((span, width), BF16),
            pltpu.VMEM((span, width), BF16),
            pltpu.VMEM((2,) + layout.slots(width), BF16),
            pltpu.VMEM((2,) + layout.slots(width), BF16),
            pltpu.VMEM((2, share, layout.experts, 8, LANES), F32),
            pltpu.VMEM((3, cut, width), F32),
            pltpu.VMEM((share, 2, width, cut), BF16),
            pltpu.VMEM((share, cut, width), BF16),
            pltpu.VMEM((levels, SMALL, width), F32),
            pltpu.VMEM((levels, SMALL, width), F32),
            dma((3,)),
            dma((2, 5)),
            dma((share, 3)),
            dma((share, 3)),
            dma((levels,)),
            dma((levels,)),
            *sums.scratch(),
        ],
        compiler_params=pltpu.CompilerParams(
            collective_id=3, has_side_effects=True, vmem_limit_bytes=60 * MIB
        ),
        cost_estimate=pl.CostEstimate(flops=1 << 30, bytes_accessed=1 << 20, transcendentals=0),
        name="weights",
    )(*own, *rows_far, cots_far, shares_far, *expert_weights, *held, *terms, small)


def local(
    tokens,
    gain_attn,
    w_qkv,
    w_out,
    gain_ffn,
    w_router,
    expert_gate,
    expert_up,
    expert_down,
    dense_gate,
    dense_up,
    dense_down,
    expert_ids,
    segments,
    cotangent,
):
    rows, width = tokens.shape
    layout = Layout(lax.axis_size("group"), lax.axis_size("expert"), rows)
    expert = lax.axis_index("expert")
    ids_row, w_router_t = jnp.transpose(expert_ids), jnp.transpose(w_router)
    places = (expert * rows + jnp.arange(rows, dtype=jnp.int32)).astype(F32)
    lane = jnp.arange(LANES)
    power = (lane % (HEAD // 2)).astype(F32) / (HEAD // 2)
    angles = places[:, None] * (10000.0 ** (-power))[None]
    cosine = jnp.cos(angles)
    sine = jnp.sin(angles) * jnp.where(lane % HEAD < HEAD // 2, -1.0, 1.0)[None]

    (
        q,
        kv,
        att_t,
        lse,
        bias,
        target,
        hidden,
        low,
        mixed,
        grad_low,
        gate_terms,
        up_terms,
        down_terms,
        cots,
        quad_cots,
        rows_in,
        shares,
        far_cot,
        far_target,
    ) = first(
        layout,
        tokens,
        gain_attn,
        w_qkv,
        cosine,
        sine,
        ids_row,
        segments,
        cotangent,
        w_out,
        gain_ffn,
        w_router_t,
        dense_gate,
        dense_up,
        dense_down,
    )
    came_back, grad_back, quad_rows, quad_shares, rows_a, gate_terms = run_experts(
        layout,
        rows_in,
        cots,
        shares,
        expert_gate,
        expert_up,
        expert_down,
        (gate_terms, up_terms, down_terms),
    )
    mixed_out, grad_tokens, proj_terms, qkv_terms, small, gate_terms, up_terms, cots_far, rows_b, shares_far = late(
        layout,
        (
            came_back,
            grad_back,
            target,
            ids_row,
            hidden,
            mixed,
            grad_low,
            low,
            cotangent,
            gain_ffn,
            w_router_t,
            w_out,
            att_t,
        ),
        (q, kv, bias, lse, tokens, gain_attn, w_qkv, cosine, sine),
        (gate_terms, up_terms, down_terms),
        far_cot,
        far_target,
        quad_rows,
        quad_shares,
    )
    gate_w, up_w, down_w, gate_sum, up_sum, down_sum, proj_sum, qkv_sum, *small = weights(
        layout,
        (quad_rows, quad_cots, quad_shares),
        (rows_a, rows_b),
        cots_far,
        shares_far,
        (expert_gate, expert_up, expert_down),
        (gate_terms, up_terms, down_terms),
        (proj_terms, qkv_terms),
        small,
    )
    return (
        mixed_out,
        grad_tokens,
        small[2],
        qkv_sum,
        proj_sum,
        small[1],
        jnp.transpose(small[0]),
        gate_w.astype(F32),
        up_w.astype(F32),
        down_w.astype(F32),
        gate_sum,
        up_sum,
        down_sum,
    )


def solution(mesh):
    in_specs = (
        P(("group", "expert"), None),
        P(),
        P(),
        P(),
        P(),
        P(),
        P("expert", None, None),
        P("expert", None, None),
        P("expert", None, None),
        P(),
        P(),
        P(),
        P(("group", "expert"), None),
        P(("group", "expert")),
        P(("group", "expert"), None),
    )
    out_specs = (
        P(("group", "expert"), None),
        P(("group", "expert"), None),
        P(),
        P("group", "expert"),
        P("group", "expert"),
        P(),
        P(),
        P("expert", None, "group"),
        P("expert", None, "group"),
        P("expert", "group", None),
        P("group", "expert"),
        P("group", "expert"),
        P("group", "expert"),
    )
    return jax.shard_map(local, mesh=mesh, in_specs=in_specs, out_specs=out_specs, check_vma=False)
```
